512 devices in a mesh: tile: 32 (over y, x, core), feat: 16 (over z).
Axes of the slice: x: 4, y: 4, z: 16, core: 2. Of those that a mesh axis runs over, the one named last changes fastest.
Arguments:
- gen_points: bfloat16 [6144, 1024], P('tile', 'feat')
- reference_embeddings: bfloat16 [6144, 1024], P('tile', 'feat')
- gen_count: int32 [32], replicated, may hold values from 1 to 192, 4608 in all
- ref_count: int32 [32], replicated, may hold values from 1 to 192, 4608 in all
Outputs:
- gen_pot: float32 [6144], P('tile')
- ref_pot: float32 [6144], P('tile')
- gen_self: float32 [6144], P('tile')
- ref_self: float32 [6144], P('tile')
- divergence: float32 [], replicated
The draws below stay inside these ranges and needn't reach their ends.
Inputs may be any that keep to these rules, and one draw needn't show every extreme that they name: The valid generated points of a block are its first gen_count entries; the counts sum to 4608 and some block is full. The valid reference points of a block are its first ref_count entries; the counts sum to 4608 and some block is full.
All inputs are finite; a program needn't handle non-finite values.
Results may differ from the reference program's by a relative error of at most 0.0003.
Values may be sent and summed in bfloat16 or wider, within the bound.
No kernel may reach another device: no remote copies, remote signals or barrier semaphores. Data moves between devices by JAX's collectives and lax.ppermute only.
A program may use at most 64 MiB of HBM per device.

```python
import math
import jax
import jax.numpy as jnp
import numpy as np
from jax import lax

D = 1024
POINTS_PER_BLOCK = 192
ITERS = 3
NBLK = 32
NPTS = 6144


def shared_centres(key):
    number = max(NPTS // 48, 4)
    centres = jax.random.normal(key, (number, D), jnp.float32) * math.sqrt(1.5 / D)
    return (centres, number)


def cloud(key, centres, number, noise_field):
    labels = jax.random.randint(jax.random.fold_in(key, 11), (NPTS,), 0, number)
    offsets = jax.random.normal(jax.random.fold_in(key, 12), (number, D), jnp.float32) * math.sqrt(0.25 / D)
    return (centres + offsets)[labels] + noise_field / math.sqrt(D)


def draw_gen_points(key, part):
    centres, number = shared_centres(key)
    key = jax.random.fold_in(key, 3)
    noise_field = jax.random.normal(jax.random.fold_in(key, 1), (NPTS, D), jnp.float32)
    return cloud(key, centres, number, noise_field).astype(jnp.bfloat16)


def draw_reference_embeddings(key, part):
    centres, number = shared_centres(key)
    key = jax.random.fold_in(key, 5)
    noise_field = jax.random.normal(jax.random.fold_in(key, 1), (NPTS, D), jnp.float32)
    return cloud(key, centres, number, noise_field).astype(jnp.bfloat16)


def split_up(count, total, reach, skew):
    portions = [(1 << 20) // math.isqrt(grade ** skew) + 1 for grade in range(2, count + 1)]
    surplus, given = total - reach - (count - 1), [1] * (count - 1)
    while surplus > 0:
        movable = [i for i in range(count - 1) if given[i] < reach]
        whole, remaining = sum([portions[i] for i in movable]), surplus
        for i in movable:
            more = min(reach - given[i], max(1, remaining * portions[i] // whole), surplus)
            given[i] = given[i] + more
            surplus = surplus - more
    return np.array([reach] + given)


def uneven_parts(key, count, total, limit, skew):
    if count == 2:
        one = jax.random.randint(key, (), max(1, total - limit), min(limit, total - 1) + 1)
        return jnp.stack([one, total - one])
    tallies = jnp.asarray(split_up(count, total, limit, skew), jnp.int32)
    pairs = (count - 1) // 2
    source_of, receiver = tallies[1:1 + 2 * pairs:2], tallies[2:2 + 2 * pairs:2]
    slack = jnp.minimum(source_of - 1, limit - receiver)
    shifted = jax.random.randint(jax.random.fold_in(key, 1), (pairs,), 0, 1 << 20) % (slack + 1)
    tallies = tallies.at[1:1 + 2 * pairs:2].set(source_of - shifted).at[2:2 + 2 * pairs:2].set(receiver + shifted)
    return tallies[jax.random.permutation(jax.random.fold_in(key, 2), count)]


def setup_inputs(seed: int = 0) -> dict:
    key_of = jax.random.split(jax.random.key(seed), 5)
    return {
        "gen_points": draw_gen_points(jax.random.fold_in(key_of[4], 71), 0),
        "reference_embeddings": draw_reference_embeddings(jax.random.fold_in(key_of[4], 71), 0),
        "gen_count": uneven_parts(key_of[2], NBLK, NPTS * 3 // 4, POINTS_PER_BLOCK, 2).astype(jnp.int32),
        "ref_count": uneven_parts(key_of[3], NBLK, NPTS * 3 // 4, POINTS_PER_BLOCK, 2).astype(jnp.int32),
    }


epsilon = 0.25
far_below = -1.0e30


def cost_over_epsilon(row_points, row_norms, col_points, col_norms):
    inner_prod = jnp.dot(row_points, col_points.T, preferred_element_type=jnp.float32)
    return (0.5 * row_norms[:, None] + 0.5 * col_norms[None, :] - inner_prod) / epsilon


def row_portion(scores):
    highest = jnp.max(scores, axis=1)
    return highest, jnp.sum(jnp.exp(scores - highest[:, None]), axis=1)


def column_part(scores):
    highest = jnp.max(scores, axis=0)
    return highest, jnp.sum(jnp.exp(scores - highest[None, :]), axis=0)


def joined(first_high, first_mass, second_high, second_mass):
    highest = jnp.maximum(first_high, second_high)
    return highest, first_mass * jnp.exp(first_high - highest) + second_mass * jnp.exp(second_high - highest)


def settle(highest, amount):
    return -(highest + jnp.log(amount))


def valid_points(counts):
    position = jnp.arange(NPTS, dtype=jnp.int32)
    return (position % POINTS_PER_BLOCK) < counts[position // POINTS_PER_BLOCK]


def sweep(gen_points, reference_embeddings, gen_sq, reference_squared_norm, gen_ok, ref_ok, gen_weight, ref_weight, gen_pot, ref_pot, gen_self, ref_self):
    ref_lift = jnp.where(ref_ok, ref_pot + ref_weight, far_below)
    gen_lift = jnp.where(gen_ok, gen_pot + gen_weight, far_below)
    gself_lift = jnp.where(gen_ok, gen_self + gen_weight, far_below)
    reference_self_shift = jnp.where(ref_ok, ref_self + ref_weight, far_below)
    blocks = NPTS // POINTS_PER_BLOCK

    def block_step(running, block_index):
        leading_row = (block_index * POINTS_PER_BLOCK).astype(jnp.int32)
        gen_block = lax.dynamic_slice_in_dim(gen_points, leading_row, POINTS_PER_BLOCK, 0)
        reference_block = lax.dynamic_slice_in_dim(reference_embeddings, leading_row, POINTS_PER_BLOCK, 0)
        gsq_block = lax.dynamic_slice_in_dim(gen_sq, leading_row, POINTS_PER_BLOCK, 0)
        reference_squared_block = lax.dynamic_slice_in_dim(reference_squared_norm, leading_row, POINTS_PER_BLOCK, 0)
        glift_block = lax.dynamic_slice_in_dim(gen_lift, leading_row, POINTS_PER_BLOCK, 0)
        cross_cost = cost_over_epsilon(gen_block, gsq_block, reference_embeddings, reference_squared_norm)
        gen_high, gen_mass = row_portion(ref_lift[None, :] - cross_cost)
        col_high, col_mass = column_part(glift_block[:, None] - cross_cost)
        running = joined(running[0], running[1], col_high, col_mass)
        gself_high, gself_mass = row_portion(gself_lift[None, :] - cost_over_epsilon(gen_block, gsq_block, gen_points, gen_sq))
        reference_self_peak, reference_self_logsum = row_portion(reference_self_shift[None, :] - cost_over_epsilon(reference_block, reference_squared_block, reference_embeddings, reference_squared_norm))
        return running, (settle(gen_high, gen_mass), settle(gself_high, gself_mass), settle(reference_self_peak, reference_self_logsum))

    starting = (jnp.full((NPTS,), far_below, jnp.float32), jnp.zeros((NPTS,), jnp.float32))
    running, updated = lax.scan(block_step, starting, jnp.arange(blocks, dtype=jnp.int32))
    return (updated[0].reshape(NPTS), settle(running[0], running[1]), updated[1].reshape(NPTS), updated[2].reshape(NPTS))


def reference(gen_points, reference_embeddings, gen_count, ref_count):
    gen_sq = jnp.sum(jnp.square(gen_points.astype(jnp.float32)), axis=1)
    reference_squared_norm = jnp.sum(jnp.square(reference_embeddings.astype(jnp.float32)), axis=1)
    gen_ok = valid_points(gen_count)
    ref_ok = valid_points(ref_count)
    gen_total = jnp.sum(gen_count).astype(jnp.float32)
    ref_total = jnp.sum(ref_count).astype(jnp.float32)
    gen_weight = -jnp.log(gen_total)
    ref_weight = -jnp.log(ref_total)
    zero_pot = jnp.zeros((NPTS,), jnp.float32)
    current = sweep(gen_points, reference_embeddings, gen_sq, reference_squared_norm, gen_ok, ref_ok, gen_weight, ref_weight, zero_pot, zero_pot, zero_pot, zero_pot)
    for repeat_index in range(ITERS):
        updated = sweep(gen_points, reference_embeddings, gen_sq, reference_squared_norm, gen_ok, ref_ok, gen_weight, ref_weight, current[0], current[1], current[2], current[3])
        current = tuple(0.5 * (before + renewed) for before, renewed in zip(current, updated))
    gen_pot, ref_pot, gen_self, ref_self = current
    divergence = jnp.sum(jnp.where(gen_ok, gen_pot - gen_self, 0.0)) / gen_total + jnp.sum(jnp.where(ref_ok, ref_pot - ref_self, 0.0)) / ref_total
    return gen_pot, ref_pot, gen_self, ref_self, divergence
```

```python
import functools

import jax
import jax.numpy as jnp
from jax import lax
from jax.experimental import pallas as pl
from jax.experimental.pallas import tpu as pltpu
from jax.sharding import Mesh, PartitionSpec as P

EPSILON = 0.25
LOG2E = 1.4426950408889634
LN2 = 0.6931471805599453
FAR = -1.0e30

BLOCK = 192
D = 1024
NI = 8 * BLOCK
NJ = 4 * BLOCK
RI = NI // 128
RJ = NJ // 128

VMEM = pl.BlockSpec(memory_space=pltpu.VMEM)
SMEM = pl.BlockSpec(memory_space=pltpu.SMEM)
PARAMS = pltpu.CompilerParams(vmem_limit_bytes=40 * 1024 * 1024)


def f32(*shape):
    return jax.ShapeDtypeStruct(shape, jnp.float32)


def call(body, outs, ins, scratch=(), cost=None):
    return pl.pallas_call(
        body,
        out_shape=outs,
        in_specs=ins,
        out_specs=jax.tree.map(lambda _: VMEM, outs),
        scratch_shapes=list(scratch),
        compiler_params=PARAMS,
        cost_estimate=cost,
    )


def merge(parts):
    high = functools.reduce(jnp.maximum, parts)
    mass = functools.reduce(jnp.add, [jnp.exp2(part - high) for part in parts])
    return high + jnp.log(mass) * LOG2E


def lifted(pot, lift):
    return jnp.where(lift > -1.0e29, pot + lift, FAR)


def reduce_lanes(k_ref, heads, high_ref, mass_ref):
    count = len(heads)

    def step(group, carry):
        rows = pl.ds(pl.multiple_of(group * 16, 16), 16)
        tiles = [k_ref[rows, r * 128 : (r + 1) * 128] for r in range(RI)]
        for v in range(count):
            xs = [heads[v][r : r + 1, :] - tiles[r] for r in range(RI)]
            high = functools.reduce(jnp.maximum, xs)
            mass = functools.reduce(jnp.add, [jnp.exp2(x - high) for x in xs])
            high_ref[v, rows, :] = high
            mass_ref[v, rows, :] = mass
        return carry

    lax.fori_loop(0, NJ // 16, step, 0)
    results = []
    for v in range(count):
        rows_out = []
        for b in range(RJ):
            part = slice(b * 128, (b + 1) * 128)
            high = jnp.transpose(high_ref[v, part, :])
            mass = jnp.transpose(mass_ref[v, part, :])
            top = jnp.max(high, axis=0, keepdims=True)
            total = jnp.sum(mass * jnp.exp2(high - top), axis=0, keepdims=True)
            rows_out.append(top + jnp.log(total) * LOG2E)
        results.append(jnp.concatenate(rows_out, axis=0))
    return results


def reduce_rows(k_ref, heads, wide_ref):
    count = len(heads)
    for v in range(count):
        for b in range(RJ):
            row = jnp.broadcast_to(heads[v][b : b + 1, :], (128, 128))
            wide_ref[v, b * 128 : (b + 1) * 128, :] = jnp.transpose(row)
    rows_out = [[] for _ in range(count)]
    span = 4
    chunk = 32
    for t in range(RI // span):
        cols = [slice((t * span + q) * 128, (t * span + q + 1) * 128) for q in range(span)]

        def highest(group, tops):
            base = pl.multiple_of(group * chunk, chunk)
            tops = list(tops)
            for s in range(chunk // 8):
                rows = pl.ds(base + s * 8, 8)
                wides = [wide_ref[v, rows, :] for v in range(count)]
                for q in range(span):
                    tile = k_ref[rows, cols[q]]
                    for v in range(count):
                        tops[v * span + q] = jnp.maximum(tops[v * span + q], wides[v] - tile)
            return tuple(tops)

        tops = lax.fori_loop(
            0, NJ // chunk, highest, tuple(jnp.full((8, 128), -3.0e38, jnp.float32) for _ in range(count * span))
        )

        def summed(group, sums):
            base = pl.multiple_of(group * chunk, chunk)
            sums = list(sums)
            for s in range(chunk // 8):
                rows = pl.ds(base + s * 8, 8)
                wides = [wide_ref[v, rows, :] for v in range(count)]
                for q in range(span):
                    tile = k_ref[rows, cols[q]]
                    for v in range(count):
                        n = v * span + q
                        sums[n] = sums[n] + jnp.exp2((wides[v] - tile) - tops[n])
            return tuple(sums)

        sums = lax.fori_loop(
            0, NJ // chunk, summed, tuple(jnp.zeros((8, 128), jnp.float32) for _ in range(count * span))
        )
        for v in range(count):
            for q in range(span):
                high, mass = tops[v * span + q], sums[v * span + q]
                top = jnp.max(high, axis=0, keepdims=True)
                total = jnp.sum(mass * jnp.exp2(high - top), axis=0, keepdims=True)
                rows_out[v].append(top + jnp.log(total) * LOG2E)
    return [jnp.concatenate(rows, axis=0) for rows in rows_out]


def unpack_body(info, raw, a_out, b_out):
    a_is_gen = info[0] == 1
    b_is_gen = info[1] == 1
    for k in range(D // 128):
        even = raw[2 * k]
        odd = raw[2 * k + 1]
        gen = jnp.concatenate([even[:, :64], odd[:, :64]], axis=1)
        ref = jnp.concatenate([even[:, 64:], odd[:, 64:]], axis=1)
        cols = slice(k * 128, (k + 1) * 128)
        a = jnp.where(a_is_gen, gen, ref)
        for n in range(4):
            a_out[n, :, cols] = a
        b_out[:, cols] = jnp.where(b_is_gen, gen, ref)


def norm_parts(values):
    values = values.astype(jnp.float32)
    values = values * values
    return functools.reduce(jnp.add, [values[:, k * 128 : (k + 1) * 128] for k in range(D // 128)])


def cost_body(info, own, other, cols, lift_i, k_ref, part_out, sq_ref, high_ref, mass_ref):
    scale = LOG2E / EPSILON
    for b in range(RJ):
        part = slice(b * 128, (b + 1) * 128)
        total = jnp.sum(norm_parts(cols[part, :]), axis=1, keepdims=True)
        sq_ref[part, :] = jnp.broadcast_to(total * (0.5 * scale), (128, 128))
    for which, source in enumerate((own, other)):
        half = jnp.where(info[2] == which, 0, 1)
        for t in range(3):
            rows = source[t * 256 : (t + 1) * 256, :]
            norms = []
            for s in range(2):
                turned = jnp.transpose(norm_parts(rows[s * 128 : (s + 1) * 128, :]))
                norms.append(jnp.sum(turned, axis=0, keepdims=True) * (0.5 * scale))
            for b in range(3):
                part = slice(b * 256, (b + 1) * 256)
                inner = lax.dot_general(
                    cols[part, :], rows, (((1,), (1,)), ((), ())), preferred_element_type=jnp.float32
                )
                for s in range(2):
                    place = pl.ds(pl.multiple_of(half * (NI // 2) + t * 256 + s * 128, 128), 128)
                    k_ref[part, place] = (norms[s] + sq_ref[part, :]) - scale * inner[:, s * 128 : (s + 1) * 128]
    (result,) = reduce_lanes(k_ref, [lift_i[...]], high_ref, mass_ref)
    for n in range(4):
        part_out[n, 0:RJ, :] = result
        part_out[n, RJ:8, :] = jnp.zeros((8 - RJ, 128), jnp.float32)


def second_body(k_ref, got, lift_j, out, g1_out, wide_ref):
    g1 = -merge([got[n, 0:RJ, :] for n in range(4)])
    g1_out[...] = g1
    lift = lift_j[...]
    results = reduce_rows(k_ref, [lift, lifted(g1, lift)], wide_ref)
    for n in range(8):
        for v in range(2):
            out[n, v * RI : (v + 1) * RI, :] = results[v]


def third_body(k_ref, got, lift_i, out, f2_out, high_ref, mass_ref):
    f1 = -merge([got[n, 0:RI, :] for n in range(8)])
    f2 = 0.5 * (f1 - merge([got[n, RI : 2 * RI, :] for n in range(8)]))
    f2_out[...] = f2
    lift = lift_i[...]
    results = reduce_lanes(k_ref, [lifted(f1, lift), lifted(f2, lift)], high_ref, mass_ref)
    for n in range(4):
        for v in range(2):
            out[n, v * 8 : v * 8 + RJ, :] = results[v]
            out[n, v * 8 + RJ : v * 8 + 8, :] = jnp.zeros((8 - RJ, 128), jnp.float32)


def fourth_body(k_ref, got, lift_j, g1, out, g3_out, wide_ref):
    g2 = 0.5 * (g1[...] - merge([got[n, 0:RJ, :] for n in range(4)]))
    g3 = 0.5 * (g2 - merge([got[n, 8 : 8 + RJ, :] for n in range(4)]))
    g3_out[...] = g3
    lift = lift_j[...]
    results = reduce_rows(k_ref, [lifted(g2, lift), lifted(g3, lift)], wide_ref)
    for n in range(8):
        for v in range(2):
            out[n, v * RI : (v + 1) * RI, :] = results[v]


def fifth_body(info, k_ref, got, lift_i, f2, g3, out, f4_ref, high_ref, mass_ref):
    f3 = 0.5 * (f2[...] - merge([got[n, 0:RI, :] for n in range(8)]))
    f4 = 0.5 * (f3 - merge([got[n, RI : 2 * RI, :] for n in range(8)]))
    f4_ref[0:RI, :] = f4
    lift = lift_i[...]
    (result,) = reduce_lanes(k_ref, [lifted(f3, lift)], high_ref, mass_ref)
    mine = f4_ref[pl.ds(info[3], 2), :]
    for n in range(16):
        out[n, 0:RJ, :] = result
        out[n, RJ : 2 * RJ, :] = g3[...]
        out[n, 2 * RJ : 2 * RJ + 2, :] = mine
        out[n, 2 * RJ + 2 : 16, :] = jnp.zeros((14 - 2 * RJ, 128), jnp.float32)


def last_body(got, gen_weight, ref_weight, ref_full_weight, pots, g4_out, share):
    cross = [got[n * 4 + 1] for n in range(4)]
    g4 = 0.5 * (cross[0][RJ : 2 * RJ, :] - merge([part[0:RJ, :] for part in cross])) * LN2
    g4_out[0:RJ, :] = g4
    g4_out[RJ:8, :] = jnp.zeros((8 - RJ, 128), jnp.float32)
    total = jnp.sum(jnp.where(ref_full_weight[...] > 0.0, g4 * ref_full_weight[...], 0.0))
    for n in range(4):
        own = slice(2 * RJ, 2 * RJ + 2)
        gen_pot = got[n * 4 + 1][own, :] * LN2
        gen_self = got[n * 4][own, :] * LN2
        ref_self = got[n * 4 + 3][own, :] * LN2
        pots[n, 0:2, :] = gen_pot
        pots[n, 2:4, :] = gen_self
        pots[n, 4:6, :] = ref_self
        pots[n, 6:8, :] = jnp.zeros((2, 128), jnp.float32)
        total += jnp.sum(jnp.where(gen_weight[n] > 0.0, (gen_pot - gen_self) * gen_weight[n], 0.0))
        total -= jnp.sum(jnp.where(ref_weight[n] > 0.0, ref_self * ref_weight[n], 0.0))
    for n in range(8):
        share[n, :, :] = jnp.full((8, 128), total, jnp.float32)


def spread(operand, axes):
    return lax.all_to_all(operand, axes, 0, 0, tiled=True)


def local(gen_points, reference_embeddings, gen_count, ref_count):
    y, x, c, zl = (lax.axis_index(name) for name in ("y", "x", "c", "zl"))
    a_is_gen = zl < 3
    b_is_gen = zl == 0
    packed = jnp.concatenate([gen_points, reference_embeddings], axis=1)
    raw = lax.all_gather(packed, ("zh", "zl"))

    info = jnp.stack(
        [a_is_gen.astype(jnp.int32), b_is_gen.astype(jnp.int32), c, c * 6 + (3 * x) // 2]
    ).astype(jnp.int32)
    counts = jnp.stack([gen_count, ref_count]).reshape(2, 4, 4, 2)
    totals = jnp.sum(counts, axis=(1, 2, 3)).astype(jnp.float32)
    weights2 = -jnp.log(totals) * LOG2E
    place = jnp.arange(BLOCK, dtype=jnp.int32)
    a_set = jnp.where(a_is_gen, 0, 1)
    b_set = jnp.where(b_is_gen, 0, 1)
    count_i = jnp.transpose(counts[a_set, y]).reshape(8)
    count_j = counts[b_set, :, x, c]
    lift_i = jnp.where(place[None, :] < count_i[:, None], weights2[a_set], FAR).reshape(RI, 128)
    lift_j = jnp.where(place[None, :] < count_j[:, None], weights2[b_set], FAR).reshape(RJ, 128)
    spots = jnp.arange(256, dtype=jnp.int32) - 64 * (x % 2)
    inside = spots >= 0
    gen_in = inside[None, :] & (spots[None, :] < counts[0, :, x, c][:, None])
    ref_in = inside[None, :] & (spots[None, :] < counts[1, :, x, c][:, None])
    gen_weight = jnp.where(gen_in, 1.0 / totals[0], 0.0).reshape(4, 2, 128)
    ref_weight = jnp.where(ref_in, 1.0 / totals[1], 0.0).reshape(4, 2, 128)
    ref_full = jnp.where(place[None, :] < counts[1, :, x, c][:, None], 1.0 / totals[1], 0.0).reshape(RJ, 128)

    bf16 = jnp.bfloat16
    a_wide, b_own = call(
        unpack_body,
        (jax.ShapeDtypeStruct((4, BLOCK, D), bf16), jax.ShapeDtypeStruct((BLOCK, D), bf16)),
        [SMEM, VMEM],
    )(info, raw)
    b_all = lax.all_gather(b_own, "y")
    a_half = spread(a_wide, "x")
    a_other = lax.ppermute(a_half, "c", [(0, 1), (1, 0)])

    passes = [pltpu.VMEM((1, NJ, 128), jnp.float32)] * 2
    passes2 = [pltpu.VMEM((2, NJ, 128), jnp.float32)] * 2
    cost, part = call(
        cost_body,
        (f32(NJ, NI), f32(4, 8, 128)),
        [SMEM, VMEM, VMEM, VMEM, VMEM],
        [pltpu.VMEM((NJ, 128), jnp.float32)] + passes,
    )(info, a_half.reshape(NJ, D), a_other.reshape(NJ, D), b_all.reshape(NJ, D), lift_i)
    got = spread(part, "y")
    part, g1 = call(
        second_body, (f32(8, 2 * RI, 128), f32(RJ, 128)), [VMEM] * 3, passes2[:1]
    )(cost, got, lift_j)
    got = spread(part, ("x", "c"))
    part, f2 = call(
        third_body, (f32(4, 16, 128), f32(RI, 128)), [VMEM] * 3, passes2
    )(cost, got, lift_i)
    got = spread(part, "y")
    part, g3 = call(
        fourth_body, (f32(8, 2 * RI, 128), f32(RJ, 128)), [VMEM] * 4, passes2[:1]
    )(cost, got, lift_j, g1)
    got = spread(part, ("x", "c"))
    part = call(
        fifth_body,
        f32(16, 16, 128),
        [SMEM] + [VMEM] * 5,
        [pltpu.VMEM((16, 128), jnp.float32)] + passes,
    )(info, cost, got, lift_i, f2, g3)
    got = spread(part, ("y", "zl"))
    pots, g4, share = call(
        last_body, (f32(4, 8, 128), f32(8, 128), f32(8, 8, 128)), [VMEM] * 4
    )(got, gen_weight, ref_weight, ref_full)
    divergence = jnp.sum(spread(share, ("x", "c"))[:, 0, 0])

    mine = lax.dynamic_index_in_dim(pots, y, 0, keepdims=False)
    mine = lax.dynamic_slice_in_dim(mine.reshape(4, 256), 64 * (x % 2), BLOCK, 1)
    ref_pot = lax.dynamic_slice_in_dim(g4.reshape(1024), y * BLOCK, BLOCK, 0)
    return mine[0], ref_pot, mine[1], mine[2], divergence


def solution(mesh):
    fine = Mesh(mesh.devices.reshape(4, 4, 2, 4, 4), ("y", "x", "c", "zh", "zl"))
    tile, feat = ("y", "x", "c"), ("zh", "zl")
    return jax.shard_map(
        local,
        mesh=fine,
        in_specs=(P(tile, feat), P(tile, feat), P(), P()),
        out_specs=(P(tile), P(tile), P(tile), P(tile), P()),
        check_vma=False,
    )
```

```python
import functools

import jax
import jax.numpy as jnp
from jax import lax
from jax.experimental import pallas as pl
from jax.experimental.pallas import tpu as pltpu
from jax.sharding import Mesh, PartitionSpec as P

EPSILON = 0.25
LOG2E = 1.4426950408889634
LN2 = 0.6931471805599453
FAR = -1.0e30

BLOCK = 192
D = 1024
NI = 8 * BLOCK
NJ = 4 * BLOCK
RI = NI // 128
RJ = NJ // 128
SPAN = 4
CHUNK = 32
ROWS = 8
UNROLL = 4

VMEM = pl.BlockSpec(memory_space=pltpu.VMEM)
HBM = pl.BlockSpec(memory_space=pltpu.HBM)
SMEM = pl.BlockSpec(memory_space=pltpu.SMEM)
PARAMS = pltpu.CompilerParams(vmem_limit_bytes=40 * 1024 * 1024)


def f32(*shape):
    return jax.ShapeDtypeStruct(shape, jnp.float32)


def call(body, outs, ins, scratch=(), out_specs=None):
    return pl.pallas_call(
        body,
        out_shape=outs,
        in_specs=ins,
        out_specs=jax.tree.map(lambda _: VMEM, outs) if out_specs is None else out_specs,
        scratch_shapes=list(scratch),
        compiler_params=PARAMS,
    )


def merge(parts):
    high = functools.reduce(jnp.maximum, parts)
    mass = functools.reduce(jnp.add, [jnp.exp2(part - high) for part in parts])
    return high + jnp.log(mass) * LOG2E


def lifted(pot, lift):
    return jnp.where(lift > -1.0e29, pot + lift, FAR)


def row_chunks(k_hbm, k_ref, sems):
    parts = [pl.ds(b * 128, 128) for b in range(RJ)]
    return [pltpu.make_async_copy(k_hbm.at[p], k_ref.at[p], sems.at[b]) for b, p in enumerate(parts)]


def column_chunks(k_hbm, k_ref, sems):
    parts = [pl.ds(t * SPAN * 128, SPAN * 128) for t in range(RI // SPAN)]
    return [
        pltpu.make_async_copy(k_hbm.at[:, p], k_ref.at[:, p], sems.at[t]) for t, p in enumerate(parts)
    ]


def reduce_lanes_rows(k_ref, heads, high_ref, mass_ref, b):
    count = len(heads)

    def step(group, carry):
        rows = pl.ds(pl.multiple_of(b * 128 + group * ROWS, ROWS), ROWS)
        spot = pl.ds(pl.multiple_of(group * ROWS, ROWS), ROWS)
        tiles = [k_ref[rows, r * 128 : (r + 1) * 128] for r in range(RI)]
        for v in range(count):
            xs = [heads[v][r : r + 1, :] - tiles[r] for r in range(RI)]
            high = functools.reduce(jnp.maximum, xs)
            mass = functools.reduce(jnp.add, [jnp.exp2(x - high) for x in xs])
            high_ref[v, spot, :] = high
            mass_ref[v, spot, :] = mass
        return carry

    lax.fori_loop(0, 128 // ROWS, step, 0, unroll=UNROLL)
    results = []
    for v in range(count):
        high = jnp.transpose(high_ref[v])
        mass = jnp.transpose(mass_ref[v])
        top = jnp.max(high, axis=0, keepdims=True)
        total = jnp.sum(mass * jnp.exp2(high - top), axis=0, keepdims=True)
        results.append(top + jnp.log(total) * LOG2E)
    return results


def reduce_lanes(k_ref, heads, high_ref, mass_ref, copies):
    results = []
    for b in range(RJ):
        copies[b].wait()
        results.append(reduce_lanes_rows(k_ref, heads, high_ref, mass_ref, b))
    return [jnp.concatenate([rows[v] for rows in results], axis=0) for v in range(len(heads))]


def reduce_rows(k_ref, heads, wide_ref, copies):
    count = len(heads)
    for v in range(count):
        for b in range(RJ):
            row = jnp.broadcast_to(heads[v][b : b + 1, :], (128, 128))
            wide_ref[v, b * 128 : (b + 1) * 128, :] = jnp.transpose(row)
    rows_out = [[] for _ in range(count)]
    for t in range(RI // SPAN):
        copies[t].wait()
        cols = [slice((t * SPAN + q) * 128, (t * SPAN + q + 1) * 128) for q in range(SPAN)]

        def highest(group, tops):
            base = pl.multiple_of(group * CHUNK, CHUNK)
            tops = list(tops)
            for s in range(CHUNK // 8):
                rows = pl.ds(base + s * 8, 8)
                wides = [wide_ref[v, rows, :] for v in range(count)]
                for q in range(SPAN):
                    tile = k_ref[rows, cols[q]]
                    for v in range(count):
                        tops[v * SPAN + q] = jnp.maximum(tops[v * SPAN + q], wides[v] - tile)
            return tuple(tops)

        tops = lax.fori_loop(
            0, NJ // CHUNK, highest, tuple(jnp.full((8, 128), -3.0e38, jnp.float32) for _ in range(count * SPAN))
        )

        def summed(group, sums):
            base = pl.multiple_of(group * CHUNK, CHUNK)
            sums = list(sums)
            for s in range(CHUNK // 8):
                rows = pl.ds(base + s * 8, 8)
                wides = [wide_ref[v, rows, :] for v in range(count)]
                for q in range(SPAN):
                    tile = k_ref[rows, cols[q]]
                    for v in range(count):
                        n = v * SPAN + q
                        sums[n] = sums[n] + jnp.exp2((wides[v] - tile) - tops[n])
            return tuple(sums)

        sums = lax.fori_loop(
            0, NJ // CHUNK, summed, tuple(jnp.zeros((8, 128), jnp.float32) for _ in range(count * SPAN))
        )
        for v in range(count):
            for q in range(SPAN):
                high, mass = tops[v * SPAN + q], sums[v * SPAN + q]
                top = jnp.max(high, axis=0, keepdims=True)
                total = jnp.sum(mass * jnp.exp2(high - top), axis=0, keepdims=True)
                rows_out[v].append(top + jnp.log(total) * LOG2E)
    return [jnp.concatenate(rows, axis=0) for rows in rows_out]


def pack_body(gen, ref, out):
    both = jnp.concatenate([gen[...].astype(jnp.float32), ref[...].astype(jnp.float32)], axis=0)
    out[...] = jnp.transpose(both).astype(jnp.bfloat16)


def unpack_body(info, raw, a_out, b_out):
    a_is_gen = info[0] == 1
    b_is_gen = info[1] == 1
    for k in range(D // 128):
        even = raw[2 * k]
        odd = raw[2 * k + 1]
        gen = jnp.concatenate([even[:, :64], odd[:, :64]], axis=1)
        ref = jnp.concatenate([even[:, 64:], odd[:, 64:]], axis=1)
        cols = slice(k * 128, (k + 1) * 128)
        a = jnp.where(a_is_gen, gen, ref)
        for n in range(4):
            a_out[n, :, cols] = a
        b_out[:, cols] = jnp.where(b_is_gen, gen, ref)


def norm_parts(values):
    values = values.astype(jnp.float32)
    values = values * values
    return functools.reduce(jnp.add, [values[:, k * 128 : (k + 1) * 128] for k in range(D // 128)])


def cost_body(
    info, own, other, cols, lift_i, k_hbm, part_out, a_ref, b_ref, k_ref, high_ref, mass_ref, sq_ref, in_sems, out_sems
):
    scale = LOG2E / EPSILON
    c = info[2]
    loads = [
        pltpu.make_async_copy(own, a_ref.at[c], in_sems.at[0]),
        pltpu.make_async_copy(other, a_ref.at[1 - c], in_sems.at[1]),
    ]
    chunks = [pl.ds(b * 256, 256) for b in range(3)]
    loads += [pltpu.make_async_copy(cols.at[p], b_ref.at[p], in_sems.at[2 + b]) for b, p in enumerate(chunks)]
    for load in loads:
        load.start()
    stores = row_chunks(k_ref, k_hbm, out_sems)
    heads = [lift_i[...]]
    loads[0].wait()
    loads[1].wait()
    for which in range(2):
        for s in range(6):
            turned = jnp.transpose(norm_parts(a_ref[which, s * 128 : (s + 1) * 128, :]))
            sq_ref[which * 6 + s : which * 6 + s + 1, :] = jnp.sum(turned, axis=0, keepdims=True) * (0.5 * scale)
    result = []
    for b in range(3):
        loads[2 + b].wait()
        rows = b_ref[b * 256 : (b + 1) * 256, :]
        row_sq = jnp.sum(norm_parts(rows), axis=1, keepdims=True) * (0.5 * scale)
        for which in range(2):
            for t in range(3):
                inner = lax.dot_general(
                    rows,
                    a_ref[which, t * 256 : (t + 1) * 256, :],
                    (((1,), (1,)), ((), ())),
                    preferred_element_type=jnp.float32,
                )
                for s in range(2):
                    r = which * 6 + t * 2 + s
                    k_ref[b * 256 : (b + 1) * 256, r * 128 : (r + 1) * 128] = (
                        row_sq + sq_ref[r : r + 1, :]
                    ) - scale * inner[:, s * 128 : (s + 1) * 128]
        for half in (2 * b, 2 * b + 1):
            stores[half].start()
            result.append(reduce_lanes_rows(k_ref, heads, high_ref, mass_ref, half)[0])
    result = jnp.concatenate(result, axis=0)
    for n in range(4):
        part_out[n, 0:RJ, :] = result
        part_out[n, RJ:8, :] = jnp.zeros((8 - RJ, 128), jnp.float32)
    for store in stores:
        store.wait()


def second_body(k_hbm, got, lift_j, out, g1_out, k_ref, sems, wide_ref):
    copies = column_chunks(k_hbm, k_ref, sems)
    for copy in copies:
        copy.start()
    g1 = -merge([got[n, 0:RJ, :] for n in range(4)])
    g1_out[...] = g1
    lift = lift_j[...]
    results = reduce_rows(k_ref, [lift, lifted(g1, lift)], wide_ref, copies)
    for n in range(8):
        for v in range(2):
            out[n, v * RI : (v + 1) * RI, :] = results[v]


def third_body(k_hbm, got, lift_i, out, f2_out, k_ref, sems, high_ref, mass_ref):
    copies = row_chunks(k_hbm, k_ref, sems)
    for copy in copies:
        copy.start()
    f1 = -merge([got[n, 0:RI, :] for n in range(8)])
    f2 = 0.5 * (f1 - merge([got[n, RI : 2 * RI, :] for n in range(8)]))
    f2_out[...] = f2
    lift = lift_i[...]
    results = reduce_lanes(k_ref, [lifted(f1, lift), lifted(f2, lift)], high_ref, mass_ref, copies)
    for n in range(4):
        for v in range(2):
            out[n, v * 8 : v * 8 + RJ, :] = results[v]
            out[n, v * 8 + RJ : v * 8 + 8, :] = jnp.zeros((8 - RJ, 128), jnp.float32)


def fourth_body(k_hbm, got, lift_j, g1, out, g3_out, k_ref, sems, wide_ref):
    copies = column_chunks(k_hbm, k_ref, sems)
    for copy in copies:
        copy.start()
    g2 = 0.5 * (g1[...] - merge([got[n, 0:RJ, :] for n in range(4)]))
    g3 = 0.5 * (g2 - merge([got[n, 8 : 8 + RJ, :] for n in range(4)]))
    g3_out[...] = g3
    lift = lift_j[...]
    results = reduce_rows(k_ref, [lifted(g2, lift), lifted(g3, lift)], wide_ref, copies)
    for n in range(8):
        for v in range(2):
            out[n, v * RI : (v + 1) * RI, :] = results[v]


def fifth_body(info, k_hbm, got, lift_i, f2, g3, out, k_ref, sems, f4_ref, high_ref, mass_ref):
    copies = row_chunks(k_hbm, k_ref, sems)
    for copy in copies:
        copy.start()
    f3 = 0.5 * (f2[...] - merge([got[n, 0:RI, :] for n in range(8)]))
    f4 = 0.5 * (f3 - merge([got[n, RI : 2 * RI, :] for n in range(8)]))
    f4_ref[0:RI, :] = f4
    lift = lift_i[...]
    (result,) = reduce_lanes(k_ref, [lifted(f3, lift)], high_ref, mass_ref, copies)
    shifted = result - g3[...]
    mine = f4_ref[pl.ds(info[3], 2), :]
    for n in range(16):
        out[n, 0:RJ, :] = shifted
        out[n, RJ : RJ + 2, :] = mine


def last_body(got, gen_weight, ref_weight, ref_full_weight, pots, g4_out, share):
    g4 = merge([got[n * 4 + 1][0:RJ, :] for n in range(4)]) * (-0.5 * LN2)
    g4_out[0:RJ, :] = g4
    g4_out[RJ:8, :] = jnp.zeros((8 - RJ, 128), jnp.float32)
    total = jnp.sum(jnp.where(ref_full_weight[...] > 0.0, g4 * ref_full_weight[...], 0.0))
    for n in range(4):
        own = slice(RJ, RJ + 2)
        gen_pot = got[n * 4 + 1][own, :] * LN2
        gen_self = got[n * 4][own, :] * LN2
        ref_self = got[n * 4 + 3][own, :] * LN2
        pots[n, 0:2, :] = gen_pot
        pots[n, 2:4, :] = gen_self
        pots[n, 4:6, :] = ref_self
        pots[n, 6:8, :] = jnp.zeros((2, 128), jnp.float32)
        total += jnp.sum(jnp.where(gen_weight[n] > 0.0, (gen_pot - gen_self) * gen_weight[n], 0.0))
        total -= jnp.sum(jnp.where(ref_weight[n] > 0.0, ref_self * ref_weight[n], 0.0))
    for n in range(8):
        share[n, :, :] = jnp.full((8, 128), total, jnp.float32)


def held(chunks):
    return [pltpu.VMEM((NJ, NI), jnp.float32), pltpu.SemaphoreType.DMA((chunks,))]


def partials(count):
    return [pltpu.VMEM((count, 128, 128), jnp.float32)] * 2


def wide(count):
    return [pltpu.VMEM((count, NJ, 128), jnp.float32)]


def stage_cost(*args):
    scratch = [
        pltpu.VMEM((2, NJ, D), jnp.bfloat16),
        pltpu.VMEM((NJ, D), jnp.bfloat16),
        pltpu.VMEM((NJ, NI), jnp.float32),
        *partials(1),
        pltpu.VMEM((16, 128), jnp.float32),
        pltpu.SemaphoreType.DMA((5,)),
        pltpu.SemaphoreType.DMA((RJ,)),
    ]
    outs = (f32(NJ, NI), f32(4, 8, 128))
    return call(cost_body, outs, [SMEM, HBM, HBM, HBM, VMEM], scratch, (HBM, VMEM))(*args)


def stage_second(*args):
    outs = (f32(8, 2 * RI, 128), f32(RJ, 128))
    return call(second_body, outs, [HBM, VMEM, VMEM], held(RI // SPAN) + wide(2))(*args)


def stage_third(*args):
    outs = (f32(4, 16, 128), f32(RI, 128))
    return call(third_body, outs, [HBM, VMEM, VMEM], held(RJ) + partials(2))(*args)


def stage_fourth(*args):
    outs = (f32(8, 2 * RI, 128), f32(RJ, 128))
    return call(fourth_body, outs, [HBM, VMEM, VMEM, VMEM], held(RI // SPAN) + wide(2))(*args)


def stage_fifth(*args):
    scratch = held(RJ) + [pltpu.VMEM((16, 128), jnp.float32)] + partials(1)
    return call(fifth_body, f32(16, 8, 128), [SMEM, HBM] + [VMEM] * 4, scratch)(*args)


def spread(operand, axes):
    return lax.all_to_all(operand, axes, 0, 0, tiled=True)


def local(gen_points, reference_embeddings, gen_count, ref_count):
    y, x, c, zl = (lax.axis_index(name) for name in ("y", "x", "c", "zl"))
    a_is_gen = zl < 3
    b_is_gen = zl == 0
    bf16 = jnp.bfloat16
    packed = call(pack_body, jax.ShapeDtypeStruct((BLOCK, 128), bf16), [VMEM, VMEM])(
        jnp.transpose(gen_points), jnp.transpose(reference_embeddings)
    )
    raw = lax.all_gather(packed, ("zh", "zl"))

    info = jnp.stack(
        [a_is_gen.astype(jnp.int32), b_is_gen.astype(jnp.int32), c, c * 6 + (3 * y) // 2]
    ).astype(jnp.int32)
    counts = jnp.stack([gen_count, ref_count]).reshape(2, 4, 4, 2)
    totals = jnp.sum(counts, axis=(1, 2, 3)).astype(jnp.float32)
    weights2 = -jnp.log(totals) * LOG2E
    place = jnp.arange(BLOCK, dtype=jnp.int32)
    a_set = jnp.where(a_is_gen, 0, 1)
    b_set = jnp.where(b_is_gen, 0, 1)
    count_i = jnp.transpose(counts[a_set, :, x]).reshape(8)
    count_j = counts[b_set, y, :, c]
    lift_i = jnp.where(place[None, :] < count_i[:, None], weights2[a_set], FAR).reshape(RI, 128)
    lift_j = jnp.where(place[None, :] < count_j[:, None], weights2[b_set], FAR).reshape(RJ, 128)
    spots = jnp.arange(256, dtype=jnp.int32) - 64 * (y % 2)
    inside = spots >= 0
    gen_in = inside[None, :] & (spots[None, :] < counts[0, y, :, c][:, None])
    ref_in = inside[None, :] & (spots[None, :] < counts[1, y, :, c][:, None])
    gen_weight = jnp.where(gen_in, 1.0 / totals[0], 0.0).reshape(4, 2, 128)
    ref_weight = jnp.where(ref_in, 1.0 / totals[1], 0.0).reshape(4, 2, 128)
    ref_full = jnp.where(place[None, :] < counts[1, y, :, c][:, None], 1.0 / totals[1], 0.0).reshape(RJ, 128)

    a_wide, b_own = call(
        unpack_body,
        (jax.ShapeDtypeStruct((4, BLOCK, D), bf16), jax.ShapeDtypeStruct((BLOCK, D), bf16)),
        [SMEM, VMEM],
    )(info, raw)
    b_all = lax.all_gather(b_own, "x")
    a_half = spread(a_wide, "y")
    a_other = lax.ppermute(a_half, "c", [(0, 1), (1, 0)])

    cost, part = stage_cost(info, a_half.reshape(NJ, D), a_other.reshape(NJ, D), b_all.reshape(NJ, D), lift_i)
    part, g1 = stage_second(cost, spread(part, "x"), lift_j)
    part, f2 = stage_third(cost, spread(part, ("y", "c")), lift_i)
    part, g3 = stage_fourth(cost, spread(part, "x"), lift_j, g1)
    part = stage_fifth(info, cost, spread(part, ("y", "c")), lift_i, f2, g3)
    got = spread(part, ("x", "zl"))
    pots, g4, share = call(
        last_body, (f32(4, 8, 128), f32(8, 128), f32(8, 8, 128)), [VMEM] * 4
    )(got, gen_weight, ref_weight, ref_full)
    divergence = jnp.sum(spread(share, ("y", "c"))[:, 0, 0])

    mine = lax.dynamic_index_in_dim(pots, x, 0, keepdims=False)
    mine = lax.dynamic_slice_in_dim(mine.reshape(4, 256), 64 * (y % 2), BLOCK, 1)
    ref_pot = lax.dynamic_slice_in_dim(g4.reshape(1024), x * BLOCK, BLOCK, 0)
    return mine[0], ref_pot, mine[1], mine[2], divergence


def solution(mesh):
    fine = Mesh(mesh.devices.reshape(4, 4, 2, 4, 4), ("y", "x", "c", "zh", "zl"))
    tile, feat = ("y", "x", "c"), ("zh", "zl")
    return jax.shard_map(
        local,
        mesh=fine,
        in_specs=(P(tile, feat), P(tile, feat), P(), P()),
        out_specs=(P(tile), P(tile), P(tile), P(tile), P()),
        check_vma=False,
    )
```

```python
import functools

import jax
import jax.numpy as jnp
from jax import lax
from jax.experimental import pallas as pl
from jax.experimental.pallas import tpu as pltpu
from jax.sharding import Mesh, PartitionSpec as P

EPSILON = 0.25
LOG2E = 1.4426950408889634
LN2 = 0.6931471805599453
FAR = -1.0e30

BLOCK = 192
D = 1024
NI = 8 * BLOCK
NJ = 4 * BLOCK
RI = NI // 128
RJ = NJ // 128
NEAR = 8
N1 = NEAR * 128
N2 = NI - N1

VMEM = pl.BlockSpec(memory_space=pltpu.VMEM)
HBM = pl.BlockSpec(memory_space=pltpu.HBM)
SMEM = pl.BlockSpec(memory_space=pltpu.SMEM)
PARAMS = pltpu.CompilerParams(vmem_limit_bytes=60 * 1024 * 1024)


def f32(*shape):
    return jax.ShapeDtypeStruct(shape, jnp.float32)


def call(body, outs, ins, scratch=(), out_specs=None):
    return pl.pallas_call(
        body,
        out_shape=outs,
        in_specs=ins,
        out_specs=jax.tree.map(lambda _: VMEM, outs) if out_specs is None else out_specs,
        scratch_shapes=list(scratch),
        compiler_params=PARAMS,
    )


def merge(got, count):
    parts = [got[n] for n in range(count)]
    high = functools.reduce(jnp.maximum, parts)
    mass = functools.reduce(jnp.add, [jnp.exp2(part - high) for part in parts])
    return high + jnp.log(mass) * LOG2E


def lifted(pot, lift):
    return jnp.where(lift > -1.0e29, pot + lift, FAR)


def tree(op, values):
    values = list(values)
    while len(values) > 1:
        values = [op(*values[n : n + 2]) if n + 1 < len(values) else values[n] for n in range(0, len(values), 2)]
    return values[0]


def fetch(k2_hbm, k2_ref, sems, b):
    rows = pl.ds(b * 128, 128)
    return pltpu.make_async_copy(k2_hbm.at[rows], k2_ref.at[rows], sems.at[b])


def start_fetch(k2_hbm, k2_ref, sems):
    for b in range(RJ):
        fetch(k2_hbm, k2_ref, sems, b).start()


def k_tile(k1_ref, k2_ref, rows, r):
    if r < NEAR:
        return k1_ref[rows, r * 128 : (r + 1) * 128]
    return k2_ref[rows, (r - NEAR) * 128 : (r - NEAR + 1) * 128]


def lanes_block(k1_ref, k2_ref, heads, high_ref, mass_ref, base):
    for group in range(16):
        rows = pl.ds(base + group * 8, 8)
        tiles = [k_tile(k1_ref, k2_ref, rows, r) for r in range(RI)]
        for v in range(len(heads)):
            xs = [heads[v][r : r + 1, :] - tiles[r] for r in range(RI)]
            high = tree(jnp.maximum, xs)
            high_ref[v, rows, :] = high
            mass_ref[v, rows, :] = tree(jnp.add, [jnp.exp2(x - high) for x in xs])


def lanes_result(count, high_ref, mass_ref):
    results = []
    for v in range(count):
        rows_out = []
        for b in range(RJ):
            high = jnp.transpose(high_ref[v, b * 128 : (b + 1) * 128, :])
            mass = jnp.transpose(mass_ref[v, b * 128 : (b + 1) * 128, :])
            top = jnp.max(high, axis=0, keepdims=True)
            total = jnp.sum(mass * jnp.exp2(high - top), axis=0, keepdims=True)
            rows_out.append((top, total))
        top = jnp.concatenate([row[0] for row in rows_out], axis=0)
        total = jnp.concatenate([row[1] for row in rows_out], axis=0)
        results.append(top + jnp.log(total) * LOG2E)
    return results


def reduce_lanes(k1_ref, k2_hbm, k2_ref, sems, heads, high_ref, mass_ref):
    def step(b, carry):
        fetch(k2_hbm, k2_ref, sems, b).wait()
        lanes_block(k1_ref, k2_ref, heads, high_ref, mass_ref, pl.multiple_of(b * 128, 128))
        return carry

    lax.fori_loop(0, RJ, step, 0)
    return lanes_result(len(heads), high_ref, mass_ref)


def reduce_rows(k1_ref, k2_hbm, k2_ref, sems, heads, head_ref, high_ref, mass_ref):
    count = len(heads)
    for v in range(count):
        head_ref[v, 0:RJ, :] = heads[v]

    def step(b, carry):
        fetch(k2_hbm, k2_ref, sems, b).wait()
        wides = [
            jnp.transpose(jnp.broadcast_to(head_ref[v, pl.ds(b, 1), :], (128, 128))) for v in range(count)
        ]
        spot = pl.ds(pl.multiple_of(b * 8, 8), 8)
        for r in range(RI):
            cols = slice(r * 128, (r + 1) * 128)
            tiles = [k_tile(k1_ref, k2_ref, pl.ds(b * 128 + group * 8, 8), r) for group in range(16)]
            for v in range(count):
                xs = [wides[v][group * 8 : group * 8 + 8, :] - tiles[group] for group in range(16)]
                high = tree(jnp.maximum, xs)
                high_ref[v, spot, cols] = high
                mass_ref[v, spot, cols] = tree(jnp.add, [jnp.exp2(x - high) for x in xs])
        return carry

    lax.fori_loop(0, RJ, step, 0)
    results = []
    for v in range(count):
        tops, totals = [], []
        for r in range(RI):
            cols = slice(r * 128, (r + 1) * 128)
            high = high_ref[v, :, cols]
            top = jnp.max(high, axis=0, keepdims=True)
            tops.append(top)
            totals.append(jnp.sum(mass_ref[v, :, cols] * jnp.exp2(high - top), axis=0, keepdims=True))
        results.append(jnp.concatenate(tops, axis=0) + jnp.log(jnp.concatenate(totals, axis=0)) * LOG2E)
    return results


def pack_body(gen, ref, out):
    both = jnp.concatenate([gen[...].astype(jnp.float32), ref[...].astype(jnp.float32)], axis=0)
    out[...] = jnp.transpose(both).astype(jnp.bfloat16)


def select_set(is_gen, raw, k):
    even, odd = raw[2 * k], raw[2 * k + 1]
    gen = jnp.concatenate([even[:, :64], odd[:, :64]], axis=1)
    ref = jnp.concatenate([even[:, 64:], odd[:, 64:]], axis=1)
    return jnp.where(is_gen, gen, ref)


def unpack_b_body(info, raw, out):
    for k in range(D // 128):
        out[:, k * 128 : (k + 1) * 128] = select_set(info[1] == 1, raw, k)


def unpack_a_body(info, raw, out):
    for k in range(D // 128):
        part = select_set(info[0] == 1, raw, k)
        for n in range(4):
            out[n, :, k * 128 : (k + 1) * 128] = part


def norm_parts(values):
    values = values.astype(jnp.float32)
    values = values * values
    return functools.reduce(jnp.add, [values[:, k * 128 : (k + 1) * 128] for k in range(D // 128)])


def cost_body(
    info, own, other, cols, lift_i, k1_ref, k2_hbm, part_out,
    a_ref, b_ref, k2_ref, high_ref, mass_ref, sq_ref, in_sems, out_sems,
):
    scale = LOG2E / EPSILON
    c = info[2]
    loads = [
        pltpu.make_async_copy(own, a_ref.at[c], in_sems.at[0]),
        pltpu.make_async_copy(other, a_ref.at[1 - c], in_sems.at[1]),
    ]
    chunks = [pl.ds(b * 256, 256) for b in range(3)]
    loads += [pltpu.make_async_copy(cols.at[p], b_ref.at[p], in_sems.at[2 + b]) for b, p in enumerate(chunks)]
    for load in loads:
        load.start()
    heads = [lift_i[...]]
    loads[0].wait()
    loads[1].wait()
    for which in range(2):
        for s in range(6):
            turned = jnp.transpose(norm_parts(a_ref[which, s * 128 : (s + 1) * 128, :]))
            sq_ref[which * 6 + s : which * 6 + s + 1, :] = jnp.sum(turned, axis=0, keepdims=True) * (0.5 * scale)
    stores = [fetch(k2_ref, k2_hbm, out_sems, b) for b in range(RJ)]
    for b in range(4):
        if b < 3:
            loads[2 + b].wait()
            rows = b_ref[b * 256 : (b + 1) * 256, :]
            row_sq = jnp.sum(norm_parts(rows), axis=1, keepdims=True) * (0.5 * scale)
            for which in range(2):
                for t in range(3):
                    inner = lax.dot_general(
                        rows,
                        a_ref[which, t * 256 : (t + 1) * 256, :],
                        (((1,), (1,)), ((), ())),
                        preferred_element_type=jnp.float32,
                    )
                    for s in range(2):
                        r = which * 6 + t * 2 + s
                        tile = (row_sq + sq_ref[r : r + 1, :]) - scale * inner[:, s * 128 : (s + 1) * 128]
                        if r < NEAR:
                            k1_ref[b * 256 : (b + 1) * 256, r * 128 : (r + 1) * 128] = tile
                        else:
                            k2_ref[b * 256 : (b + 1) * 256, (r - NEAR) * 128 : (r - NEAR + 1) * 128] = tile
        if b > 0:
            for half in (2 * b - 2, 2 * b - 1):
                lanes_block(k1_ref, k2_ref, heads, high_ref, mass_ref, half * 128)
        if b < 3:
            stores[2 * b].start()
            stores[2 * b + 1].start()
    (result,) = lanes_result(1, high_ref, mass_ref)
    for n in range(4):
        part_out[n, 0:RJ, :] = result
        part_out[n, RJ:8, :] = jnp.zeros((8 - RJ, 128), jnp.float32)
    for store in stores:
        store.wait()


def second_body(k1_ref, k2_hbm, got, lift_j, out, g1_out, k2_ref, sems, head_ref, high_ref, mass_ref):
    start_fetch(k2_hbm, k2_ref, sems)
    g1 = -merge(got, 4)[0:RJ, :]
    g1_out[...] = g1
    lift = lift_j[...]
    heads = [lift, lifted(g1, lift)]
    results = reduce_rows(k1_ref, k2_hbm, k2_ref, sems, heads, head_ref, high_ref, mass_ref)
    for n in range(8):
        for v in range(2):
            out[n, v * RI : (v + 1) * RI, :] = results[v]


def third_body(k1_ref, k2_hbm, got, lift_i, out, f2_out, k2_ref, sems, high_ref, mass_ref):
    start_fetch(k2_hbm, k2_ref, sems)
    merged = -merge(got, 8)
    f1 = merged[0:RI, :]
    f2 = 0.5 * (f1 + merged[RI : 2 * RI, :])
    f2_out[...] = f2
    lift = lift_i[...]
    heads = [lifted(f1, lift), lifted(f2, lift)]
    results = reduce_lanes(k1_ref, k2_hbm, k2_ref, sems, heads, high_ref, mass_ref)
    for n in range(4):
        for v in range(2):
            out[n, v * 8 : v * 8 + RJ, :] = results[v]
            out[n, v * 8 + RJ : v * 8 + 8, :] = jnp.zeros((8 - RJ, 128), jnp.float32)


def fourth_body(k1_ref, k2_hbm, got, lift_j, g1, out, g3_out, k2_ref, sems, head_ref, high_ref, mass_ref):
    start_fetch(k2_hbm, k2_ref, sems)
    merged = -merge(got, 4)
    g2 = 0.5 * (g1[...] + merged[0:RJ, :])
    g3 = 0.5 * (g2 + merged[8 : 8 + RJ, :])
    g3_out[...] = g3
    lift = lift_j[...]
    heads = [lifted(g2, lift), lifted(g3, lift)]
    results = reduce_rows(k1_ref, k2_hbm, k2_ref, sems, heads, head_ref, high_ref, mass_ref)
    for n in range(8):
        for v in range(2):
            out[n, v * RI : (v + 1) * RI, :] = results[v]


def fifth_body(info, k1_ref, k2_hbm, got, lift_i, f2, g3, out, k2_ref, sems, high_ref, mass_ref, f4_ref):
    start_fetch(k2_hbm, k2_ref, sems)
    merged = -merge(got, 8)
    f3 = 0.5 * (f2[...] + merged[0:RI, :])
    f4 = 0.5 * (f3 + merged[RI : 2 * RI, :])
    f4_ref[0:RI, :] = f4
    heads = [lifted(f3, lift_i[...])]
    (result,) = reduce_lanes(k1_ref, k2_hbm, k2_ref, sems, heads, high_ref, mass_ref)
    shifted = result - g3[...]
    mine = f4_ref[pl.ds(info[3], 2), :]
    for n in range(16):
        out[n, 0:RJ, :] = shifted
        out[n, RJ : RJ + 2, :] = mine


def last_body(got, gen_weight, ref_weight, ref_full_weight, pots, g4_out, share):
    g4 = merge([got[n * 4 + 1, 0:RJ, :] for n in range(4)], 4) * (-0.5 * LN2)
    g4_out[0:RJ, :] = g4
    g4_out[RJ:8, :] = jnp.zeros((8 - RJ, 128), jnp.float32)
    total = jnp.sum(jnp.where(ref_full_weight[...] > 0.0, g4 * ref_full_weight[...], 0.0))
    for n in range(4):
        own = slice(RJ, RJ + 2)
        gen_pot = got[n * 4 + 1][own, :] * LN2
        gen_self = got[n * 4][own, :] * LN2
        ref_self = got[n * 4 + 3][own, :] * LN2
        pots[n, 0:2, :] = gen_pot
        pots[n, 2:4, :] = gen_self
        pots[n, 4:6, :] = ref_self
        pots[n, 6:8, :] = jnp.zeros((2, 128), jnp.float32)
        total += jnp.sum(jnp.where(gen_weight[n] > 0.0, (gen_pot - gen_self) * gen_weight[n], 0.0))
        total -= jnp.sum(jnp.where(ref_weight[n] > 0.0, ref_self * ref_weight[n], 0.0))
    for n in range(8):
        share[n, :, :] = jnp.full((8, 128), total, jnp.float32)


F32 = jnp.float32
BF16 = jnp.bfloat16
STREAM = [pltpu.VMEM((NJ, N2), F32), pltpu.SemaphoreType.DMA((RJ,))]


def lane_scratch(count):
    return [pltpu.VMEM((count, NJ, 128), F32)] * 2


def row_scratch(count):
    return [pltpu.VMEM((count, 8, 128), F32)] + [pltpu.VMEM((count, 8 * RJ, NI), F32)] * 2


def stage_pack(*args):
    return call(pack_body, jax.ShapeDtypeStruct((BLOCK, 128), BF16), [VMEM, VMEM])(*args)


def stage_unpack_b(*args):
    return call(unpack_b_body, jax.ShapeDtypeStruct((BLOCK, D), BF16), [SMEM, VMEM])(*args)


def stage_unpack_a(*args):
    return call(unpack_a_body, jax.ShapeDtypeStruct((4, BLOCK, D), BF16), [SMEM, VMEM])(*args)


def stage_cost(*args):
    scratch = [
        pltpu.VMEM((2, NJ, D), BF16),
        pltpu.VMEM((NJ, D), BF16),
        pltpu.VMEM((NJ, N2), F32),
        *lane_scratch(1),
        pltpu.VMEM((16, 128), F32),
        pltpu.SemaphoreType.DMA((5,)),
        pltpu.SemaphoreType.DMA((RJ,)),
    ]
    outs = (f32(NJ, N1), f32(NJ, N2), f32(4, 8, 128))
    return call(cost_body, outs, [SMEM, HBM, HBM, HBM, VMEM], scratch, (VMEM, HBM, VMEM))(*args)


def stage_second(*args):
    outs = (f32(8, 2 * RI, 128), f32(RJ, 128))
    return call(second_body, outs, [VMEM, HBM, VMEM, VMEM], STREAM + row_scratch(2))(*args)


def stage_third(*args):
    outs = (f32(4, 16, 128), f32(RI, 128))
    return call(third_body, outs, [VMEM, HBM, VMEM, VMEM], STREAM + lane_scratch(2))(*args)


def stage_fourth(*args):
    outs = (f32(8, 2 * RI, 128), f32(RJ, 128))
    return call(fourth_body, outs, [VMEM, HBM, VMEM, VMEM, VMEM], STREAM + row_scratch(2))(*args)


def stage_fifth(*args):
    scratch = STREAM + lane_scratch(1) + [pltpu.VMEM((16, 128), F32)]
    return call(fifth_body, f32(16, 8, 128), [SMEM, VMEM, HBM] + [VMEM] * 4, scratch)(*args)


def spread(operand, axes):
    return lax.all_to_all(operand, axes, 0, 0, tiled=True)


def local(gen_points, reference_embeddings, gen_count, ref_count):
    y, x, c, zl = (lax.axis_index(name) for name in ("y", "x", "c", "zl"))
    a_is_gen = zl < 3
    b_is_gen = zl == 0
    packed = stage_pack(jnp.transpose(gen_points), jnp.transpose(reference_embeddings))
    raw = lax.all_gather(packed, ("zh", "zl"))

    info = jnp.stack(
        [a_is_gen.astype(jnp.int32), b_is_gen.astype(jnp.int32), c, c * 6 + (3 * y) // 2]
    ).astype(jnp.int32)
    counts = jnp.stack([gen_count, ref_count]).reshape(2, 4, 4, 2)
    totals = jnp.sum(counts, axis=(1, 2, 3)).astype(jnp.float32)
    weights2 = -jnp.log(totals) * LOG2E
    place = jnp.arange(BLOCK, dtype=jnp.int32)
    a_set = jnp.where(a_is_gen, 0, 1)
    b_set = jnp.where(b_is_gen, 0, 1)
    count_i = jnp.transpose(counts[a_set, :, x]).reshape(8)
    count_j = counts[b_set, y, :, c]
    lift_i = jnp.where(place[None, :] < count_i[:, None], weights2[a_set], FAR).reshape(RI, 128)
    lift_j = jnp.where(place[None, :] < count_j[:, None], weights2[b_set], FAR).reshape(RJ, 128)
    spots = jnp.arange(256, dtype=jnp.int32) - 64 * (y % 2)
    inside = spots >= 0
    gen_in = inside[None, :] & (spots[None, :] < counts[0, y, :, c][:, None])
    ref_in = inside[None, :] & (spots[None, :] < counts[1, y, :, c][:, None])
    gen_weight = jnp.where(gen_in, 1.0 / totals[0], 0.0).reshape(4, 2, 128)
    ref_weight = jnp.where(ref_in, 1.0 / totals[1], 0.0).reshape(4, 2, 128)
    ref_full = jnp.where(place[None, :] < counts[1, y, :, c][:, None], 1.0 / totals[1], 0.0).reshape(RJ, 128)

    b_all = lax.all_gather(stage_unpack_b(info, raw), "x")
    a_half = spread(stage_unpack_a(info, raw), "y")
    a_other = lax.ppermute(a_half, "c", [(0, 1), (1, 0)])

    k1, k2, part = stage_cost(
        info, a_half.reshape(NJ, D), a_other.reshape(NJ, D), b_all.reshape(NJ, D), lift_i
    )
    part, g1 = stage_second(k1, k2, spread(part, "x"), lift_j)
    part, f2 = stage_third(k1, k2, spread(part, ("y", "c")), lift_i)
    part, g3 = stage_fourth(k1, k2, spread(part, "x"), lift_j, g1)
    part = stage_fifth(info, k1, k2, spread(part, ("y", "c")), lift_i, f2, g3)
    got = spread(part, ("x", "zl"))
    pots, g4, share = call(
        last_body, (f32(4, 8, 128), f32(8, 128), f32(8, 8, 128)), [VMEM] * 4
    )(got, gen_weight, ref_weight, ref_full)
    divergence = jnp.sum(spread(share, ("y", "c"))[:, 0, 0])

    mine = lax.dynamic_index_in_dim(pots, x, 0, keepdims=False)
    mine = lax.dynamic_slice_in_dim(mine.reshape(4, 256), 64 * (y % 2), BLOCK, 1)
    ref_pot = lax.dynamic_slice_in_dim(g4.reshape(1024), x * BLOCK, BLOCK, 0)
    return mine[0], ref_pot, mine[1], mine[2], divergence


def solution(mesh):
    fine = Mesh(mesh.devices.reshape(4, 4, 2, 4, 4), ("y", "x", "c", "zh", "zl"))
    tile, feat = ("y", "x", "c"), ("zh", "zl")
    return jax.shard_map(
        local,
        mesh=fine,
        in_specs=(P(tile, feat), P(tile, feat), P(), P()),
        out_specs=(P(tile), P(tile), P(tile), P(tile), P()),
        check_vma=False,
    )
```

```python
import functools

import jax
import jax.numpy as jnp
from jax import lax
from jax.experimental import pallas as pl
from jax.experimental.pallas import tpu as pltpu
from jax.sharding import Mesh, PartitionSpec as P

EPSILON = 0.25
LOG2E = 1.4426950408889634
LN2 = 0.6931471805599453
FAR = -1.0e30

BLOCK = 192
D = 1024
NI = 8 * BLOCK
NJ = 4 * BLOCK
RI = NI // 128
RJ = NJ // 128
NEAR = 8
N1 = NEAR * 128
N2 = NI - N1
ROOM = 18 * NJ

VMEM = pl.BlockSpec(memory_space=pltpu.VMEM)
HBM = pl.BlockSpec(memory_space=pltpu.HBM)
SMEM = pl.BlockSpec(memory_space=pltpu.SMEM)


def f32(*shape):
    return jax.ShapeDtypeStruct(shape, jnp.float32)


def call(body, outs, ins, scratch=(), out_specs=None, mib=40):
    return pl.pallas_call(
        body,
        out_shape=outs,
        in_specs=ins,
        out_specs=jax.tree.map(lambda _: VMEM, outs) if out_specs is None else out_specs,
        scratch_shapes=list(scratch),
        compiler_params=pltpu.CompilerParams(vmem_limit_bytes=mib * 1024 * 1024),
    )


def merge(got, count):
    parts = [got[n] for n in range(count)]
    high = functools.reduce(jnp.maximum, parts)
    mass = functools.reduce(jnp.add, [jnp.exp2(part - high) for part in parts])
    return high + jnp.log(mass) * LOG2E


def lifted(pot, lift):
    return jnp.where(lift > -1.0e29, pot + lift, FAR)


def tree(op, values):
    values = list(values)
    while len(values) > 1:
        values = [op(*values[n : n + 2]) if n + 1 < len(values) else values[n] for n in range(0, len(values), 2)]
    return values[0]


def fetch(k2_hbm, k2_ref, sems, b):
    rows = pl.ds(b * 128, 128)
    return pltpu.make_async_copy(k2_hbm.at[rows], k2_ref.at[rows], sems.at[b])


def start_fetch(k2_hbm, k2_ref, sems):
    for b in range(RJ):
        fetch(k2_hbm, k2_ref, sems, b).start()


def lanes_block(tiles_of, count, heads, high_ref, mass_ref, base, joined=False):
    for group in range(16):
        rows = pl.ds(base + group * 8, 8)
        tiles = tiles_of(rows)
        for v in range(count):
            xs = [heads[v][r : r + 1, :] - tile for r, tile in tiles]
            high = tree(jnp.maximum, xs)
            if joined:
                before = high_ref[v, rows, :]
                high = jnp.maximum(high, before)
                xs.append(before)
            masses = [jnp.exp2(x - high) for x in xs]
            if joined:
                masses[-1] = masses[-1] * mass_ref[v, rows, :]
            high_ref[v, rows, :] = high
            mass_ref[v, rows, :] = tree(jnp.add, masses)


def near_tiles(k1_ref):
    return lambda rows: [(r, k1_ref[rows, r * 128 : (r + 1) * 128]) for r in range(NEAR)]


def far_tiles(k2_ref):
    return lambda rows: [(r, k2_ref[rows, (r - NEAR) * 128 : (r - NEAR + 1) * 128]) for r in range(NEAR, RI)]


def lanes_result(count, high_ref, mass_ref):
    results = []
    for v in range(count):
        rows_out = []
        for b in range(RJ):
            high = jnp.transpose(high_ref[v, b * 128 : (b + 1) * 128, :])
            mass = jnp.transpose(mass_ref[v, b * 128 : (b + 1) * 128, :])
            top = jnp.max(high, axis=0, keepdims=True)
            total = jnp.sum(mass * jnp.exp2(high - top), axis=0, keepdims=True)
            rows_out.append((top, total))
        top = jnp.concatenate([row[0] for row in rows_out], axis=0)
        total = jnp.concatenate([row[1] for row in rows_out], axis=0)
        results.append(top + jnp.log(total) * LOG2E)
    return results


def reduce_lanes(k1_ref, k2_hbm, k2_ref, sems, heads, high_ref, mass_ref):
    count = len(heads)

    def near(b, carry):
        lanes_block(near_tiles(k1_ref), count, heads, high_ref, mass_ref, pl.multiple_of(b * 128, 128))
        return carry

    def far(b, carry):
        fetch(k2_hbm, k2_ref, sems, b).wait()
        lanes_block(far_tiles(k2_ref), count, heads, high_ref, mass_ref, pl.multiple_of(b * 128, 128), True)
        return carry

    lax.fori_loop(0, RJ, near, 0)
    lax.fori_loop(0, RJ, far, 0)
    return lanes_result(count, high_ref, mass_ref)


def reduce_rows(k1_ref, k2_hbm, k2_ref, sems, heads, head_ref, wide_ref, high_ref, mass_ref):
    count = len(heads)
    for v in range(count):
        head_ref[v, 0:RJ, :] = heads[v]

    def block(b, wides, tile, r):
        spot = pl.ds(pl.multiple_of(b * 8, 8), 8)
        cols = slice(r * 128, (r + 1) * 128)
        tiles = [tile(pl.ds(b * 128 + group * 8, 8)) for group in range(16)]
        for v in range(count):
            xs = [wides[v][group * 8 : group * 8 + 8, :] - tiles[group] for group in range(16)]
            high = tree(jnp.maximum, xs)
            high_ref[v, spot, cols] = high
            mass_ref[v, spot, cols] = tree(jnp.add, [jnp.exp2(x - high) for x in xs])

    def near(b, carry):
        wides = []
        for v in range(count):
            wides.append(jnp.transpose(jnp.broadcast_to(head_ref[v, pl.ds(b, 1), :], (128, 128))))
            wide_ref[v, pl.ds(pl.multiple_of(b * 128, 128), 128), :] = wides[v]
        for r in range(NEAR):
            block(b, wides, lambda rows: k1_ref[rows, r * 128 : (r + 1) * 128], r)
        return carry

    def far(b, carry):
        fetch(k2_hbm, k2_ref, sems, b).wait()
        wides = [wide_ref[v, pl.ds(pl.multiple_of(b * 128, 128), 128), :] for v in range(count)]
        for r in range(NEAR, RI):
            block(b, wides, lambda rows: k2_ref[rows, (r - NEAR) * 128 : (r - NEAR + 1) * 128], r)
        return carry

    lax.fori_loop(0, RJ, near, 0)
    lax.fori_loop(0, RJ, far, 0)
    results = []
    for v in range(count):
        tops, totals = [], []
        for r in range(RI):
            cols = slice(r * 128, (r + 1) * 128)
            high = high_ref[v, :, cols]
            top = jnp.max(high, axis=0, keepdims=True)
            tops.append(top)
            totals.append(jnp.sum(mass_ref[v, :, cols] * jnp.exp2(high - top), axis=0, keepdims=True))
        results.append(jnp.concatenate(tops, axis=0) + jnp.log(jnp.concatenate(totals, axis=0)) * LOG2E)
    return results


def pack_body(gen, ref, out):
    both = jnp.concatenate([gen[...].astype(jnp.float32), ref[...].astype(jnp.float32)], axis=0)
    out[...] = jnp.transpose(both).astype(jnp.bfloat16)


def select_set(is_gen, raw, k):
    even, odd = raw[2 * k], raw[2 * k + 1]
    gen = jnp.concatenate([even[:, :64], odd[:, :64]], axis=1)
    ref = jnp.concatenate([even[:, 64:], odd[:, 64:]], axis=1)
    return jnp.where(is_gen, gen, ref)


def unpack_b_body(info, raw, out):
    for k in range(D // 128):
        out[:, k * 128 : (k + 1) * 128] = select_set(info[1] == 1, raw, k)


def unpack_a_body(info, raw, out):
    for k in range(D // 128):
        part = select_set(info[0] == 1, raw, k)
        for n in range(4):
            out[n, :, k * 128 : (k + 1) * 128] = part


def norm_parts(values):
    values = values.astype(jnp.float32)
    values = values * values
    return functools.reduce(jnp.add, [values[:, k * 128 : (k + 1) * 128] for k in range(D // 128)])


def join_body(info, own, other, a_out, norm_out):
    first = info[2] == 0
    for half in range(2):
        for s in range(6):
            part = slice(s * 128, (s + 1) * 128)
            near, far = (own, other) if half == 0 else (other, own)
            rows = jnp.where(first, near[part, :], far[part, :])
            r = half * 6 + s
            a_out[r * 128 : (r + 1) * 128, :] = rows
            turned = jnp.transpose(norm_parts(rows))
            norm_out[r : r + 1, :] = jnp.sum(turned, axis=0, keepdims=True) * (0.5 * LOG2E / EPSILON)
    norm_out[RI:16, :] = jnp.zeros((16 - RI, 128), jnp.float32)


def cost_body(
    a_ref, norm_ref, b_ref, lift_i, k1_ref, k2_hbm, part_out, k2_ref, high_ref, mass_ref, sq_ref, out_sems
):
    scale = LOG2E / EPSILON
    heads = [lift_i[...]]
    for b in range(RJ):
        part = slice(b * 128, (b + 1) * 128)
        total = jnp.sum(norm_parts(b_ref[part, :]), axis=1, keepdims=True) * (0.5 * scale)
        sq_ref[part, :] = jnp.broadcast_to(total, (128, 128))
    stores = [fetch(k2_ref, k2_hbm, out_sems, b) for b in range(RJ)]
    order = [4, 5, 0, 1, 2, 3]
    for step in range(RI // 2 + 1):
        if step < RI // 2:
            n = order[step]
            inner = lax.dot_general(
                b_ref[...],
                a_ref[n * 256 : (n + 1) * 256, :],
                (((1,), (1,)), ((), ())),
                preferred_element_type=jnp.float32,
            )
            for s in range(2):
                r = 2 * n + s
                tile = (sq_ref[...] + norm_ref[r : r + 1, :]) - scale * inner[:, s * 128 : (s + 1) * 128]
                if r < NEAR:
                    k1_ref[:, r * 128 : (r + 1) * 128] = tile
                else:
                    k2_ref[:, (r - NEAR) * 128 : (r - NEAR + 1) * 128] = tile
        if step > 0:
            done = 2 * order[step - 1]
            source, at = (k1_ref, done) if done < NEAR else (k2_ref, done - NEAR)
            pair = lambda rows: [
                (done + s, source[rows, (at + s) * 128 : (at + s + 1) * 128]) for s in range(2)
            ]
            for b in range(RJ):
                lanes_block(pair, 1, heads, high_ref, mass_ref, b * 128, step > 1)
        if step == 1:
            for store in stores:
                store.start()
    (result,) = lanes_result(1, high_ref, mass_ref)
    for n in range(4):
        part_out[n, 0:RJ, :] = result
        part_out[n, RJ:8, :] = jnp.zeros((8 - RJ, 128), jnp.float32)
    for store in stores:
        store.wait()


def second_body(k1_ref, k2_hbm, got, lift_j, out, g1_out, k2_ref, sems, head_ref, wide_ref, high_ref, mass_ref):
    start_fetch(k2_hbm, k2_ref, sems)
    g1 = -merge(got, 4)[0:RJ, :]
    g1_out[...] = g1
    lift = lift_j[...]
    heads = [lift, lifted(g1, lift)]
    results = reduce_rows(k1_ref, k2_hbm, k2_ref, sems, heads, head_ref, wide_ref, high_ref, mass_ref)
    for n in range(8):
        for v in range(2):
            out[n, v * RI : (v + 1) * RI, :] = results[v]


def third_body(k1_ref, k2_hbm, got, lift_i, out, f2_out, k2_ref, sems, high_ref, mass_ref):
    start_fetch(k2_hbm, k2_ref, sems)
    merged = -merge(got, 8)
    f1 = merged[0:RI, :]
    f2 = 0.5 * (f1 + merged[RI : 2 * RI, :])
    f2_out[...] = f2
    lift = lift_i[...]
    heads = [lifted(f1, lift), lifted(f2, lift)]
    results = reduce_lanes(k1_ref, k2_hbm, k2_ref, sems, heads, high_ref, mass_ref)
    for n in range(4):
        for v in range(2):
            out[n, v * 8 : v * 8 + RJ, :] = results[v]
            out[n, v * 8 + RJ : v * 8 + 8, :] = jnp.zeros((8 - RJ, 128), jnp.float32)


def fourth_body(k1_ref, k2_hbm, got, lift_j, g1, out, g3_out, k2_ref, sems, head_ref, wide_ref, high_ref, mass_ref):
    start_fetch(k2_hbm, k2_ref, sems)
    merged = -merge(got, 4)
    g2 = 0.5 * (g1[...] + merged[0:RJ, :])
    g3 = 0.5 * (g2 + merged[8 : 8 + RJ, :])
    g3_out[...] = g3
    lift = lift_j[...]
    heads = [lifted(g2, lift), lifted(g3, lift)]
    results = reduce_rows(k1_ref, k2_hbm, k2_ref, sems, heads, head_ref, wide_ref, high_ref, mass_ref)
    for n in range(8):
        for v in range(2):
            out[n, v * RI : (v + 1) * RI, :] = results[v]


def fifth_body(info, k1_ref, k2_hbm, got, lift_i, f2, g3, out, k2_ref, sems, high_ref, mass_ref, f4_ref):
    start_fetch(k2_hbm, k2_ref, sems)
    merged = -merge(got, 8)
    f3 = 0.5 * (f2[...] + merged[0:RI, :])
    f4 = 0.5 * (f3 + merged[RI : 2 * RI, :])
    f4_ref[0:RI, :] = f4
    heads = [lifted(f3, lift_i[...])]
    (result,) = reduce_lanes(k1_ref, k2_hbm, k2_ref, sems, heads, high_ref, mass_ref)
    shifted = result - g3[...]
    mine = f4_ref[pl.ds(info[3], 2), :]
    for n in range(16):
        out[n, 0:RJ, :] = shifted
        out[n, RJ : RJ + 2, :] = mine


def last_body(got, gen_weight, ref_weight, ref_full_weight, pots, g4_out, share):
    g4 = merge([got[n * 4 + 1, 0:RJ, :] for n in range(4)], 4) * (-0.5 * LN2)
    g4_out[0:RJ, :] = g4
    g4_out[RJ:8, :] = jnp.zeros((8 - RJ, 128), jnp.float32)
    total = jnp.sum(jnp.where(ref_full_weight[...] > 0.0, g4 * ref_full_weight[...], 0.0))
    for n in range(4):
        own = slice(RJ, RJ + 2)
        gen_pot = got[n * 4 + 1][own, :] * LN2
        gen_self = got[n * 4][own, :] * LN2
        ref_self = got[n * 4 + 3][own, :] * LN2
        pots[n, 0:2, :] = gen_pot
        pots[n, 2:4, :] = gen_self
        pots[n, 4:6, :] = ref_self
        pots[n, 6:8, :] = jnp.zeros((2, 128), jnp.float32)
        total += jnp.sum(jnp.where(gen_weight[n] > 0.0, (gen_pot - gen_self) * gen_weight[n], 0.0))
        total -= jnp.sum(jnp.where(ref_weight[n] > 0.0, ref_self * ref_weight[n], 0.0))
    for n in range(8):
        share[n, :, :] = jnp.full((8, 128), total, jnp.float32)


F32 = jnp.float32
BF16 = jnp.bfloat16
STREAM = [pltpu.VMEM((NJ, N2), F32), pltpu.SemaphoreType.DMA((RJ,))]


def lane_scratch(count):
    return [pltpu.VMEM((count, NJ, 128), F32)] * 2


def row_scratch(count):
    return [pltpu.VMEM((count, 8, 128), F32), pltpu.VMEM((count, NJ, 128), F32)] + [pltpu.VMEM((count, 8 * RJ, NI), F32)] * 2


def stage_pack(*args):
    return call(pack_body, jax.ShapeDtypeStruct((BLOCK, 128), BF16), [VMEM, VMEM])(*args)


def stage_unpack_b(*args):
    return call(unpack_b_body, jax.ShapeDtypeStruct((BLOCK, D), BF16), [SMEM, VMEM])(*args)


def stage_unpack_a(*args):
    return call(unpack_a_body, jax.ShapeDtypeStruct((4, BLOCK, D), BF16), [SMEM, VMEM])(*args)


def stage_join(*args):
    outs = (jax.ShapeDtypeStruct((NI, D), BF16), f32(16, 128))
    return call(join_body, outs, [SMEM, VMEM, VMEM])(*args)


def stage_cost(*args):
    scratch = [
        pltpu.VMEM((NJ, N2), F32),
        *lane_scratch(1),
        pltpu.VMEM((NJ, 128), F32),
        pltpu.SemaphoreType.DMA((RJ,)),
    ]
    outs = (f32(NJ, N1), f32(ROOM, N2), f32(4, 8, 128))
    return call(cost_body, outs, [VMEM] * 4, scratch, (VMEM, HBM, VMEM))(*args)


def stage_second(*args):
    outs = (f32(8, 2 * RI, 128), f32(RJ, 128))
    return call(second_body, outs, [VMEM, HBM, VMEM, VMEM], STREAM + row_scratch(2))(*args)


def stage_third(*args):
    outs = (f32(4, 16, 128), f32(RI, 128))
    return call(third_body, outs, [VMEM, HBM, VMEM, VMEM], STREAM + lane_scratch(2))(*args)


def stage_fourth(*args):
    outs = (f32(8, 2 * RI, 128), f32(RJ, 128))
    return call(fourth_body, outs, [VMEM, HBM, VMEM, VMEM, VMEM], STREAM + row_scratch(2))(*args)


def stage_fifth(*args):
    scratch = STREAM + lane_scratch(1) + [pltpu.VMEM((16, 128), F32)]
    return call(fifth_body, f32(16, 8, 128), [SMEM, VMEM, HBM] + [VMEM] * 4, scratch)(*args)


def spread(operand, axes):
    return lax.all_to_all(operand, axes, 0, 0, tiled=True)


def local(gen_points, reference_embeddings, gen_count, ref_count):
    y, x, c, zl = (lax.axis_index(name) for name in ("y", "x", "c", "zl"))
    a_is_gen = zl < 3
    b_is_gen = zl == 0
    packed = stage_pack(jnp.transpose(gen_points), jnp.transpose(reference_embeddings))
    raw = lax.all_gather(packed, ("zh", "zl"))

    info = jnp.stack(
        [a_is_gen.astype(jnp.int32), b_is_gen.astype(jnp.int32), c, c * 6 + (3 * y) // 2]
    ).astype(jnp.int32)
    counts = jnp.stack([gen_count, ref_count]).reshape(2, 4, 4, 2)
    totals = jnp.sum(counts, axis=(1, 2, 3)).astype(jnp.float32)
    weights2 = -jnp.log(totals) * LOG2E
    place = jnp.arange(BLOCK, dtype=jnp.int32)
    a_set = jnp.where(a_is_gen, 0, 1)
    b_set = jnp.where(b_is_gen, 0, 1)
    count_i = jnp.transpose(counts[a_set, :, x]).reshape(8)
    count_j = counts[b_set, y, :, c]
    lift_i = jnp.where(place[None, :] < count_i[:, None], weights2[a_set], FAR).reshape(RI, 128)
    lift_j = jnp.where(place[None, :] < count_j[:, None], weights2[b_set], FAR).reshape(RJ, 128)
    spots = jnp.arange(256, dtype=jnp.int32) - 64 * (y % 2)
    inside = spots >= 0
    gen_in = inside[None, :] & (spots[None, :] < counts[0, y, :, c][:, None])
    ref_in = inside[None, :] & (spots[None, :] < counts[1, y, :, c][:, None])
    gen_weight = jnp.where(gen_in, 1.0 / totals[0], 0.0).reshape(4, 2, 128)
    ref_weight = jnp.where(ref_in, 1.0 / totals[1], 0.0).reshape(4, 2, 128)
    ref_full = jnp.where(place[None, :] < counts[1, y, :, c][:, None], 1.0 / totals[1], 0.0).reshape(RJ, 128)

    b_all = lax.all_gather(stage_unpack_b(info, raw), "x")
    a_half = spread(stage_unpack_a(info, raw), "y")
    a_other = lax.ppermute(a_half, "c", [(0, 1), (1, 0)])

    a_all, norms = stage_join(info, a_half.reshape(NJ, D), a_other.reshape(NJ, D))
    k1, k2, part = stage_cost(a_all, norms, b_all.reshape(NJ, D), lift_i)
    part, g1 = stage_second(k1, k2, spread(part, "x"), lift_j)
    part, f2 = stage_third(k1, k2, spread(part, ("y", "c")), lift_i)
    part, g3 = stage_fourth(k1, k2, spread(part, "x"), lift_j, g1)
    part = stage_fifth(info, k1, k2, spread(part, ("y", "c")), lift_i, f2, g3)
    got = spread(part, ("x", "zl"))
    pots, g4, share = call(
        last_body, (f32(4, 8, 128), f32(8, 128), f32(8, 8, 128)), [VMEM] * 4
    )(got, gen_weight, ref_weight, ref_full)
    divergence = jnp.sum(spread(share, ("y", "c"))[:, 0, 0])

    mine = lax.dynamic_index_in_dim(pots, x, 0, keepdims=False)
    mine = lax.dynamic_slice_in_dim(mine.reshape(4, 256), 64 * (y % 2), BLOCK, 1)
    ref_pot = lax.dynamic_slice_in_dim(g4.reshape(1024), x * BLOCK, BLOCK, 0)
    return mine[0], ref_pot, mine[1], mine[2], divergence


def solution(mesh):
    fine = Mesh(mesh.devices.reshape(4, 4, 2, 4, 4), ("y", "x", "c", "zh", "zl"))
    tile, feat = ("y", "x", "c"), ("zh", "zl")
    return jax.shard_map(
        local,
        mesh=fine,
        in_specs=(P(tile, feat), P(tile, feat), P(), P()),
        out_specs=(P(tile), P(tile), P(tile), P(tile), P()),
        check_vma=False,
    )
```

```python
import functools

import jax
import jax.numpy as jnp
from jax import lax
from jax.experimental import pallas as pl
from jax.experimental.pallas import tpu as pltpu
from jax.sharding import Mesh, PartitionSpec as P

EPSILON = 0.25
LOG2E = 1.4426950408889634
LN2 = 0.6931471805599453
FAR = -1.0e30

BLOCK = 192
D = 1024
NI = 8 * BLOCK
NJ = 4 * BLOCK
RI = NI // 128
RJ = NJ // 128
NEAR = 8
N1 = NEAR * 128
N2 = NI - N1
ROOM = 18 * NJ

VMEM = pl.BlockSpec(memory_space=pltpu.VMEM)
HBM = pl.BlockSpec(memory_space=pltpu.HBM)
SMEM = pl.BlockSpec(memory_space=pltpu.SMEM)


def f32(*shape):
    return jax.ShapeDtypeStruct(shape, jnp.float32)


def call(body, outs, ins, scratch=(), out_specs=None, mib=40):
    return pl.pallas_call(
        body,
        out_shape=outs,
        in_specs=ins,
        out_specs=jax.tree.map(lambda _: VMEM, outs) if out_specs is None else out_specs,
        scratch_shapes=list(scratch),
        compiler_params=pltpu.CompilerParams(vmem_limit_bytes=mib * 1024 * 1024),
    )


def merge(got, count):
    parts = [got[n] for n in range(count)]
    high = functools.reduce(jnp.maximum, parts)
    mass = functools.reduce(jnp.add, [jnp.exp2(part - high) for part in parts])
    return high + jnp.log(mass) * LOG2E


def lifted(pot, lift):
    return jnp.where(lift > -1.0e29, pot + lift, FAR)


def tree(op, values):
    values = list(values)
    while len(values) > 1:
        values = [op(*values[n : n + 2]) if n + 1 < len(values) else values[n] for n in range(0, len(values), 2)]
    return values[0]


def fetch(k2_hbm, k2_ref, sems, b):
    rows = pl.ds(b * 128, 128)
    return pltpu.make_async_copy(k2_hbm.at[rows], k2_ref.at[rows], sems.at[b])


def start_fetch(k2_hbm, k2_ref, sems):
    for b in range(RJ):
        fetch(k2_hbm, k2_ref, sems, b).start()


def lanes_block(tiles_of, count, heads, high_ref, mass_ref, base, joined=False):
    for group in range(16):
        rows = pl.ds(base + group * 8, 8)
        tiles = tiles_of(rows)
        for v in range(count):
            xs = [heads[v][r : r + 1, :] - tile for r, tile in tiles]
            high = tree(jnp.maximum, xs)
            if joined:
                before = high_ref[v, rows, :]
                high = jnp.maximum(high, before)
                xs.append(before)
            masses = [jnp.exp2(x - high) for x in xs]
            if joined:
                masses[-1] = masses[-1] * mass_ref[v, rows, :]
            high_ref[v, rows, :] = high
            mass_ref[v, rows, :] = tree(jnp.add, masses)


def near_tiles(k1_ref):
    return lambda rows: [(r, k1_ref[rows, r * 128 : (r + 1) * 128]) for r in range(NEAR)]


def far_tiles(k2_ref):
    return lambda rows: [(r, k2_ref[rows, (r - NEAR) * 128 : (r - NEAR + 1) * 128]) for r in range(NEAR, RI)]


def lanes_result(count, high_ref, mass_ref):
    results = []
    for v in range(count):
        rows_out = []
        for b in range(RJ):
            high = jnp.transpose(high_ref[v, b * 128 : (b + 1) * 128, :])
            mass = jnp.transpose(mass_ref[v, b * 128 : (b + 1) * 128, :])
            top = jnp.max(high, axis=0, keepdims=True)
            total = jnp.sum(mass * jnp.exp2(high - top), axis=0, keepdims=True)
            rows_out.append((top, total))
        top = jnp.concatenate([row[0] for row in rows_out], axis=0)
        total = jnp.concatenate([row[1] for row in rows_out], axis=0)
        results.append(top + jnp.log(total) * LOG2E)
    return results


def reduce_lanes(k1_ref, k2_hbm, k2_ref, sems, heads, high_ref, mass_ref):
    count = len(heads)

    def near(b, carry):
        lanes_block(near_tiles(k1_ref), count, heads, high_ref, mass_ref, pl.multiple_of(b * 128, 128))
        return carry

    def far(b, carry):
        fetch(k2_hbm, k2_ref, sems, b).wait()
        lanes_block(far_tiles(k2_ref), count, heads, high_ref, mass_ref, pl.multiple_of(b * 128, 128), True)
        return carry

    lax.fori_loop(0, RJ, near, 0)
    lax.fori_loop(0, RJ, far, 0)
    return lanes_result(count, high_ref, mass_ref)


def reduce_rows(k1_ref, k2_hbm, k2_ref, sems, heads, head_ref, wide_ref, high_ref, mass_ref):
    count = len(heads)
    for v in range(count):
        head_ref[v, 0:RJ, :] = heads[v]

    def block(b, wides, tile, r):
        spot = pl.ds(pl.multiple_of(b * 8, 8), 8)
        cols = slice(r * 128, (r + 1) * 128)
        tiles = [tile(pl.ds(b * 128 + group * 8, 8)) for group in range(16)]
        for v in range(count):
            xs = [wides[v][group * 8 : group * 8 + 8, :] - tiles[group] for group in range(16)]
            high = tree(jnp.maximum, xs)
            high_ref[v, spot, cols] = high
            mass_ref[v, spot, cols] = tree(jnp.add, [jnp.exp2(x - high) for x in xs])

    def near(b, carry):
        wides = []
        for v in range(count):
            wides.append(jnp.transpose(jnp.broadcast_to(head_ref[v, pl.ds(b, 1), :], (128, 128))))
            wide_ref[v, pl.ds(pl.multiple_of(b * 128, 128), 128), :] = wides[v]
        for r in range(NEAR):
            block(b, wides, lambda rows: k1_ref[rows, r * 128 : (r + 1) * 128], r)
        return carry

    def far(b, carry):
        fetch(k2_hbm, k2_ref, sems, b).wait()
        wides = [wide_ref[v, pl.ds(pl.multiple_of(b * 128, 128), 128), :] for v in range(count)]
        for r in range(NEAR, RI):
            block(b, wides, lambda rows: k2_ref[rows, (r - NEAR) * 128 : (r - NEAR + 1) * 128], r)
        return carry

    lax.fori_loop(0, RJ, near, 0)
    lax.fori_loop(0, RJ, far, 0)
    results = []
    for v in range(count):
        tops, totals = [], []
        for r in range(RI):
            cols = slice(r * 128, (r + 1) * 128)
            high = high_ref[v, :, cols]
            top = jnp.max(high, axis=0, keepdims=True)
            tops.append(top)
            totals.append(jnp.sum(mass_ref[v, :, cols] * jnp.exp2(high - top), axis=0, keepdims=True))
        results.append(jnp.concatenate(tops, axis=0) + jnp.log(jnp.concatenate(totals, axis=0)) * LOG2E)
    return results


def pack_body(gen, ref, out, both, sems):
    copies = [pltpu.make_async_copy(part, both.at[n], sems.at[n]) for n, part in enumerate((gen, ref))]
    for copy in copies:
        copy.start()
    for copy in copies:
        copy.wait()
    wide = jnp.concatenate([both[0].astype(jnp.float32), both[1].astype(jnp.float32)], axis=0)
    out[...] = jnp.transpose(wide).astype(jnp.bfloat16)


def select_set(is_gen, raw, k):
    even, odd = raw[2 * k], raw[2 * k + 1]
    gen = jnp.concatenate([even[:, :64], odd[:, :64]], axis=1)
    ref = jnp.concatenate([even[:, 64:], odd[:, 64:]], axis=1)
    return jnp.where(is_gen, gen, ref)


def unpack_b_body(info, raw, out):
    for k in range(D // 128):
        out[:, k * 128 : (k + 1) * 128] = select_set(info[1] == 1, raw, k)


def unpack_a_body(info, raw, b_own, out):
    del b_own
    for k in range(D // 128):
        part = select_set(info[0] == 1, raw, k)
        for n in range(4):
            out[n, :, k * 128 : (k + 1) * 128] = part


def norm_parts(values):
    values = values.astype(jnp.float32)
    values = values * values
    return functools.reduce(jnp.add, [values[:, k * 128 : (k + 1) * 128] for k in range(D // 128)])


def join_body(info, own, other, a_out, norm_out):
    first = info[2] == 0
    for half in range(2):
        for s in range(6):
            part = slice(s * 128, (s + 1) * 128)
            near, far = (own, other) if half == 0 else (other, own)
            rows = jnp.where(first, near[part, :], far[part, :])
            r = half * 6 + s
            a_out[r * 128 : (r + 1) * 128, :] = rows
            turned = jnp.transpose(norm_parts(rows))
            norm_out[r : r + 1, :] = jnp.sum(turned, axis=0, keepdims=True) * (0.5 * LOG2E / EPSILON)
    norm_out[RI:16, :] = jnp.zeros((16 - RI, 128), jnp.float32)


def cost_body(
    a_ref, norm_ref, b_ref, lift_i, k1_ref, k2_hbm, part_out, k2_ref, high_ref, mass_ref, sq_ref, out_sems
):
    scale = LOG2E / EPSILON
    heads = [lift_i[...]]
    for b in range(RJ):
        part = slice(b * 128, (b + 1) * 128)
        total = jnp.sum(norm_parts(b_ref[part, :]), axis=1, keepdims=True) * (0.5 * scale)
        sq_ref[part, :] = jnp.broadcast_to(total, (128, 128))
    stores = [fetch(k2_ref, k2_hbm, out_sems, b) for b in range(RJ)]
    order = [4, 5, 0, 1, 2, 3]
    for step in range(RI // 2 + 1):
        if step < RI // 2:
            n = order[step]
            inner = lax.dot_general(
                b_ref[...],
                a_ref[n * 256 : (n + 1) * 256, :],
                (((1,), (1,)), ((), ())),
                preferred_element_type=jnp.float32,
            )
            for s in range(2):
                r = 2 * n + s
                tile = (sq_ref[...] + norm_ref[r : r + 1, :]) - scale * inner[:, s * 128 : (s + 1) * 128]
                if r < NEAR:
                    k1_ref[:, r * 128 : (r + 1) * 128] = tile
                else:
                    k2_ref[:, (r - NEAR) * 128 : (r - NEAR + 1) * 128] = tile
        if step > 0:
            done = 2 * order[step - 1]
            source, at = (k1_ref, done) if done < NEAR else (k2_ref, done - NEAR)
            pair = lambda rows: [
                (done + s, source[rows, (at + s) * 128 : (at + s + 1) * 128]) for s in range(2)
            ]
            for b in range(RJ):
                lanes_block(pair, 1, heads, high_ref, mass_ref, b * 128, step > 1)
        if step == 1:
            for store in stores:
                store.start()
    (result,) = lanes_result(1, high_ref, mass_ref)
    for n in range(4):
        part_out[n, 0:RJ, :] = result
        part_out[n, RJ:8, :] = jnp.zeros((8 - RJ, 128), jnp.float32)
    for store in stores:
        store.wait()


def second_body(k1_ref, k2_hbm, got, lift_j, out, g1_out, k2_ref, sems, head_ref, wide_ref, high_ref, mass_ref):
    start_fetch(k2_hbm, k2_ref, sems)
    g1 = -merge(got, 4)[0:RJ, :]
    g1_out[...] = g1
    lift = lift_j[...]
    heads = [lift, lifted(g1, lift)]
    results = reduce_rows(k1_ref, k2_hbm, k2_ref, sems, heads, head_ref, wide_ref, high_ref, mass_ref)
    for n in range(8):
        for v in range(2):
            out[n, v * RI : (v + 1) * RI, :] = results[v]


def third_body(k1_ref, k2_hbm, got, lift_i, out, f2_out, k2_ref, sems, high_ref, mass_ref):
    start_fetch(k2_hbm, k2_ref, sems)
    merged = -merge(got, 8)
    f1 = merged[0:RI, :]
    f2 = 0.5 * (f1 + merged[RI : 2 * RI, :])
    f2_out[...] = f2
    lift = lift_i[...]
    heads = [lifted(f1, lift), lifted(f2, lift)]
    results = reduce_lanes(k1_ref, k2_hbm, k2_ref, sems, heads, high_ref, mass_ref)
    for n in range(4):
        for v in range(2):
            out[n, v * 8 : v * 8 + RJ, :] = results[v]
            out[n, v * 8 + RJ : v * 8 + 8, :] = jnp.zeros((8 - RJ, 128), jnp.float32)


def fourth_body(k1_ref, k2_hbm, got, lift_j, g1, out, g3_out, k2_ref, sems, head_ref, wide_ref, high_ref, mass_ref):
    start_fetch(k2_hbm, k2_ref, sems)
    merged = -merge(got, 4)
    g2 = 0.5 * (g1[...] + merged[0:RJ, :])
    g3 = 0.5 * (g2 + merged[8 : 8 + RJ, :])
    g3_out[...] = g3
    lift = lift_j[...]
    heads = [lifted(g2, lift), lifted(g3, lift)]
    results = reduce_rows(k1_ref, k2_hbm, k2_ref, sems, heads, head_ref, wide_ref, high_ref, mass_ref)
    for n in range(8):
        for v in range(2):
            out[n, v * RI : (v + 1) * RI, :] = results[v]


def fifth_body(info, k1_ref, k2_hbm, got, lift_i, f2, g3, out, k2_ref, sems, high_ref, mass_ref, f4_ref):
    start_fetch(k2_hbm, k2_ref, sems)
    merged = -merge(got, 8)
    f3 = 0.5 * (f2[...] + merged[0:RI, :])
    f4 = 0.5 * (f3 + merged[RI : 2 * RI, :])
    f4_ref[0:RI, :] = f4
    heads = [lifted(f3, lift_i[...])]
    (result,) = reduce_lanes(k1_ref, k2_hbm, k2_ref, sems, heads, high_ref, mass_ref)
    shifted = result - g3[...]
    mine = f4_ref[pl.ds(info[3], 2), :]
    for n in range(16):
        out[n, 0:RJ, :] = shifted
        out[n, RJ : RJ + 2, :] = mine


def last_body(got, gen_weight, ref_weight, ref_full_weight, pots, g4_out, share):
    g4 = merge([got[n * 4 + 1, 0:RJ, :] for n in range(4)], 4) * (-0.5 * LN2)
    g4_out[0:RJ, :] = g4
    g4_out[RJ:8, :] = jnp.zeros((8 - RJ, 128), jnp.float32)
    total = jnp.sum(jnp.where(ref_full_weight[...] > 0.0, g4 * ref_full_weight[...], 0.0))
    for n in range(4):
        own = slice(RJ, RJ + 2)
        gen_pot = got[n * 4 + 1][own, :] * LN2
        gen_self = got[n * 4][own, :] * LN2
        ref_self = got[n * 4 + 3][own, :] * LN2
        pots[n, 0:2, :] = gen_pot
        pots[n, 2:4, :] = gen_self
        pots[n, 4:6, :] = ref_self
        pots[n, 6:8, :] = jnp.zeros((2, 128), jnp.float32)
        total += jnp.sum(jnp.where(gen_weight[n] > 0.0, (gen_pot - gen_self) * gen_weight[n], 0.0))
        total -= jnp.sum(jnp.where(ref_weight[n] > 0.0, ref_self * ref_weight[n], 0.0))
    for n in range(8):
        share[n, :, :] = jnp.full((8, 128), total, jnp.float32)


F32 = jnp.float32
BF16 = jnp.bfloat16
STREAM = [pltpu.VMEM((NJ, N2), F32), pltpu.SemaphoreType.DMA((RJ,))]


def lane_scratch(count):
    return [pltpu.VMEM((count, NJ, 128), F32)] * 2


def row_scratch(count):
    return [pltpu.VMEM((count, 8, 128), F32), pltpu.VMEM((count, NJ, 128), F32)] + [pltpu.VMEM((count, 8 * RJ, NI), F32)] * 2


def stage_pack(*args):
    scratch = [pltpu.VMEM((2, 64, BLOCK), BF16), pltpu.SemaphoreType.DMA((2,))]
    out = jax.ShapeDtypeStruct((BLOCK, 128), BF16)
    return call(pack_body, out, [HBM, HBM], scratch, mib=60)(*args)


def stage_unpack_b(*args):
    return call(unpack_b_body, jax.ShapeDtypeStruct((BLOCK, D), BF16), [SMEM, VMEM])(*args)


def stage_unpack_a(*args):
    return call(unpack_a_body, jax.ShapeDtypeStruct((4, BLOCK, D), BF16), [SMEM, VMEM, HBM])(*args)


def stage_join(*args):
    outs = (jax.ShapeDtypeStruct((NI, D), BF16), f32(16, 128))
    return call(join_body, outs, [SMEM, VMEM, VMEM])(*args)


def stage_cost(*args):
    scratch = [
        pltpu.VMEM((NJ, N2), F32),
        *lane_scratch(1),
        pltpu.VMEM((NJ, 128), F32),
        pltpu.SemaphoreType.DMA((RJ,)),
    ]
    outs = (f32(NJ, N1), f32(ROOM, N2), f32(4, 8, 128))
    return call(cost_body, outs, [VMEM] * 4, scratch, (VMEM, HBM, VMEM))(*args)


def stage_second(*args):
    outs = (f32(8, 2 * RI, 128), f32(RJ, 128))
    return call(second_body, outs, [VMEM, HBM, VMEM, VMEM], STREAM + row_scratch(2))(*args)


def stage_third(*args):
    outs = (f32(4, 16, 128), f32(RI, 128))
    return call(third_body, outs, [VMEM, HBM, VMEM, VMEM], STREAM + lane_scratch(2))(*args)


def stage_fourth(*args):
    outs = (f32(8, 2 * RI, 128), f32(RJ, 128))
    return call(fourth_body, outs, [VMEM, HBM, VMEM, VMEM, VMEM], STREAM + row_scratch(2))(*args)


def stage_fifth(*args):
    scratch = STREAM + lane_scratch(1) + [pltpu.VMEM((16, 128), F32)]
    return call(fifth_body, f32(16, 8, 128), [SMEM, VMEM, HBM] + [VMEM] * 4, scratch)(*args)


def spread(operand, axes):
    return lax.all_to_all(operand, axes, 0, 0, tiled=True)


def local(gen_points, reference_embeddings, gen_count, ref_count):
    y, x, c, zl = (lax.axis_index(name) for name in ("y", "x", "c", "zl"))
    a_is_gen = zl < 3
    b_is_gen = zl == 0
    packed = stage_pack(jnp.transpose(gen_points), jnp.transpose(reference_embeddings))
    raw = lax.all_gather(packed, ("zh", "zl"))

    info = jnp.stack(
        [a_is_gen.astype(jnp.int32), b_is_gen.astype(jnp.int32), c, c * 6 + (3 * y) // 2]
    ).astype(jnp.int32)
    counts = jnp.stack([gen_count, ref_count]).reshape(2, 4, 4, 2)
    totals = jnp.sum(counts, axis=(1, 2, 3)).astype(jnp.float32)
    weights2 = -jnp.log(totals) * LOG2E
    place = jnp.arange(BLOCK, dtype=jnp.int32)
    a_set = jnp.where(a_is_gen, 0, 1)
    b_set = jnp.where(b_is_gen, 0, 1)
    count_i = jnp.transpose(counts[a_set, :, x]).reshape(8)
    count_j = counts[b_set, y, :, c]
    lift_i = jnp.where(place[None, :] < count_i[:, None], weights2[a_set], FAR).reshape(RI, 128)
    lift_j = jnp.where(place[None, :] < count_j[:, None], weights2[b_set], FAR).reshape(RJ, 128)
    spots = jnp.arange(256, dtype=jnp.int32) - 64 * (y % 2)
    inside = spots >= 0
    gen_in = inside[None, :] & (spots[None, :] < counts[0, y, :, c][:, None])
    ref_in = inside[None, :] & (spots[None, :] < counts[1, y, :, c][:, None])
    gen_weight = jnp.where(gen_in, 1.0 / totals[0], 0.0).reshape(4, 2, 128)
    ref_weight = jnp.where(ref_in, 1.0 / totals[1], 0.0).reshape(4, 2, 128)
    ref_full = jnp.where(place[None, :] < counts[1, y, :, c][:, None], 1.0 / totals[1], 0.0).reshape(RJ, 128)

    b_own = stage_unpack_b(info, raw)
    b_all = lax.all_gather(b_own, "x")
    a_half = spread(stage_unpack_a(info, raw, b_own), "y")
    a_other = lax.ppermute(a_half, "c", [(0, 1), (1, 0)])

    a_all, norms = stage_join(info, a_half.reshape(NJ, D), a_other.reshape(NJ, D))
    k1, k2, part = stage_cost(a_all, norms, b_all.reshape(NJ, D), lift_i)
    part, g1 = stage_second(k1, k2, spread(part, "x"), lift_j)
    part, f2 = stage_third(k1, k2, spread(part, ("y", "c")), lift_i)
    part, g3 = stage_fourth(k1, k2, spread(part, "x"), lift_j, g1)
    part = stage_fifth(info, k1, k2, spread(part, ("y", "c")), lift_i, f2, g3)
    got = spread(part, ("x", "zl"))
    pots, g4, share = call(
        last_body, (f32(4, 8, 128), f32(8, 128), f32(8, 8, 128)), [VMEM] * 4
    )(got, gen_weight, ref_weight, ref_full)
    divergence = jnp.sum(spread(share, ("y", "c"))[:, 0, 0])

    mine = lax.dynamic_index_in_dim(pots, x, 0, keepdims=False)
    mine = lax.dynamic_slice_in_dim(mine.reshape(4, 256), 64 * (y % 2), BLOCK, 1)
    ref_pot = lax.dynamic_slice_in_dim(g4.reshape(1024), x * BLOCK, BLOCK, 0)
    return mine[0], ref_pot, mine[1], mine[2], divergence


def solution(mesh):
    fine = Mesh(mesh.devices.reshape(4, 4, 2, 4, 4), ("y", "x", "c", "zh", "zl"))
    tile, feat = ("y", "x", "c"), ("zh", "zl")
    return jax.shard_map(
        local,
        mesh=fine,
        in_specs=(P(tile, feat), P(tile, feat), P(), P()),
        out_specs=(P(tile), P(tile), P(tile), P(tile), P()),
        check_vma=False,
    )
```

```python
import functools

import jax
import jax.numpy as jnp
from jax import lax
from jax.experimental import pallas as pl
from jax.experimental.pallas import tpu as pltpu
from jax.sharding import Mesh, PartitionSpec as P

EPSILON = 0.25
LOG2E = 1.4426950408889634
LN2 = 0.6931471805599453
FAR = -1.0e30

BLOCK = 192
D = 1024
NI = 8 * BLOCK
NJ = 4 * BLOCK
RI = NI // 128
RJ = NJ // 128
NEAR = 8
N1 = NEAR * 128
N2 = NI - N1
ROOM = 18 * NJ

VMEM = pl.BlockSpec(memory_space=pltpu.VMEM)
HBM = pl.BlockSpec(memory_space=pltpu.HBM)
SMEM = pl.BlockSpec(memory_space=pltpu.SMEM)


def f32(*shape):
    return jax.ShapeDtypeStruct(shape, jnp.float32)


def call(body, outs, ins, scratch=(), out_specs=None, mib=40):
    return pl.pallas_call(
        body,
        out_shape=outs,
        in_specs=ins,
        out_specs=jax.tree.map(lambda _: VMEM, outs) if out_specs is None else out_specs,
        scratch_shapes=list(scratch),
        compiler_params=pltpu.CompilerParams(vmem_limit_bytes=mib * 1024 * 1024),
    )


def merge(got, count):
    parts = [got[n] for n in range(count)]
    high = functools.reduce(jnp.maximum, parts)
    mass = functools.reduce(jnp.add, [jnp.exp2(part - high) for part in parts])
    return high + jnp.log(mass) * LOG2E


def lifted(pot, lift):
    return jnp.where(lift > -1.0e29, pot + lift, FAR)


def tree(op, values):
    values = list(values)
    while len(values) > 1:
        values = [op(*values[n : n + 2]) if n + 1 < len(values) else values[n] for n in range(0, len(values), 2)]
    return values[0]


def fetch(k2_hbm, k2_ref, sems, b):
    rows = pl.ds(b * 128, 128)
    return pltpu.make_async_copy(k2_hbm.at[rows], k2_ref.at[rows], sems.at[b])


def start_fetch(k2_hbm, k2_ref, sems):
    for b in range(RJ):
        fetch(k2_hbm, k2_ref, sems, b).start()


def lanes_block(tiles_of, count, heads, high_ref, mass_ref, base, joined=False):
    for group in range(16):
        rows = pl.ds(base + group * 8, 8)
        tiles = tiles_of(rows)
        for v in range(count):
            xs = [heads[v][r : r + 1, :] - tile for r, tile in tiles]
            high = tree(jnp.maximum, xs)
            if joined:
                before = high_ref[v, rows, :]
                high = jnp.maximum(high, before)
                xs.append(before)
            masses = [jnp.exp2(x - high) for x in xs]
            if joined:
                masses[-1] = masses[-1] * mass_ref[v, rows, :]
            high_ref[v, rows, :] = high
            mass_ref[v, rows, :] = tree(jnp.add, masses)


def near_tiles(k1_ref):
    return lambda rows: [(r, k1_ref[rows, r * 128 : (r + 1) * 128]) for r in range(NEAR)]


def far_tiles(k2_ref):
    return lambda rows: [(r, k2_ref[rows, (r - NEAR) * 128 : (r - NEAR + 1) * 128]) for r in range(NEAR, RI)]


def lanes_result(count, high_ref, mass_ref):
    results = []
    for v in range(count):
        rows_out = []
        for b in range(RJ):
            high = jnp.transpose(high_ref[v, b * 128 : (b + 1) * 128, :])
            mass = jnp.transpose(mass_ref[v, b * 128 : (b + 1) * 128, :])
            top = jnp.max(high, axis=0, keepdims=True)
            total = jnp.sum(mass * jnp.exp2(high - top), axis=0, keepdims=True)
            rows_out.append((top, total))
        top = jnp.concatenate([row[0] for row in rows_out], axis=0)
        total = jnp.concatenate([row[1] for row in rows_out], axis=0)
        results.append(top + jnp.log(total) * LOG2E)
    return results


def reduce_lanes(k1_ref, k2_hbm, k2_ref, sems, heads, high_ref, mass_ref):
    count = len(heads)

    def near(b, carry):
        lanes_block(near_tiles(k1_ref), count, heads, high_ref, mass_ref, pl.multiple_of(b * 128, 128))
        return carry

    def far(b, carry):
        fetch(k2_hbm, k2_ref, sems, b).wait()
        lanes_block(far_tiles(k2_ref), count, heads, high_ref, mass_ref, pl.multiple_of(b * 128, 128), True)
        return carry

    lax.fori_loop(0, RJ, near, 0)
    lax.fori_loop(0, RJ, far, 0)
    return lanes_result(count, high_ref, mass_ref)


def reduce_rows(k1_ref, k2_hbm, k2_ref, sems, heads, head_ref, wide_ref, high_ref, mass_ref):
    count = len(heads)
    for v in range(count):
        head_ref[v, 0:RJ, :] = heads[v]

    def block(b, wides, tile, r):
        spot = pl.ds(pl.multiple_of(b * 8, 8), 8)
        cols = slice(r * 128, (r + 1) * 128)
        tiles = [tile(pl.ds(b * 128 + group * 8, 8)) for group in range(16)]
        for v in range(count):
            xs = [wides[v][group * 8 : group * 8 + 8, :] - tiles[group] for group in range(16)]
            high = tree(jnp.maximum, xs)
            high_ref[v, spot, cols] = high
            mass_ref[v, spot, cols] = tree(jnp.add, [jnp.exp2(x - high) for x in xs])

    def near(b, carry):
        wides = []
        for v in range(count):
            wides.append(jnp.transpose(jnp.broadcast_to(head_ref[v, pl.ds(b, 1), :], (128, 128))))
            wide_ref[v, pl.ds(pl.multiple_of(b * 128, 128), 128), :] = wides[v]
        for r in range(NEAR):
            block(b, wides, lambda rows: k1_ref[rows, r * 128 : (r + 1) * 128], r)
        return carry

    def far(b, carry):
        fetch(k2_hbm, k2_ref, sems, b).wait()
        wides = [wide_ref[v, pl.ds(pl.multiple_of(b * 128, 128), 128), :] for v in range(count)]
        for r in range(NEAR, RI):
            block(b, wides, lambda rows: k2_ref[rows, (r - NEAR) * 128 : (r - NEAR + 1) * 128], r)
        return carry

    lax.fori_loop(0, RJ, near, 0)
    lax.fori_loop(0, RJ, far, 0)
    results = []
    for v in range(count):
        tops, totals = [], []
        for r in range(RI):
            cols = slice(r * 128, (r + 1) * 128)
            high = high_ref[v, :, cols]
            top = jnp.max(high, axis=0, keepdims=True)
            tops.append(top)
            totals.append(jnp.sum(mass_ref[v, :, cols] * jnp.exp2(high - top), axis=0, keepdims=True))
        results.append(jnp.concatenate(tops, axis=0) + jnp.log(jnp.concatenate(totals, axis=0)) * LOG2E)
    return results


def pack_body(gen, ref, out, both, sems):
    copies = [pltpu.make_async_copy(part, both.at[n], sems.at[n]) for n, part in enumerate((gen, ref))]
    for copy in copies:
        copy.start()
    for copy in copies:
        copy.wait()
    wide = jnp.concatenate([both[0].astype(jnp.float32), both[1].astype(jnp.float32)], axis=0)
    out[...] = jnp.transpose(wide).astype(jnp.bfloat16)


def unpack_body(info, raw, a_out, b_out):
    for k in range(D // 128):
        cols = slice(k * 128, (k + 1) * 128)
        even, odd = raw[2 * k], raw[2 * k + 1]
        gen = jnp.concatenate([even[:, :64], odd[:, :64]], axis=1)
        ref = jnp.concatenate([even[:, 64:], odd[:, 64:]], axis=1)
        a = jnp.where(info[0] == 1, gen, ref)
        b = jnp.where(info[1] == 1, gen, ref)
        for n in range(4):
            a_out[n, :, cols] = a
            b_out[n, :, cols] = b


def norm_parts(values):
    values = values.astype(jnp.float32)
    values = values * values
    return functools.reduce(jnp.add, [values[:, k * 128 : (k + 1) * 128] for k in range(D // 128)])


def join_body(info, own, other, cols, a_out, norm_out):
    del cols
    first = info[2] == 0
    for half in range(2):
        for s in range(6):
            part = slice(s * 128, (s + 1) * 128)
            near, far = (own, other) if half == 0 else (other, own)
            rows = jnp.where(first, near[part, :], far[part, :])
            r = half * 6 + s
            a_out[r * 128 : (r + 1) * 128, :] = rows
            turned = jnp.transpose(norm_parts(rows))
            norm_out[r : r + 1, :] = jnp.sum(turned, axis=0, keepdims=True) * (0.5 * LOG2E / EPSILON)
    norm_out[RI:16, :] = jnp.zeros((16 - RI, 128), jnp.float32)


def cost_body(
    a_ref, norm_ref, b_ref, lift_i, k1_ref, k2_hbm, part_out, k2_ref, high_ref, mass_ref, sq_ref, out_sems
):
    scale = LOG2E / EPSILON
    heads = [lift_i[...]]
    for b in range(RJ):
        part = slice(b * 128, (b + 1) * 128)
        total = jnp.sum(norm_parts(b_ref[part, :]), axis=1, keepdims=True) * (0.5 * scale)
        sq_ref[part, :] = jnp.broadcast_to(total, (128, 128))
    stores = [fetch(k2_ref, k2_hbm, out_sems, b) for b in range(RJ)]
    order = [4, 5, 0, 1, 2, 3]
    for step in range(RI // 2 + 1):
        if step < RI // 2:
            n = order[step]
            inner = lax.dot_general(
                b_ref[...],
                a_ref[n * 256 : (n + 1) * 256, :],
                (((1,), (1,)), ((), ())),
                preferred_element_type=jnp.float32,
            )
            for s in range(2):
                r = 2 * n + s
                tile = (sq_ref[...] + norm_ref[r : r + 1, :]) - scale * inner[:, s * 128 : (s + 1) * 128]
                if r < NEAR:
                    k1_ref[:, r * 128 : (r + 1) * 128] = tile
                else:
                    k2_ref[:, (r - NEAR) * 128 : (r - NEAR + 1) * 128] = tile
        if step > 0:
            done = 2 * order[step - 1]
            source, at = (k1_ref, done) if done < NEAR else (k2_ref, done - NEAR)
            pair = lambda rows: [
                (done + s, source[rows, (at + s) * 128 : (at + s + 1) * 128]) for s in range(2)
            ]
            for b in range(RJ):
                lanes_block(pair, 1, heads, high_ref, mass_ref, b * 128, step > 1)
        if step == 1:
            for store in stores:
                store.start()
    (result,) = lanes_result(1, high_ref, mass_ref)
    for n in range(4):
        part_out[n, 0:RJ, :] = result
        part_out[n, RJ:8, :] = jnp.zeros((8 - RJ, 128), jnp.float32)
    for store in stores:
        store.wait()


def second_body(k1_ref, k2_hbm, got, lift_j, out, g1_out, k2_ref, sems, head_ref, wide_ref, high_ref, mass_ref):
    start_fetch(k2_hbm, k2_ref, sems)
    g1 = -merge(got, 4)[0:RJ, :]
    g1_out[...] = g1
    lift = lift_j[...]
    heads = [lift, lifted(g1, lift)]
    results = reduce_rows(k1_ref, k2_hbm, k2_ref, sems, heads, head_ref, wide_ref, high_ref, mass_ref)
    for n in range(8):
        for v in range(2):
            out[n, v * RI : (v + 1) * RI, :] = results[v]


def third_body(k1_ref, k2_hbm, got, lift_i, out, f2_out, k2_ref, sems, high_ref, mass_ref):
    start_fetch(k2_hbm, k2_ref, sems)
    merged = -merge(got, 8)
    f1 = merged[0:RI, :]
    f2 = 0.5 * (f1 + merged[RI : 2 * RI, :])
    f2_out[...] = f2
    lift = lift_i[...]
    heads = [lifted(f1, lift), lifted(f2, lift)]
    results = reduce_lanes(k1_ref, k2_hbm, k2_ref, sems, heads, high_ref, mass_ref)
    for n in range(4):
        for v in range(2):
            out[n, v * 8 : v * 8 + RJ, :] = results[v]
            out[n, v * 8 + RJ : v * 8 + 8, :] = jnp.zeros((8 - RJ, 128), jnp.float32)


def fourth_body(k1_ref, k2_hbm, got, lift_j, g1, out, g3_out, k2_ref, sems, head_ref, wide_ref, high_ref, mass_ref):
    start_fetch(k2_hbm, k2_ref, sems)
    merged = -merge(got, 4)
    g2 = 0.5 * (g1[...] + merged[0:RJ, :])
    g3 = 0.5 * (g2 + merged[8 : 8 + RJ, :])
    g3_out[...] = g3
    lift = lift_j[...]
    heads = [lifted(g2, lift), lifted(g3, lift)]
    results = reduce_rows(k1_ref, k2_hbm, k2_ref, sems, heads, head_ref, wide_ref, high_ref, mass_ref)
    for n in range(8):
        for v in range(2):
            out[n, v * RI : (v + 1) * RI, :] = results[v]


def fifth_body(info, k1_ref, k2_hbm, got, lift_i, f2, g3, out, k2_ref, sems, high_ref, mass_ref, f4_ref):
    start_fetch(k2_hbm, k2_ref, sems)
    merged = -merge(got, 8)
    f3 = 0.5 * (f2[...] + merged[0:RI, :])
    f4 = 0.5 * (f3 + merged[RI : 2 * RI, :])
    f4_ref[0:RI, :] = f4
    heads = [lifted(f3, lift_i[...])]
    (result,) = reduce_lanes(k1_ref, k2_hbm, k2_ref, sems, heads, high_ref, mass_ref)
    shifted = result - g3[...]
    mine = f4_ref[pl.ds(info[3], 2), :]
    for n in range(16):
        out[n, 0:RJ, :] = shifted
        out[n, RJ : RJ + 2, :] = mine


def last_body(got, gen_weight, ref_weight, ref_full_weight, pots, g4_out, share):
    g4 = merge([got[n * 4 + 1, 0:RJ, :] for n in range(4)], 4) * (-0.5 * LN2)
    g4_out[0:RJ, :] = g4
    g4_out[RJ:8, :] = jnp.zeros((8 - RJ, 128), jnp.float32)
    total = jnp.sum(jnp.where(ref_full_weight[...] > 0.0, g4 * ref_full_weight[...], 0.0))
    for n in range(4):
        own = slice(RJ, RJ + 2)
        gen_pot = got[n * 4 + 1][own, :] * LN2
        gen_self = got[n * 4][own, :] * LN2
        ref_self = got[n * 4 + 3][own, :] * LN2
        pots[n, 0:2, :] = gen_pot
        pots[n, 2:4, :] = gen_self
        pots[n, 4:6, :] = ref_self
        pots[n, 6:8, :] = jnp.zeros((2, 128), jnp.float32)
        total += jnp.sum(jnp.where(gen_weight[n] > 0.0, (gen_pot - gen_self) * gen_weight[n], 0.0))
        total -= jnp.sum(jnp.where(ref_weight[n] > 0.0, ref_self * ref_weight[n], 0.0))
    for n in range(8):
        share[n, :, :] = jnp.full((8, 128), total, jnp.float32)


F32 = jnp.float32
BF16 = jnp.bfloat16
STREAM = [pltpu.VMEM((NJ, N2), F32), pltpu.SemaphoreType.DMA((RJ,))]


def lane_scratch(count):
    return [pltpu.VMEM((count, NJ, 128), F32)] * 2


def row_scratch(count):
    return [pltpu.VMEM((count, 8, 128), F32), pltpu.VMEM((count, NJ, 128), F32)] + [pltpu.VMEM((count, 8 * RJ, NI), F32)] * 2


def stage_pack(*args):
    scratch = [pltpu.VMEM((2, 64, BLOCK), BF16), pltpu.SemaphoreType.DMA((2,))]
    out = jax.ShapeDtypeStruct((BLOCK, 128), BF16)
    return call(pack_body, out, [HBM, HBM], scratch, mib=60)(*args)


def stage_unpack(*args):
    outs = (jax.ShapeDtypeStruct((4, BLOCK, D), BF16),) * 2
    return call(unpack_body, outs, [SMEM, VMEM])(*args)


def stage_join(*args):
    outs = (jax.ShapeDtypeStruct((NI, D), BF16), f32(16, 128))
    return call(join_body, outs, [SMEM, VMEM, VMEM, HBM])(*args)


def stage_cost(*args):
    scratch = [
        pltpu.VMEM((NJ, N2), F32),
        *lane_scratch(1),
        pltpu.VMEM((NJ, 128), F32),
        pltpu.SemaphoreType.DMA((RJ,)),
    ]
    outs = (f32(NJ, N1), f32(ROOM, N2), f32(4, 8, 128))
    return call(cost_body, outs, [VMEM] * 4, scratch, (VMEM, HBM, VMEM))(*args)


def stage_second(*args):
    outs = (f32(8, 2 * RI, 128), f32(RJ, 128))
    return call(second_body, outs, [VMEM, HBM, VMEM, VMEM], STREAM + row_scratch(2))(*args)


def stage_third(*args):
    outs = (f32(4, 16, 128), f32(RI, 128))
    return call(third_body, outs, [VMEM, HBM, VMEM, VMEM], STREAM + lane_scratch(2))(*args)


def stage_fourth(*args):
    outs = (f32(8, 2 * RI, 128), f32(RJ, 128))
    return call(fourth_body, outs, [VMEM, HBM, VMEM, VMEM, VMEM], STREAM + row_scratch(2))(*args)


def stage_fifth(*args):
    scratch = STREAM + lane_scratch(1) + [pltpu.VMEM((16, 128), F32)]
    return call(fifth_body, f32(16, 8, 128), [SMEM, VMEM, HBM] + [VMEM] * 4, scratch)(*args)


def spread(operand, axes):
    return lax.all_to_all(operand, axes, 0, 0, tiled=True)


def local(gen_points, reference_embeddings, gen_count, ref_count):
    y, x, c, zl = (lax.axis_index(name) for name in ("y", "x", "c", "zl"))
    a_is_gen = zl < 3
    b_is_gen = zl == 0
    packed = stage_pack(jnp.transpose(gen_points), jnp.transpose(reference_embeddings))
    raw = lax.all_gather(packed, ("zh", "zl"))

    info = jnp.stack(
        [a_is_gen.astype(jnp.int32), b_is_gen.astype(jnp.int32), c, c * 6 + (3 * y) // 2]
    ).astype(jnp.int32)
    counts = jnp.stack([gen_count, ref_count]).reshape(2, 4, 4, 2)
    totals = jnp.sum(counts, axis=(1, 2, 3)).astype(jnp.float32)
    weights2 = -jnp.log(totals) * LOG2E
    place = jnp.arange(BLOCK, dtype=jnp.int32)
    a_set = jnp.where(a_is_gen, 0, 1)
    b_set = jnp.where(b_is_gen, 0, 1)
    count_i = jnp.transpose(counts[a_set, :, x]).reshape(8)
    count_j = counts[b_set, y, :, c]
    lift_i = jnp.where(place[None, :] < count_i[:, None], weights2[a_set], FAR).reshape(RI, 128)
    lift_j = jnp.where(place[None, :] < count_j[:, None], weights2[b_set], FAR).reshape(RJ, 128)
    spots = jnp.arange(256, dtype=jnp.int32) - 64 * (y % 2)
    inside = spots >= 0
    gen_in = inside[None, :] & (spots[None, :] < counts[0, y, :, c][:, None])
    ref_in = inside[None, :] & (spots[None, :] < counts[1, y, :, c][:, None])
    gen_weight = jnp.where(gen_in, 1.0 / totals[0], 0.0).reshape(4, 2, 128)
    ref_weight = jnp.where(ref_in, 1.0 / totals[1], 0.0).reshape(4, 2, 128)
    ref_full = jnp.where(place[None, :] < counts[1, y, :, c][:, None], 1.0 / totals[1], 0.0).reshape(RJ, 128)

    a_wide, b_wide = stage_unpack(info, raw)
    a_half = spread(a_wide, "y")
    a_other = lax.ppermute(a_half, "c", [(0, 1), (1, 0)])
    b_all = spread(b_wide, "x")

    b_all = b_all.reshape(NJ, D)
    a_all, norms = stage_join(info, a_half.reshape(NJ, D), a_other.reshape(NJ, D), b_all)
    k1, k2, part = stage_cost(a_all, norms, b_all, lift_i)
    part, g1 = stage_second(k1, k2, spread(part, "x"), lift_j)
    part, f2 = stage_third(k1, k2, spread(part, ("y", "c")), lift_i)
    part, g3 = stage_fourth(k1, k2, spread(part, "x"), lift_j, g1)
    part = stage_fifth(info, k1, k2, spread(part, ("y", "c")), lift_i, f2, g3)
    got = spread(part, ("x", "zl"))
    pots, g4, share = call(
        last_body, (f32(4, 8, 128), f32(8, 128), f32(8, 8, 128)), [VMEM] * 4
    )(got, gen_weight, ref_weight, ref_full)
    divergence = jnp.sum(spread(share, ("y", "c"))[:, 0, 0])

    mine = lax.dynamic_index_in_dim(pots, x, 0, keepdims=False)
    mine = lax.dynamic_slice_in_dim(mine.reshape(4, 256), 64 * (y % 2), BLOCK, 1)
    ref_pot = lax.dynamic_slice_in_dim(g4.reshape(1024), x * BLOCK, BLOCK, 0)
    return mine[0], ref_pot, mine[1], mine[2], divergence


def solution(mesh):
    fine = Mesh(mesh.devices.reshape(4, 4, 2, 4, 4), ("y", "x", "c", "zh", "zl"))
    tile, feat = ("y", "x", "c"), ("zh", "zl")
    return jax.shard_map(
        local,
        mesh=fine,
        in_specs=(P(tile, feat), P(tile, feat), P(), P()),
        out_specs=(P(tile), P(tile), P(tile), P(tile), P()),
        check_vma=False,
    )
```

```python
import functools

import jax
import jax.numpy as jnp
from jax import lax
from jax.experimental import pallas as pl
from jax.experimental.pallas import tpu as pltpu
from jax.sharding import Mesh, PartitionSpec as P

EPSILON = 0.25
LOG2E = 1.4426950408889634
LN2 = 0.6931471805599453
FAR = -1.0e30

BLOCK = 192
D = 1024
NI = 8 * BLOCK
NJ = 4 * BLOCK
RI = NI // 128
RJ = NJ // 128
NEAR = 8
N1 = NEAR * 128
N2 = NI - N1
ROOM = 18 * NJ

VMEM = pl.BlockSpec(memory_space=pltpu.VMEM)
HBM = pl.BlockSpec(memory_space=pltpu.HBM)
SMEM = pl.BlockSpec(memory_space=pltpu.SMEM)


def f32(*shape):
    return jax.ShapeDtypeStruct(shape, jnp.float32)


def call(body, outs, ins, scratch=(), out_specs=None, mib=40):
    return pl.pallas_call(
        body,
        out_shape=outs,
        in_specs=ins,
        out_specs=jax.tree.map(lambda _: VMEM, outs) if out_specs is None else out_specs,
        scratch_shapes=list(scratch),
        compiler_params=pltpu.CompilerParams(vmem_limit_bytes=mib * 1024 * 1024),
    )


def merge(got, count):
    parts = [got[n] for n in range(count)]
    high = functools.reduce(jnp.maximum, parts)
    mass = functools.reduce(jnp.add, [jnp.exp2(part - high) for part in parts])
    return high + jnp.log(mass) * LOG2E


def lifted(pot, lift):
    return jnp.where(lift > -1.0e29, pot + lift, FAR)


def tree(op, values):
    values = list(values)
    while len(values) > 1:
        values = [op(*values[n : n + 2]) if n + 1 < len(values) else values[n] for n in range(0, len(values), 2)]
    return values[0]


def fetch(k2_hbm, k2_ref, sems, b):
    rows = pl.ds(b * 128, 128)
    return pltpu.make_async_copy(k2_hbm.at[rows], k2_ref.at[rows], sems.at[b])


def start_fetch(k2_hbm, k2_ref, sems):
    for b in range(RJ):
        fetch(k2_hbm, k2_ref, sems, b).start()


def lanes_block(tiles_of, count, heads, high_ref, mass_ref, base, joined=False):
    for group in range(16):
        rows = pl.ds(base + group * 8, 8)
        tiles = tiles_of(rows)
        for v in range(count):
            xs = [heads[v][r : r + 1, :] - tile for r, tile in tiles]
            high = tree(jnp.maximum, xs)
            if joined:
                before = high_ref[v, rows, :]
                high = jnp.maximum(high, before)
                xs.append(before)
            masses = [jnp.exp2(x - high) for x in xs]
            if joined:
                masses[-1] = masses[-1] * mass_ref[v, rows, :]
            high_ref[v, rows, :] = high
            mass_ref[v, rows, :] = tree(jnp.add, masses)


def near_tiles(k1_ref):
    return lambda rows: [(r, k1_ref[rows, r * 128 : (r + 1) * 128]) for r in range(NEAR)]


def far_tiles(k2_ref):
    return lambda rows: [(r, k2_ref[rows, (r - NEAR) * 128 : (r - NEAR + 1) * 128]) for r in range(NEAR, RI)]


def lanes_result(count, high_ref, mass_ref):
    results = []
    for v in range(count):
        rows_out = []
        for b in range(RJ):
            high = jnp.transpose(high_ref[v, b * 128 : (b + 1) * 128, :])
            mass = jnp.transpose(mass_ref[v, b * 128 : (b + 1) * 128, :])
            top = jnp.max(high, axis=0, keepdims=True)
            total = jnp.sum(mass * jnp.exp2(high - top), axis=0, keepdims=True)
            rows_out.append((top, total))
        top = jnp.concatenate([row[0] for row in rows_out], axis=0)
        total = jnp.concatenate([row[1] for row in rows_out], axis=0)
        results.append(top + jnp.log(total) * LOG2E)
    return results


def reduce_lanes(k1_ref, k2_hbm, k2_ref, sems, heads, high_ref, mass_ref):
    count = len(heads)

    def near(b, carry):
        lanes_block(near_tiles(k1_ref), count, heads, high_ref, mass_ref, pl.multiple_of(b * 128, 128))
        return carry

    def far(b, carry):
        fetch(k2_hbm, k2_ref, sems, b).wait()
        lanes_block(far_tiles(k2_ref), count, heads, high_ref, mass_ref, pl.multiple_of(b * 128, 128), True)
        return carry

    lax.fori_loop(0, RJ, near, 0)
    lax.fori_loop(0, RJ, far, 0)
    return lanes_result(count, high_ref, mass_ref)


def reduce_rows(k1_ref, k2_hbm, k2_ref, sems, heads, head_ref, wide_ref, high_ref, mass_ref):
    count = len(heads)
    for v in range(count):
        head_ref[v, 0:RJ, :] = heads[v]

    def block(b, wides, tile, r):
        spot = pl.ds(pl.multiple_of(b * 8, 8), 8)
        cols = slice(r * 128, (r + 1) * 128)
        tiles = [tile(pl.ds(b * 128 + group * 8, 8)) for group in range(16)]
        for v in range(count):
            xs = [wides[v][group * 8 : group * 8 + 8, :] - tiles[group] for group in range(16)]
            high = tree(jnp.maximum, xs)
            high_ref[v, spot, cols] = high
            mass_ref[v, spot, cols] = tree(jnp.add, [jnp.exp2(x - high) for x in xs])

    def near(b, carry):
        wides = []
        for v in range(count):
            wides.append(jnp.transpose(jnp.broadcast_to(head_ref[v, pl.ds(b, 1), :], (128, 128))))
            wide_ref[v, pl.ds(pl.multiple_of(b * 128, 128), 128), :] = wides[v]
        for r in range(NEAR):
            block(b, wides, lambda rows: k1_ref[rows, r * 128 : (r + 1) * 128], r)
        return carry

    def far(b, carry):
        fetch(k2_hbm, k2_ref, sems, b).wait()
        wides = [wide_ref[v, pl.ds(pl.multiple_of(b * 128, 128), 128), :] for v in range(count)]
        for r in range(NEAR, RI):
            block(b, wides, lambda rows: k2_ref[rows, (r - NEAR) * 128 : (r - NEAR + 1) * 128], r)
        return carry

    lax.fori_loop(0, RJ, near, 0)
    lax.fori_loop(0, RJ, far, 0)
    results = []
    for v in range(count):
        tops, totals = [], []
        for r in range(RI):
            cols = slice(r * 128, (r + 1) * 128)
            high = high_ref[v, :, cols]
            top = jnp.max(high, axis=0, keepdims=True)
            tops.append(top)
            totals.append(jnp.sum(mass_ref[v, :, cols] * jnp.exp2(high - top), axis=0, keepdims=True))
        results.append(jnp.concatenate(tops, axis=0) + jnp.log(jnp.concatenate(totals, axis=0)) * LOG2E)
    return results


def pack_body(gen, ref, out, both, sems):
    copies = [pltpu.make_async_copy(part, both.at[n], sems.at[n]) for n, part in enumerate((gen, ref))]
    for copy in copies:
        copy.start()
    for copy in copies:
        copy.wait()
    wide = jnp.concatenate([both[0].astype(jnp.float32), both[1].astype(jnp.float32)], axis=0)
    out[...] = jnp.transpose(wide).astype(jnp.bfloat16)


def unpack_body(which, info, raw, *refs):
    out = refs[-1]
    for k in range(D // 128):
        cols = slice(k * 128, (k + 1) * 128)
        even, odd = raw[2 * k], raw[2 * k + 1]
        gen = jnp.concatenate([even[:, :64], odd[:, :64]], axis=1)
        ref = jnp.concatenate([even[:, 64:], odd[:, 64:]], axis=1)
        part = jnp.where(info[which] == 1, gen, ref)
        for n in range(4):
            out[n, :, cols] = part


def norm_parts(values):
    values = values.astype(jnp.float32)
    values = values * values
    return functools.reduce(jnp.add, [values[:, k * 128 : (k + 1) * 128] for k in range(D // 128)])


def join_body(info, gen_count, ref_count, own, other, cols, a_out, norm_out, lift_i, lift_j, weights):
    del cols
    c, x, y = info[2], info[4], info[5]
    first = c == 0
    for half in range(2):
        for s in range(6):
            part = slice(s * 128, (s + 1) * 128)
            near, far = (own, other) if half == 0 else (other, own)
            rows = jnp.where(first, near[part, :], far[part, :])
            r = half * 6 + s
            a_out[r * 128 : (r + 1) * 128, :] = rows
            turned = jnp.transpose(norm_parts(rows))
            norm_out[r : r + 1, :] = jnp.sum(turned, axis=0, keepdims=True) * (0.5 * LOG2E / EPSILON)
    norm_out[RI:16, :] = jnp.zeros((16 - RI, 128), jnp.float32)

    def total(counts):
        return jnp.full((8, 128), functools.reduce(jnp.add, [counts[n] for n in range(32)]).astype(jnp.float32))

    def number(is_gen, t):
        return jnp.where(is_gen, gen_count[t], ref_count[t])

    def flat(rows):
        shape = (rows, 128)
        return lax.broadcasted_iota(jnp.int32, shape, 0) * 128 + lax.broadcasted_iota(jnp.int32, shape, 1)

    def valid(spots, starts, counts):
        inside = [(spots >= start) & (spots < start + count) for start, count in zip(starts, counts)]
        return functools.reduce(jnp.logical_or, inside)

    a_is_gen, b_is_gen = info[0] == 1, info[1] == 1
    totals = total(gen_count), total(ref_count)
    gen_log, ref_log = (-jnp.log(value) * LOG2E for value in totals)
    counts = [number(a_is_gen, ((n % 4) * 4 + x) * 2 + n // 4) for n in range(8)]
    ok = valid(flat(16), [n * BLOCK for n in range(8)], counts)
    log_a = jnp.where(a_is_gen, gen_log, ref_log)
    lift_i[...] = jnp.where(ok, jnp.concatenate([log_a, log_a], axis=0), FAR)
    here = [(y * 4 + n) * 2 + c for n in range(4)]
    starts = [n * BLOCK for n in range(4)]
    ok = valid(flat(8), starts, [number(b_is_gen, t) for t in here])
    lift_j[...] = jnp.where(ok, jnp.where(b_is_gen, gen_log, ref_log), FAR)
    shift = 64 * lax.rem(y, 2)
    windows = [n * 256 + shift for n in range(4)]
    for n, counts in enumerate((gen_count, ref_count)):
        ok = valid(flat(8), windows, [counts[t] for t in here])
        weights[n * 8 : n * 8 + 8, :] = jnp.where(ok, 1.0 / totals[n], 0.0)
    ok = valid(flat(8), starts, [ref_count[t] for t in here])
    weights[16:24, :] = jnp.where(ok, 1.0 / totals[1], 0.0)


def cost_body(
    a_ref, norm_ref, b_ref, lift_i, k1_ref, k2_hbm, part_out, k2_ref, high_ref, mass_ref, sq_ref, out_sems
):
    scale = LOG2E / EPSILON
    heads = [lift_i[0:RI, :]]
    for b in range(RJ):
        part = slice(b * 128, (b + 1) * 128)
        total = jnp.sum(norm_parts(b_ref[part, :]), axis=1, keepdims=True) * (0.5 * scale)
        sq_ref[part, :] = jnp.broadcast_to(total, (128, 128))
    stores = [fetch(k2_ref, k2_hbm, out_sems, b) for b in range(RJ)]
    order = [4, 5, 0, 1, 2, 3]
    for step in range(RI // 2 + 1):
        if step < RI // 2:
            n = order[step]
            inner = lax.dot_general(
                b_ref[...],
                a_ref[n * 256 : (n + 1) * 256, :],
                (((1,), (1,)), ((), ())),
                preferred_element_type=jnp.float32,
            )
            for s in range(2):
                r = 2 * n + s
                tile = (sq_ref[...] + norm_ref[r : r + 1, :]) - scale * inner[:, s * 128 : (s + 1) * 128]
                if r < NEAR:
                    k1_ref[:, r * 128 : (r + 1) * 128] = tile
                else:
                    k2_ref[:, (r - NEAR) * 128 : (r - NEAR + 1) * 128] = tile
        if step > 0:
            done = 2 * order[step - 1]
            source, at = (k1_ref, done) if done < NEAR else (k2_ref, done - NEAR)
            pair = lambda rows: [
                (done + s, source[rows, (at + s) * 128 : (at + s + 1) * 128]) for s in range(2)
            ]
            for b in range(RJ):
                lanes_block(pair, 1, heads, high_ref, mass_ref, b * 128, step > 1)
        if step == 1:
            for store in stores:
                store.start()
    (result,) = lanes_result(1, high_ref, mass_ref)
    for n in range(4):
        part_out[n, 0:RJ, :] = result
        part_out[n, RJ:8, :] = jnp.zeros((8 - RJ, 128), jnp.float32)
    for store in stores:
        store.wait()


def second_body(k1_ref, k2_hbm, got, lift_j, out, g1_out, k2_ref, sems, head_ref, wide_ref, high_ref, mass_ref):
    start_fetch(k2_hbm, k2_ref, sems)
    g1 = -merge(got, 4)[0:RJ, :]
    g1_out[...] = g1
    lift = lift_j[0:RJ, :]
    heads = [lift, lifted(g1, lift)]
    results = reduce_rows(k1_ref, k2_hbm, k2_ref, sems, heads, head_ref, wide_ref, high_ref, mass_ref)
    for n in range(8):
        for v in range(2):
            out[n, v * RI : (v + 1) * RI, :] = results[v]


def third_body(k1_ref, k2_hbm, got, lift_i, out, f2_out, k2_ref, sems, high_ref, mass_ref):
    start_fetch(k2_hbm, k2_ref, sems)
    merged = -merge(got, 8)
    f1 = merged[0:RI, :]
    f2 = 0.5 * (f1 + merged[RI : 2 * RI, :])
    f2_out[...] = f2
    lift = lift_i[0:RI, :]
    heads = [lifted(f1, lift), lifted(f2, lift)]
    results = reduce_lanes(k1_ref, k2_hbm, k2_ref, sems, heads, high_ref, mass_ref)
    for n in range(4):
        for v in range(2):
            out[n, v * 8 : v * 8 + RJ, :] = results[v]
            out[n, v * 8 + RJ : v * 8 + 8, :] = jnp.zeros((8 - RJ, 128), jnp.float32)


def fourth_body(k1_ref, k2_hbm, got, lift_j, g1, out, g3_out, k2_ref, sems, head_ref, wide_ref, high_ref, mass_ref):
    start_fetch(k2_hbm, k2_ref, sems)
    merged = -merge(got, 4)
    g2 = 0.5 * (g1[...] + merged[0:RJ, :])
    g3 = 0.5 * (g2 + merged[8 : 8 + RJ, :])
    g3_out[...] = g3
    lift = lift_j[0:RJ, :]
    heads = [lifted(g2, lift), lifted(g3, lift)]
    results = reduce_rows(k1_ref, k2_hbm, k2_ref, sems, heads, head_ref, wide_ref, high_ref, mass_ref)
    for n in range(8):
        for v in range(2):
            out[n, v * RI : (v + 1) * RI, :] = results[v]


def fifth_body(info, k1_ref, k2_hbm, got, lift_i, f2, g3, out, k2_ref, sems, high_ref, mass_ref, f4_ref):
    start_fetch(k2_hbm, k2_ref, sems)
    merged = -merge(got, 8)
    f3 = 0.5 * (f2[...] + merged[0:RI, :])
    f4 = 0.5 * (f3 + merged[RI : 2 * RI, :])
    f4_ref[0:RI, :] = f4
    heads = [lifted(f3, lift_i[0:RI, :])]
    (result,) = reduce_lanes(k1_ref, k2_hbm, k2_ref, sems, heads, high_ref, mass_ref)
    shifted = result - g3[...]
    mine = f4_ref[pl.ds(info[3], 2), :]
    for n in range(16):
        out[n, 0:RJ, :] = shifted
        out[n, RJ : RJ + 2, :] = mine


def last_body(got, weights, pots, g4_out, share):
    g4 = merge([got[n * 4 + 1, 0:RJ, :] for n in range(4)], 4) * (-0.5 * LN2)
    g4_out[0:RJ, :] = g4
    g4_out[RJ:8, :] = jnp.zeros((8 - RJ, 128), jnp.float32)
    weight = weights[16 : 16 + RJ, :]
    total = jnp.sum(jnp.where(weight > 0.0, g4 * weight, 0.0))
    for n in range(4):
        own = slice(RJ, RJ + 2)
        gen_pot = got[n * 4 + 1][own, :] * LN2
        gen_self = got[n * 4][own, :] * LN2
        ref_self = got[n * 4 + 3][own, :] * LN2
        pots[n, 0:2, :] = gen_pot
        pots[n, 2:4, :] = gen_self
        pots[n, 4:6, :] = ref_self
        pots[n, 6:8, :] = jnp.zeros((2, 128), jnp.float32)
        weight = weights[2 * n : 2 * n + 2, :]
        total += jnp.sum(jnp.where(weight > 0.0, (gen_pot - gen_self) * weight, 0.0))
        weight = weights[8 + 2 * n : 8 + 2 * n + 2, :]
        total -= jnp.sum(jnp.where(weight > 0.0, ref_self * weight, 0.0))
    for n in range(8):
        share[n, :, :] = jnp.full((8, 128), total, jnp.float32)


F32 = jnp.float32
BF16 = jnp.bfloat16
STREAM = [pltpu.VMEM((NJ, N2), F32), pltpu.SemaphoreType.DMA((RJ,))]


def lane_scratch(count):
    return [pltpu.VMEM((count, NJ, 128), F32)] * 2


def row_scratch(count):
    return [pltpu.VMEM((count, 8, 128), F32), pltpu.VMEM((count, NJ, 128), F32)] + [pltpu.VMEM((count, 8 * RJ, NI), F32)] * 2


def stage_pack(*args):
    scratch = [pltpu.VMEM((2, 64, BLOCK), BF16), pltpu.SemaphoreType.DMA((2,))]
    out = jax.ShapeDtypeStruct((BLOCK, 128), BF16)
    return call(pack_body, out, [HBM, HBM], scratch, mib=60)(*args)


def stage_unpack(which, *args):
    out = jax.ShapeDtypeStruct((4, BLOCK, D), BF16)
    return call(functools.partial(unpack_body, which), out, [SMEM, VMEM, HBM][: len(args)])(*args)


def stage_join(*args):
    outs = (jax.ShapeDtypeStruct((NI, D), BF16), f32(16, 128), f32(16, 128), f32(8, 128), f32(24, 128))
    return call(join_body, outs, [SMEM, SMEM, SMEM, VMEM, VMEM, HBM])(*args)


def stage_cost(*args):
    scratch = [
        pltpu.VMEM((NJ, N2), F32),
        *lane_scratch(1),
        pltpu.VMEM((NJ, 128), F32),
        pltpu.SemaphoreType.DMA((RJ,)),
    ]
    outs = (f32(NJ, N1), f32(ROOM, N2), f32(4, 8, 128))
    return call(cost_body, outs, [VMEM] * 4, scratch, (VMEM, HBM, VMEM))(*args)


def stage_second(*args):
    outs = (f32(8, 2 * RI, 128), f32(RJ, 128))
    return call(second_body, outs, [VMEM, HBM, VMEM, VMEM], STREAM + row_scratch(2))(*args)


def stage_third(*args):
    outs = (f32(4, 16, 128), f32(RI, 128))
    return call(third_body, outs, [VMEM, HBM, VMEM, VMEM], STREAM + lane_scratch(2))(*args)


def stage_fourth(*args):
    outs = (f32(8, 2 * RI, 128), f32(RJ, 128))
    return call(fourth_body, outs, [VMEM, HBM, VMEM, VMEM, VMEM], STREAM + row_scratch(2))(*args)


def stage_fifth(*args):
    scratch = STREAM + lane_scratch(1) + [pltpu.VMEM((16, 128), F32)]
    return call(fifth_body, f32(16, 8, 128), [SMEM, VMEM, HBM] + [VMEM] * 4, scratch)(*args)


def spread(operand, axes):
    return lax.all_to_all(operand, axes, 0, 0, tiled=True)


def local(gen_points, reference_embeddings, gen_count, ref_count):
    y, x, c, zl = (lax.axis_index(name) for name in ("y", "x", "c", "zl"))
    a_is_gen = zl < 3
    b_is_gen = zl == 0
    packed = stage_pack(jnp.transpose(gen_points), jnp.transpose(reference_embeddings))
    raw = lax.all_gather(packed, ("zh", "zl"))

    info = jnp.stack(
        [a_is_gen.astype(jnp.int32), b_is_gen.astype(jnp.int32), c, c * 6 + (3 * y) // 2, x, y]
    ).astype(jnp.int32)
    a_half = spread(stage_unpack(0, info, raw), "y")
    a_other = lax.ppermute(a_half, "c", [(0, 1), (1, 0)])
    b_all = spread(stage_unpack(1, info, raw, a_half), "x")
    b_all = b_all.reshape(NJ, D)
    a_all, norms, lift_i, lift_j, weights = stage_join(
        info, gen_count, ref_count, a_half.reshape(NJ, D), a_other.reshape(NJ, D), b_all
    )
    k1, k2, part = stage_cost(a_all, norms, b_all, lift_i)
    part, g1 = stage_second(k1, k2, spread(part, "x"), lift_j)
    part, f2 = stage_third(k1, k2, spread(part, ("y", "c")), lift_i)
    part, g3 = stage_fourth(k1, k2, spread(part, "x"), lift_j, g1)
    part = stage_fifth(info, k1, k2, spread(part, ("y", "c")), lift_i, f2, g3)
    got = spread(part, ("x", "zl"))
    pots, g4, share = call(last_body, (f32(4, 8, 128), f32(8, 128), f32(8, 8, 128)), [VMEM, VMEM])(got, weights)
    divergence = jnp.sum(spread(share, ("y", "c"))[:, 0, 0])

    mine = lax.dynamic_index_in_dim(pots, x, 0, keepdims=False)
    mine = lax.dynamic_slice_in_dim(mine.reshape(4, 256), 64 * (y % 2), BLOCK, 1)
    ref_pot = lax.dynamic_slice_in_dim(g4.reshape(1024), x * BLOCK, BLOCK, 0)
    return mine[0], ref_pot, mine[1], mine[2], divergence


def solution(mesh):
    fine = Mesh(mesh.devices.reshape(4, 4, 2, 4, 4), ("y", "x", "c", "zh", "zl"))
    tile, feat = ("y", "x", "c"), ("zh", "zl")
    return jax.shard_map(
        local,
        mesh=fine,
        in_specs=(P(tile, feat), P(tile, feat), P(), P()),
        out_specs=(P(tile), P(tile), P(tile), P(tile), P()),
        check_vma=False,
    )
```

```python
import functools

import jax
import jax.numpy as jnp
from jax import lax
from jax.experimental import pallas as pl
from jax.experimental.pallas import tpu as pltpu
from jax.sharding import Mesh, PartitionSpec as P

EPSILON = 0.25
LOG2E = 1.4426950408889634
LN2 = 0.6931471805599453
FAR = -1.0e30

BLOCK = 192
D = 1024
NI = 8 * BLOCK
NJ = 4 * BLOCK
RI = NI // 128
RJ = NJ // 128
NEAR = 8
N1 = NEAR * 128
N2 = NI - N1
ROOM = 18 * NJ

VMEM = pl.BlockSpec(memory_space=pltpu.VMEM)
HBM = pl.BlockSpec(memory_space=pltpu.HBM)
SMEM = pl.BlockSpec(memory_space=pltpu.SMEM)


def f32(*shape):
    return jax.ShapeDtypeStruct(shape, jnp.float32)


def call(body, outs, ins, scratch=(), out_specs=None, mib=40):
    return pl.pallas_call(
        body,
        out_shape=outs,
        in_specs=ins,
        out_specs=jax.tree.map(lambda _: VMEM, outs) if out_specs is None else out_specs,
        scratch_shapes=list(scratch),
        compiler_params=pltpu.CompilerParams(vmem_limit_bytes=mib * 1024 * 1024),
    )


def merge(got, count):
    parts = [got[n] for n in range(count)]
    high = functools.reduce(jnp.maximum, parts)
    mass = functools.reduce(jnp.add, [jnp.exp2(part - high) for part in parts])
    return high + jnp.log(mass) * LOG2E


def lifted(pot, lift):
    return jnp.where(lift > -1.0e29, pot + lift, FAR)


def tree(op, values):
    values = list(values)
    while len(values) > 1:
        values = [op(*values[n : n + 2]) if n + 1 < len(values) else values[n] for n in range(0, len(values), 2)]
    return values[0]


def fetch(k2_hbm, k2_ref, sems, b):
    rows = pl.ds(b * 128, 128)
    return pltpu.make_async_copy(k2_hbm.at[rows], k2_ref.at[rows], sems.at[b])


def start_fetch(k2_hbm, k2_ref, sems):
    for b in range(RJ):
        fetch(k2_hbm, k2_ref, sems, b).start()


def lanes_block(tiles_of, count, heads, high_ref, mass_ref, base, joined=False):
    for group in range(16):
        rows = pl.ds(base + group * 8, 8)
        tiles = tiles_of(rows)
        for v in range(count):
            xs = [heads[v][r : r + 1, :] - tile for r, tile in tiles]
            high = tree(jnp.maximum, xs)
            if joined:
                before = high_ref[v, rows, :]
                high = jnp.maximum(high, before)
                xs.append(before)
            masses = [jnp.exp2(x - high) for x in xs]
            if joined:
                masses[-1] = masses[-1] * mass_ref[v, rows, :]
            high_ref[v, rows, :] = high
            mass_ref[v, rows, :] = tree(jnp.add, masses)


def near_tiles(k1_ref):
    return lambda rows: [(r, k1_ref[rows, r * 128 : (r + 1) * 128]) for r in range(NEAR)]


def far_tiles(k2_ref):
    return lambda rows: [(r, k2_ref[rows, (r - NEAR) * 128 : (r - NEAR + 1) * 128]) for r in range(NEAR, RI)]


def lanes_result(count, high_ref, mass_ref):
    results = []
    for v in range(count):
        rows_out = []
        for b in range(RJ):
            high = jnp.transpose(high_ref[v, b * 128 : (b + 1) * 128, :])
            mass = jnp.transpose(mass_ref[v, b * 128 : (b + 1) * 128, :])
            top = jnp.max(high, axis=0, keepdims=True)
            total = jnp.sum(mass * jnp.exp2(high - top), axis=0, keepdims=True)
            rows_out.append((top, total))
        top = jnp.concatenate([row[0] for row in rows_out], axis=0)
        total = jnp.concatenate([row[1] for row in rows_out], axis=0)
        results.append(top + jnp.log(total) * LOG2E)
    return results


def reduce_lanes(k1_ref, k2_hbm, k2_ref, sems, heads, high_ref, mass_ref):
    count = len(heads)

    def near(b, carry):
        lanes_block(near_tiles(k1_ref), count, heads, high_ref, mass_ref, pl.multiple_of(b * 128, 128))
        return carry

    def far(b, carry):
        fetch(k2_hbm, k2_ref, sems, b).wait()
        lanes_block(far_tiles(k2_ref), count, heads, high_ref, mass_ref, pl.multiple_of(b * 128, 128), True)
        return carry

    lax.fori_loop(0, RJ, near, 0)
    lax.fori_loop(0, RJ, far, 0)
    return lanes_result(count, high_ref, mass_ref)


def reduce_rows(k1_ref, k2_hbm, k2_ref, sems, heads, head_ref, wide_ref, high_ref, mass_ref):
    count = len(heads)
    for v in range(count):
        head_ref[v, 0:RJ, :] = heads[v]

    def block(b, wides, tile, r):
        spot = pl.ds(pl.multiple_of(b * 8, 8), 8)
        cols = slice(r * 128, (r + 1) * 128)
        tiles = [tile(pl.ds(b * 128 + group * 8, 8)) for group in range(16)]
        for v in range(count):
            xs = [wides[v][group * 8 : group * 8 + 8, :] - tiles[group] for group in range(16)]
            high = tree(jnp.maximum, xs)
            high_ref[v, spot, cols] = high
            mass_ref[v, spot, cols] = tree(jnp.add, [jnp.exp2(x - high) for x in xs])

    def near(b, carry):
        wides = []
        for v in range(count):
            wides.append(jnp.transpose(jnp.broadcast_to(head_ref[v, pl.ds(b, 1), :], (128, 128))))
            wide_ref[v, pl.ds(pl.multiple_of(b * 128, 128), 128), :] = wides[v]
        for r in range(NEAR):
            block(b, wides, lambda rows: k1_ref[rows, r * 128 : (r + 1) * 128], r)
        return carry

    def far(b, carry):
        fetch(k2_hbm, k2_ref, sems, b).wait()
        wides = [wide_ref[v, pl.ds(pl.multiple_of(b * 128, 128), 128), :] for v in range(count)]
        for r in range(NEAR, RI):
            block(b, wides, lambda rows: k2_ref[rows, (r - NEAR) * 128 : (r - NEAR + 1) * 128], r)
        return carry

    lax.fori_loop(0, RJ, near, 0)
    lax.fori_loop(0, RJ, far, 0)
    results = []
    for v in range(count):
        tops, totals = [], []
        for r in range(RI):
            cols = slice(r * 128, (r + 1) * 128)
            high = high_ref[v, :, cols]
            top = jnp.max(high, axis=0, keepdims=True)
            tops.append(top)
            totals.append(jnp.sum(mass_ref[v, :, cols] * jnp.exp2(high - top), axis=0, keepdims=True))
        results.append(jnp.concatenate(tops, axis=0) + jnp.log(jnp.concatenate(totals, axis=0)) * LOG2E)
    return results


def pack_body(gen, ref, out, both, sems):
    copies = [pltpu.make_async_copy(part, both.at[n], sems.at[n]) for n, part in enumerate((gen, ref))]
    for copy in copies:
        copy.start()
    for copy in copies:
        copy.wait()
    wide = jnp.concatenate([both[0].astype(jnp.float32), both[1].astype(jnp.float32)], axis=0)
    out[...] = jnp.transpose(wide).astype(jnp.bfloat16)


def unpack_body(which, info, raw, *refs):
    out = refs[-1]
    for k in range(D // 128):
        cols = slice(k * 128, (k + 1) * 128)
        even, odd = raw[2 * k], raw[2 * k + 1]
        gen = jnp.concatenate([even[:, :64], odd[:, :64]], axis=1)
        ref = jnp.concatenate([even[:, 64:], odd[:, 64:]], axis=1)
        part = jnp.where(info[6 + which] == 1, gen, ref)
        for n in range(4):
            out[n, :, cols] = part


def norm_parts(values):
    values = values.astype(jnp.float32)
    values = values * values
    return functools.reduce(jnp.add, [values[:, k * 128 : (k + 1) * 128] for k in range(D // 128)])


def join_body(
    info, gen_count, ref_count, one, two, from_0, from_1, a_out, b_out, norm_out, lift_i, lift_j, weights
):
    c, x, y = info[2], info[4], info[5]
    first = c == 0
    for s in range(6):
        part = slice(s * 128, (s + 1) * 128)
        b_out[part, :] = jnp.where(first, two[part, :], one[part, :])
    for half in range(2):
        for s in range(6):
            part = slice(s * 128, (s + 1) * 128)
            on_0, on_1 = (one, from_0) if half == 0 else (from_1, two)
            rows = jnp.where(first, on_0[part, :], on_1[part, :])
            r = half * 6 + s
            a_out[r * 128 : (r + 1) * 128, :] = rows
            turned = jnp.transpose(norm_parts(rows))
            norm_out[r : r + 1, :] = jnp.sum(turned, axis=0, keepdims=True) * (0.5 * LOG2E / EPSILON)
    norm_out[RI:16, :] = jnp.zeros((16 - RI, 128), jnp.float32)

    def total(counts):
        return jnp.full((8, 128), functools.reduce(jnp.add, [counts[n] for n in range(32)]).astype(jnp.float32))

    def number(is_gen, t):
        return jnp.where(is_gen, gen_count[t], ref_count[t])

    def flat(rows):
        shape = (rows, 128)
        return lax.broadcasted_iota(jnp.int32, shape, 0) * 128 + lax.broadcasted_iota(jnp.int32, shape, 1)

    def valid(spots, starts, counts):
        inside = [(spots >= start) & (spots < start + count) for start, count in zip(starts, counts)]
        return functools.reduce(jnp.logical_or, inside)

    a_is_gen, b_is_gen = info[0] == 1, info[1] == 1
    totals = total(gen_count), total(ref_count)
    gen_log, ref_log = (-jnp.log(value) * LOG2E for value in totals)
    counts = [number(a_is_gen, ((n % 4) * 4 + x) * 2 + n // 4) for n in range(8)]
    ok = valid(flat(16), [n * BLOCK for n in range(8)], counts)
    log_a = jnp.where(a_is_gen, gen_log, ref_log)
    lift_i[...] = jnp.where(ok, jnp.concatenate([log_a, log_a], axis=0), FAR)
    here = [(y * 4 + n) * 2 + c for n in range(4)]
    starts = [n * BLOCK for n in range(4)]
    ok = valid(flat(8), starts, [number(b_is_gen, t) for t in here])
    lift_j[...] = jnp.where(ok, jnp.where(b_is_gen, gen_log, ref_log), FAR)
    shift = 64 * lax.rem(y, 2)
    windows = [n * 256 + shift for n in range(4)]
    for n, counts in enumerate((gen_count, ref_count)):
        ok = valid(flat(8), windows, [counts[t] for t in here])
        weights[n * 8 : n * 8 + 8, :] = jnp.where(ok, 1.0 / totals[n], 0.0)
    ok = valid(flat(8), starts, [ref_count[t] for t in here])
    weights[16:24, :] = jnp.where(ok, 1.0 / totals[1], 0.0)


def cost_body(
    a_ref, norm_ref, b_ref, lift_i, k1_ref, k2_hbm, part_out, k2_ref, high_ref, mass_ref, sq_ref, out_sems
):
    scale = LOG2E / EPSILON
    heads = [lift_i[0:RI, :]]
    for b in range(RJ):
        part = slice(b * 128, (b + 1) * 128)
        total = jnp.sum(norm_parts(b_ref[part, :]), axis=1, keepdims=True) * (0.5 * scale)
        sq_ref[part, :] = jnp.broadcast_to(total, (128, 128))
    stores = [fetch(k2_ref, k2_hbm, out_sems, b) for b in range(RJ)]
    order = [4, 5, 0, 1, 2, 3]
    for step in range(RI // 2 + 1):
        if step < RI // 2:
            n = order[step]
            inner = lax.dot_general(
                b_ref[...],
                a_ref[n * 256 : (n + 1) * 256, :],
                (((1,), (1,)), ((), ())),
                preferred_element_type=jnp.float32,
            )
            for s in range(2):
                r = 2 * n + s
                tile = (sq_ref[...] + norm_ref[r : r + 1, :]) - scale * inner[:, s * 128 : (s + 1) * 128]
                if r < NEAR:
                    k1_ref[:, r * 128 : (r + 1) * 128] = tile
                else:
                    k2_ref[:, (r - NEAR) * 128 : (r - NEAR + 1) * 128] = tile
        if step > 0:
            done = 2 * order[step - 1]
            source, at = (k1_ref, done) if done < NEAR else (k2_ref, done - NEAR)
            pair = lambda rows: [
                (done + s, source[rows, (at + s) * 128 : (at + s + 1) * 128]) for s in range(2)
            ]
            for b in range(RJ):
                lanes_block(pair, 1, heads, high_ref, mass_ref, b * 128, step > 1)
        if step == 1:
            for store in stores:
                store.start()
    (result,) = lanes_result(1, high_ref, mass_ref)
    for n in range(4):
        part_out[n, 0:RJ, :] = result
        part_out[n, RJ:8, :] = jnp.zeros((8 - RJ, 128), jnp.float32)
    for store in stores:
        store.wait()


def second_body(k1_ref, k2_hbm, got, lift_j, out, g1_out, k2_ref, sems, head_ref, wide_ref, high_ref, mass_ref):
    start_fetch(k2_hbm, k2_ref, sems)
    g1 = -merge(got, 4)[0:RJ, :]
    g1_out[...] = g1
    lift = lift_j[0:RJ, :]
    heads = [lift, lifted(g1, lift)]
    results = reduce_rows(k1_ref, k2_hbm, k2_ref, sems, heads, head_ref, wide_ref, high_ref, mass_ref)
    for n in range(8):
        for v in range(2):
            out[n, v * RI : (v + 1) * RI, :] = results[v]


def third_body(k1_ref, k2_hbm, got, lift_i, out, f2_out, k2_ref, sems, high_ref, mass_ref):
    start_fetch(k2_hbm, k2_ref, sems)
    merged = -merge(got, 8)
    f1 = merged[0:RI, :]
    f2 = 0.5 * (f1 + merged[RI : 2 * RI, :])
    f2_out[...] = f2
    lift = lift_i[0:RI, :]
    heads = [lifted(f1, lift), lifted(f2, lift)]
    results = reduce_lanes(k1_ref, k2_hbm, k2_ref, sems, heads, high_ref, mass_ref)
    for n in range(4):
        for v in range(2):
            out[n, v * 8 : v * 8 + RJ, :] = results[v]
            out[n, v * 8 + RJ : v * 8 + 8, :] = jnp.zeros((8 - RJ, 128), jnp.float32)


def fourth_body(k1_ref, k2_hbm, got, lift_j, g1, out, g3_out, k2_ref, sems, head_ref, wide_ref, high_ref, mass_ref):
    start_fetch(k2_hbm, k2_ref, sems)
    merged = -merge(got, 4)
    g2 = 0.5 * (g1[...] + merged[0:RJ, :])
    g3 = 0.5 * (g2 + merged[8 : 8 + RJ, :])
    g3_out[...] = g3
    lift = lift_j[0:RJ, :]
    heads = [lifted(g2, lift), lifted(g3, lift)]
    results = reduce_rows(k1_ref, k2_hbm, k2_ref, sems, heads, head_ref, wide_ref, high_ref, mass_ref)
    for n in range(8):
        for v in range(2):
            out[n, v * RI : (v + 1) * RI, :] = results[v]


def fifth_body(info, k1_ref, k2_hbm, got, lift_i, f2, g3, out, k2_ref, sems, high_ref, mass_ref, f4_ref):
    start_fetch(k2_hbm, k2_ref, sems)
    merged = -merge(got, 8)
    f3 = 0.5 * (f2[...] + merged[0:RI, :])
    f4 = 0.5 * (f3 + merged[RI : 2 * RI, :])
    f4_ref[0:RI, :] = f4
    heads = [lifted(f3, lift_i[0:RI, :])]
    (result,) = reduce_lanes(k1_ref, k2_hbm, k2_ref, sems, heads, high_ref, mass_ref)
    shifted = result - g3[...]
    mine = f4_ref[pl.ds(info[3], 2), :]
    for n in range(16):
        out[n, 0:RJ, :] = shifted
        out[n, RJ : RJ + 2, :] = mine


def last_body(got, weights, pots, g4_out, share):
    g4 = merge([got[n * 4 + 1, 0:RJ, :] for n in range(4)], 4) * (-0.5 * LN2)
    g4_out[0:RJ, :] = g4
    g4_out[RJ:8, :] = jnp.zeros((8 - RJ, 128), jnp.float32)
    weight = weights[16 : 16 + RJ, :]
    total = jnp.sum(jnp.where(weight > 0.0, g4 * weight, 0.0))
    for n in range(4):
        own = slice(RJ, RJ + 2)
        gen_pot = got[n * 4 + 1][own, :] * LN2
        gen_self = got[n * 4][own, :] * LN2
        ref_self = got[n * 4 + 3][own, :] * LN2
        pots[n, 0:2, :] = gen_pot
        pots[n, 2:4, :] = gen_self
        pots[n, 4:6, :] = ref_self
        pots[n, 6:8, :] = jnp.zeros((2, 128), jnp.float32)
        weight = weights[2 * n : 2 * n + 2, :]
        total += jnp.sum(jnp.where(weight > 0.0, (gen_pot - gen_self) * weight, 0.0))
        weight = weights[8 + 2 * n : 8 + 2 * n + 2, :]
        total -= jnp.sum(jnp.where(weight > 0.0, ref_self * weight, 0.0))
    for n in range(8):
        share[n, :, :] = jnp.full((8, 128), total, jnp.float32)


F32 = jnp.float32
BF16 = jnp.bfloat16
STREAM = [pltpu.VMEM((NJ, N2), F32), pltpu.SemaphoreType.DMA((RJ,))]


def lane_scratch(count):
    return [pltpu.VMEM((count, NJ, 128), F32)] * 2


def row_scratch(count):
    return [pltpu.VMEM((count, 8, 128), F32), pltpu.VMEM((count, NJ, 128), F32)] + [pltpu.VMEM((count, 8 * RJ, NI), F32)] * 2


def stage_pack(*args):
    scratch = [pltpu.VMEM((2, 64, BLOCK), BF16), pltpu.SemaphoreType.DMA((2,))]
    out = jax.ShapeDtypeStruct((BLOCK, 128), BF16)
    return call(pack_body, out, [HBM, HBM], scratch, mib=60)(*args)


def stage_unpack(which, *args):
    out = jax.ShapeDtypeStruct((4, BLOCK, D), BF16)
    return call(functools.partial(unpack_body, which), out, [SMEM, VMEM, HBM][: len(args)])(*args)


def stage_join(*args):
    points = tuple(jax.ShapeDtypeStruct((rows, D), BF16) for rows in (NI, NJ))
    outs = points + (f32(16, 128), f32(16, 128), f32(8, 128), f32(24, 128))
    return call(join_body, outs, [SMEM] * 3 + [VMEM] * 4)(*args)


def stage_cost(*args):
    scratch = [
        pltpu.VMEM((NJ, N2), F32),
        *lane_scratch(1),
        pltpu.VMEM((NJ, 128), F32),
        pltpu.SemaphoreType.DMA((RJ,)),
    ]
    outs = (f32(NJ, N1), f32(ROOM, N2), f32(4, 8, 128))
    return call(cost_body, outs, [VMEM] * 4, scratch, (VMEM, HBM, VMEM))(*args)


def stage_second(*args):
    outs = (f32(8, 2 * RI, 128), f32(RJ, 128))
    return call(second_body, outs, [VMEM, HBM, VMEM, VMEM], STREAM + row_scratch(2))(*args)


def stage_third(*args):
    outs = (f32(4, 16, 128), f32(RI, 128))
    return call(third_body, outs, [VMEM, HBM, VMEM, VMEM], STREAM + lane_scratch(2))(*args)


def stage_fourth(*args):
    outs = (f32(8, 2 * RI, 128), f32(RJ, 128))
    return call(fourth_body, outs, [VMEM, HBM, VMEM, VMEM, VMEM], STREAM + row_scratch(2))(*args)


def stage_fifth(*args):
    scratch = STREAM + lane_scratch(1) + [pltpu.VMEM((16, 128), F32)]
    return call(fifth_body, f32(16, 8, 128), [SMEM, VMEM, HBM] + [VMEM] * 4, scratch)(*args)


def spread(operand, axes, groups=None):
    return lax.all_to_all(operand, axes, 0, 0, tiled=True, axis_index_groups=groups)


def local(gen_points, reference_embeddings, gen_count, ref_count):
    y, x, c, zl = (lax.axis_index(name) for name in ("y", "x", "c", "zl"))
    a_is_gen = zl < 3
    b_is_gen = zl == 0
    packed = stage_pack(jnp.transpose(gen_points), jnp.transpose(reference_embeddings))
    raw = lax.all_gather(packed, ("zh", "zl"))

    info = jnp.stack(
        [
            a_is_gen.astype(jnp.int32),
            b_is_gen.astype(jnp.int32),
            c,
            c * 6 + (3 * y) // 2,
            x,
            y,
            jnp.where(c == 0, a_is_gen, b_is_gen).astype(jnp.int32),
            jnp.where(c == 0, b_is_gen, a_is_gen).astype(jnp.int32),
        ]
    ).astype(jnp.int32)
    along_y = [[[(i * 4 + n) * 2 + core for i in range(4)] for n in range(4)] for core in range(2)]
    along_x = [[[(n * 4 + i) * 2 + core for i in range(4)] for n in range(4)] for core in range(2)]
    one = spread(stage_unpack(0, info, raw), ("y", "x", "c"), along_y[0] + along_x[1])
    from_0 = lax.ppermute(one, "c", [(0, 1)])
    two = spread(stage_unpack(1, info, raw, one), ("y", "x", "c"), along_x[0] + along_y[1])
    from_1 = lax.ppermute(two, "c", [(1, 0)])
    blocks = [part.reshape(NJ, D) for part in (one, two, from_0, from_1)]
    a_all, b_all, norms, lift_i, lift_j, weights = stage_join(info, gen_count, ref_count, *blocks)
    k1, k2, part = stage_cost(a_all, norms, b_all, lift_i)
    part, g1 = stage_second(k1, k2, spread(part, "x"), lift_j)
    part, f2 = stage_third(k1, k2, spread(part, ("y", "c")), lift_i)
    part, g3 = stage_fourth(k1, k2, spread(part, "x"), lift_j, g1)
    part = stage_fifth(info, k1, k2, spread(part, ("y", "c")), lift_i, f2, g3)
    got = spread(part, ("x", "zl"))
    pots, g4, share = call(last_body, (f32(4, 8, 128), f32(8, 128), f32(8, 8, 128)), [VMEM, VMEM])(got, weights)
    divergence = jnp.sum(spread(share, ("y", "c"))[:, 0, 0])

    mine = lax.dynamic_index_in_dim(pots, x, 0, keepdims=False)
    mine = lax.dynamic_slice_in_dim(mine.reshape(4, 256), 64 * (y % 2), BLOCK, 1)
    ref_pot = lax.dynamic_slice_in_dim(g4.reshape(1024), x * BLOCK, BLOCK, 0)
    return mine[0], ref_pot, mine[1], mine[2], divergence


def solution(mesh):
    fine = Mesh(mesh.devices.reshape(4, 4, 2, 4, 4), ("y", "x", "c", "zh", "zl"))
    tile, feat = ("y", "x", "c"), ("zh", "zl")
    return jax.shard_map(
        local,
        mesh=fine,
        in_specs=(P(tile, feat), P(tile, feat), P(), P()),
        out_specs=(P(tile), P(tile), P(tile), P(tile), P()),
        check_vma=False,
    )
```

```python
import functools

import jax
import jax.numpy as jnp
from jax import lax
from jax.experimental import pallas as pl
from jax.experimental.pallas import tpu as pltpu
from jax.sharding import Mesh, PartitionSpec as P

EPSILON = 0.25
LOG2E = 1.4426950408889634
LN2 = 0.6931471805599453
FAR = -1.0e30

BLOCK = 192
D = 1024
NI = 8 * BLOCK
NJ = 4 * BLOCK
RI = NI // 128
RH = RI // 2
RJ = NJ // 128
NEAR = 8
N2 = NI - NEAR * 128
ROOM = 18 * NJ

VMEM = pl.BlockSpec(memory_space=pltpu.VMEM)
HBM = pl.BlockSpec(memory_space=pltpu.HBM)
SMEM = pl.BlockSpec(memory_space=pltpu.SMEM)


def f32(*shape):
    return jax.ShapeDtypeStruct(shape, jnp.float32)


def call(body, outs, ins, scratch=(), out_specs=None, mib=40):
    return pl.pallas_call(
        body,
        out_shape=outs,
        in_specs=ins,
        out_specs=jax.tree.map(lambda _: VMEM, outs) if out_specs is None else out_specs,
        scratch_shapes=list(scratch),
        compiler_params=pltpu.CompilerParams(vmem_limit_bytes=mib * 1024 * 1024),
    )


def merge(got, count):
    parts = [got[n] for n in range(count)]
    high = functools.reduce(jnp.maximum, parts)
    mass = functools.reduce(jnp.add, [jnp.exp2(part - high) for part in parts])
    return high + jnp.log(mass) * LOG2E


def lifted(pot, lift):
    return jnp.where(lift > -1.0e29, pot + lift, FAR)


def tree(op, values):
    values = list(values)
    while len(values) > 1:
        values = [op(*values[n : n + 2]) if n + 1 < len(values) else values[n] for n in range(0, len(values), 2)]
    return values[0]


def fetch(k2_hbm, k2_ref, sems, b):
    rows = pl.ds(b * 128, 128)
    return pltpu.make_async_copy(k2_hbm.at[rows], k2_ref.at[rows], sems.at[b])


def start_fetch(k2_hbm, k2_ref, sems):
    for b in range(RJ):
        fetch(k2_hbm, k2_ref, sems, b).start()


def lanes_block(tiles_of, count, heads, high_ref, mass_ref, base, joined=False):
    for group in range(16):
        rows = pl.ds(base + group * 8, 8)
        tiles = tiles_of(rows)
        for v in range(count):
            xs = [heads[v][r : r + 1, :] - tile for r, tile in tiles]
            high = tree(jnp.maximum, xs)
            if joined:
                before = high_ref[v, rows, :]
                high = jnp.maximum(high, before)
                xs.append(before)
            masses = [jnp.exp2(x - high) for x in xs]
            if joined:
                masses[-1] = masses[-1] * mass_ref[v, rows, :]
            high_ref[v, rows, :] = high
            mass_ref[v, rows, :] = tree(jnp.add, masses)


def near_tile(k1a_ref, k1b_ref, rows, r):
    if r < RH:
        return k1a_ref[rows, r * 128 : (r + 1) * 128]
    return k1b_ref[rows, (r - RH) * 128 : (r - RH + 1) * 128]


def near_tiles(k1a_ref, k1b_ref):
    return lambda rows: [(r, near_tile(k1a_ref, k1b_ref, rows, r)) for r in range(NEAR)]


def far_tiles(k2_ref):
    return lambda rows: [(r, k2_ref[rows, (r - NEAR) * 128 : (r - NEAR + 1) * 128]) for r in range(NEAR, RI)]


def turned(swap, value):
    return jnp.where(swap, jnp.concatenate([value[RH:RI, :], value[0:RH, :]], axis=0), value)


def lanes_result(count, high_ref, mass_ref):
    results = []
    for v in range(count):
        rows_out = []
        for b in range(RJ):
            high = jnp.transpose(high_ref[v, b * 128 : (b + 1) * 128, :])
            mass = jnp.transpose(mass_ref[v, b * 128 : (b + 1) * 128, :])
            top = jnp.max(high, axis=0, keepdims=True)
            total = jnp.sum(mass * jnp.exp2(high - top), axis=0, keepdims=True)
            rows_out.append((top, total))
        top = jnp.concatenate([row[0] for row in rows_out], axis=0)
        total = jnp.concatenate([row[1] for row in rows_out], axis=0)
        results.append(top + jnp.log(total) * LOG2E)
    return results


def reduce_lanes(k1a_ref, k1b_ref, k2_hbm, k2_ref, sems, heads, high_ref, mass_ref):
    count = len(heads)

    def near(b, carry):
        lanes_block(near_tiles(k1a_ref, k1b_ref), count, heads, high_ref, mass_ref, pl.multiple_of(b * 128, 128))
        return carry

    def far(b, carry):
        fetch(k2_hbm, k2_ref, sems, b).wait()
        lanes_block(far_tiles(k2_ref), count, heads, high_ref, mass_ref, pl.multiple_of(b * 128, 128), True)
        return carry

    lax.fori_loop(0, RJ, near, 0)
    lax.fori_loop(0, RJ, far, 0)
    return lanes_result(count, high_ref, mass_ref)


def reduce_rows(k1a_ref, k1b_ref, k2_hbm, k2_ref, sems, heads, head_ref, wide_ref, high_ref, mass_ref):
    count = len(heads)
    for v in range(count):
        head_ref[v, 0:RJ, :] = heads[v]

    def block(b, wides, tile, r):
        spot = pl.ds(pl.multiple_of(b * 8, 8), 8)
        cols = slice(r * 128, (r + 1) * 128)
        tiles = [tile(pl.ds(b * 128 + group * 8, 8)) for group in range(16)]
        for v in range(count):
            xs = [wides[v][group * 8 : group * 8 + 8, :] - tiles[group] for group in range(16)]
            high = tree(jnp.maximum, xs)
            high_ref[v, spot, cols] = high
            mass_ref[v, spot, cols] = tree(jnp.add, [jnp.exp2(x - high) for x in xs])

    def near(b, carry):
        wides = []
        for v in range(count):
            wides.append(jnp.transpose(jnp.broadcast_to(head_ref[v, pl.ds(b, 1), :], (128, 128))))
            wide_ref[v, pl.ds(pl.multiple_of(b * 128, 128), 128), :] = wides[v]
        for r in range(NEAR):
            block(b, wides, lambda rows: near_tile(k1a_ref, k1b_ref, rows, r), r)
        return carry

    def far(b, carry):
        fetch(k2_hbm, k2_ref, sems, b).wait()
        wides = [wide_ref[v, pl.ds(pl.multiple_of(b * 128, 128), 128), :] for v in range(count)]
        for r in range(NEAR, RI):
            block(b, wides, lambda rows: k2_ref[rows, (r - NEAR) * 128 : (r - NEAR + 1) * 128], r)
        return carry

    lax.fori_loop(0, RJ, near, 0)
    lax.fori_loop(0, RJ, far, 0)
    results = []
    for v in range(count):
        tops, totals = [], []
        for r in range(RI):
            cols = slice(r * 128, (r + 1) * 128)
            high = high_ref[v, :, cols]
            top = jnp.max(high, axis=0, keepdims=True)
            tops.append(top)
            totals.append(jnp.sum(mass_ref[v, :, cols] * jnp.exp2(high - top), axis=0, keepdims=True))
        results.append(jnp.concatenate(tops, axis=0) + jnp.log(jnp.concatenate(totals, axis=0)) * LOG2E)
    return results


def pack_body(gen, ref, out, both, sems):
    copies = [pltpu.make_async_copy(part, both.at[n], sems.at[n]) for n, part in enumerate((gen, ref))]
    for copy in copies:
        copy.start()
    for copy in copies:
        copy.wait()
    wide = jnp.concatenate([both[0].astype(jnp.float32), both[1].astype(jnp.float32)], axis=0)
    out[...] = jnp.transpose(wide).astype(jnp.bfloat16)


def unpack_body(which, info, raw, *refs):
    out = refs[-1]
    for k in range(D // 128):
        cols = slice(k * 128, (k + 1) * 128)
        even, odd = raw[2 * k], raw[2 * k + 1]
        gen = jnp.concatenate([even[:, :64], odd[:, :64]], axis=1)
        ref = jnp.concatenate([even[:, 64:], odd[:, 64:]], axis=1)
        part = jnp.where(info[6 + which] == 1, gen, ref)
        for n in range(4):
            out[n, :, cols] = part


def norm_parts(values):
    values = values.astype(jnp.float32)
    values = values * values
    return functools.reduce(jnp.add, [values[:, k * 128 : (k + 1) * 128] for k in range(D // 128)])


def join_body(info, gen_count, ref_count, one, two, a_out, b_out, lift_i, lift_j, weights):
    c, x, y = info[2], info[4], info[5]
    for s in range(6):
        part = slice(s * 128, (s + 1) * 128)
        a_out[part, :] = jnp.where(c == 0, one[part, :], two[part, :])
        b_out[part, :] = jnp.where(c == 0, two[part, :], one[part, :])

    def total(counts):
        return jnp.full((8, 128), functools.reduce(jnp.add, [counts[n] for n in range(32)]).astype(jnp.float32))

    def number(is_gen, t):
        return jnp.where(is_gen, gen_count[t], ref_count[t])

    def flat(rows):
        shape = (rows, 128)
        return lax.broadcasted_iota(jnp.int32, shape, 0) * 128 + lax.broadcasted_iota(jnp.int32, shape, 1)

    def valid(spots, starts, counts):
        inside = [(spots >= start) & (spots < start + count) for start, count in zip(starts, counts)]
        return functools.reduce(jnp.logical_or, inside)

    a_is_gen, b_is_gen = info[0] == 1, info[1] == 1
    totals = total(gen_count), total(ref_count)
    gen_log, ref_log = (-jnp.log(value) * LOG2E for value in totals)
    counts = [number(a_is_gen, ((n % 4) * 4 + x) * 2 + (c if n < 4 else 1 - c)) for n in range(8)]
    ok = valid(flat(16), [n * BLOCK for n in range(8)], counts)
    log_a = jnp.where(a_is_gen, gen_log, ref_log)
    lift_i[...] = jnp.where(ok, jnp.concatenate([log_a, log_a], axis=0), FAR)
    here = [(y * 4 + n) * 2 + c for n in range(4)]
    starts = [n * BLOCK for n in range(4)]
    ok = valid(flat(8), starts, [number(b_is_gen, t) for t in here])
    lift_j[...] = jnp.where(ok, jnp.where(b_is_gen, gen_log, ref_log), FAR)
    shift = 64 * lax.rem(y, 2)
    windows = [n * 256 + shift for n in range(4)]
    for n, counts in enumerate((gen_count, ref_count)):
        ok = valid(flat(8), windows, [counts[t] for t in here])
        weights[n * 8 : n * 8 + 8, :] = jnp.where(ok, 1.0 / totals[n], 0.0)
    ok = valid(flat(8), starts, [ref_count[t] for t in here])
    weights[16:24, :] = jnp.where(ok, 1.0 / totals[1], 0.0)


def a_norms(a_ref):
    rows = []
    for s in range(RH):
        flipped = jnp.transpose(norm_parts(a_ref[s * 128 : (s + 1) * 128, :]))
        rows.append(jnp.sum(flipped, axis=0, keepdims=True) * (0.5 * LOG2E / EPSILON))
    return rows


def cost_tiles(a_ref, b_ref, sq_ref, norms, n):
    inner = lax.dot_general(
        b_ref[...],
        a_ref[n * 256 : (n + 1) * 256, :],
        (((1,), (1,)), ((), ())),
        preferred_element_type=jnp.float32,
    )
    scale = LOG2E / EPSILON
    return [(sq_ref[...] + norms[2 * n + s]) - scale * inner[:, s * 128 : (s + 1) * 128] for s in range(2)]


def reduce_pair(head, source, at, high_ref, mass_ref, base, joined):
    heads = [head[base : base + 2, :]]
    pair = lambda rows: [(s, source[rows, at + s * 128 : at + (s + 1) * 128]) for s in range(2)]
    for b in range(RJ):
        lanes_block(pair, 1, heads, high_ref, mass_ref, b * 128, joined)


def cost_own_body(a_ref, b_ref, lift_i, k1a_ref, high_ref, mass_ref, sq_ref):
    head = lift_i[...]
    norms = a_norms(a_ref)
    for b in range(RJ):
        part = slice(b * 128, (b + 1) * 128)
        total = jnp.sum(norm_parts(b_ref[part, :]), axis=1, keepdims=True) * (0.5 * LOG2E / EPSILON)
        sq_ref[part, :] = jnp.broadcast_to(total, (128, 128))
    for n in range(4):
        if n < 3:
            for s, tile in enumerate(cost_tiles(a_ref, b_ref, sq_ref, norms, n)):
                k1a_ref[:, (2 * n + s) * 128 : (2 * n + s + 1) * 128] = tile
        if n > 0:
            reduce_pair(head, k1a_ref, (n - 1) * 256, high_ref, mass_ref, 2 * n - 2, n > 1)


def cost_other_body(
    a_ref, b_ref, lift_i, high_in, mass_in, sq_ref, k1b_ref, k2_hbm, part_out, k2_ref, high_ref, mass_ref, out_sems
):
    head = lift_i[...]
    norms = a_norms(a_ref)
    high_ref[...] = high_in[...]
    mass_ref[...] = mass_in[...]
    stores = [fetch(k2_ref, k2_hbm, out_sems, b) for b in range(RJ)]
    order = [1, 2, 0]
    for step in range(4):
        if step < 3:
            n = order[step]
            target, at = (k1b_ref, 0) if n == 0 else (k2_ref, (n - 1) * 256)
            for s, tile in enumerate(cost_tiles(a_ref, b_ref, sq_ref, norms, n)):
                target[:, at + s * 128 : at + (s + 1) * 128] = tile
        if step > 0:
            n = order[step - 1]
            source, at = (k1b_ref, 0) if n == 0 else (k2_ref, (n - 1) * 256)
            reduce_pair(head, source, at, high_ref, mass_ref, RH + 2 * n, True)
        if step == 1:
            for store in stores:
                store.start()
    (result,) = lanes_result(1, high_ref, mass_ref)
    for n in range(4):
        part_out[n, 0:RJ, :] = result
        part_out[n, RJ:8, :] = jnp.zeros((8 - RJ, 128), jnp.float32)
    for store in stores:
        store.wait()


def second_body(info, k1a_ref, k1b_ref, k2_hbm, got, lift_j, out, g1_out, k2_ref, sems, head_ref, wide_ref, high_ref, mass_ref):
    start_fetch(k2_hbm, k2_ref, sems)
    g1 = -merge(got, 4)[0:RJ, :]
    g1_out[...] = g1
    lift = lift_j[0:RJ, :]
    heads = [lift, lifted(g1, lift)]
    results = reduce_rows(k1a_ref, k1b_ref, k2_hbm, k2_ref, sems, heads, head_ref, wide_ref, high_ref, mass_ref)
    sent = [turned(info[2] == 1, value) for value in results]
    for n in range(8):
        for v in range(2):
            out[n, v * RI : (v + 1) * RI, :] = sent[v]


def third_body(info, k1a_ref, k1b_ref, k2_hbm, got, lift_i, out, f2_out, k2_ref, sems, high_ref, mass_ref):
    start_fetch(k2_hbm, k2_ref, sems)
    merged = -merge(got, 8)
    f1 = turned(info[2] == 1, merged[0:RI, :])
    f2 = 0.5 * (f1 + turned(info[2] == 1, merged[RI : 2 * RI, :]))
    f2_out[...] = f2
    lift = lift_i[0:RI, :]
    heads = [lifted(f1, lift), lifted(f2, lift)]
    results = reduce_lanes(k1a_ref, k1b_ref, k2_hbm, k2_ref, sems, heads, high_ref, mass_ref)
    for n in range(4):
        for v in range(2):
            out[n, v * 8 : v * 8 + RJ, :] = results[v]
            out[n, v * 8 + RJ : v * 8 + 8, :] = jnp.zeros((8 - RJ, 128), jnp.float32)


def fourth_body(info, k1a_ref, k1b_ref, k2_hbm, got, lift_j, g1, out, g3_out, k2_ref, sems, head_ref, wide_ref, high_ref, mass_ref):
    start_fetch(k2_hbm, k2_ref, sems)
    merged = -merge(got, 4)
    g2 = 0.5 * (g1[...] + merged[0:RJ, :])
    g3 = 0.5 * (g2 + merged[8 : 8 + RJ, :])
    g3_out[...] = g3
    lift = lift_j[0:RJ, :]
    heads = [lifted(g2, lift), lifted(g3, lift)]
    results = reduce_rows(k1a_ref, k1b_ref, k2_hbm, k2_ref, sems, heads, head_ref, wide_ref, high_ref, mass_ref)
    sent = [turned(info[2] == 1, value) for value in results]
    for n in range(8):
        for v in range(2):
            out[n, v * RI : (v + 1) * RI, :] = sent[v]


def fifth_body(info, k1a_ref, k1b_ref, k2_hbm, got, lift_i, f2, g3, out, k2_ref, sems, high_ref, mass_ref, f4_ref):
    start_fetch(k2_hbm, k2_ref, sems)
    merged = -merge(got, 8)
    f3 = 0.5 * (f2[...] + turned(info[2] == 1, merged[0:RI, :]))
    f4 = 0.5 * (f3 + turned(info[2] == 1, merged[RI : 2 * RI, :]))
    f4_ref[0:RI, :] = f4
    heads = [lifted(f3, lift_i[0:RI, :])]
    (result,) = reduce_lanes(k1a_ref, k1b_ref, k2_hbm, k2_ref, sems, heads, high_ref, mass_ref)
    shifted = result - g3[...]
    mine = f4_ref[pl.ds(info[3], 2), :]
    for n in range(16):
        out[n, 0:RJ, :] = shifted
        out[n, RJ : RJ + 2, :] = mine


def last_body(got, weights, pots, g4_out, share):
    g4 = merge([got[n * 4 + 1, 0:RJ, :] for n in range(4)], 4) * (-0.5 * LN2)
    g4_out[0:RJ, :] = g4
    g4_out[RJ:8, :] = jnp.zeros((8 - RJ, 128), jnp.float32)
    weight = weights[16 : 16 + RJ, :]
    total = jnp.sum(jnp.where(weight > 0.0, g4 * weight, 0.0))
    for n in range(4):
        own = slice(RJ, RJ + 2)
        gen_pot = got[n * 4 + 1][own, :] * LN2
        gen_self = got[n * 4][own, :] * LN2
        ref_self = got[n * 4 + 3][own, :] * LN2
        pots[n, 0:2, :] = gen_pot
        pots[n, 2:4, :] = gen_self
        pots[n, 4:6, :] = ref_self
        pots[n, 6:8, :] = jnp.zeros((2, 128), jnp.float32)
        weight = weights[2 * n : 2 * n + 2, :]
        total += jnp.sum(jnp.where(weight > 0.0, (gen_pot - gen_self) * weight, 0.0))
        weight = weights[8 + 2 * n : 8 + 2 * n + 2, :]
        total -= jnp.sum(jnp.where(weight > 0.0, ref_self * weight, 0.0))
    for n in range(8):
        share[n, :, :] = jnp.full((8, 128), total, jnp.float32)


F32 = jnp.float32
BF16 = jnp.bfloat16
STREAM = [pltpu.VMEM((NJ, N2), F32), pltpu.SemaphoreType.DMA((RJ,))]


def lane_scratch(count):
    return [pltpu.VMEM((count, NJ, 128), F32)] * 2


def row_scratch(count):
    return [pltpu.VMEM((count, 8, 128), F32), pltpu.VMEM((count, NJ, 128), F32)] + [pltpu.VMEM((count, 8 * RJ, NI), F32)] * 2


def stage_pack(*args):
    scratch = [pltpu.VMEM((2, 64, BLOCK), BF16), pltpu.SemaphoreType.DMA((2,))]
    out = jax.ShapeDtypeStruct((BLOCK, 128), BF16)
    return call(pack_body, out, [HBM, HBM], scratch, mib=60)(*args)


def stage_unpack(which, *args):
    out = jax.ShapeDtypeStruct((4, BLOCK, D), BF16)
    return call(functools.partial(unpack_body, which), out, [SMEM, VMEM, HBM][: len(args)])(*args)


def stage_join(*args):
    points = (jax.ShapeDtypeStruct((NJ, D), BF16),) * 2
    outs = points + (f32(16, 128), f32(8, 128), f32(24, 128))
    return call(join_body, outs, [SMEM] * 3 + [VMEM] * 2)(*args)


def stage_cost_own(*args):
    outs = (f32(NJ, NI // 2), f32(1, NJ, 128), f32(1, NJ, 128), f32(NJ, 128))
    return call(cost_own_body, outs, [VMEM] * 3)(*args)


def stage_cost_other(*args):
    scratch = [pltpu.VMEM((NJ, N2), F32), *lane_scratch(1), pltpu.SemaphoreType.DMA((RJ,))]
    outs = (f32(NJ, NI // 2 - N2), f32(ROOM, N2), f32(4, 8, 128))
    return call(cost_other_body, outs, [VMEM] * 6, scratch, (VMEM, HBM, VMEM))(*args)


K_SPECS = [SMEM, VMEM, VMEM, HBM]


def stage_second(*args):
    outs = (f32(8, 2 * RI, 128), f32(RJ, 128))
    return call(second_body, outs, K_SPECS + [VMEM] * 2, STREAM + row_scratch(2))(*args)


def stage_third(*args):
    outs = (f32(4, 16, 128), f32(RI, 128))
    return call(third_body, outs, K_SPECS + [VMEM] * 2, STREAM + lane_scratch(2))(*args)


def stage_fourth(*args):
    outs = (f32(8, 2 * RI, 128), f32(RJ, 128))
    return call(fourth_body, outs, K_SPECS + [VMEM] * 3, STREAM + row_scratch(2))(*args)


def stage_fifth(*args):
    scratch = STREAM + lane_scratch(1) + [pltpu.VMEM((16, 128), F32)]
    return call(fifth_body, f32(16, 8, 128), K_SPECS + [VMEM] * 4, scratch)(*args)


def spread(operand, axes, groups=None):
    return lax.all_to_all(operand, axes, 0, 0, tiled=True, axis_index_groups=groups)


def local(gen_points, reference_embeddings, gen_count, ref_count):
    y, x, c, zl = (lax.axis_index(name) for name in ("y", "x", "c", "zl"))
    a_is_gen = zl < 3
    b_is_gen = zl == 0
    packed = stage_pack(jnp.transpose(gen_points), jnp.transpose(reference_embeddings))
    raw = lax.all_gather(packed, ("zh", "zl"))

    info = jnp.stack(
        [
            a_is_gen.astype(jnp.int32),
            b_is_gen.astype(jnp.int32),
            c,
            (3 * y) // 2,
            x,
            y,
            jnp.where(c == 0, a_is_gen, b_is_gen).astype(jnp.int32),
            jnp.where(c == 0, b_is_gen, a_is_gen).astype(jnp.int32),
        ]
    ).astype(jnp.int32)
    along_y = [[[(i * 4 + n) * 2 + core for i in range(4)] for n in range(4)] for core in range(2)]
    along_x = [[[(n * 4 + i) * 2 + core for i in range(4)] for n in range(4)] for core in range(2)]
    one = spread(stage_unpack(0, info, raw), ("y", "x", "c"), along_y[0] + along_x[1])
    two = spread(stage_unpack(1, info, raw, one), ("y", "x", "c"), along_x[0] + along_y[1])
    a_own, b_all, lift_i, lift_j, weights = stage_join(
        info, gen_count, ref_count, one.reshape(NJ, D), two.reshape(NJ, D)
    )
    a_other = lax.ppermute(a_own, "c", [(0, 1), (1, 0)])
    k1a, high, mass, b_norms = stage_cost_own(a_own, b_all, lift_i)
    k1b, k2, part = stage_cost_other(a_other, b_all, lift_i, high, mass, b_norms)
    k = (info, k1a, k1b, k2)
    part, g1 = stage_second(*k, spread(part, "x"), lift_j)
    part, f2 = stage_third(*k, spread(part, ("y", "c")), lift_i)
    part, g3 = stage_fourth(*k, spread(part, "x"), lift_j, g1)
    part = stage_fifth(*k, spread(part, ("y", "c")), lift_i, f2, g3)
    got = spread(part, ("x", "zl"))
    pots, g4, share = call(last_body, (f32(4, 8, 128), f32(8, 128), f32(8, 8, 128)), [VMEM, VMEM])(got, weights)
    divergence = jnp.sum(spread(share, ("y", "c"))[:, 0, 0])

    mine = lax.dynamic_index_in_dim(pots, x, 0, keepdims=False)
    mine = lax.dynamic_slice_in_dim(mine.reshape(4, 256), 64 * (y % 2), BLOCK, 1)
    ref_pot = lax.dynamic_slice_in_dim(g4.reshape(1024), x * BLOCK, BLOCK, 0)
    return mine[0], ref_pot, mine[1], mine[2], divergence


def solution(mesh):
    fine = Mesh(mesh.devices.reshape(4, 4, 2, 4, 4), ("y", "x", "c", "zh", "zl"))
    tile, feat = ("y", "x", "c"), ("zh", "zl")
    return jax.shard_map(
        local,
        mesh=fine,
        in_specs=(P(tile, feat), P(tile, feat), P(), P()),
        out_specs=(P(tile), P(tile), P(tile), P(tile), P()),
        check_vma=False,
    )
```

```python
import functools

import jax
import jax.numpy as jnp
from jax import lax
from jax.experimental import pallas as pl
from jax.experimental.pallas import tpu as pltpu
from jax.sharding import Mesh, PartitionSpec as P

EPSILON = 0.25
LOG2E = 1.4426950408889634
LN2 = 0.6931471805599453
FAR = -1.0e30

BLOCK = 192
D = 1024
NI = 8 * BLOCK
NJ = 4 * BLOCK
RI = NI // 128
RH = RI // 2
RJ = NJ // 128
NEAR = 8
N2 = NI - NEAR * 128
ROOM = 18 * NJ

VMEM = pl.BlockSpec(memory_space=pltpu.VMEM)
HBM = pl.BlockSpec(memory_space=pltpu.HBM)
SMEM = pl.BlockSpec(memory_space=pltpu.SMEM)


def f32(*shape):
    return jax.ShapeDtypeStruct(shape, jnp.float32)


def call(body, outs, ins, scratch=(), out_specs=None, mib=40):
    return pl.pallas_call(
        body,
        out_shape=outs,
        in_specs=ins,
        out_specs=jax.tree.map(lambda _: VMEM, outs) if out_specs is None else out_specs,
        scratch_shapes=list(scratch),
        compiler_params=pltpu.CompilerParams(vmem_limit_bytes=mib * 1024 * 1024),
    )


def merge(got, count):
    parts = [got[n] for n in range(count)]
    high = functools.reduce(jnp.maximum, parts)
    mass = functools.reduce(jnp.add, [jnp.exp2(part - high) for part in parts])
    return high + jnp.log(mass) * LOG2E


def lifted(pot, lift):
    return jnp.where(lift > -1.0e29, pot + lift, FAR)


def tree(op, values):
    values = list(values)
    while len(values) > 1:
        values = [op(*values[n : n + 2]) if n + 1 < len(values) else values[n] for n in range(0, len(values), 2)]
    return values[0]


def fetch(k2_hbm, k2_ref, sems, b):
    rows = pl.ds(b * 128, 128)
    return pltpu.make_async_copy(k2_hbm.at[rows], k2_ref.at[rows], sems.at[b])


def start_fetch(k2_hbm, k2_ref, sems):
    for b in range(RJ):
        fetch(k2_hbm, k2_ref, sems, b).start()


def lanes_block(tiles_of, count, heads, high_ref, mass_ref, base, joined=False):
    for group in range(16):
        rows = pl.ds(base + group * 8, 8)
        tiles = tiles_of(rows)
        for v in range(count):
            xs = [heads[v][r : r + 1, :] - tile for r, tile in tiles]
            high = tree(jnp.maximum, xs)
            if joined:
                before = high_ref[v, rows, :]
                high = jnp.maximum(high, before)
                xs.append(before)
            masses = [jnp.exp2(x - high) for x in xs]
            if joined:
                masses[-1] = masses[-1] * mass_ref[v, rows, :]
            high_ref[v, rows, :] = high
            mass_ref[v, rows, :] = tree(jnp.add, masses)


def near_tile(k1a_ref, k1b_ref, rows, r):
    if r < RH:
        return k1a_ref[rows, r * 128 : (r + 1) * 128]
    return k1b_ref[rows, (r - RH) * 128 : (r - RH + 1) * 128]


def near_tiles(k1a_ref, k1b_ref):
    return lambda rows: [(r, near_tile(k1a_ref, k1b_ref, rows, r)) for r in range(NEAR)]


def far_tiles(k2_ref):
    return lambda rows: [(r, k2_ref[rows, (r - NEAR) * 128 : (r - NEAR + 1) * 128]) for r in range(NEAR, RI)]


def turned(core, value):
    return jnp.where(core > 0.5, jnp.concatenate([value[RH:RI, :], value[0:RH, :]], axis=0), value)


def lanes_result(count, high_ref, mass_ref):
    results = []
    for v in range(count):
        rows_out = []
        for b in range(RJ):
            high = jnp.transpose(high_ref[v, b * 128 : (b + 1) * 128, :])
            mass = jnp.transpose(mass_ref[v, b * 128 : (b + 1) * 128, :])
            top = jnp.max(high, axis=0, keepdims=True)
            total = jnp.sum(mass * jnp.exp2(high - top), axis=0, keepdims=True)
            rows_out.append((top, total))
        top = jnp.concatenate([row[0] for row in rows_out], axis=0)
        total = jnp.concatenate([row[1] for row in rows_out], axis=0)
        results.append(top + jnp.log(total) * LOG2E)
    return results


def reduce_lanes(k1a_ref, k1b_ref, k2_hbm, k2_ref, sems, heads, high_ref, mass_ref):
    count = len(heads)

    def near(b, carry):
        lanes_block(near_tiles(k1a_ref, k1b_ref), count, heads, high_ref, mass_ref, pl.multiple_of(b * 128, 128))
        return carry

    def far(b, carry):
        fetch(k2_hbm, k2_ref, sems, b).wait()
        lanes_block(far_tiles(k2_ref), count, heads, high_ref, mass_ref, pl.multiple_of(b * 128, 128), True)
        return carry

    lax.fori_loop(0, RJ, near, 0)
    lax.fori_loop(0, RJ, far, 0)
    return lanes_result(count, high_ref, mass_ref)


def reduce_rows(k1a_ref, k1b_ref, k2_hbm, k2_ref, sems, heads, head_ref, wide_ref, high_ref, mass_ref):
    count = len(heads)
    for v in range(count):
        head_ref[v, 0:RJ, :] = heads[v]

    def block(b, wides, tile, r):
        spot = pl.ds(pl.multiple_of(b * 8, 8), 8)
        cols = slice(r * 128, (r + 1) * 128)
        tiles = [tile(pl.ds(b * 128 + group * 8, 8)) for group in range(16)]
        for v in range(count):
            xs = [wides[v][group * 8 : group * 8 + 8, :] - tiles[group] for group in range(16)]
            high = tree(jnp.maximum, xs)
            high_ref[v, spot, cols] = high
            mass_ref[v, spot, cols] = tree(jnp.add, [jnp.exp2(x - high) for x in xs])

    def near(b, carry):
        wides = []
        for v in range(count):
            wides.append(jnp.transpose(jnp.broadcast_to(head_ref[v, pl.ds(b, 1), :], (128, 128))))
            wide_ref[v, pl.ds(pl.multiple_of(b * 128, 128), 128), :] = wides[v]
        for r in range(NEAR):
            block(b, wides, lambda rows: near_tile(k1a_ref, k1b_ref, rows, r), r)
        return carry

    def far(b, carry):
        fetch(k2_hbm, k2_ref, sems, b).wait()
        wides = [wide_ref[v, pl.ds(pl.multiple_of(b * 128, 128), 128), :] for v in range(count)]
        for r in range(NEAR, RI):
            block(b, wides, lambda rows: k2_ref[rows, (r - NEAR) * 128 : (r - NEAR + 1) * 128], r)
        return carry

    lax.fori_loop(0, RJ, near, 0)
    lax.fori_loop(0, RJ, far, 0)
    results = []
    for v in range(count):
        tops, totals = [], []
        for r in range(RI):
            cols = slice(r * 128, (r + 1) * 128)
            high = high_ref[v, :, cols]
            top = jnp.max(high, axis=0, keepdims=True)
            tops.append(top)
            totals.append(jnp.sum(mass_ref[v, :, cols] * jnp.exp2(high - top), axis=0, keepdims=True))
        results.append(jnp.concatenate(tops, axis=0) + jnp.log(jnp.concatenate(totals, axis=0)) * LOG2E)
    return results


def pack_body(gen, ref, out, both, sems):
    copies = [pltpu.make_async_copy(part, both.at[n], sems.at[n]) for n, part in enumerate((gen, ref))]
    for copy in copies:
        copy.start()
    for copy in copies:
        copy.wait()
    wide = jnp.concatenate([both[0].astype(jnp.float32), both[1].astype(jnp.float32)], axis=0)
    out[...] = jnp.transpose(wide).astype(jnp.bfloat16)


def unpack_body(which, info, raw, *refs):
    out = refs[-1]
    for k in range(D // 128):
        cols = slice(k * 128, (k + 1) * 128)
        even, odd = raw[2 * k], raw[2 * k + 1]
        gen = jnp.concatenate([even[:, :64], odd[:, :64]], axis=1)
        ref = jnp.concatenate([even[:, 64:], odd[:, 64:]], axis=1)
        part = jnp.where(info[5 + which] == 1, gen, ref)
        for n in range(4):
            out[n, :, cols] = part


def norm_parts(values):
    values = values.astype(jnp.float32)
    values = values * values
    return functools.reduce(jnp.add, [values[:, k * 128 : (k + 1) * 128] for k in range(D // 128)])


def join_body(info, gen_count, ref_count, one, two, a_out, b_out, lift_i, lift_j, weights):
    c, x, y = info[2], info[3], info[4]
    for s in range(6):
        part = slice(s * 128, (s + 1) * 128)
        a_out[part, :] = jnp.where(c == 0, one[part, :], two[part, :])
        b_out[part, :] = jnp.where(c == 0, two[part, :], one[part, :])

    def total(counts):
        return jnp.full((8, 128), functools.reduce(jnp.add, [counts[n] for n in range(32)]).astype(jnp.float32))

    def number(is_gen, t):
        return jnp.where(is_gen, gen_count[t], ref_count[t])

    def flat(rows):
        shape = (rows, 128)
        return lax.broadcasted_iota(jnp.int32, shape, 0) * 128 + lax.broadcasted_iota(jnp.int32, shape, 1)

    def valid(spots, starts, counts):
        inside = [(spots >= start) & (spots < start + count) for start, count in zip(starts, counts)]
        return functools.reduce(jnp.logical_or, inside)

    a_is_gen, b_is_gen = info[0] == 1, info[1] == 1
    totals = total(gen_count), total(ref_count)
    gen_log, ref_log = (-jnp.log(value) * LOG2E for value in totals)
    counts = [number(a_is_gen, ((n % 4) * 4 + x) * 2 + (c if n < 4 else 1 - c)) for n in range(8)]
    ok = valid(flat(16), [n * BLOCK for n in range(8)], counts)
    log_a = jnp.where(a_is_gen, gen_log, ref_log)
    lift_i[...] = jnp.where(ok, jnp.concatenate([log_a, log_a], axis=0), FAR)
    core = jnp.full((1, 128), c.astype(jnp.float32))
    lift_i[14:15, :] = core
    lift_i[15:16, :] = jnp.full((1, 128), y.astype(jnp.float32))
    here = [(y * 4 + n) * 2 + c for n in range(4)]
    starts = [n * BLOCK for n in range(4)]
    ok = valid(flat(8), starts, [number(b_is_gen, t) for t in here])
    lift_j[...] = jnp.where(ok, jnp.where(b_is_gen, gen_log, ref_log), FAR)
    lift_j[6:7, :] = core
    shift = 64 * lax.rem(y, 2)
    windows = [n * 256 + shift for n in range(4)]
    for n, counts in enumerate((gen_count, ref_count)):
        ok = valid(flat(8), windows, [counts[t] for t in here])
        weights[n * 8 : n * 8 + 8, :] = jnp.where(ok, 1.0 / totals[n], 0.0)
    ok = valid(flat(8), starts, [ref_count[t] for t in here])
    weights[16:24, :] = jnp.where(ok, 1.0 / totals[1], 0.0)


def a_norms(a_ref):
    rows = []
    for s in range(RH):
        flipped = jnp.transpose(norm_parts(a_ref[s * 128 : (s + 1) * 128, :]))
        rows.append(jnp.sum(flipped, axis=0, keepdims=True) * (0.5 * LOG2E / EPSILON))
    return rows


def cost_tiles(a_ref, b_ref, sq_ref, norms, n):
    inner = lax.dot_general(
        b_ref[...],
        a_ref[n * 256 : (n + 1) * 256, :],
        (((1,), (1,)), ((), ())),
        preferred_element_type=jnp.float32,
    )
    scale = LOG2E / EPSILON
    return [(sq_ref[...] + norms[2 * n + s]) - scale * inner[:, s * 128 : (s + 1) * 128] for s in range(2)]


def reduce_pair(head, source, at, high_ref, mass_ref, base, joined):
    heads = [head[base : base + 2, :]]
    pair = lambda rows: [(s, source[rows, at + s * 128 : at + (s + 1) * 128]) for s in range(2)]
    for b in range(RJ):
        lanes_block(pair, 1, heads, high_ref, mass_ref, b * 128, joined)


def cost_own_body(a_ref, b_ref, lift_i, k1a_ref, high_ref, mass_ref, sq_ref):
    head = lift_i[...]
    norms = a_norms(a_ref)
    for b in range(RJ):
        part = slice(b * 128, (b + 1) * 128)
        total = jnp.sum(norm_parts(b_ref[part, :]), axis=1, keepdims=True) * (0.5 * LOG2E / EPSILON)
        sq_ref[part, :] = jnp.broadcast_to(total, (128, 128))
    for n in range(4):
        if n < 3:
            for s, tile in enumerate(cost_tiles(a_ref, b_ref, sq_ref, norms, n)):
                k1a_ref[:, (2 * n + s) * 128 : (2 * n + s + 1) * 128] = tile
        if n > 0:
            reduce_pair(head, k1a_ref, (n - 1) * 256, high_ref, mass_ref, 2 * n - 2, n > 1)


def cost_other_body(
    a_ref, b_ref, lift_i, high_in, mass_in, sq_ref, k1b_ref, k2_hbm, part_out, k2_ref, high_ref, mass_ref, out_sems
):
    head = lift_i[...]
    norms = a_norms(a_ref)
    high_ref[...] = high_in[...]
    mass_ref[...] = mass_in[...]
    stores = [fetch(k2_ref, k2_hbm, out_sems, b) for b in range(RJ)]
    order = [1, 2, 0]
    for step in range(4):
        if step < 3:
            n = order[step]
            target, at = (k1b_ref, 0) if n == 0 else (k2_ref, (n - 1) * 256)
            for s, tile in enumerate(cost_tiles(a_ref, b_ref, sq_ref, norms, n)):
                target[:, at + s * 128 : at + (s + 1) * 128] = tile
        if step > 0:
            n = order[step - 1]
            source, at = (k1b_ref, 0) if n == 0 else (k2_ref, (n - 1) * 256)
            reduce_pair(head, source, at, high_ref, mass_ref, RH + 2 * n, True)
        if step == 1:
            for store in stores:
                store.start()
    (result,) = lanes_result(1, high_ref, mass_ref)
    for n in range(4):
        part_out[n, 0:RJ, :] = result
        part_out[n, RJ:8, :] = jnp.zeros((8 - RJ, 128), jnp.float32)
    for store in stores:
        store.wait()


def second_body(k1a_ref, k1b_ref, k2_hbm, got, lift_j, out, g1_out, k2_ref, sems, head_ref, wide_ref, high_ref, mass_ref):
    core = lift_j[6:7, :]
    start_fetch(k2_hbm, k2_ref, sems)
    g1 = -merge(got, 4)[0:RJ, :]
    g1_out[...] = g1
    lift = lift_j[0:RJ, :]
    heads = [lift, lifted(g1, lift)]
    results = reduce_rows(k1a_ref, k1b_ref, k2_hbm, k2_ref, sems, heads, head_ref, wide_ref, high_ref, mass_ref)
    sent = [turned(core, value) for value in results]
    for n in range(8):
        for v in range(2):
            out[n, v * RI : (v + 1) * RI, :] = sent[v]


def third_body(k1a_ref, k1b_ref, k2_hbm, got, lift_i, out, f2_out, k2_ref, sems, high_ref, mass_ref):
    core = lift_i[14:15, :]
    start_fetch(k2_hbm, k2_ref, sems)
    merged = -merge(got, 8)
    f1 = turned(core, merged[0:RI, :])
    f2 = 0.5 * (f1 + turned(core, merged[RI : 2 * RI, :]))
    f2_out[...] = f2
    lift = lift_i[0:RI, :]
    heads = [lifted(f1, lift), lifted(f2, lift)]
    results = reduce_lanes(k1a_ref, k1b_ref, k2_hbm, k2_ref, sems, heads, high_ref, mass_ref)
    for n in range(4):
        for v in range(2):
            out[n, v * 8 : v * 8 + RJ, :] = results[v]
            out[n, v * 8 + RJ : v * 8 + 8, :] = jnp.zeros((8 - RJ, 128), jnp.float32)


def fourth_body(k1a_ref, k1b_ref, k2_hbm, got, lift_j, g1, out, g3_out, k2_ref, sems, head_ref, wide_ref, high_ref, mass_ref):
    core = lift_j[6:7, :]
    start_fetch(k2_hbm, k2_ref, sems)
    merged = -merge(got, 4)
    g2 = 0.5 * (g1[...] + merged[0:RJ, :])
    g3 = 0.5 * (g2 + merged[8 : 8 + RJ, :])
    g3_out[...] = g3
    lift = lift_j[0:RJ, :]
    heads = [lifted(g2, lift), lifted(g3, lift)]
    results = reduce_rows(k1a_ref, k1b_ref, k2_hbm, k2_ref, sems, heads, head_ref, wide_ref, high_ref, mass_ref)
    sent = [turned(core, value) for value in results]
    for n in range(8):
        for v in range(2):
            out[n, v * RI : (v + 1) * RI, :] = sent[v]


def fifth_body(k1a_ref, k1b_ref, k2_hbm, got, lift_i, f2, g3, out, k2_ref, sems, high_ref, mass_ref):
    core = lift_i[14:15, :]
    start_fetch(k2_hbm, k2_ref, sems)
    merged = -merge(got, 8)
    f3 = 0.5 * (f2[...] + turned(core, merged[0:RI, :]))
    f4 = 0.5 * (f3 + turned(core, merged[RI : 2 * RI, :]))
    heads = [lifted(f3, lift_i[0:RI, :])]
    (result,) = reduce_lanes(k1a_ref, k1b_ref, k2_hbm, k2_ref, sems, heads, high_ref, mass_ref)
    shifted = result - g3[...]
    along_y = lift_i[15:16, :]
    mine = f4[4:6, :]
    for n, row in ((2, 3), (1, 1), (0, 0)):
        mine = jnp.where(along_y < n + 0.5, f4[row : row + 2, :], mine)
    for n in range(16):
        out[n, 0:RJ, :] = shifted
        out[n, RJ : RJ + 2, :] = mine


def last_body(got, weights, pots, g4_out, share):
    g4 = merge([got[n * 4 + 1, 0:RJ, :] for n in range(4)], 4) * (-0.5 * LN2)
    g4_out[0:RJ, :] = g4
    g4_out[RJ:8, :] = jnp.zeros((8 - RJ, 128), jnp.float32)
    weight = weights[16 : 16 + RJ, :]
    total = jnp.sum(jnp.where(weight > 0.0, g4 * weight, 0.0))
    for n in range(4):
        own = slice(RJ, RJ + 2)
        gen_pot = got[n * 4 + 1][own, :] * LN2
        gen_self = got[n * 4][own, :] * LN2
        ref_self = got[n * 4 + 3][own, :] * LN2
        pots[n, 0:2, :] = gen_pot
        pots[n, 2:4, :] = gen_self
        pots[n, 4:6, :] = ref_self
        pots[n, 6:8, :] = jnp.zeros((2, 128), jnp.float32)
        weight = weights[2 * n : 2 * n + 2, :]
        total += jnp.sum(jnp.where(weight > 0.0, (gen_pot - gen_self) * weight, 0.0))
        weight = weights[8 + 2 * n : 8 + 2 * n + 2, :]
        total -= jnp.sum(jnp.where(weight > 0.0, ref_self * weight, 0.0))
    for n in range(8):
        share[n, :, :] = jnp.full((8, 128), total, jnp.float32)


F32 = jnp.float32
BF16 = jnp.bfloat16
STREAM = [pltpu.VMEM((NJ, N2), F32), pltpu.SemaphoreType.DMA((RJ,))]


def lane_scratch(count):
    return [pltpu.VMEM((count, NJ, 128), F32)] * 2


def row_scratch(count):
    return [pltpu.VMEM((count, 8, 128), F32), pltpu.VMEM((count, NJ, 128), F32)] + [pltpu.VMEM((count, 8 * RJ, NI), F32)] * 2


def stage_pack(*args):
    scratch = [pltpu.VMEM((2, 64, BLOCK), BF16), pltpu.SemaphoreType.DMA((2,))]
    out = jax.ShapeDtypeStruct((BLOCK, 128), BF16)
    return call(pack_body, out, [HBM, HBM], scratch, mib=60)(*args)


def stage_unpack(which, *args):
    out = jax.ShapeDtypeStruct((4, BLOCK, D), BF16)
    return call(functools.partial(unpack_body, which), out, [SMEM, VMEM, HBM][: len(args)])(*args)


def stage_join(*args):
    points = (jax.ShapeDtypeStruct((NJ, D), BF16),) * 2
    outs = points + (f32(16, 128), f32(8, 128), f32(24, 128))
    return call(join_body, outs, [SMEM] * 3 + [VMEM] * 2)(*args)


def stage_cost_own(*args):
    outs = (f32(NJ, NI // 2), f32(1, NJ, 128), f32(1, NJ, 128), f32(NJ, 128))
    return call(cost_own_body, outs, [VMEM] * 3)(*args)


def stage_cost_other(*args):
    scratch = [pltpu.VMEM((NJ, N2), F32), *lane_scratch(1), pltpu.SemaphoreType.DMA((RJ,))]
    outs = (f32(NJ, NI // 2 - N2), f32(ROOM, N2), f32(4, 8, 128))
    return call(cost_other_body, outs, [VMEM] * 6, scratch, (VMEM, HBM, VMEM))(*args)


K_SPECS = [VMEM, VMEM, HBM]


def stage_second(*args):
    outs = (f32(8, 2 * RI, 128), f32(RJ, 128))
    return call(second_body, outs, K_SPECS + [VMEM] * 2, STREAM + row_scratch(2))(*args)


def stage_third(*args):
    outs = (f32(4, 16, 128), f32(RI, 128))
    return call(third_body, outs, K_SPECS + [VMEM] * 2, STREAM + lane_scratch(2))(*args)


def stage_fourth(*args):
    outs = (f32(8, 2 * RI, 128), f32(RJ, 128))
    return call(fourth_body, outs, K_SPECS + [VMEM] * 3, STREAM + row_scratch(2))(*args)


def stage_fifth(*args):
    return call(fifth_body, f32(16, 8, 128), K_SPECS + [VMEM] * 4, STREAM + lane_scratch(1))(*args)


def spread(operand, axes, groups=None):
    return lax.all_to_all(operand, axes, 0, 0, tiled=True, axis_index_groups=groups)


def local(gen_points, reference_embeddings, gen_count, ref_count):
    y, x, c, zl = (lax.axis_index(name) for name in ("y", "x", "c", "zl"))
    a_is_gen = zl < 3
    b_is_gen = zl == 0
    packed = stage_pack(jnp.transpose(gen_points), jnp.transpose(reference_embeddings))
    raw = lax.all_gather(packed, ("zh", "zl"))

    info = jnp.stack(
        [
            a_is_gen.astype(jnp.int32),
            b_is_gen.astype(jnp.int32),
            c,
            x,
            y,
            jnp.where(c == 0, a_is_gen, b_is_gen).astype(jnp.int32),
            jnp.where(c == 0, b_is_gen, a_is_gen).astype(jnp.int32),
        ]
    ).astype(jnp.int32)
    along_y = [[[(i * 4 + n) * 2 + core for i in range(4)] for n in range(4)] for core in range(2)]
    along_x = [[[(n * 4 + i) * 2 + core for i in range(4)] for n in range(4)] for core in range(2)]
    one = spread(stage_unpack(0, info, raw), ("y", "x", "c"), along_y[0] + along_x[1])
    two = spread(stage_unpack(1, info, raw, one), ("y", "x", "c"), along_x[0] + along_y[1])
    a_own, b_all, lift_i, lift_j, weights = stage_join(
        info, gen_count, ref_count, one.reshape(NJ, D), two.reshape(NJ, D)
    )
    a_other = lax.ppermute(a_own, "c", [(0, 1), (1, 0)])
    k1a, high, mass, b_norms = stage_cost_own(a_own, b_all, lift_i)
    k1b, k2, part = stage_cost_other(a_other, b_all, lift_i, high, mass, b_norms)
    k = (k1a, k1b, k2)
    part, g1 = stage_second(*k, spread(part, "x"), lift_j)
    part, f2 = stage_third(*k, spread(part, ("y", "c")), lift_i)
    part, g3 = stage_fourth(*k, spread(part, "x"), lift_j, g1)
    part = stage_fifth(*k, spread(part, ("y", "c")), lift_i, f2, g3)
    got = spread(part, ("x", "zl"))
    pots, g4, share = call(last_body, (f32(4, 8, 128), f32(8, 128), f32(8, 8, 128)), [VMEM, VMEM])(got, weights)
    divergence = jnp.sum(spread(share, ("y", "c"))[:, 0, 0])

    mine = lax.dynamic_index_in_dim(pots, x, 0, keepdims=False)
    mine = lax.dynamic_slice_in_dim(mine.reshape(4, 256), 64 * (y % 2), BLOCK, 1)
    ref_pot = lax.dynamic_slice_in_dim(g4.reshape(1024), x * BLOCK, BLOCK, 0)
    return mine[0], ref_pot, mine[1], mine[2], divergence


def solution(mesh):
    fine = Mesh(mesh.devices.reshape(4, 4, 2, 4, 4), ("y", "x", "c", "zh", "zl"))
    tile, feat = ("y", "x", "c"), ("zh", "zl")
    return jax.shard_map(
        local,
        mesh=fine,
        in_specs=(P(tile, feat), P(tile, feat), P(), P()),
        out_specs=(P(tile), P(tile), P(tile), P(tile), P()),
        check_vma=False,
    )
```

```python
import functools

import jax
import jax.numpy as jnp
from jax import lax
from jax.experimental import pallas as pl
from jax.experimental.pallas import tpu as pltpu
from jax.sharding import Mesh, PartitionSpec as P

EPSILON = 0.25
LOG2E = 1.4426950408889634
LN2 = 0.6931471805599453
FAR = -1.0e30

BLOCK = 192
D = 1024
NI = 8 * BLOCK
NJ = 4 * BLOCK
RI = NI // 128
RH = RI // 2
RJ = NJ // 128
NEAR = 8
N2 = NI - NEAR * 128
PACK_MIB = 40
ROOM = 18 * NJ

VMEM = pl.BlockSpec(memory_space=pltpu.VMEM)
HBM = pl.BlockSpec(memory_space=pltpu.HBM)
SMEM = pl.BlockSpec(memory_space=pltpu.SMEM)


def f32(*shape):
    return jax.ShapeDtypeStruct(shape, jnp.float32)


def call(body, outs, ins, scratch=(), out_specs=None, mib=40):
    return pl.pallas_call(
        body,
        out_shape=outs,
        in_specs=ins,
        out_specs=jax.tree.map(lambda _: VMEM, outs) if out_specs is None else out_specs,
        scratch_shapes=list(scratch),
        compiler_params=pltpu.CompilerParams(vmem_limit_bytes=mib * 1024 * 1024),
    )


def merge(got, count):
    parts = [got[n] for n in range(count)]
    high = functools.reduce(jnp.maximum, parts)
    mass = functools.reduce(jnp.add, [jnp.exp2(part - high) for part in parts])
    return high + jnp.log(mass) * LOG2E


def lifted(pot, lift):
    return jnp.where(lift > -1.0e29, pot + lift, FAR)


def tree(op, values):
    values = list(values)
    while len(values) > 1:
        values = [op(*values[n : n + 2]) if n + 1 < len(values) else values[n] for n in range(0, len(values), 2)]
    return values[0]


def fetch(k2_hbm, k2_ref, sems, b):
    rows = pl.ds(b * 128, 128)
    return pltpu.make_async_copy(k2_hbm.at[rows], k2_ref.at[rows], sems.at[b])


def start_fetch(k2_hbm, k2_ref, sems):
    for b in range(RJ):
        fetch(k2_hbm, k2_ref, sems, b).start()


def lanes_block(tiles_of, count, heads, high_ref, mass_ref, base, joined=False):
    for group in range(16):
        rows = pl.ds(base + group * 8, 8)
        tiles = tiles_of(rows)
        for v in range(count):
            xs = [heads[v][r : r + 1, :] - tile for r, tile in tiles]
            high = tree(jnp.maximum, xs)
            if joined:
                before = high_ref[v, rows, :]
                high = jnp.maximum(high, before)
                xs.append(before)
            masses = [jnp.exp2(x - high) for x in xs]
            if joined:
                masses[-1] = masses[-1] * mass_ref[v, rows, :]
            high_ref[v, rows, :] = high
            mass_ref[v, rows, :] = tree(jnp.add, masses)


def near_tile(k1a_ref, k1b_ref, rows, r):
    if r < RH:
        return k1a_ref[rows, r * 128 : (r + 1) * 128]
    return k1b_ref[rows, (r - RH) * 128 : (r - RH + 1) * 128]


def near_tiles(k1a_ref, k1b_ref):
    return lambda rows: [(r, near_tile(k1a_ref, k1b_ref, rows, r)) for r in range(NEAR)]


def far_tiles(k2_ref):
    return lambda rows: [(r, k2_ref[rows, (r - NEAR) * 128 : (r - NEAR + 1) * 128]) for r in range(NEAR, RI)]


def turned(core, value):
    return jnp.where(core > 0.5, jnp.concatenate([value[RH:RI, :], value[0:RH, :]], axis=0), value)


def lanes_result(count, high_ref, mass_ref):
    results = []
    for v in range(count):
        rows_out = []
        for b in range(RJ):
            high = jnp.transpose(high_ref[v, b * 128 : (b + 1) * 128, :])
            mass = jnp.transpose(mass_ref[v, b * 128 : (b + 1) * 128, :])
            top = jnp.max(high, axis=0, keepdims=True)
            total = jnp.sum(mass * jnp.exp2(high - top), axis=0, keepdims=True)
            rows_out.append((top, total))
        top = jnp.concatenate([row[0] for row in rows_out], axis=0)
        total = jnp.concatenate([row[1] for row in rows_out], axis=0)
        results.append(top + jnp.log(total) * LOG2E)
    return results


def reduce_lanes(k1a_ref, k1b_ref, k2_hbm, k2_ref, sems, heads, high_ref, mass_ref):
    count = len(heads)

    def near(b, carry):
        lanes_block(near_tiles(k1a_ref, k1b_ref), count, heads, high_ref, mass_ref, pl.multiple_of(b * 128, 128))
        return carry

    def far(b, carry):
        fetch(k2_hbm, k2_ref, sems, b).wait()
        lanes_block(far_tiles(k2_ref), count, heads, high_ref, mass_ref, pl.multiple_of(b * 128, 128), True)
        return carry

    lax.fori_loop(0, RJ, near, 0)
    lax.fori_loop(0, RJ, far, 0)
    return lanes_result(count, high_ref, mass_ref)


def reduce_rows(k1a_ref, k1b_ref, k2_hbm, k2_ref, sems, heads, head_ref, wide_ref, high_ref, mass_ref):
    count = len(heads)
    for v in range(count):
        head_ref[v, 0:RJ, :] = heads[v]

    def block(b, wides, tile, r):
        spot = pl.ds(pl.multiple_of(b * 8, 8), 8)
        cols = slice(r * 128, (r + 1) * 128)
        tiles = [tile(pl.ds(b * 128 + group * 8, 8)) for group in range(16)]
        for v in range(count):
            xs = [wides[v][group * 8 : group * 8 + 8, :] - tiles[group] for group in range(16)]
            high = tree(jnp.maximum, xs)
            high_ref[v, spot, cols] = high
            mass_ref[v, spot, cols] = tree(jnp.add, [jnp.exp2(x - high) for x in xs])

    def near(b, carry):
        wides = []
        for v in range(count):
            wides.append(jnp.transpose(jnp.broadcast_to(head_ref[v, pl.ds(b, 1), :], (128, 128))))
            wide_ref[v, pl.ds(pl.multiple_of(b * 128, 128), 128), :] = wides[v]
        for r in range(NEAR):
            block(b, wides, lambda rows: near_tile(k1a_ref, k1b_ref, rows, r), r)
        return carry

    def far(b, carry):
        fetch(k2_hbm, k2_ref, sems, b).wait()
        wides = [wide_ref[v, pl.ds(pl.multiple_of(b * 128, 128), 128), :] for v in range(count)]
        for r in range(NEAR, RI):
            block(b, wides, lambda rows: k2_ref[rows, (r - NEAR) * 128 : (r - NEAR + 1) * 128], r)
        return carry

    lax.fori_loop(0, RJ, near, 0)
    lax.fori_loop(0, RJ, far, 0)
    results = []
    for v in range(count):
        tops, totals = [], []
        for r in range(RI):
            cols = slice(r * 128, (r + 1) * 128)
            high = high_ref[v, :, cols]
            top = jnp.max(high, axis=0, keepdims=True)
            tops.append(top)
            totals.append(jnp.sum(mass_ref[v, :, cols] * jnp.exp2(high - top), axis=0, keepdims=True))
        results.append(jnp.concatenate(tops, axis=0) + jnp.log(jnp.concatenate(totals, axis=0)) * LOG2E)
    return results


def pack_body(gen, ref, out, both, sems):
    copies = [pltpu.make_async_copy(part, both.at[n], sems.at[n]) for n, part in enumerate((gen, ref))]
    for copy in copies:
        copy.start()
    for copy in copies:
        copy.wait()
    for n in range(2):
        points = jnp.transpose(both[n].astype(jnp.float32))
        rows = jnp.concatenate([points[:96, :], points[96:, :]], axis=1).astype(jnp.bfloat16)
        for z in range(16):
            if (z % 4) // 2 == n:
                out[z] = rows


def unpack_body(raw, own_out, wide_out):
    for k in range(D // 128):
        cols = slice(k * 128, (k + 1) * 128)
        even, odd = raw[2 * k], raw[2 * k + 1]
        for half, lanes in enumerate((slice(0, 64), slice(64, 128))):
            part = jnp.concatenate([even[:, lanes], odd[:, lanes]], axis=1)
            rows = slice(half * 96, half * 96 + 96)
            own_out[rows, cols] = part
            for n in range(4):
                wide_out[n, rows, cols] = part


def widen_body(info, own, swapped, out):
    part = jnp.where(info[0] != info[1], swapped[...], own[...])
    for n in range(4):
        out[n] = part


def norm_parts(values):
    values = values.astype(jnp.float32)
    values = values * values
    return functools.reduce(jnp.add, [values[:, k * 128 : (k + 1) * 128] for k in range(D // 128)])


def masks(info, gen_count, ref_count, lift_i, lift_j, weights):
    c, x, y = info[2], info[3], info[4]

    def total(counts):
        return jnp.full((8, 128), functools.reduce(jnp.add, [counts[n] for n in range(32)]).astype(jnp.float32))

    def number(is_gen, t):
        return jnp.where(is_gen, gen_count[t], ref_count[t])

    def flat(rows):
        shape = (rows, 128)
        return lax.broadcasted_iota(jnp.int32, shape, 0) * 128 + lax.broadcasted_iota(jnp.int32, shape, 1)

    def valid(spots, starts, counts):
        inside = [(spots >= start) & (spots < start + count) for start, count in zip(starts, counts)]
        return functools.reduce(jnp.logical_or, inside)

    a_is_gen, b_is_gen = info[0] == 1, info[1] == 1
    totals = total(gen_count), total(ref_count)
    gen_log, ref_log = (-jnp.log(value) * LOG2E for value in totals)
    counts = [number(a_is_gen, ((n % 4) * 4 + x) * 2 + (c if n < 4 else 1 - c)) for n in range(8)]
    ok = valid(flat(16), [n * BLOCK for n in range(8)], counts)
    log_a = jnp.where(a_is_gen, gen_log, ref_log)
    lift_i[...] = jnp.where(ok, jnp.concatenate([log_a, log_a], axis=0), FAR)
    core = jnp.full((1, 128), c.astype(jnp.float32))
    lift_i[14:15, :] = core
    lift_i[15:16, :] = jnp.full((1, 128), y.astype(jnp.float32))
    here = [(y * 4 + n) * 2 + c for n in range(4)]
    starts = [n * BLOCK for n in range(4)]
    ok = valid(flat(8), starts, [number(b_is_gen, t) for t in here])
    lift_j[...] = jnp.where(ok, jnp.where(b_is_gen, gen_log, ref_log), FAR)
    lift_j[6:7, :] = core
    shift = 64 * lax.rem(y, 2)
    windows = [n * 256 + shift for n in range(4)]
    for n, counts in enumerate((gen_count, ref_count)):
        ok = valid(flat(8), windows, [counts[t] for t in here])
        weights[n * 8 : n * 8 + 8, :] = jnp.where(ok, 1.0 / totals[n], 0.0)
    ok = valid(flat(8), starts, [ref_count[t] for t in here])
    weights[16:24, :] = jnp.where(ok, 1.0 / totals[1], 0.0)


def a_norms(a_ref):
    rows = []
    for s in range(RH):
        flipped = jnp.transpose(norm_parts(a_ref[s * 128 : (s + 1) * 128, :]))
        rows.append(jnp.sum(flipped, axis=0, keepdims=True) * (0.5 * LOG2E / EPSILON))
    return rows


def cost_tiles(a_ref, b_ref, sq_ref, norms, n):
    inner = lax.dot_general(
        b_ref[...],
        a_ref[n * 256 : (n + 1) * 256, :],
        (((1,), (1,)), ((), ())),
        preferred_element_type=jnp.float32,
    )
    scale = LOG2E / EPSILON
    return [(sq_ref[...] + norms[2 * n + s]) - scale * inner[:, s * 128 : (s + 1) * 128] for s in range(2)]


def reduce_pair(head, source, at, high_ref, mass_ref, base, joined):
    heads = [head[base : base + 2, :]]
    pair = lambda rows: [(s, source[rows, at + s * 128 : at + (s + 1) * 128]) for s in range(2)]
    for b in range(RJ):
        lanes_block(pair, 1, heads, high_ref, mass_ref, b * 128, joined)


def cost_own_body(
    info, gen_count, ref_count, a_ref, b_ref, k1a_ref, high_ref, mass_ref, sq_ref, lift_i, lift_j, weights
):
    masks(info, gen_count, ref_count, lift_i, lift_j, weights)
    head = lift_i[...]
    norms = a_norms(a_ref)
    for b in range(RJ):
        part = slice(b * 128, (b + 1) * 128)
        total = jnp.sum(norm_parts(b_ref[part, :]), axis=1, keepdims=True) * (0.5 * LOG2E / EPSILON)
        sq_ref[part, :] = jnp.broadcast_to(total, (128, 128))
    for n in range(4):
        if n < 3:
            for s, tile in enumerate(cost_tiles(a_ref, b_ref, sq_ref, norms, n)):
                k1a_ref[:, (2 * n + s) * 128 : (2 * n + s + 1) * 128] = tile
        if n > 0:
            reduce_pair(head, k1a_ref, (n - 1) * 256, high_ref, mass_ref, 2 * n - 2, n > 1)


def cost_other_body(
    a_ref, b_ref, lift_i, high_in, mass_in, sq_ref, k1b_ref, k2_hbm, part_out, k2_ref, high_ref, mass_ref, out_sems
):
    head = lift_i[...]
    norms = a_norms(a_ref)
    high_ref[...] = high_in[...]
    mass_ref[...] = mass_in[...]
    stores = [fetch(k2_ref, k2_hbm, out_sems, b) for b in range(RJ)]
    order = [1, 2, 0]
    for step in range(4):
        if step < 3:
            n = order[step]
            target, at = (k1b_ref, 0) if n == 0 else (k2_ref, (n - 1) * 256)
            for s, tile in enumerate(cost_tiles(a_ref, b_ref, sq_ref, norms, n)):
                target[:, at + s * 128 : at + (s + 1) * 128] = tile
        if step > 0:
            n = order[step - 1]
            source, at = (k1b_ref, 0) if n == 0 else (k2_ref, (n - 1) * 256)
            reduce_pair(head, source, at, high_ref, mass_ref, RH + 2 * n, True)
        if step == 1:
            for store in stores:
                store.start()
    (result,) = lanes_result(1, high_ref, mass_ref)
    for n in range(4):
        part_out[n, 0:RJ, :] = result
        part_out[n, RJ:8, :] = jnp.zeros((8 - RJ, 128), jnp.float32)
    for store in stores:
        store.wait()


def second_body(k1a_ref, k1b_ref, k2_hbm, got, lift_j, out, g1_out, k2_ref, sems, head_ref, wide_ref, high_ref, mass_ref):
    core = lift_j[6:7, :]
    start_fetch(k2_hbm, k2_ref, sems)
    g1 = -merge(got, 4)[0:RJ, :]
    g1_out[...] = g1
    lift = lift_j[0:RJ, :]
    heads = [lift, lifted(g1, lift)]
    results = reduce_rows(k1a_ref, k1b_ref, k2_hbm, k2_ref, sems, heads, head_ref, wide_ref, high_ref, mass_ref)
    sent = [turned(core, value) for value in results]
    for n in range(8):
        for v in range(2):
            out[n, v * RI : (v + 1) * RI, :] = sent[v]


def third_body(k1a_ref, k1b_ref, k2_hbm, got, lift_i, out, f2_out, k2_ref, sems, high_ref, mass_ref):
    core = lift_i[14:15, :]
    start_fetch(k2_hbm, k2_ref, sems)
    merged = -merge(got, 8)
    f1 = turned(core, merged[0:RI, :])
    f2 = 0.5 * (f1 + turned(core, merged[RI : 2 * RI, :]))
    f2_out[...] = f2
    lift = lift_i[0:RI, :]
    heads = [lifted(f1, lift), lifted(f2, lift)]
    results = reduce_lanes(k1a_ref, k1b_ref, k2_hbm, k2_ref, sems, heads, high_ref, mass_ref)
    for n in range(4):
        for v in range(2):
            out[n, v * 8 : v * 8 + RJ, :] = results[v]
            out[n, v * 8 + RJ : v * 8 + 8, :] = jnp.zeros((8 - RJ, 128), jnp.float32)


def fourth_body(k1a_ref, k1b_ref, k2_hbm, got, lift_j, g1, out, g3_out, k2_ref, sems, head_ref, wide_ref, high_ref, mass_ref):
    core = lift_j[6:7, :]
    start_fetch(k2_hbm, k2_ref, sems)
    merged = -merge(got, 4)
    g2 = 0.5 * (g1[...] + merged[0:RJ, :])
    g3 = 0.5 * (g2 + merged[8 : 8 + RJ, :])
    g3_out[...] = g3
    lift = lift_j[0:RJ, :]
    heads = [lifted(g2, lift), lifted(g3, lift)]
    results = reduce_rows(k1a_ref, k1b_ref, k2_hbm, k2_ref, sems, heads, head_ref, wide_ref, high_ref, mass_ref)
    sent = [turned(core, value) for value in results]
    for n in range(8):
        for v in range(2):
            out[n, v * RI : (v + 1) * RI, :] = sent[v]


def fifth_body(k1a_ref, k1b_ref, k2_hbm, got, lift_i, f2, g3, out, k2_ref, sems, high_ref, mass_ref):
    core = lift_i[14:15, :]
    start_fetch(k2_hbm, k2_ref, sems)
    merged = -merge(got, 8)
    f3 = 0.5 * (f2[...] + turned(core, merged[0:RI, :]))
    f4 = 0.5 * (f3 + turned(core, merged[RI : 2 * RI, :]))
    heads = [lifted(f3, lift_i[0:RI, :])]
    (result,) = reduce_lanes(k1a_ref, k1b_ref, k2_hbm, k2_ref, sems, heads, high_ref, mass_ref)
    shifted = result - g3[...]
    along_y = lift_i[15:16, :]
    mine = f4[4:6, :]
    for n, row in ((2, 3), (1, 1), (0, 0)):
        mine = jnp.where(along_y < n + 0.5, f4[row : row + 2, :], mine)
    for n in range(16):
        out[n, 0:RJ, :] = shifted
        out[n, RJ : RJ + 2, :] = mine


def last_body(got, weights, pots, g4_out, share):
    g4 = merge([got[n * 4 + 1, 0:RJ, :] for n in range(4)], 4) * (-0.5 * LN2)
    g4_out[0:RJ, :] = g4
    g4_out[RJ:8, :] = jnp.zeros((8 - RJ, 128), jnp.float32)
    weight = weights[16 : 16 + RJ, :]
    total = jnp.sum(jnp.where(weight > 0.0, g4 * weight, 0.0))
    for n in range(4):
        own = slice(RJ, RJ + 2)
        gen_pot = got[n * 4 + 1][own, :] * LN2
        gen_self = got[n * 4][own, :] * LN2
        ref_self = got[n * 4 + 3][own, :] * LN2
        pots[n, 0:2, :] = gen_pot
        pots[n, 2:4, :] = gen_self
        pots[n, 4:6, :] = ref_self
        pots[n, 6:8, :] = jnp.zeros((2, 128), jnp.float32)
        weight = weights[2 * n : 2 * n + 2, :]
        total += jnp.sum(jnp.where(weight > 0.0, (gen_pot - gen_self) * weight, 0.0))
        weight = weights[8 + 2 * n : 8 + 2 * n + 2, :]
        total -= jnp.sum(jnp.where(weight > 0.0, ref_self * weight, 0.0))
    for n in range(8):
        share[n, :, :] = jnp.full((8, 128), total, jnp.float32)


F32 = jnp.float32
BF16 = jnp.bfloat16
STREAM = [pltpu.VMEM((NJ, N2), F32), pltpu.SemaphoreType.DMA((RJ,))]


def lane_scratch(count):
    return [pltpu.VMEM((count, NJ, 128), F32)] * 2


def row_scratch(count):
    return [pltpu.VMEM((count, 8, 128), F32), pltpu.VMEM((count, NJ, 128), F32)] + [pltpu.VMEM((count, 8 * RJ, NI), F32)] * 2


def bf16(*shape):
    return jax.ShapeDtypeStruct(shape, BF16)


def stage_pack(*args):
    scratch = [pltpu.VMEM((2, 64, BLOCK), BF16), pltpu.SemaphoreType.DMA((2,))]
    return call(pack_body, bf16(16, 96, 128), [HBM, HBM], scratch, mib=PACK_MIB)(*args)


def stage_unpack(*args):
    return call(unpack_body, (bf16(BLOCK, D), bf16(4, BLOCK, D)), [VMEM])(*args)


def stage_widen(*args):
    return call(widen_body, bf16(4, BLOCK, D), [SMEM, VMEM, VMEM])(*args)


def stage_cost_own(*args):
    outs = (f32(NJ, NI // 2), f32(1, NJ, 128), f32(1, NJ, 128), f32(NJ, 128))
    outs += (f32(16, 128), f32(8, 128), f32(24, 128))
    return call(cost_own_body, outs, [SMEM] * 3 + [VMEM] * 2)(*args)


def stage_cost_other(*args):
    scratch = [pltpu.VMEM((NJ, N2), F32), *lane_scratch(1), pltpu.SemaphoreType.DMA((RJ,))]
    outs = (f32(NJ, NI // 2 - N2), f32(ROOM, N2), f32(4, 8, 128))
    return call(cost_other_body, outs, [VMEM] * 6, scratch, (VMEM, HBM, VMEM))(*args)


K_SPECS = [VMEM, VMEM, HBM]


def stage_second(*args):
    outs = (f32(8, 2 * RI, 128), f32(RJ, 128))
    return call(second_body, outs, K_SPECS + [VMEM] * 2, STREAM + row_scratch(2))(*args)


def stage_third(*args):
    outs = (f32(4, 16, 128), f32(RI, 128))
    return call(third_body, outs, K_SPECS + [VMEM] * 2, STREAM + lane_scratch(2))(*args)


def stage_fourth(*args):
    outs = (f32(8, 2 * RI, 128), f32(RJ, 128))
    return call(fourth_body, outs, K_SPECS + [VMEM] * 3, STREAM + row_scratch(2))(*args)


def stage_fifth(*args):
    return call(fifth_body, f32(16, 8, 128), K_SPECS + [VMEM] * 4, STREAM + lane_scratch(1))(*args)


def spread(operand, axes):
    return lax.all_to_all(operand, axes, 0, 0, tiled=True)


def local(gen_points, reference_embeddings, gen_count, ref_count):
    y, x, c, zl = (lax.axis_index(name) for name in ("y", "x", "c", "zl"))
    a_is_gen = zl < 2
    b_is_gen = (zl == 0) | (zl == 2)
    packed = stage_pack(jnp.transpose(gen_points), jnp.transpose(reference_embeddings))
    raw = spread(packed, ("zh", "zl"))
    info = jnp.stack(
        [
            a_is_gen.astype(jnp.int32),
            b_is_gen.astype(jnp.int32),
            c,
            x,
            y,
        ]
    ).astype(jnp.int32)
    own, wide_a = stage_unpack(raw)
    swapped = lax.ppermute(own, "zl", [(1, 2), (2, 1)])
    one = spread(wide_a, "y")
    two = spread(stage_widen(info, own, swapped), "x")
    a_own, b_all = lax.optimization_barrier((one.reshape(NJ, D), two.reshape(NJ, D)))
    a_other = lax.ppermute(a_own, "c", [(0, 1), (1, 0)])
    k1a, high, mass, b_norms, lift_i, lift_j, weights = stage_cost_own(
        info, gen_count, ref_count, a_own, b_all
    )
    k1b, k2, part = stage_cost_other(a_other, b_all, lift_i, high, mass, b_norms)
    k = (k1a, k1b, k2)
    part, g1 = stage_second(*k, spread(part, "x"), lift_j)
    part, f2 = stage_third(*k, spread(part, ("y", "c")), lift_i)
    part, g3 = stage_fourth(*k, spread(part, "x"), lift_j, g1)
    part = stage_fifth(*k, spread(part, ("y", "c")), lift_i, f2, g3)
    got = spread(part, ("x", "zl"))
    pots, g4, share = call(last_body, (f32(4, 8, 128), f32(8, 128), f32(8, 8, 128)), [VMEM, VMEM])(got, weights)
    divergence = jnp.sum(spread(share, ("y", "c"))[:, 0, 0])

    mine = lax.dynamic_index_in_dim(pots, x, 0, keepdims=False)
    mine = lax.dynamic_slice_in_dim(mine.reshape(4, 256), 64 * (y % 2), BLOCK, 1)
    ref_pot = lax.dynamic_slice_in_dim(g4.reshape(1024), x * BLOCK, BLOCK, 0)
    return mine[0], ref_pot, mine[1], mine[2], divergence


def solution(mesh):
    fine = Mesh(mesh.devices.reshape(4, 4, 2, 4, 4), ("y", "x", "c", "zh", "zl"))
    tile, feat = ("y", "x", "c"), ("zh", "zl")
    return jax.shard_map(
        local,
        mesh=fine,
        in_specs=(P(tile, feat), P(tile, feat), P(), P()),
        out_specs=(P(tile), P(tile), P(tile), P(tile), P()),
        check_vma=False,
    )
```

```python
import functools

import jax
import jax.numpy as jnp
from jax import lax
from jax.experimental import pallas as pl
from jax.experimental.pallas import tpu as pltpu
from jax.sharding import Mesh, PartitionSpec as P

EPSILON = 0.25
LOG2E = 1.4426950408889634
LN2 = 0.6931471805599453
FAR = -1.0e30

BLOCK = 192
D = 1024
NI = 8 * BLOCK
NJ = 4 * BLOCK
RI = NI // 128
RH = RI // 2
RJ = NJ // 128
NEAR = 8
N2 = NI - NEAR * 128
ROOM = 18 * NJ

VMEM = pl.BlockSpec(memory_space=pltpu.VMEM)
HBM = pl.BlockSpec(memory_space=pltpu.HBM)
SMEM = pl.BlockSpec(memory_space=pltpu.SMEM)


def f32(*shape):
    return jax.ShapeDtypeStruct(shape, jnp.float32)


def call(body, outs, ins, scratch=(), out_specs=None, mib=40):
    return pl.pallas_call(
        body,
        out_shape=outs,
        in_specs=ins,
        out_specs=jax.tree.map(lambda _: VMEM, outs) if out_specs is None else out_specs,
        scratch_shapes=list(scratch),
        compiler_params=pltpu.CompilerParams(vmem_limit_bytes=mib * 1024 * 1024),
    )


def merge(got, count):
    parts = [got[n] for n in range(count)]
    high = functools.reduce(jnp.maximum, parts)
    mass = functools.reduce(jnp.add, [jnp.exp2(part - high) for part in parts])
    return high + jnp.log(mass) * LOG2E


def lifted(pot, lift):
    return jnp.where(lift > -1.0e29, pot + lift, FAR)


def tree(op, values):
    values = list(values)
    while len(values) > 1:
        values = [op(*values[n : n + 2]) if n + 1 < len(values) else values[n] for n in range(0, len(values), 2)]
    return values[0]


def fetch(k2_hbm, k2_ref, sems, b):
    rows = pl.ds(b * 128, 128)
    return pltpu.make_async_copy(k2_hbm.at[rows], k2_ref.at[rows], sems.at[b])


def start_fetch(k2_hbm, k2_ref, sems):
    for b in range(RJ):
        fetch(k2_hbm, k2_ref, sems, b).start()


def lanes_block(tiles_of, count, heads, high_ref, mass_ref, base, joined=False):
    for group in range(16):
        rows = pl.ds(base + group * 8, 8)
        tiles = tiles_of(rows)
        for v in range(count):
            xs = [heads[v][r : r + 1, :] - tile for r, tile in tiles]
            high = tree(jnp.maximum, xs)
            if joined:
                before = high_ref[v, rows, :]
                high = jnp.maximum(high, before)
                xs.append(before)
            masses = [jnp.exp2(x - high) for x in xs]
            if joined:
                masses[-1] = masses[-1] * mass_ref[v, rows, :]
            high_ref[v, rows, :] = high
            mass_ref[v, rows, :] = tree(jnp.add, masses)


def near_tile(k1a_ref, k1b_ref, rows, r):
    if r < RH:
        return k1a_ref[rows, r * 128 : (r + 1) * 128]
    return k1b_ref[rows, (r - RH) * 128 : (r - RH + 1) * 128]


def near_tiles(k1a_ref, k1b_ref):
    return lambda rows: [(r, near_tile(k1a_ref, k1b_ref, rows, r)) for r in range(NEAR)]


def far_tiles(k2_ref):
    return lambda rows: [(r, k2_ref[rows, (r - NEAR) * 128 : (r - NEAR + 1) * 128]) for r in range(NEAR, RI)]


def turned(core, value):
    return jnp.where(core > 0.5, jnp.concatenate([value[RH:RI, :], value[0:RH, :]], axis=0), value)


def lanes_result(count, high_ref, mass_ref):
    results = []
    for v in range(count):
        rows_out = []
        for b in range(RJ):
            high = jnp.transpose(high_ref[v, b * 128 : (b + 1) * 128, :])
            mass = jnp.transpose(mass_ref[v, b * 128 : (b + 1) * 128, :])
            top = jnp.max(high, axis=0, keepdims=True)
            total = jnp.sum(mass * jnp.exp2(high - top), axis=0, keepdims=True)
            rows_out.append((top, total))
        top = jnp.concatenate([row[0] for row in rows_out], axis=0)
        total = jnp.concatenate([row[1] for row in rows_out], axis=0)
        results.append(top + jnp.log(total) * LOG2E)
    return results


def reduce_lanes(k1a_ref, k1b_ref, k2_hbm, k2_ref, sems, heads, high_ref, mass_ref):
    count = len(heads)

    def near(b, carry):
        lanes_block(near_tiles(k1a_ref, k1b_ref), count, heads, high_ref, mass_ref, pl.multiple_of(b * 128, 128))
        return carry

    def far(b, carry):
        fetch(k2_hbm, k2_ref, sems, b).wait()
        lanes_block(far_tiles(k2_ref), count, heads, high_ref, mass_ref, pl.multiple_of(b * 128, 128), True)
        return carry

    lax.fori_loop(0, RJ, near, 0)
    lax.fori_loop(0, RJ, far, 0)
    return lanes_result(count, high_ref, mass_ref)


def reduce_rows(k1a_ref, k1b_ref, k2_hbm, k2_ref, sems, heads, head_ref, wide_ref, high_ref, mass_ref):
    count = len(heads)
    for v in range(count):
        head_ref[v, 0:RJ, :] = heads[v]

    def block(b, wides, tile, r):
        spot = pl.ds(pl.multiple_of(b * 8, 8), 8)
        cols = slice(r * 128, (r + 1) * 128)
        tiles = [tile(pl.ds(b * 128 + group * 8, 8)) for group in range(16)]
        for v in range(count):
            xs = [wides[v][group * 8 : group * 8 + 8, :] - tiles[group] for group in range(16)]
            high = tree(jnp.maximum, xs)
            high_ref[v, spot, cols] = high
            mass_ref[v, spot, cols] = tree(jnp.add, [jnp.exp2(x - high) for x in xs])

    def near(b, carry):
        wides = []
        for v in range(count):
            wides.append(jnp.transpose(jnp.broadcast_to(head_ref[v, pl.ds(b, 1), :], (128, 128))))
            wide_ref[v, pl.ds(pl.multiple_of(b * 128, 128), 128), :] = wides[v]
        for r in range(NEAR):
            block(b, wides, lambda rows: near_tile(k1a_ref, k1b_ref, rows, r), r)
        return carry

    def far(b, carry):
        fetch(k2_hbm, k2_ref, sems, b).wait()
        wides = [wide_ref[v, pl.ds(pl.multiple_of(b * 128, 128), 128), :] for v in range(count)]
        for r in range(NEAR, RI):
            block(b, wides, lambda rows: k2_ref[rows, (r - NEAR) * 128 : (r - NEAR + 1) * 128], r)
        return carry

    lax.fori_loop(0, RJ, near, 0)
    lax.fori_loop(0, RJ, far, 0)
    results = []
    for v in range(count):
        tops, totals = [], []
        for r in range(RI):
            cols = slice(r * 128, (r + 1) * 128)
            high = high_ref[v, :, cols]
            top = jnp.max(high, axis=0, keepdims=True)
            tops.append(top)
            totals.append(jnp.sum(mass_ref[v, :, cols] * jnp.exp2(high - top), axis=0, keepdims=True))
        results.append(jnp.concatenate(tops, axis=0) + jnp.log(jnp.concatenate(totals, axis=0)) * LOG2E)
    return results


def pack_body(gen, ref, out, both, sems):
    copies = [pltpu.make_async_copy(part, both.at[n], sems.at[n]) for n, part in enumerate((gen, ref))]
    for copy in copies:
        copy.start()
    for copy in copies:
        copy.wait()
    wide = jnp.concatenate([both[0].astype(jnp.float32), both[1].astype(jnp.float32)], axis=0)
    out[...] = jnp.transpose(wide).astype(jnp.bfloat16)


def unpack_body(which, info, raw, *refs):
    out = refs[-1]
    for k in range(D // 128):
        cols = slice(k * 128, (k + 1) * 128)
        even, odd = raw[2 * k], raw[2 * k + 1]
        gen = jnp.concatenate([even[:, :64], odd[:, :64]], axis=1)
        ref = jnp.concatenate([even[:, 64:], odd[:, 64:]], axis=1)
        part = jnp.where(info[which] == 1, gen, ref)
        for n in range(4):
            out[n, :, cols] = part


def norm_parts(values):
    values = values.astype(jnp.float32)
    values = values * values
    return functools.reduce(jnp.add, [values[:, k * 128 : (k + 1) * 128] for k in range(D // 128)])


def masks(info, gen_count, ref_count, lift_i, lift_j, weights):
    c, x, y = info[2], info[3], info[4]

    def total(counts):
        return jnp.full((8, 128), functools.reduce(jnp.add, [counts[n] for n in range(32)]).astype(jnp.float32))

    def number(is_gen, t):
        return jnp.where(is_gen, gen_count[t], ref_count[t])

    def flat(rows):
        shape = (rows, 128)
        return lax.broadcasted_iota(jnp.int32, shape, 0) * 128 + lax.broadcasted_iota(jnp.int32, shape, 1)

    def valid(spots, starts, counts):
        inside = [(spots >= start) & (spots < start + count) for start, count in zip(starts, counts)]
        return functools.reduce(jnp.logical_or, inside)

    a_is_gen, b_is_gen = info[0] == 1, info[1] == 1
    totals = total(gen_count), total(ref_count)
    gen_log, ref_log = (-jnp.log(value) * LOG2E for value in totals)
    counts = [number(a_is_gen, ((n % 4) * 4 + x) * 2 + (c if n < 4 else 1 - c)) for n in range(8)]
    ok = valid(flat(16), [n * BLOCK for n in range(8)], counts)
    log_a = jnp.where(a_is_gen, gen_log, ref_log)
    lift_i[...] = jnp.where(ok, jnp.concatenate([log_a, log_a], axis=0), FAR)
    core = jnp.full((1, 128), c.astype(jnp.float32))
    lift_i[14:15, :] = core
    lift_i[15:16, :] = jnp.full((1, 128), y.astype(jnp.float32))
    here = [(y * 4 + n) * 2 + c for n in range(4)]
    starts = [n * BLOCK for n in range(4)]
    ok = valid(flat(8), starts, [number(b_is_gen, t) for t in here])
    lift_j[...] = jnp.where(ok, jnp.where(b_is_gen, gen_log, ref_log), FAR)
    lift_j[6:7, :] = core
    shift = 64 * lax.rem(y, 2)
    windows = [n * 256 + shift for n in range(4)]
    for n, counts in enumerate((gen_count, ref_count)):
        ok = valid(flat(8), windows, [counts[t] for t in here])
        weights[n * 8 : n * 8 + 8, :] = jnp.where(ok, 1.0 / totals[n], 0.0)
    ok = valid(flat(8), starts, [ref_count[t] for t in here])
    weights[16:24, :] = jnp.where(ok, 1.0 / totals[1], 0.0)
    weights[22:23, :] = jnp.full((1, 128), x.astype(jnp.float32))
    weights[23:24, :] = jnp.full((1, 128), lax.rem(y, 2).astype(jnp.float32))


def a_norms(a_ref):
    rows = []
    for s in range(RH):
        flipped = jnp.transpose(norm_parts(a_ref[s * 128 : (s + 1) * 128, :]))
        rows.append(jnp.sum(flipped, axis=0, keepdims=True) * (0.5 * LOG2E / EPSILON))
    return rows


def cost_tiles(a_ref, b_ref, sq_ref, norms, n):
    inner = lax.dot_general(
        b_ref[...],
        a_ref[n * 256 : (n + 1) * 256, :],
        (((1,), (1,)), ((), ())),
        preferred_element_type=jnp.float32,
    )
    scale = LOG2E / EPSILON
    return [(sq_ref[...] + norms[2 * n + s]) - scale * inner[:, s * 128 : (s + 1) * 128] for s in range(2)]


def reduce_pair(head, source, at, high_ref, mass_ref, base, joined):
    heads = [head[base : base + 2, :]]
    pair = lambda rows: [(s, source[rows, at + s * 128 : at + (s + 1) * 128]) for s in range(2)]
    for b in range(RJ):
        lanes_block(pair, 1, heads, high_ref, mass_ref, b * 128, joined)


def cost_own_body(
    info, gen_count, ref_count, a_ref, b_ref, k1a_ref, high_ref, mass_ref, sq_ref, lift_i, lift_j, weights
):
    masks(info, gen_count, ref_count, lift_i, lift_j, weights)
    head = lift_i[...]
    norms = a_norms(a_ref)
    for b in range(RJ):
        part = slice(b * 128, (b + 1) * 128)
        total = jnp.sum(norm_parts(b_ref[part, :]), axis=1, keepdims=True) * (0.5 * LOG2E / EPSILON)
        sq_ref[part, :] = jnp.broadcast_to(total, (128, 128))
    for n in range(4):
        if n < 3:
            for s, tile in enumerate(cost_tiles(a_ref, b_ref, sq_ref, norms, n)):
                k1a_ref[:, (2 * n + s) * 128 : (2 * n + s + 1) * 128] = tile
        if n > 0:
            reduce_pair(head, k1a_ref, (n - 1) * 256, high_ref, mass_ref, 2 * n - 2, n > 1)


def cost_other_body(
    a_ref, b_ref, lift_i, high_in, mass_in, sq_ref, k1b_ref, k2_hbm, part_out, k2_ref, high_ref, mass_ref, out_sems
):
    head = lift_i[...]
    norms = a_norms(a_ref)
    high_ref[...] = high_in[...]
    mass_ref[...] = mass_in[...]
    stores = [fetch(k2_ref, k2_hbm, out_sems, b) for b in range(RJ)]
    order = [1, 2, 0]
    for step in range(4):
        if step < 3:
            n = order[step]
            target, at = (k1b_ref, 0) if n == 0 else (k2_ref, (n - 1) * 256)
            for s, tile in enumerate(cost_tiles(a_ref, b_ref, sq_ref, norms, n)):
                target[:, at + s * 128 : at + (s + 1) * 128] = tile
        if step > 0:
            n = order[step - 1]
            source, at = (k1b_ref, 0) if n == 0 else (k2_ref, (n - 1) * 256)
            reduce_pair(head, source, at, high_ref, mass_ref, RH + 2 * n, True)
        if step == 1:
            for store in stores:
                store.start()
    (result,) = lanes_result(1, high_ref, mass_ref)
    for n in range(4):
        part_out[n, 0:RJ, :] = result
        part_out[n, RJ:8, :] = jnp.zeros((8 - RJ, 128), jnp.float32)
    for store in stores:
        store.wait()


def second_body(k1a_ref, k1b_ref, k2_hbm, got, lift_j, out, g1_out, k2_ref, sems, head_ref, wide_ref, high_ref, mass_ref):
    core = lift_j[6:7, :]
    start_fetch(k2_hbm, k2_ref, sems)
    g1 = -merge(got, 4)[0:RJ, :]
    g1_out[...] = g1
    lift = lift_j[0:RJ, :]
    heads = [lift, lifted(g1, lift)]
    results = reduce_rows(k1a_ref, k1b_ref, k2_hbm, k2_ref, sems, heads, head_ref, wide_ref, high_ref, mass_ref)
    sent = [turned(core, value) for value in results]
    for n in range(8):
        for v in range(2):
            out[n, v * RI : (v + 1) * RI, :] = sent[v]


def third_body(k1a_ref, k1b_ref, k2_hbm, got, lift_i, out, f2_out, k2_ref, sems, high_ref, mass_ref):
    core = lift_i[14:15, :]
    start_fetch(k2_hbm, k2_ref, sems)
    merged = -merge(got, 8)
    f1 = turned(core, merged[0:RI, :])
    f2 = 0.5 * (f1 + turned(core, merged[RI : 2 * RI, :]))
    f2_out[...] = f2
    lift = lift_i[0:RI, :]
    heads = [lifted(f1, lift), lifted(f2, lift)]
    results = reduce_lanes(k1a_ref, k1b_ref, k2_hbm, k2_ref, sems, heads, high_ref, mass_ref)
    for n in range(4):
        for v in range(2):
            out[n, v * 8 : v * 8 + RJ, :] = results[v]
            out[n, v * 8 + RJ : v * 8 + 8, :] = jnp.zeros((8 - RJ, 128), jnp.float32)


def fourth_body(k1a_ref, k1b_ref, k2_hbm, got, lift_j, g1, out, g3_out, k2_ref, sems, head_ref, wide_ref, high_ref, mass_ref):
    core = lift_j[6:7, :]
    start_fetch(k2_hbm, k2_ref, sems)
    merged = -merge(got, 4)
    g2 = 0.5 * (g1[...] + merged[0:RJ, :])
    g3 = 0.5 * (g2 + merged[8 : 8 + RJ, :])
    g3_out[...] = g3
    lift = lift_j[0:RJ, :]
    heads = [lifted(g2, lift), lifted(g3, lift)]
    results = reduce_rows(k1a_ref, k1b_ref, k2_hbm, k2_ref, sems, heads, head_ref, wide_ref, high_ref, mass_ref)
    sent = [turned(core, value) for value in results]
    for n in range(8):
        for v in range(2):
            out[n, v * RI : (v + 1) * RI, :] = sent[v]


def fifth_body(k1a_ref, k1b_ref, k2_hbm, got, lift_i, f2, g3, out, k2_ref, sems, high_ref, mass_ref):
    core = lift_i[14:15, :]
    start_fetch(k2_hbm, k2_ref, sems)
    merged = -merge(got, 8)
    f3 = 0.5 * (f2[...] + turned(core, merged[0:RI, :]))
    f4 = 0.5 * (f3 + turned(core, merged[RI : 2 * RI, :]))
    heads = [lifted(f3, lift_i[0:RI, :])]
    (result,) = reduce_lanes(k1a_ref, k1b_ref, k2_hbm, k2_ref, sems, heads, high_ref, mass_ref)
    shifted = result - g3[...]
    along_y = lift_i[15:16, :]
    mine = f4[4:6, :]
    for n, row in ((2, 3), (1, 1), (0, 0)):
        mine = jnp.where(along_y < n + 0.5, f4[row : row + 2, :], mine)
    for n in range(16):
        out[n, 0:RJ, :] = shifted
        out[n, RJ : RJ + 2, :] = mine


def last_body(got, weights, gen_pot, ref_pot, gen_self, ref_self, share):
    g4 = merge([got[n * 4 + 1, 0:RJ, :] for n in range(4)], 4) * (-0.5 * LN2)
    weight = weights[16 : 16 + RJ, :]
    total = jnp.sum(jnp.where(weight > 0.0, g4 * weight, 0.0))
    own = [[got[n * 4 + plane, RJ : RJ + 2, :] * LN2 for n in range(4)] for plane in (1, 0, 3)]
    for n in range(4):
        weight = weights[2 * n : 2 * n + 2, :]
        total += jnp.sum(jnp.where(weight > 0.0, (own[0][n] - own[1][n]) * weight, 0.0))
        weight = weights[8 + 2 * n : 8 + 2 * n + 2, :]
        total -= jnp.sum(jnp.where(weight > 0.0, own[2][n] * weight, 0.0))
    for n in range(8):
        share[n, :, :] = jnp.full((8, 128), total, jnp.float32)

    along_x, odd_y = weights[22:23, :], weights[23:24, :]
    low = lax.broadcasted_iota(jnp.int32, (1, 128), 1) < 64

    def chosen(rows):
        result = rows[0]
        for n in range(1, 4):
            result = jnp.where(along_x > n - 0.5, rows[n], result)
        return result

    def write(out, window, late):
        rolled = jnp.concatenate([window[:, 64:], window[:, :64]], axis=1)
        first = jnp.where(late, jnp.where(low, rolled[0:1, :], rolled[1:2, :]), window[0:1, :])
        second = jnp.where(late, rolled[1:2, :], window[1:2, :])
        out[0:1, 0:128] = first
        out[0:1, 128:192] = second[:, 0:64]

    for out, rows in zip((gen_pot, gen_self, ref_self), own):
        write(out, chosen(rows), odd_y > 0.5)
    odd_x = ((along_x > 0.5) & (along_x < 1.5)) | (along_x > 2.5)
    write(ref_pot, chosen([g4[row : row + 2, :] for row in (0, 1, 3, 4)]), odd_x)


F32 = jnp.float32
BF16 = jnp.bfloat16
STREAM = [pltpu.VMEM((NJ, N2), F32), pltpu.SemaphoreType.DMA((RJ,))]


def lane_scratch(count):
    return [pltpu.VMEM((count, NJ, 128), F32)] * 2


def row_scratch(count):
    return [pltpu.VMEM((count, 8, 128), F32), pltpu.VMEM((count, NJ, 128), F32)] + [pltpu.VMEM((count, 8 * RJ, NI), F32)] * 2


def stage_pack(*args):
    scratch = [pltpu.VMEM((2, 64, BLOCK), BF16), pltpu.SemaphoreType.DMA((2,))]
    out = jax.ShapeDtypeStruct((BLOCK, 128), BF16)
    return call(pack_body, out, [HBM, HBM], scratch, mib=60)(*args)


def stage_unpack(which, *args):
    out = jax.ShapeDtypeStruct((4, BLOCK, D), BF16)
    return call(functools.partial(unpack_body, which), out, [SMEM, VMEM, HBM][: len(args)])(*args)


def stage_cost_own(*args):
    outs = (f32(NJ, NI // 2), f32(1, NJ, 128), f32(1, NJ, 128), f32(NJ, 128))
    outs += (f32(16, 128), f32(8, 128), f32(24, 128))
    return call(cost_own_body, outs, [SMEM] * 3 + [VMEM] * 2)(*args)


def stage_cost_other(*args):
    scratch = [pltpu.VMEM((NJ, N2), F32), *lane_scratch(1), pltpu.SemaphoreType.DMA((RJ,))]
    outs = (f32(NJ, NI // 2 - N2), f32(ROOM, N2), f32(4, 8, 128))
    return call(cost_other_body, outs, [VMEM] * 6, scratch, (VMEM, HBM, VMEM))(*args)


K_SPECS = [VMEM, VMEM, HBM]


def stage_second(*args):
    outs = (f32(8, 2 * RI, 128), f32(RJ, 128))
    return call(second_body, outs, K_SPECS + [VMEM] * 2, STREAM + row_scratch(2))(*args)


def stage_third(*args):
    outs = (f32(4, 16, 128), f32(RI, 128))
    return call(third_body, outs, K_SPECS + [VMEM] * 2, STREAM + lane_scratch(2))(*args)


def stage_fourth(*args):
    outs = (f32(8, 2 * RI, 128), f32(RJ, 128))
    return call(fourth_body, outs, K_SPECS + [VMEM] * 3, STREAM + row_scratch(2))(*args)


def stage_fifth(*args):
    return call(fifth_body, f32(16, 8, 128), K_SPECS + [VMEM] * 4, STREAM + lane_scratch(1))(*args)


def spread(operand, axes):
    return lax.all_to_all(operand, axes, 0, 0, tiled=True)


def local(gen_points, reference_embeddings, gen_count, ref_count):
    y, x, c, zl = (lax.axis_index(name) for name in ("y", "x", "c", "zl"))
    a_is_gen = zl < 3
    b_is_gen = zl == 0
    packed = stage_pack(jnp.transpose(gen_points), jnp.transpose(reference_embeddings))
    raw = lax.all_gather(packed, ("zh", "zl"))

    info = jnp.stack(
        [
            a_is_gen.astype(jnp.int32),
            b_is_gen.astype(jnp.int32),
            c,
            x,
            y,
        ]
    ).astype(jnp.int32)
    one = spread(stage_unpack(0, info, raw), "y")
    two = spread(stage_unpack(1, info, raw, one), "x")
    a_own, b_all = lax.optimization_barrier((one.reshape(NJ, D), two.reshape(NJ, D)))
    a_other = lax.ppermute(a_own, "c", [(0, 1), (1, 0)])
    k1a, high, mass, b_norms, lift_i, lift_j, weights = stage_cost_own(
        info, gen_count, ref_count, a_own, b_all
    )
    k1b, k2, part = stage_cost_other(a_other, b_all, lift_i, high, mass, b_norms)
    k = (k1a, k1b, k2)
    part, g1 = stage_second(*k, spread(part, "x"), lift_j)
    part, f2 = stage_third(*k, spread(part, ("y", "c")), lift_i)
    part, g3 = stage_fourth(*k, spread(part, "x"), lift_j, g1)
    part = stage_fifth(*k, spread(part, ("y", "c")), lift_i, f2, g3)
    got = spread(part, ("x", "zl"))
    outs = (f32(1, BLOCK),) * 4 + (f32(8, 8, 128),)
    *pots, share = call(last_body, outs, [VMEM, VMEM])(got, weights)
    divergence = jnp.sum(spread(share, ("y", "c"))[:, 0, 0])
    return *(pot.reshape(BLOCK) for pot in pots), divergence


def solution(mesh):
    fine = Mesh(mesh.devices.reshape(4, 4, 2, 4, 4), ("y", "x", "c", "zh", "zl"))
    tile, feat = ("y", "x", "c"), ("zh", "zl")
    return jax.shard_map(
        local,
        mesh=fine,
        in_specs=(P(tile, feat), P(tile, feat), P(), P()),
        out_specs=(P(tile), P(tile), P(tile), P(tile), P()),
        check_vma=False,
    )
```

```python
import functools

import jax
import jax.numpy as jnp
from jax import lax
from jax.experimental import pallas as pl
from jax.experimental.pallas import tpu as pltpu
from jax.sharding import Mesh, PartitionSpec as P

EPSILON = 0.25
LOG2E = 1.4426950408889634
LN2 = 0.6931471805599453
FAR = -1.0e30

BLOCK = 192
D = 1024
NI = 8 * BLOCK
NJ = 4 * BLOCK
RI = NI // 128
RH = RI // 2
RJ = NJ // 128
NEAR = 8
N2 = NI - NEAR * 128
UNPACK_MIB = 60
ROOM = 18 * NJ

VMEM = pl.BlockSpec(memory_space=pltpu.VMEM)
HBM = pl.BlockSpec(memory_space=pltpu.HBM)
SMEM = pl.BlockSpec(memory_space=pltpu.SMEM)


def f32(*shape):
    return jax.ShapeDtypeStruct(shape, jnp.float32)


def call(body, outs, ins, scratch=(), out_specs=None, mib=40, cost=None):
    return pl.pallas_call(
        body,
        out_shape=outs,
        in_specs=ins,
        out_specs=jax.tree.map(lambda _: VMEM, outs) if out_specs is None else out_specs,
        scratch_shapes=list(scratch),
        compiler_params=pltpu.CompilerParams(vmem_limit_bytes=mib * 1024 * 1024),
        cost_estimate=cost,
    )


def merge(got, count):
    parts = [got[n] for n in range(count)]
    high = functools.reduce(jnp.maximum, parts)
    mass = functools.reduce(jnp.add, [jnp.exp2(part - high) for part in parts])
    return high + jnp.log(mass) * LOG2E


def lifted(pot, lift):
    return jnp.where(lift > -1.0e29, pot + lift, FAR)


def tree(op, values):
    values = list(values)
    while len(values) > 1:
        values = [op(*values[n : n + 2]) if n + 1 < len(values) else values[n] for n in range(0, len(values), 2)]
    return values[0]


def fetch(k2_hbm, k2_ref, sems, b):
    rows = pl.ds(b * 128, 128)
    return pltpu.make_async_copy(k2_hbm.at[rows], k2_ref.at[rows], sems.at[b])


def start_fetch(k2_hbm, k2_ref, sems):
    for b in range(RJ):
        fetch(k2_hbm, k2_ref, sems, b).start()


def lanes_block(tiles_of, count, heads, high_ref, mass_ref, base, joined=False):
    for group in range(16):
        rows = pl.ds(base + group * 8, 8)
        tiles = tiles_of(rows)
        for v in range(count):
            xs = [heads[v][r : r + 1, :] - tile for r, tile in tiles]
            high = tree(jnp.maximum, xs)
            if joined:
                before = high_ref[v, rows, :]
                high = jnp.maximum(high, before)
                xs.append(before)
            masses = [jnp.exp2(x - high) for x in xs]
            if joined:
                masses[-1] = masses[-1] * mass_ref[v, rows, :]
            high_ref[v, rows, :] = high
            mass_ref[v, rows, :] = tree(jnp.add, masses)


def near_tile(k1a_ref, k1b_ref, rows, r):
    if r < RH:
        return k1a_ref[rows, r * 128 : (r + 1) * 128]
    return k1b_ref[rows, (r - RH) * 128 : (r - RH + 1) * 128]


def near_tiles(k1a_ref, k1b_ref):
    return lambda rows: [(r, near_tile(k1a_ref, k1b_ref, rows, r)) for r in range(NEAR)]


def far_tiles(k2_ref):
    return lambda rows: [(r, k2_ref[rows, (r - NEAR) * 128 : (r - NEAR + 1) * 128]) for r in range(NEAR, RI)]


def turned(core, value):
    return jnp.where(core > 0.5, jnp.concatenate([value[RH:RI, :], value[0:RH, :]], axis=0), value)


def lanes_result(count, high_ref, mass_ref):
    results = []
    for v in range(count):
        rows_out = []
        for b in range(RJ):
            high = jnp.transpose(high_ref[v, b * 128 : (b + 1) * 128, :])
            mass = jnp.transpose(mass_ref[v, b * 128 : (b + 1) * 128, :])
            top = jnp.max(high, axis=0, keepdims=True)
            total = jnp.sum(mass * jnp.exp2(high - top), axis=0, keepdims=True)
            rows_out.append((top, total))
        top = jnp.concatenate([row[0] for row in rows_out], axis=0)
        total = jnp.concatenate([row[1] for row in rows_out], axis=0)
        results.append(top + jnp.log(total) * LOG2E)
    return results


def reduce_lanes(k1a_ref, k1b_ref, k2_hbm, k2_ref, sems, heads, high_ref, mass_ref):
    count = len(heads)

    def near(b, carry):
        lanes_block(near_tiles(k1a_ref, k1b_ref), count, heads, high_ref, mass_ref, pl.multiple_of(b * 128, 128))
        return carry

    def far(b, carry):
        fetch(k2_hbm, k2_ref, sems, b).wait()
        lanes_block(far_tiles(k2_ref), count, heads, high_ref, mass_ref, pl.multiple_of(b * 128, 128), True)
        return carry

    lax.fori_loop(0, RJ, near, 0)
    lax.fori_loop(0, RJ, far, 0)
    return lanes_result(count, high_ref, mass_ref)


def reduce_rows(k1a_ref, k1b_ref, k2_hbm, k2_ref, sems, heads, head_ref, wide_ref, high_ref, mass_ref):
    count = len(heads)
    for v in range(count):
        head_ref[v, 0:RJ, :] = heads[v]

    def block(b, wides, tile, r):
        spot = pl.ds(pl.multiple_of(b * 8, 8), 8)
        cols = slice(r * 128, (r + 1) * 128)
        tiles = [tile(pl.ds(b * 128 + group * 8, 8)) for group in range(16)]
        for v in range(count):
            xs = [wides[v][group * 8 : group * 8 + 8, :] - tiles[group] for group in range(16)]
            high = tree(jnp.maximum, xs)
            high_ref[v, spot, cols] = high
            mass_ref[v, spot, cols] = tree(jnp.add, [jnp.exp2(x - high) for x in xs])

    def near(b, carry):
        wides = []
        for v in range(count):
            wides.append(jnp.transpose(jnp.broadcast_to(head_ref[v, pl.ds(b, 1), :], (128, 128))))
            wide_ref[v, pl.ds(pl.multiple_of(b * 128, 128), 128), :] = wides[v]
        for r in range(NEAR):
            block(b, wides, lambda rows: near_tile(k1a_ref, k1b_ref, rows, r), r)
        return carry

    def far(b, carry):
        fetch(k2_hbm, k2_ref, sems, b).wait()
        wides = [wide_ref[v, pl.ds(pl.multiple_of(b * 128, 128), 128), :] for v in range(count)]
        for r in range(NEAR, RI):
            block(b, wides, lambda rows: k2_ref[rows, (r - NEAR) * 128 : (r - NEAR + 1) * 128], r)
        return carry

    lax.fori_loop(0, RJ, near, 0)
    lax.fori_loop(0, RJ, far, 0)
    results = []
    for v in range(count):
        tops, totals = [], []
        for r in range(RI):
            cols = slice(r * 128, (r + 1) * 128)
            high = high_ref[v, :, cols]
            top = jnp.max(high, axis=0, keepdims=True)
            tops.append(top)
            totals.append(jnp.sum(mass_ref[v, :, cols] * jnp.exp2(high - top), axis=0, keepdims=True))
        results.append(jnp.concatenate(tops, axis=0) + jnp.log(jnp.concatenate(totals, axis=0)) * LOG2E)
    return results


def pack_body(gen, ref, out, both, sems):
    copies = [pltpu.make_async_copy(part, both.at[n], sems.at[n]) for n, part in enumerate((gen, ref))]
    for copy in copies:
        copy.start()
    for copy in copies:
        copy.wait()
    wide = jnp.concatenate([both[0].astype(jnp.float32), both[1].astype(jnp.float32)], axis=0)
    out[...] = jnp.transpose(wide).astype(jnp.bfloat16)


def unpack_body(which, info, raw, *refs):
    out = refs[-1]
    for k in range(D // 128):
        cols = slice(k * 128, (k + 1) * 128)
        even, odd = raw[2 * k], raw[2 * k + 1]
        gen = jnp.concatenate([even[:, :64], odd[:, :64]], axis=1)
        ref = jnp.concatenate([even[:, 64:], odd[:, 64:]], axis=1)
        part = jnp.where(info[which] == 1, gen, ref)
        for n in range(4):
            out[n, :, cols] = part


def norm_parts(values):
    values = values.astype(jnp.float32)
    values = values * values
    return functools.reduce(jnp.add, [values[:, k * 128 : (k + 1) * 128] for k in range(D // 128)])


def masks(info, gen_count, ref_count, lift_i, lift_j, weights):
    c, x, y = info[2], info[3], info[4]

    def total(counts):
        return jnp.full((8, 128), functools.reduce(jnp.add, [counts[n] for n in range(32)]).astype(jnp.float32))

    def number(is_gen, t):
        return jnp.where(is_gen, gen_count[t], ref_count[t])

    def flat(rows):
        shape = (rows, 128)
        return lax.broadcasted_iota(jnp.int32, shape, 0) * 128 + lax.broadcasted_iota(jnp.int32, shape, 1)

    def valid(spots, starts, counts):
        inside = [(spots >= start) & (spots < start + count) for start, count in zip(starts, counts)]
        return functools.reduce(jnp.logical_or, inside)

    a_is_gen, b_is_gen = info[0] == 1, info[1] == 1
    totals = total(gen_count), total(ref_count)
    gen_log, ref_log = (-jnp.log(value) * LOG2E for value in totals)
    counts = [number(a_is_gen, ((n % 4) * 4 + x) * 2 + (c if n < 4 else 1 - c)) for n in range(8)]
    ok = valid(flat(16), [n * BLOCK for n in range(8)], counts)
    log_a = jnp.where(a_is_gen, gen_log, ref_log)
    lift_i[...] = jnp.where(ok, jnp.concatenate([log_a, log_a], axis=0), FAR)
    core = jnp.full((1, 128), c.astype(jnp.float32))
    lift_i[14:15, :] = core
    lift_i[15:16, :] = jnp.full((1, 128), y.astype(jnp.float32))
    here = [(y * 4 + n) * 2 + c for n in range(4)]
    starts = [n * BLOCK for n in range(4)]
    ok = valid(flat(8), starts, [number(b_is_gen, t) for t in here])
    lift_j[...] = jnp.where(ok, jnp.where(b_is_gen, gen_log, ref_log), FAR)
    lift_j[6:7, :] = core
    shift = 64 * lax.rem(y, 2)
    windows = [n * 256 + shift for n in range(4)]
    for n, counts in enumerate((gen_count, ref_count)):
        ok = valid(flat(8), windows, [counts[t] for t in here])
        weights[n * 8 : n * 8 + 8, :] = jnp.where(ok, 1.0 / totals[n], 0.0)
    ok = valid(flat(8), starts, [ref_count[t] for t in here])
    weights[16:24, :] = jnp.where(ok, 1.0 / totals[1], 0.0)
    weights[22:23, :] = jnp.full((1, 128), x.astype(jnp.float32))
    weights[23:24, :] = jnp.full((1, 128), lax.rem(y, 2).astype(jnp.float32))


def a_norms(a_ref):
    rows = []
    for s in range(RH):
        flipped = jnp.transpose(norm_parts(a_ref[s * 128 : (s + 1) * 128, :]))
        rows.append(jnp.sum(flipped, axis=0, keepdims=True) * (0.5 * LOG2E / EPSILON))
    return rows


def cost_tiles(a_ref, b_ref, sq_ref, norms, n):
    inner = lax.dot_general(
        b_ref[...],
        a_ref[n * 256 : (n + 1) * 256, :],
        (((1,), (1,)), ((), ())),
        preferred_element_type=jnp.float32,
    )
    scale = LOG2E / EPSILON
    return [(sq_ref[...] + norms[2 * n + s]) - scale * inner[:, s * 128 : (s + 1) * 128] for s in range(2)]


def reduce_pair(head, source, at, high_ref, mass_ref, base, joined):
    heads = [head[base : base + 2, :]]
    pair = lambda rows: [(s, source[rows, at + s * 128 : at + (s + 1) * 128]) for s in range(2)]
    for b in range(RJ):
        lanes_block(pair, 1, heads, high_ref, mass_ref, b * 128, joined)


def cost_own_body(
    info, gen_count, ref_count, a_ref, b_ref, k1a_ref, high_ref, mass_ref, sq_ref, lift_i, lift_j, weights
):
    masks(info, gen_count, ref_count, lift_i, lift_j, weights)
    head = lift_i[...]
    norms = a_norms(a_ref)
    for b in range(RJ):
        part = slice(b * 128, (b + 1) * 128)
        total = jnp.sum(norm_parts(b_ref[part, :]), axis=1, keepdims=True) * (0.5 * LOG2E / EPSILON)
        sq_ref[part, :] = jnp.broadcast_to(total, (128, 128))
    for n in range(4):
        if n < 3:
            for s, tile in enumerate(cost_tiles(a_ref, b_ref, sq_ref, norms, n)):
                k1a_ref[:, (2 * n + s) * 128 : (2 * n + s + 1) * 128] = tile
        if n > 0:
            reduce_pair(head, k1a_ref, (n - 1) * 256, high_ref, mass_ref, 2 * n - 2, n > 1)


def cost_other_body(
    a_ref, b_ref, lift_i, high_in, mass_in, sq_ref, k1b_ref, k2_hbm, part_out, k2_ref, high_ref, mass_ref, out_sems
):
    head = lift_i[...]
    norms = a_norms(a_ref)
    high_ref[...] = high_in[...]
    mass_ref[...] = mass_in[...]
    stores = [fetch(k2_ref, k2_hbm, out_sems, b) for b in range(RJ)]
    order = [1, 2, 0]
    for step in range(4):
        if step < 3:
            n = order[step]
            target, at = (k1b_ref, 0) if n == 0 else (k2_ref, (n - 1) * 256)
            for s, tile in enumerate(cost_tiles(a_ref, b_ref, sq_ref, norms, n)):
                target[:, at + s * 128 : at + (s + 1) * 128] = tile
        if step > 0:
            n = order[step - 1]
            source, at = (k1b_ref, 0) if n == 0 else (k2_ref, (n - 1) * 256)
            reduce_pair(head, source, at, high_ref, mass_ref, RH + 2 * n, True)
        if step == 1:
            for store in stores:
                store.start()
    (result,) = lanes_result(1, high_ref, mass_ref)
    for n in range(4):
        part_out[n, 0:RJ, :] = result
        part_out[n, RJ:8, :] = jnp.zeros((8 - RJ, 128), jnp.float32)
    for store in stores:
        store.wait()


def second_body(k1a_ref, k1b_ref, k2_hbm, got, lift_j, out, g1_out, k2_ref, sems, head_ref, wide_ref, high_ref, mass_ref):
    core = lift_j[6:7, :]
    start_fetch(k2_hbm, k2_ref, sems)
    g1 = -merge(got, 4)[0:RJ, :]
    g1_out[...] = g1
    lift = lift_j[0:RJ, :]
    heads = [lift, lifted(g1, lift)]
    results = reduce_rows(k1a_ref, k1b_ref, k2_hbm, k2_ref, sems, heads, head_ref, wide_ref, high_ref, mass_ref)
    sent = [turned(core, value) for value in results]
    for n in range(8):
        for v in range(2):
            out[n, v * RI : (v + 1) * RI, :] = sent[v]


def third_body(k1a_ref, k1b_ref, k2_hbm, got, lift_i, out, f2_out, k2_ref, sems, high_ref, mass_ref):
    core = lift_i[14:15, :]
    start_fetch(k2_hbm, k2_ref, sems)
    merged = -merge(got, 8)
    f1 = turned(core, merged[0:RI, :])
    f2 = 0.5 * (f1 + turned(core, merged[RI : 2 * RI, :]))
    f2_out[...] = f2
    lift = lift_i[0:RI, :]
    heads = [lifted(f1, lift), lifted(f2, lift)]
    results = reduce_lanes(k1a_ref, k1b_ref, k2_hbm, k2_ref, sems, heads, high_ref, mass_ref)
    for n in range(4):
        for v in range(2):
            out[n, v * 8 : v * 8 + RJ, :] = results[v]
            out[n, v * 8 + RJ : v * 8 + 8, :] = jnp.zeros((8 - RJ, 128), jnp.float32)


def fourth_body(k1a_ref, k1b_ref, k2_hbm, got, lift_j, g1, out, g3_out, k2_ref, sems, head_ref, wide_ref, high_ref, mass_ref):
    core = lift_j[6:7, :]
    start_fetch(k2_hbm, k2_ref, sems)
    merged = -merge(got, 4)
    g2 = 0.5 * (g1[...] + merged[0:RJ, :])
    g3 = 0.5 * (g2 + merged[8 : 8 + RJ, :])
    g3_out[...] = g3
    lift = lift_j[0:RJ, :]
    heads = [lifted(g2, lift), lifted(g3, lift)]
    results = reduce_rows(k1a_ref, k1b_ref, k2_hbm, k2_ref, sems, heads, head_ref, wide_ref, high_ref, mass_ref)
    sent = [turned(core, value) for value in results]
    for n in range(8):
        for v in range(2):
            out[n, v * RI : (v + 1) * RI, :] = sent[v]


def fifth_body(k1a_ref, k1b_ref, k2_hbm, got, lift_i, f2, g3, out, k2_ref, sems, high_ref, mass_ref):
    core = lift_i[14:15, :]
    start_fetch(k2_hbm, k2_ref, sems)
    merged = -merge(got, 8)
    f3 = 0.5 * (f2[...] + turned(core, merged[0:RI, :]))
    f4 = 0.5 * (f3 + turned(core, merged[RI : 2 * RI, :]))
    heads = [lifted(f3, lift_i[0:RI, :])]
    (result,) = reduce_lanes(k1a_ref, k1b_ref, k2_hbm, k2_ref, sems, heads, high_ref, mass_ref)
    shifted = result - g3[...]
    along_y = lift_i[15:16, :]
    mine = f4[4:6, :]
    for n, row in ((2, 3), (1, 1), (0, 0)):
        mine = jnp.where(along_y < n + 0.5, f4[row : row + 2, :], mine)
    for n in range(16):
        out[n, 0:RJ, :] = shifted
        out[n, RJ : RJ + 2, :] = mine


def last_body(got, weights, gen_pot, ref_pot, gen_self, ref_self, share):
    g4 = merge([got[n * 4 + 1, 0:RJ, :] for n in range(4)], 4) * (-0.5 * LN2)
    weight = weights[16 : 16 + RJ, :]
    total = jnp.sum(jnp.where(weight > 0.0, g4 * weight, 0.0))
    own = [[got[n * 4 + plane, RJ : RJ + 2, :] * LN2 for n in range(4)] for plane in (1, 0, 3)]
    for n in range(4):
        weight = weights[2 * n : 2 * n + 2, :]
        total += jnp.sum(jnp.where(weight > 0.0, (own[0][n] - own[1][n]) * weight, 0.0))
        weight = weights[8 + 2 * n : 8 + 2 * n + 2, :]
        total -= jnp.sum(jnp.where(weight > 0.0, own[2][n] * weight, 0.0))
    for n in range(8):
        share[n, :, :] = jnp.full((8, 128), total, jnp.float32)

    along_x, odd_y = weights[22:23, :], weights[23:24, :]
    low = lax.broadcasted_iota(jnp.int32, (1, 128), 1) < 64

    def chosen(rows):
        result = rows[0]
        for n in range(1, 4):
            result = jnp.where(along_x > n - 0.5, rows[n], result)
        return result

    def write(out, window, late):
        rolled = jnp.concatenate([window[:, 64:], window[:, :64]], axis=1)
        first = jnp.where(late, jnp.where(low, rolled[0:1, :], rolled[1:2, :]), window[0:1, :])
        second = jnp.where(late, rolled[1:2, :], window[1:2, :])
        out[0:1, 0:128] = first
        out[0:1, 128:192] = second[:, 0:64]

    for out, rows in zip((gen_pot, gen_self, ref_self), own):
        write(out, chosen(rows), odd_y > 0.5)
    odd_x = ((along_x > 0.5) & (along_x < 1.5)) | (along_x > 2.5)
    write(ref_pot, chosen([g4[row : row + 2, :] for row in (0, 1, 3, 4)]), odd_x)


F32 = jnp.float32
BF16 = jnp.bfloat16
STREAM = [pltpu.VMEM((NJ, N2), F32), pltpu.SemaphoreType.DMA((RJ,))]


def lane_scratch(count):
    return [pltpu.VMEM((count, NJ, 128), F32)] * 2


def row_scratch(count):
    return [pltpu.VMEM((count, 8, 128), F32), pltpu.VMEM((count, NJ, 128), F32)] + [pltpu.VMEM((count, 8 * RJ, NI), F32)] * 2


def stage_pack(*args):
    scratch = [pltpu.VMEM((2, 64, BLOCK), BF16), pltpu.SemaphoreType.DMA((2,))]
    out = jax.ShapeDtypeStruct((BLOCK, 128), BF16)
    return call(pack_body, out, [HBM, HBM], scratch, mib=60)(*args)


def stage_unpack(which, *args):
    out = jax.ShapeDtypeStruct((4, BLOCK, D), BF16)
    return call(functools.partial(unpack_body, which), out, [SMEM, VMEM, HBM][: len(args)], mib=(40, UNPACK_MIB)[which])(*args)


def stage_cost_own(*args):
    outs = (f32(NJ, NI // 2), f32(1, NJ, 128), f32(1, NJ, 128), f32(NJ, 128))
    outs += (f32(16, 128), f32(8, 128), f32(24, 128))
    cost = pl.CostEstimate(flops=10**10, bytes_accessed=1, transcendentals=0)
    return call(cost_own_body, outs, [SMEM] * 3 + [VMEM] * 2, cost=cost)(*args)


def stage_cost_other(*args):
    scratch = [pltpu.VMEM((NJ, N2), F32), *lane_scratch(1), pltpu.SemaphoreType.DMA((RJ,))]
    outs = (f32(NJ, NI // 2 - N2), f32(ROOM, N2), f32(4, 8, 128))
    return call(cost_other_body, outs, [VMEM] * 6, scratch, (VMEM, HBM, VMEM))(*args)


K_SPECS = [VMEM, VMEM, HBM]


def stage_second(*args):
    outs = (f32(8, 2 * RI, 128), f32(RJ, 128))
    return call(second_body, outs, K_SPECS + [VMEM] * 2, STREAM + row_scratch(2))(*args)


def stage_third(*args):
    outs = (f32(4, 16, 128), f32(RI, 128))
    return call(third_body, outs, K_SPECS + [VMEM] * 2, STREAM + lane_scratch(2))(*args)


def stage_fourth(*args):
    outs = (f32(8, 2 * RI, 128), f32(RJ, 128))
    return call(fourth_body, outs, K_SPECS + [VMEM] * 3, STREAM + row_scratch(2))(*args)


def stage_fifth(*args):
    return call(fifth_body, f32(16, 8, 128), K_SPECS + [VMEM] * 4, STREAM + lane_scratch(1))(*args)


def spread(operand, axes):
    return lax.all_to_all(operand, axes, 0, 0, tiled=True)


def local(gen_points, reference_embeddings, gen_count, ref_count):
    y, x, c, zl = (lax.axis_index(name) for name in ("y", "x", "c", "zl"))
    a_is_gen = zl < 3
    b_is_gen = zl == 0
    packed = stage_pack(jnp.transpose(gen_points), jnp.transpose(reference_embeddings))
    raw = lax.all_gather(packed, ("zh", "zl"))

    info = jnp.stack(
        [
            a_is_gen.astype(jnp.int32),
            b_is_gen.astype(jnp.int32),
            c,
            x,
            y,
        ]
    ).astype(jnp.int32)
    one = spread(stage_unpack(0, info, raw), "y")
    two = spread(stage_unpack(1, info, raw, one), "x")
    a_own, b_all = one.reshape(NJ, D), two.reshape(NJ, D)
    a_other = lax.ppermute(a_own, "c", [(0, 1), (1, 0)])
    k1a, high, mass, b_norms, lift_i, lift_j, weights = stage_cost_own(
        info, gen_count, ref_count, a_own, b_all
    )
    k1b, k2, part = stage_cost_other(a_other, b_all, lift_i, high, mass, b_norms)
    k = (k1a, k1b, k2)
    part, g1 = stage_second(*k, spread(part, "x"), lift_j)
    part, f2 = stage_third(*k, spread(part, ("y", "c")), lift_i)
    part, g3 = stage_fourth(*k, spread(part, "x"), lift_j, g1)
    part = stage_fifth(*k, spread(part, ("y", "c")), lift_i, f2, g3)
    got = spread(part, ("x", "zl"))
    outs = (f32(1, BLOCK),) * 4 + (f32(8, 8, 128),)
    *pots, share = call(last_body, outs, [VMEM, VMEM])(got, weights)
    divergence = jnp.sum(spread(share, ("y", "c"))[:, 0, 0])
    return *(pot.reshape(BLOCK) for pot in pots), divergence


def solution(mesh):
    fine = Mesh(mesh.devices.reshape(4, 4, 2, 4, 4), ("y", "x", "c", "zh", "zl"))
    tile, feat = ("y", "x", "c"), ("zh", "zl")
    return jax.shard_map(
        local,
        mesh=fine,
        in_specs=(P(tile, feat), P(tile, feat), P(), P()),
        out_specs=(P(tile), P(tile), P(tile), P(tile), P()),
        check_vma=False,
    )
```

```python
import functools

import jax
import jax.numpy as jnp
from jax import lax
from jax.experimental import pallas as pl
from jax.experimental.pallas import tpu as pltpu
from jax.sharding import Mesh, PartitionSpec as P

EPSILON = 0.25
LOG2E = 1.4426950408889634
LN2 = 0.6931471805599453
FAR = -1.0e30

BLOCK = 192
D = 1024
NI = 8 * BLOCK
NJ = 4 * BLOCK
RI = NI // 128
RH = RI // 2
RJ = NJ // 128
NEAR = 8
N2 = NI - NEAR * 128
ROOM = 18 * NJ

VMEM = pl.BlockSpec(memory_space=pltpu.VMEM)
HBM = pl.BlockSpec(memory_space=pltpu.HBM)
SMEM = pl.BlockSpec(memory_space=pltpu.SMEM)


def f32(*shape):
    return jax.ShapeDtypeStruct(shape, jnp.float32)


def call(body, outs, ins, scratch=(), out_specs=None, mib=40):
    return pl.pallas_call(
        body,
        out_shape=outs,
        in_specs=ins,
        out_specs=jax.tree.map(lambda _: VMEM, outs) if out_specs is None else out_specs,
        scratch_shapes=list(scratch),
        compiler_params=pltpu.CompilerParams(vmem_limit_bytes=mib * 1024 * 1024),
    )


def merge(got, count):
    parts = [got[n] for n in range(count)]
    high = functools.reduce(jnp.maximum, parts)
    mass = functools.reduce(jnp.add, [jnp.exp2(part - high) for part in parts])
    return high + jnp.log(mass) * LOG2E


def lifted(pot, lift):
    return jnp.where(lift > -1.0e29, pot + lift, FAR)


def tree(op, values):
    values = list(values)
    while len(values) > 1:
        values = [op(*values[n : n + 2]) if n + 1 < len(values) else values[n] for n in range(0, len(values), 2)]
    return values[0]


def fetch(k2_hbm, k2_ref, sems, b):
    rows = pl.ds(b * 128, 128)
    return pltpu.make_async_copy(k2_hbm.at[rows], k2_ref.at[rows], sems.at[b])


def start_fetch(k2_hbm, k2_ref, sems):
    for b in range(RJ):
        fetch(k2_hbm, k2_ref, sems, b).start()


def lanes_block(tiles_of, count, heads, high_ref, mass_ref, base, before=None):
    for group in range(16):
        rows = pl.ds(base + group * 8, 8)
        tiles = tiles_of(rows)
        for v in range(count):
            xs = [heads[v][r : r + 1, :] - tile for r, tile in tiles]
            high = tree(jnp.maximum, xs)
            if before:
                above = before[0][v, rows, :]
                high = jnp.maximum(high, above)
                xs.append(above)
            masses = [jnp.exp2(x - high) for x in xs]
            if before:
                masses[-1] = masses[-1] * before[1][v, rows, :]
            high_ref[v, rows, :] = high
            mass_ref[v, rows, :] = tree(jnp.add, masses)


def near_tile(k1a_ref, k1b_ref, rows, r):
    if r < RH:
        return k1a_ref[rows, r * 128 : (r + 1) * 128]
    return k1b_ref[rows, (r - RH) * 128 : (r - RH + 1) * 128]


def near_tiles(k1a_ref, k1b_ref):
    return lambda rows: [(r, near_tile(k1a_ref, k1b_ref, rows, r)) for r in range(NEAR)]


def far_tiles(k2_ref):
    return lambda rows: [(r, k2_ref[rows, (r - NEAR) * 128 : (r - NEAR + 1) * 128]) for r in range(NEAR, RI)]


def turned(core, value):
    return jnp.where(core > 0.5, jnp.concatenate([value[RH:RI, :], value[0:RH, :]], axis=0), value)


def lanes_result(count, high_ref, mass_ref):
    results = []
    for v in range(count):
        rows_out = []
        for b in range(RJ):
            high = jnp.transpose(high_ref[v, b * 128 : (b + 1) * 128, :])
            mass = jnp.transpose(mass_ref[v, b * 128 : (b + 1) * 128, :])
            top = jnp.max(high, axis=0, keepdims=True)
            total = jnp.sum(mass * jnp.exp2(high - top), axis=0, keepdims=True)
            rows_out.append((top, total))
        top = jnp.concatenate([row[0] for row in rows_out], axis=0)
        total = jnp.concatenate([row[1] for row in rows_out], axis=0)
        results.append(top + jnp.log(total) * LOG2E)
    return results


def reduce_lanes(k1a_ref, k1b_ref, k2_hbm, k2_ref, sems, heads, high_ref, mass_ref):
    count = len(heads)

    def near(b, carry):
        lanes_block(near_tiles(k1a_ref, k1b_ref), count, heads, high_ref, mass_ref, pl.multiple_of(b * 128, 128))
        return carry

    def far(b, carry):
        fetch(k2_hbm, k2_ref, sems, b).wait()
        start = pl.multiple_of(b * 128, 128)
        lanes_block(far_tiles(k2_ref), count, heads, high_ref, mass_ref, start, (high_ref, mass_ref))
        return carry

    lax.fori_loop(0, RJ, near, 0)
    lax.fori_loop(0, RJ, far, 0)
    return lanes_result(count, high_ref, mass_ref)


def reduce_rows(k1a_ref, k1b_ref, k2_hbm, k2_ref, sems, heads, wide_ref, high_ref, mass_ref):
    count = len(heads)
    for v in range(count):
        for b in range(RJ):
            row = jnp.broadcast_to(heads[v][b : b + 1, :], (128, 128))
            wide_ref[v, b * 128 : (b + 1) * 128, :] = jnp.transpose(row)

    def block(b, wides, tile, r):
        spot = pl.ds(pl.multiple_of(b * 8, 8), 8)
        cols = slice(r * 128, (r + 1) * 128)
        tiles = [tile(pl.ds(b * 128 + group * 8, 8)) for group in range(16)]
        for v in range(count):
            xs = [wides[v][group * 8 : group * 8 + 8, :] - tiles[group] for group in range(16)]
            high = tree(jnp.maximum, xs)
            high_ref[v, spot, cols] = high
            mass_ref[v, spot, cols] = tree(jnp.add, [jnp.exp2(x - high) for x in xs])

    def near(b, carry):
        wides = [wide_ref[v, pl.ds(pl.multiple_of(b * 128, 128), 128), :] for v in range(count)]
        for r in range(NEAR):
            block(b, wides, lambda rows: near_tile(k1a_ref, k1b_ref, rows, r), r)
        return carry

    def far(b, carry):
        fetch(k2_hbm, k2_ref, sems, b).wait()
        wides = [wide_ref[v, pl.ds(pl.multiple_of(b * 128, 128), 128), :] for v in range(count)]
        for r in range(NEAR, RI):
            block(b, wides, lambda rows: k2_ref[rows, (r - NEAR) * 128 : (r - NEAR + 1) * 128], r)
        return carry

    lax.fori_loop(0, RJ, near, 0)
    lax.fori_loop(0, RJ, far, 0)
    results = []
    for v in range(count):
        tops, totals = [], []
        for r in range(RI):
            cols = slice(r * 128, (r + 1) * 128)
            high = high_ref[v, :, cols]
            top = jnp.max(high, axis=0, keepdims=True)
            tops.append(top)
            totals.append(jnp.sum(mass_ref[v, :, cols] * jnp.exp2(high - top), axis=0, keepdims=True))
        results.append(jnp.concatenate(tops, axis=0) + jnp.log(jnp.concatenate(totals, axis=0)) * LOG2E)
    return results


def pack_body(gen, ref, out, both, sems):
    copies = [pltpu.make_async_copy(part, both.at[n], sems.at[n]) for n, part in enumerate((gen, ref))]
    for copy in copies:
        copy.start()
    for copy in copies:
        copy.wait()
    wide = jnp.concatenate([both[0].astype(jnp.float32), both[1].astype(jnp.float32)], axis=0)
    out[...] = jnp.transpose(wide).astype(jnp.bfloat16)


def unpack_body(info, raw, a_out, b_out):
    for k in range(D // 128):
        cols = slice(k * 128, (k + 1) * 128)
        even, odd = raw[2 * k], raw[2 * k + 1]
        gen = jnp.concatenate([even[:, :64], odd[:, :64]], axis=1)
        ref = jnp.concatenate([even[:, 64:], odd[:, 64:]], axis=1)
        a = jnp.where(info[0] == 1, gen, ref)
        b_out[:, cols] = jnp.where(info[1] == 1, gen, ref)
        for n in range(4):
            a_out[n, :, cols] = a


def widen_body(own, a_half, out):
    del a_half
    for n in range(4):
        out[n] = own[...]


def norm_parts(values):
    values = values.astype(jnp.float32)
    values = values * values
    return functools.reduce(jnp.add, [values[:, k * 128 : (k + 1) * 128] for k in range(D // 128)])


def masks(info, gen_count, ref_count, lift_i, lift_j, weights):
    c, x, y = info[2], info[3], info[4]

    def total(counts):
        return jnp.full((8, 128), functools.reduce(jnp.add, [counts[n] for n in range(32)]).astype(jnp.float32))

    def number(is_gen, t):
        return jnp.where(is_gen, gen_count[t], ref_count[t])

    def flat(rows):
        shape = (rows, 128)
        return lax.broadcasted_iota(jnp.int32, shape, 0) * 128 + lax.broadcasted_iota(jnp.int32, shape, 1)

    def valid(spots, starts, counts):
        inside = [(spots >= start) & (spots < start + count) for start, count in zip(starts, counts)]
        return functools.reduce(jnp.logical_or, inside)

    a_is_gen, b_is_gen = info[0] == 1, info[1] == 1
    totals = total(gen_count), total(ref_count)
    gen_log, ref_log = (-jnp.log(value) * LOG2E for value in totals)
    counts = [number(a_is_gen, ((n % 4) * 4 + x) * 2 + (c if n < 4 else 1 - c)) for n in range(8)]
    ok = valid(flat(16), [n * BLOCK for n in range(8)], counts)
    log_a = jnp.where(a_is_gen, gen_log, ref_log)
    lift_i[...] = jnp.where(ok, jnp.concatenate([log_a, log_a], axis=0), FAR)
    core = jnp.full((1, 128), c.astype(jnp.float32))
    lift_i[14:15, :] = core
    lift_i[15:16, :] = jnp.full((1, 128), y.astype(jnp.float32))
    here = [(y * 4 + n) * 2 + c for n in range(4)]
    starts = [n * BLOCK for n in range(4)]
    ok = valid(flat(8), starts, [number(b_is_gen, t) for t in here])
    lift_j[...] = jnp.where(ok, jnp.where(b_is_gen, gen_log, ref_log), FAR)
    lift_j[6:7, :] = core
    shift = 64 * lax.rem(y, 2)
    windows = [n * 256 + shift for n in range(4)]
    for n, counts in enumerate((gen_count, ref_count)):
        ok = valid(flat(8), windows, [counts[t] for t in here])
        weights[n * 8 : n * 8 + 8, :] = jnp.where(ok, 1.0 / totals[n], 0.0)
    ok = valid(flat(8), starts, [ref_count[t] for t in here])
    weights[16:24, :] = jnp.where(ok, 1.0 / totals[1], 0.0)
    weights[22:23, :] = jnp.full((1, 128), x.astype(jnp.float32))
    weights[23:24, :] = jnp.full((1, 128), lax.rem(y, 2).astype(jnp.float32))


def a_norms(a_ref):
    rows = []
    for s in range(RH):
        flipped = jnp.transpose(norm_parts(a_ref[s * 128 : (s + 1) * 128, :]))
        rows.append(jnp.sum(flipped, axis=0, keepdims=True) * (0.5 * LOG2E / EPSILON))
    return rows


def cost_tiles(a_ref, b_ref, sq_ref, norms, n):
    inner = lax.dot_general(
        b_ref[...],
        a_ref[n * 256 : (n + 1) * 256, :],
        (((1,), (1,)), ((), ())),
        preferred_element_type=jnp.float32,
    )
    scale = LOG2E / EPSILON
    return [(sq_ref[...] + norms[2 * n + s]) - scale * inner[:, s * 128 : (s + 1) * 128] for s in range(2)]


def reduce_pair(head, source, at, high_ref, mass_ref, base, before):
    heads = [head[base : base + 2, :]]
    pair = lambda rows: [(s, source[rows, at + s * 128 : at + (s + 1) * 128]) for s in range(2)]
    for b in range(RJ):
        lanes_block(pair, 1, heads, high_ref, mass_ref, b * 128, before)


def cost_own_body(
    info, gen_count, ref_count, a_ref, b_ref, k1a_ref, high_ref, mass_ref, sq_ref, lift_i, lift_j, weights
):
    masks(info, gen_count, ref_count, lift_i, lift_j, weights)
    head = lift_i[...]
    norms = a_norms(a_ref)
    for b in range(RJ):
        part = slice(b * 128, (b + 1) * 128)
        total = jnp.sum(norm_parts(b_ref[part, :]), axis=1, keepdims=True) * (0.5 * LOG2E / EPSILON)
        sq_ref[part, :] = jnp.broadcast_to(total, (128, 128))
    for n in range(4):
        if n < 3:
            for s, tile in enumerate(cost_tiles(a_ref, b_ref, sq_ref, norms, n)):
                k1a_ref[:, (2 * n + s) * 128 : (2 * n + s + 1) * 128] = tile
        if n > 0:
            before = (high_ref, mass_ref) if n > 1 else None
            reduce_pair(head, k1a_ref, (n - 1) * 256, high_ref, mass_ref, 2 * n - 2, before)


def cost_other_body(
    a_ref, b_ref, lift_i, high_in, mass_in, sq_ref, k1b_ref, k2_hbm, part_out, k2_ref, high_ref, mass_ref, out_sems
):
    head = lift_i[...]
    norms = a_norms(a_ref)
    stores = [fetch(k2_ref, k2_hbm, out_sems, b) for b in range(RJ)]
    order = [1, 2, 0]
    for step in range(4):
        if step < 3:
            n = order[step]
            target, at = (k1b_ref, 0) if n == 0 else (k2_ref, (n - 1) * 256)
            for s, tile in enumerate(cost_tiles(a_ref, b_ref, sq_ref, norms, n)):
                target[:, at + s * 128 : at + (s + 1) * 128] = tile
        if step > 0:
            n = order[step - 1]
            source, at = (k1b_ref, 0) if n == 0 else (k2_ref, (n - 1) * 256)
            before = (high_ref, mass_ref) if step > 1 else (high_in, mass_in)
            reduce_pair(head, source, at, high_ref, mass_ref, RH + 2 * n, before)
        if step == 1:
            for store in stores:
                store.start()
    (result,) = lanes_result(1, high_ref, mass_ref)
    for n in range(4):
        part_out[n, 0:RJ, :] = result
        part_out[n, RJ:8, :] = jnp.zeros((8 - RJ, 128), jnp.float32)
    for store in stores:
        store.wait()


def second_body(k1a_ref, k1b_ref, k2_hbm, got, lift_j, out, g1_out, k2_ref, sems, wide_ref, high_ref, mass_ref):
    core = lift_j[6:7, :]
    start_fetch(k2_hbm, k2_ref, sems)
    g1 = -merge(got, 4)[0:RJ, :]
    g1_out[...] = g1
    lift = lift_j[0:RJ, :]
    heads = [lift, lifted(g1, lift)]
    results = reduce_rows(k1a_ref, k1b_ref, k2_hbm, k2_ref, sems, heads, wide_ref, high_ref, mass_ref)
    sent = [turned(core, value) for value in results]
    for n in range(8):
        for v in range(2):
            out[n, v * RI : (v + 1) * RI, :] = sent[v]


def third_body(k1a_ref, k1b_ref, k2_hbm, got, lift_i, out, f2_out, k2_ref, sems, high_ref, mass_ref):
    core = lift_i[14:15, :]
    start_fetch(k2_hbm, k2_ref, sems)
    merged = -merge(got, 8)
    f1 = turned(core, merged[0:RI, :])
    f2 = 0.5 * (f1 + turned(core, merged[RI : 2 * RI, :]))
    f2_out[...] = f2
    lift = lift_i[0:RI, :]
    heads = [lifted(f1, lift), lifted(f2, lift)]
    results = reduce_lanes(k1a_ref, k1b_ref, k2_hbm, k2_ref, sems, heads, high_ref, mass_ref)
    for n in range(4):
        for v in range(2):
            out[n, v * 8 : v * 8 + RJ, :] = results[v]
            out[n, v * 8 + RJ : v * 8 + 8, :] = jnp.zeros((8 - RJ, 128), jnp.float32)


def fourth_body(k1a_ref, k1b_ref, k2_hbm, got, lift_j, g1, out, g3_out, k2_ref, sems, wide_ref, high_ref, mass_ref):
    core = lift_j[6:7, :]
    start_fetch(k2_hbm, k2_ref, sems)
    merged = -merge(got, 4)
    g2 = 0.5 * (g1[...] + merged[0:RJ, :])
    g3 = 0.5 * (g2 + merged[8 : 8 + RJ, :])
    g3_out[...] = g3
    lift = lift_j[0:RJ, :]
    heads = [lifted(g2, lift), lifted(g3, lift)]
    results = reduce_rows(k1a_ref, k1b_ref, k2_hbm, k2_ref, sems, heads, wide_ref, high_ref, mass_ref)
    sent = [turned(core, value) for value in results]
    for n in range(8):
        for v in range(2):
            out[n, v * RI : (v + 1) * RI, :] = sent[v]


def fifth_body(k1a_ref, k1b_ref, k2_hbm, got, lift_i, f2, g3, out, k2_ref, sems, high_ref, mass_ref):
    core = lift_i[14:15, :]
    start_fetch(k2_hbm, k2_ref, sems)
    merged = -merge(got, 8)
    f3 = 0.5 * (f2[...] + turned(core, merged[0:RI, :]))
    f4 = 0.5 * (f3 + turned(core, merged[RI : 2 * RI, :]))
    heads = [lifted(f3, lift_i[0:RI, :])]
    (result,) = reduce_lanes(k1a_ref, k1b_ref, k2_hbm, k2_ref, sems, heads, high_ref, mass_ref)
    shifted = result - g3[...]
    along_y = lift_i[15:16, :]
    mine = f4[4:6, :]
    for n, row in ((2, 3), (1, 1), (0, 0)):
        mine = jnp.where(along_y < n + 0.5, f4[row : row + 2, :], mine)
    for n in range(16):
        out[n, 0:RJ, :] = shifted
        out[n, RJ : RJ + 2, :] = mine


def last_body(got, weights, gen_pot, ref_pot, gen_self, ref_self, share):
    g4 = merge([got[n * 4 + 1, 0:RJ, :] for n in range(4)], 4) * (-0.5 * LN2)
    weight = weights[16 : 16 + RJ, :]
    total = jnp.sum(jnp.where(weight > 0.0, g4 * weight, 0.0))
    own = [[got[n * 4 + plane, RJ : RJ + 2, :] * LN2 for n in range(4)] for plane in (1, 0, 3)]
    for n in range(4):
        weight = weights[2 * n : 2 * n + 2, :]
        total += jnp.sum(jnp.where(weight > 0.0, (own[0][n] - own[1][n]) * weight, 0.0))
        weight = weights[8 + 2 * n : 8 + 2 * n + 2, :]
        total -= jnp.sum(jnp.where(weight > 0.0, own[2][n] * weight, 0.0))
    for n in range(8):
        share[n, :, :] = jnp.full((8, 128), total, jnp.float32)

    along_x, odd_y = weights[22:23, :], weights[23:24, :]
    low = lax.broadcasted_iota(jnp.int32, (1, 128), 1) < 64

    def chosen(rows):
        result = rows[0]
        for n in range(1, 4):
            result = jnp.where(along_x > n - 0.5, rows[n], result)
        return result

    def write(out, window, late):
        rolled = jnp.concatenate([window[:, 64:], window[:, :64]], axis=1)
        first = jnp.where(late, jnp.where(low, rolled[0:1, :], rolled[1:2, :]), window[0:1, :])
        second = jnp.where(late, rolled[1:2, :], window[1:2, :])
        out[0:1, 0:128] = first
        out[0:1, 128:192] = second[:, 0:64]

    for out, rows in zip((gen_pot, gen_self, ref_self), own):
        write(out, chosen(rows), odd_y > 0.5)
    odd_x = ((along_x > 0.5) & (along_x < 1.5)) | (along_x > 2.5)
    write(ref_pot, chosen([g4[row : row + 2, :] for row in (0, 1, 3, 4)]), odd_x)


F32 = jnp.float32
BF16 = jnp.bfloat16
STREAM = [pltpu.VMEM((NJ, N2), F32), pltpu.SemaphoreType.DMA((RJ,))]


def lane_scratch(count):
    return [pltpu.VMEM((count, NJ, 128), F32)] * 2


def row_scratch(count):
    return [pltpu.VMEM((count, NJ, 128), F32)] + [pltpu.VMEM((count, 8 * RJ, NI), F32)] * 2


def stage_pack(*args):
    scratch = [pltpu.VMEM((2, 64, BLOCK), BF16), pltpu.SemaphoreType.DMA((2,))]
    out = jax.ShapeDtypeStruct((BLOCK, 128), BF16)
    return call(pack_body, out, [HBM, HBM], scratch, mib=60)(*args)


def bf16(*shape):
    return jax.ShapeDtypeStruct(shape, BF16)


def stage_unpack(*args):
    return call(unpack_body, (bf16(4, BLOCK, D), bf16(BLOCK, D)), [SMEM, VMEM])(*args)


def stage_widen(*args):
    return call(widen_body, bf16(4, BLOCK, D), [VMEM, HBM])(*args)


def stage_cost_own(*args):
    outs = (f32(NJ, NI // 2), f32(1, NJ, 128), f32(1, NJ, 128), f32(NJ, 128))
    outs += (f32(16, 128), f32(8, 128), f32(24, 128))
    return call(cost_own_body, outs, [SMEM] * 3 + [VMEM] * 2)(*args)


def stage_cost_other(*args):
    scratch = [pltpu.VMEM((NJ, N2), F32), *lane_scratch(1), pltpu.SemaphoreType.DMA((RJ,))]
    outs = (f32(NJ, NI // 2 - N2), f32(ROOM, N2), f32(4, 8, 128))
    return call(cost_other_body, outs, [VMEM] * 6, scratch, (VMEM, HBM, VMEM))(*args)


K_SPECS = [VMEM, VMEM, HBM]


def stage_second(*args):
    outs = (f32(8, 2 * RI, 128), f32(RJ, 128))
    return call(second_body, outs, K_SPECS + [VMEM] * 2, STREAM + row_scratch(2))(*args)


def stage_third(*args):
    outs = (f32(4, 16, 128), f32(RI, 128))
    return call(third_body, outs, K_SPECS + [VMEM] * 2, STREAM + lane_scratch(2))(*args)


def stage_fourth(*args):
    outs = (f32(8, 2 * RI, 128), f32(RJ, 128))
    return call(fourth_body, outs, K_SPECS + [VMEM] * 3, STREAM + row_scratch(2))(*args)


def stage_fifth(*args):
    return call(fifth_body, f32(16, 8, 128), K_SPECS + [VMEM] * 4, STREAM + lane_scratch(1))(*args)


def spread(operand, axes):
    return lax.all_to_all(operand, axes, 0, 0, tiled=True)


def local(gen_points, reference_embeddings, gen_count, ref_count):
    y, x, c, zl = (lax.axis_index(name) for name in ("y", "x", "c", "zl"))
    a_is_gen = zl < 3
    b_is_gen = zl == 0
    packed = stage_pack(jnp.transpose(gen_points), jnp.transpose(reference_embeddings))
    raw = lax.all_gather(packed, ("zh", "zl"))

    info = jnp.stack(
        [
            a_is_gen.astype(jnp.int32),
            b_is_gen.astype(jnp.int32),
            c,
            x,
            y,
        ]
    ).astype(jnp.int32)
    a_wide, b_own = stage_unpack(info, raw)
    one = spread(a_wide, "y")
    two = spread(stage_widen(b_own, one), "x")
    a_own, b_all = lax.optimization_barrier((one.reshape(NJ, D), two.reshape(NJ, D)))
    a_other = lax.ppermute(a_own, "c", [(0, 1), (1, 0)])
    k1a, high, mass, b_norms, lift_i, lift_j, weights = stage_cost_own(
        info, gen_count, ref_count, a_own, b_all
    )
    k1b, k2, part = stage_cost_other(a_other, b_all, lift_i, high, mass, b_norms)
    k = (k1a, k1b, k2)
    part, g1 = stage_second(*k, spread(part, "x"), lift_j)
    part, f2 = stage_third(*k, spread(part, ("y", "c")), lift_i)
    part, g3 = stage_fourth(*k, spread(part, "x"), lift_j, g1)
    part = stage_fifth(*k, spread(part, ("y", "c")), lift_i, f2, g3)
    got = spread(part, ("x", "zl"))
    outs = (f32(1, BLOCK),) * 4 + (f32(8, 8, 128),)
    *pots, share = call(last_body, outs, [VMEM, VMEM])(got, weights)
    divergence = jnp.sum(spread(share, ("y", "c"))[:, 0, 0])
    return *(pot.reshape(BLOCK) for pot in pots), divergence


def solution(mesh):
    fine = Mesh(mesh.devices.reshape(4, 4, 2, 4, 4), ("y", "x", "c", "zh", "zl"))
    tile, feat = ("y", "x", "c"), ("zh", "zl")
    return jax.shard_map(
        local,
        mesh=fine,
        in_specs=(P(tile, feat), P(tile, feat), P(), P()),
        out_specs=(P(tile), P(tile), P(tile), P(tile), P()),
        check_vma=False,
    )
```

```python
import functools

import jax
import jax.numpy as jnp
from jax import lax
from jax.experimental import pallas as pl
from jax.experimental.pallas import tpu as pltpu
from jax.sharding import Mesh, PartitionSpec as P

EPSILON = 0.25
LOG2E = 1.4426950408889634
LN2 = 0.6931471805599453
FAR = -1.0e30

BLOCK = 192
D = 1024
NI = 8 * BLOCK
NJ = 4 * BLOCK
RI = NI // 128
RH = RI // 2
RJ = NJ // 128
NEAR = 8
N2 = NI - NEAR * 128
ROOM = 18 * NJ

VMEM = pl.BlockSpec(memory_space=pltpu.VMEM)
HBM = pl.BlockSpec(memory_space=pltpu.HBM)
SMEM = pl.BlockSpec(memory_space=pltpu.SMEM)


def f32(*shape):
    return jax.ShapeDtypeStruct(shape, jnp.float32)


def call(body, outs, ins, scratch=(), out_specs=None, mib=40):
    return pl.pallas_call(
        body,
        out_shape=outs,
        in_specs=ins,
        out_specs=jax.tree.map(lambda _: VMEM, outs) if out_specs is None else out_specs,
        scratch_shapes=list(scratch),
        compiler_params=pltpu.CompilerParams(vmem_limit_bytes=mib * 1024 * 1024),
    )


def merge(got, count):
    parts = [got[n] for n in range(count)]
    high = functools.reduce(jnp.maximum, parts)
    mass = functools.reduce(jnp.add, [jnp.exp2(part - high) for part in parts])
    return high + jnp.log(mass) * LOG2E


def lifted(pot, lift):
    return jnp.where(lift > -1.0e29, pot + lift, FAR)


def tree(op, values):
    values = list(values)
    while len(values) > 1:
        values = [op(*values[n : n + 2]) if n + 1 < len(values) else values[n] for n in range(0, len(values), 2)]
    return values[0]


def fetch(k2_hbm, k2_ref, sems, b):
    rows = pl.ds(b * 128, 128)
    return pltpu.make_async_copy(k2_hbm.at[rows], k2_ref.at[rows], sems.at[b])


def start_fetch(k2_hbm, k2_ref, sems):
    for b in range(RJ):
        fetch(k2_hbm, k2_ref, sems, b).start()


def lanes_block(tiles_of, count, heads, high_ref, mass_ref, base, before=None):
    for group in range(16):
        rows = pl.ds(base + group * 8, 8)
        tiles = tiles_of(rows)
        for v in range(count):
            xs = [heads[v][r : r + 1, :] - tile for r, tile in tiles]
            high = tree(jnp.maximum, xs)
            if before:
                above = before[0][v, rows, :]
                high = jnp.maximum(high, above)
                xs.append(above)
            masses = [jnp.exp2(x - high) for x in xs]
            if before:
                masses[-1] = masses[-1] * before[1][v, rows, :]
            high_ref[v, rows, :] = high
            mass_ref[v, rows, :] = tree(jnp.add, masses)


def near_tile(k1a_ref, k1b_ref, rows, r):
    if r < RH:
        return k1a_ref[rows, r * 128 : (r + 1) * 128]
    return k1b_ref[rows, (r - RH) * 128 : (r - RH + 1) * 128]


def near_tiles(k1a_ref, k1b_ref):
    return lambda rows: [(r, near_tile(k1a_ref, k1b_ref, rows, r)) for r in range(NEAR)]


def far_tiles(k2_ref):
    return lambda rows: [(r, k2_ref[rows, (r - NEAR) * 128 : (r - NEAR + 1) * 128]) for r in range(NEAR, RI)]


def turned(core, value):
    return jnp.where(core > 0.5, jnp.concatenate([value[RH:RI, :], value[0:RH, :]], axis=0), value)


def lanes_result(count, high_ref, mass_ref):
    results = []
    for v in range(count):
        rows_out = []
        for b in range(RJ):
            high = jnp.transpose(high_ref[v, b * 128 : (b + 1) * 128, :])
            mass = jnp.transpose(mass_ref[v, b * 128 : (b + 1) * 128, :])
            top = jnp.max(high, axis=0, keepdims=True)
            total = jnp.sum(mass * jnp.exp2(high - top), axis=0, keepdims=True)
            rows_out.append((top, total))
        top = jnp.concatenate([row[0] for row in rows_out], axis=0)
        total = jnp.concatenate([row[1] for row in rows_out], axis=0)
        results.append(top + jnp.log(total) * LOG2E)
    return results


def reduce_lanes(k1a_ref, k1b_ref, k2_hbm, k2_ref, sems, heads, high_ref, mass_ref):
    count = len(heads)

    def near(b, carry):
        lanes_block(near_tiles(k1a_ref, k1b_ref), count, heads, high_ref, mass_ref, pl.multiple_of(b * 128, 128))
        return carry

    def far(b, carry):
        fetch(k2_hbm, k2_ref, sems, b).wait()
        start = pl.multiple_of(b * 128, 128)
        lanes_block(far_tiles(k2_ref), count, heads, high_ref, mass_ref, start, (high_ref, mass_ref))
        return carry

    lax.fori_loop(0, RJ, near, 0, unroll=2)
    lax.fori_loop(0, RJ, far, 0, unroll=2)
    return lanes_result(count, high_ref, mass_ref)


def reduce_rows(k1a_ref, k1b_ref, k2_hbm, k2_ref, sems, heads, wide_ref, high_ref, mass_ref):
    count = len(heads)
    for v in range(count):
        for b in range(RJ):
            row = jnp.broadcast_to(heads[v][b : b + 1, :], (128, 128))
            wide_ref[v, b * 128 : (b + 1) * 128, :] = jnp.transpose(row)

    def block(b, wides, tile, r):
        spot = pl.ds(pl.multiple_of(b * 8, 8), 8)
        cols = slice(r * 128, (r + 1) * 128)
        tiles = [tile(pl.ds(b * 128 + group * 8, 8)) for group in range(16)]
        for v in range(count):
            xs = [wides[v][group * 8 : group * 8 + 8, :] - tiles[group] for group in range(16)]
            high = tree(jnp.maximum, xs)
            high_ref[v, spot, cols] = high
            mass_ref[v, spot, cols] = tree(jnp.add, [jnp.exp2(x - high) for x in xs])

    def near(b, carry):
        wides = [wide_ref[v, pl.ds(pl.multiple_of(b * 128, 128), 128), :] for v in range(count)]
        for r in range(NEAR):
            block(b, wides, lambda rows: near_tile(k1a_ref, k1b_ref, rows, r), r)
        return carry

    def far(b, carry):
        fetch(k2_hbm, k2_ref, sems, b).wait()
        wides = [wide_ref[v, pl.ds(pl.multiple_of(b * 128, 128), 128), :] for v in range(count)]
        for r in range(NEAR, RI):
            block(b, wides, lambda rows: k2_ref[rows, (r - NEAR) * 128 : (r - NEAR + 1) * 128], r)
        return carry

    lax.fori_loop(0, RJ, near, 0, unroll=2)
    lax.fori_loop(0, RJ, far, 0, unroll=2)
    results = []
    for v in range(count):
        tops, totals = [], []
        for r in range(RI):
            cols = slice(r * 128, (r + 1) * 128)
            high = high_ref[v, :, cols]
            top = jnp.max(high, axis=0, keepdims=True)
            tops.append(top)
            totals.append(jnp.sum(mass_ref[v, :, cols] * jnp.exp2(high - top), axis=0, keepdims=True))
        results.append(jnp.concatenate(tops, axis=0) + jnp.log(jnp.concatenate(totals, axis=0)) * LOG2E)
    return results


def pack_body(gen, ref, out, both, sems):
    copies = [pltpu.make_async_copy(part, both.at[n], sems.at[n]) for n, part in enumerate((gen, ref))]
    for copy in copies:
        copy.start()
    for copy in copies:
        copy.wait()
    wide = jnp.concatenate([both[0].astype(jnp.float32), both[1].astype(jnp.float32)], axis=0)
    out[...] = jnp.transpose(wide).astype(jnp.bfloat16)


def unpack_body(info, raw, a_out, b_out):
    for k in range(D // 128):
        cols = slice(k * 128, (k + 1) * 128)
        even, odd = raw[2 * k], raw[2 * k + 1]
        gen = jnp.concatenate([even[:, :64], odd[:, :64]], axis=1)
        ref = jnp.concatenate([even[:, 64:], odd[:, 64:]], axis=1)
        a = jnp.where(info[0] == 1, gen, ref)
        b_out[:, cols] = jnp.where(info[1] == 1, gen, ref)
        for n in range(4):
            a_out[n, :, cols] = a


def widen_body(own, a_half, out):
    del a_half
    for n in range(4):
        out[n] = own[...]


def norm_parts(values):
    values = values.astype(jnp.float32)
    values = values * values
    return functools.reduce(jnp.add, [values[:, k * 128 : (k + 1) * 128] for k in range(D // 128)])


def masks(info, gen_count, ref_count, lift_i, lift_j, weights):
    c, x, y = info[2], info[3], info[4]

    def total(counts):
        return jnp.full((8, 128), functools.reduce(jnp.add, [counts[n] for n in range(32)]).astype(jnp.float32))

    def number(is_gen, t):
        return jnp.where(is_gen, gen_count[t], ref_count[t])

    def flat(rows):
        shape = (rows, 128)
        return lax.broadcasted_iota(jnp.int32, shape, 0) * 128 + lax.broadcasted_iota(jnp.int32, shape, 1)

    def valid(spots, starts, counts):
        inside = [(spots >= start) & (spots < start + count) for start, count in zip(starts, counts)]
        return functools.reduce(jnp.logical_or, inside)

    a_is_gen, b_is_gen = info[0] == 1, info[1] == 1
    totals = total(gen_count), total(ref_count)
    gen_log, ref_log = (-jnp.log(value) * LOG2E for value in totals)
    counts = [number(a_is_gen, ((n % 4) * 4 + x) * 2 + (c if n < 4 else 1 - c)) for n in range(8)]
    ok = valid(flat(16), [n * BLOCK for n in range(8)], counts)
    log_a = jnp.where(a_is_gen, gen_log, ref_log)
    lift_i[...] = jnp.where(ok, jnp.concatenate([log_a, log_a], axis=0), FAR)
    core = jnp.full((1, 128), c.astype(jnp.float32))
    lift_i[14:15, :] = core
    lift_i[15:16, :] = jnp.full((1, 128), y.astype(jnp.float32))
    here = [(y * 4 + n) * 2 + c for n in range(4)]
    starts = [n * BLOCK for n in range(4)]
    ok = valid(flat(8), starts, [number(b_is_gen, t) for t in here])
    lift_j[...] = jnp.where(ok, jnp.where(b_is_gen, gen_log, ref_log), FAR)
    lift_j[6:7, :] = core
    shift = 64 * lax.rem(y, 2)
    windows = [n * 256 + shift for n in range(4)]
    for n, counts in enumerate((gen_count, ref_count)):
        ok = valid(flat(8), windows, [counts[t] for t in here])
        weights[n * 8 : n * 8 + 8, :] = jnp.where(ok, 1.0 / totals[n], 0.0)
    ok = valid(flat(8), starts, [ref_count[t] for t in here])
    weights[16:24, :] = jnp.where(ok, 1.0 / totals[1], 0.0)
    weights[22:23, :] = jnp.full((1, 128), x.astype(jnp.float32))
    weights[23:24, :] = jnp.full((1, 128), lax.rem(y, 2).astype(jnp.float32))


def a_norms(a_ref):
    rows = []
    for s in range(RH):
        flipped = jnp.transpose(norm_parts(a_ref[s * 128 : (s + 1) * 128, :]))
        rows.append(jnp.sum(flipped, axis=0, keepdims=True) * (0.5 * LOG2E / EPSILON))
    return rows


def cost_tiles(a_ref, b_ref, sq_ref, norms, n):
    inner = lax.dot_general(
        b_ref[...],
        a_ref[n * 256 : (n + 1) * 256, :],
        (((1,), (1,)), ((), ())),
        preferred_element_type=jnp.float32,
    )
    scale = LOG2E / EPSILON
    return [(sq_ref[...] + norms[2 * n + s]) - scale * inner[:, s * 128 : (s + 1) * 128] for s in range(2)]


def reduce_pair(head, source, at, high_ref, mass_ref, base, before):
    heads = [head[base : base + 2, :]]
    pair = lambda rows: [(s, source[rows, at + s * 128 : at + (s + 1) * 128]) for s in range(2)]
    for b in range(RJ):
        lanes_block(pair, 1, heads, high_ref, mass_ref, b * 128, before)


def cost_own_body(
    info, gen_count, ref_count, a_ref, b_ref, k1a_ref, high_ref, mass_ref, sq_ref, lift_i, lift_j, weights
):
    masks(info, gen_count, ref_count, lift_i, lift_j, weights)
    head = lift_i[...]
    norms = a_norms(a_ref)
    for b in range(RJ):
        part = slice(b * 128, (b + 1) * 128)
        total = jnp.sum(norm_parts(b_ref[part, :]), axis=1, keepdims=True) * (0.5 * LOG2E / EPSILON)
        sq_ref[part, :] = jnp.broadcast_to(total, (128, 128))
    for n in range(4):
        if n < 3:
            for s, tile in enumerate(cost_tiles(a_ref, b_ref, sq_ref, norms, n)):
                k1a_ref[:, (2 * n + s) * 128 : (2 * n + s + 1) * 128] = tile
        if n > 0:
            before = (high_ref, mass_ref) if n > 1 else None
            reduce_pair(head, k1a_ref, (n - 1) * 256, high_ref, mass_ref, 2 * n - 2, before)


def cost_other_body(
    a_ref, b_ref, lift_i, high_in, mass_in, sq_ref, k1b_ref, k2_hbm, part_out, k2_ref, high_ref, mass_ref, out_sems
):
    head = lift_i[...]
    norms = a_norms(a_ref)
    stores = [fetch(k2_ref, k2_hbm, out_sems, b) for b in range(RJ)]
    order = [1, 2, 0]
    for step in range(4):
        if step < 3:
            n = order[step]
            target, at = (k1b_ref, 0) if n == 0 else (k2_ref, (n - 1) * 256)
            for s, tile in enumerate(cost_tiles(a_ref, b_ref, sq_ref, norms, n)):
                target[:, at + s * 128 : at + (s + 1) * 128] = tile
        if step > 0:
            n = order[step - 1]
            source, at = (k1b_ref, 0) if n == 0 else (k2_ref, (n - 1) * 256)
            before = (high_ref, mass_ref) if step > 1 else (high_in, mass_in)
            reduce_pair(head, source, at, high_ref, mass_ref, RH + 2 * n, before)
        if step == 1:
            for store in stores:
                store.start()
    (result,) = lanes_result(1, high_ref, mass_ref)
    for n in range(4):
        part_out[n, 0:RJ, :] = result
        part_out[n, RJ:8, :] = jnp.zeros((8 - RJ, 128), jnp.float32)
    for store in stores:
        store.wait()


def second_body(k1a_ref, k1b_ref, k2_hbm, got, lift_j, out, g1_out, k2_ref, sems, wide_ref, high_ref, mass_ref):
    core = lift_j[6:7, :]
    start_fetch(k2_hbm, k2_ref, sems)
    g1 = -merge(got, 4)[0:RJ, :]
    g1_out[...] = g1
    lift = lift_j[0:RJ, :]
    heads = [lift, lifted(g1, lift)]
    results = reduce_rows(k1a_ref, k1b_ref, k2_hbm, k2_ref, sems, heads, wide_ref, high_ref, mass_ref)
    sent = [turned(core, value) for value in results]
    for n in range(8):
        for v in range(2):
            out[n, v * RI : (v + 1) * RI, :] = sent[v]


def third_body(k1a_ref, k1b_ref, k2_hbm, got, lift_i, out, f2_out, k2_ref, sems, high_ref, mass_ref):
    core = lift_i[14:15, :]
    start_fetch(k2_hbm, k2_ref, sems)
    merged = -merge(got, 8)
    f1 = turned(core, merged[0:RI, :])
    f2 = 0.5 * (f1 + turned(core, merged[RI : 2 * RI, :]))
    f2_out[...] = f2
    lift = lift_i[0:RI, :]
    heads = [lifted(f1, lift), lifted(f2, lift)]
    results = reduce_lanes(k1a_ref, k1b_ref, k2_hbm, k2_ref, sems, heads, high_ref, mass_ref)
    for n in range(4):
        for v in range(2):
            out[n, v * 8 : v * 8 + RJ, :] = results[v]
            out[n, v * 8 + RJ : v * 8 + 8, :] = jnp.zeros((8 - RJ, 128), jnp.float32)


def fourth_body(k1a_ref, k1b_ref, k2_hbm, got, lift_j, g1, out, g3_out, k2_ref, sems, wide_ref, high_ref, mass_ref):
    core = lift_j[6:7, :]
    start_fetch(k2_hbm, k2_ref, sems)
    merged = -merge(got, 4)
    g2 = 0.5 * (g1[...] + merged[0:RJ, :])
    g3 = 0.5 * (g2 + merged[8 : 8 + RJ, :])
    g3_out[...] = g3
    lift = lift_j[0:RJ, :]
    heads = [lifted(g2, lift), lifted(g3, lift)]
    results = reduce_rows(k1a_ref, k1b_ref, k2_hbm, k2_ref, sems, heads, wide_ref, high_ref, mass_ref)
    sent = [turned(core, value) for value in results]
    for n in range(8):
        for v in range(2):
            out[n, v * RI : (v + 1) * RI, :] = sent[v]


def fifth_body(k1a_ref, k1b_ref, k2_hbm, got, lift_i, f2, g3, out, k2_ref, sems, high_ref, mass_ref):
    core = lift_i[14:15, :]
    start_fetch(k2_hbm, k2_ref, sems)
    merged = -merge(got, 8)
    f3 = 0.5 * (f2[...] + turned(core, merged[0:RI, :]))
    f4 = 0.5 * (f3 + turned(core, merged[RI : 2 * RI, :]))
    heads = [lifted(f3, lift_i[0:RI, :])]
    (result,) = reduce_lanes(k1a_ref, k1b_ref, k2_hbm, k2_ref, sems, heads, high_ref, mass_ref)
    shifted = result - g3[...]
    along_y = lift_i[15:16, :]
    mine = f4[4:6, :]
    for n, row in ((2, 3), (1, 1), (0, 0)):
        mine = jnp.where(along_y < n + 0.5, f4[row : row + 2, :], mine)
    for n in range(16):
        out[n, 0:RJ, :] = shifted
        out[n, RJ : RJ + 2, :] = mine


def last_body(got, weights, gen_pot, ref_pot, gen_self, ref_self, share):
    g4 = merge([got[n * 4 + 1, 0:RJ, :] for n in range(4)], 4) * (-0.5 * LN2)
    weight = weights[16 : 16 + RJ, :]
    total = jnp.sum(jnp.where(weight > 0.0, g4 * weight, 0.0))
    own = [[got[n * 4 + plane, RJ : RJ + 2, :] * LN2 for n in range(4)] for plane in (1, 0, 3)]
    for n in range(4):
        weight = weights[2 * n : 2 * n + 2, :]
        total += jnp.sum(jnp.where(weight > 0.0, (own[0][n] - own[1][n]) * weight, 0.0))
        weight = weights[8 + 2 * n : 8 + 2 * n + 2, :]
        total -= jnp.sum(jnp.where(weight > 0.0, own[2][n] * weight, 0.0))
    for n in range(8):
        share[n, :, :] = jnp.full((8, 128), total, jnp.float32)

    along_x, odd_y = weights[22:23, :], weights[23:24, :]
    low = lax.broadcasted_iota(jnp.int32, (1, 128), 1) < 64

    def chosen(rows):
        result = rows[0]
        for n in range(1, 4):
            result = jnp.where(along_x > n - 0.5, rows[n], result)
        return result

    def write(out, window, late):
        rolled = jnp.concatenate([window[:, 64:], window[:, :64]], axis=1)
        first = jnp.where(late, jnp.where(low, rolled[0:1, :], rolled[1:2, :]), window[0:1, :])
        second = jnp.where(late, rolled[1:2, :], window[1:2, :])
        out[0:1, 0:128] = first
        out[0:1, 128:192] = second[:, 0:64]

    for out, rows in zip((gen_pot, gen_self, ref_self), own):
        write(out, chosen(rows), odd_y > 0.5)
    odd_x = ((along_x > 0.5) & (along_x < 1.5)) | (along_x > 2.5)
    write(ref_pot, chosen([g4[row : row + 2, :] for row in (0, 1, 3, 4)]), odd_x)


F32 = jnp.float32
BF16 = jnp.bfloat16
STREAM = [pltpu.VMEM((NJ, N2), F32), pltpu.SemaphoreType.DMA((RJ,))]


def lane_scratch(count):
    return [pltpu.VMEM((count, NJ, 128), F32)] * 2


def row_scratch(count):
    return [pltpu.VMEM((count, NJ, 128), F32)] + [pltpu.VMEM((count, 8 * RJ, NI), F32)] * 2


def stage_pack(*args):
    scratch = [pltpu.VMEM((2, 64, BLOCK), BF16), pltpu.SemaphoreType.DMA((2,))]
    out = jax.ShapeDtypeStruct((BLOCK, 128), BF16)
    return call(pack_body, out, [HBM, HBM], scratch, mib=60)(*args)


def bf16(*shape):
    return jax.ShapeDtypeStruct(shape, BF16)


def stage_unpack(*args):
    return call(unpack_body, (bf16(4, BLOCK, D), bf16(BLOCK, D)), [SMEM, VMEM])(*args)


def stage_widen(*args):
    return call(widen_body, bf16(4, BLOCK, D), [VMEM, HBM])(*args)


def stage_cost_own(*args):
    outs = (f32(NJ, NI // 2), f32(1, NJ, 128), f32(1, NJ, 128), f32(NJ, 128))
    outs += (f32(16, 128), f32(8, 128), f32(24, 128))
    return call(cost_own_body, outs, [SMEM] * 3 + [VMEM] * 2)(*args)


def stage_cost_other(*args):
    scratch = [pltpu.VMEM((NJ, N2), F32), *lane_scratch(1), pltpu.SemaphoreType.DMA((RJ,))]
    outs = (f32(NJ, NI // 2 - N2), f32(ROOM, N2), f32(4, 8, 128))
    return call(cost_other_body, outs, [VMEM] * 6, scratch, (VMEM, HBM, VMEM))(*args)


K_SPECS = [VMEM, VMEM, HBM]


def stage_second(*args):
    outs = (f32(8, 2 * RI, 128), f32(RJ, 128))
    return call(second_body, outs, K_SPECS + [VMEM] * 2, STREAM + row_scratch(2))(*args)


def stage_third(*args):
    outs = (f32(4, 16, 128), f32(RI, 128))
    return call(third_body, outs, K_SPECS + [VMEM] * 2, STREAM + lane_scratch(2))(*args)


def stage_fourth(*args):
    outs = (f32(8, 2 * RI, 128), f32(RJ, 128))
    return call(fourth_body, outs, K_SPECS + [VMEM] * 3, STREAM + row_scratch(2))(*args)


def stage_fifth(*args):
    return call(fifth_body, f32(16, 8, 128), K_SPECS + [VMEM] * 4, STREAM + lane_scratch(1))(*args)


def spread(operand, axes):
    return lax.all_to_all(operand, axes, 0, 0, tiled=True)


def local(gen_points, reference_embeddings, gen_count, ref_count):
    y, x, c, zl = (lax.axis_index(name) for name in ("y", "x", "c", "zl"))
    a_is_gen = zl < 3
    b_is_gen = zl == 0
    packed = stage_pack(jnp.transpose(gen_points), jnp.transpose(reference_embeddings))
    raw = lax.all_gather(packed, ("zh", "zl"))

    info = jnp.stack(
        [
            a_is_gen.astype(jnp.int32),
            b_is_gen.astype(jnp.int32),
            c,
            x,
            y,
        ]
    ).astype(jnp.int32)
    a_wide, b_own = stage_unpack(info, raw)
    one = spread(a_wide, "y")
    two = spread(stage_widen(b_own, one), "x")
    a_own, b_all = lax.optimization_barrier((one.reshape(NJ, D), two.reshape(NJ, D)))
    a_other = lax.ppermute(a_own, "c", [(0, 1), (1, 0)])
    k1a, high, mass, b_norms, lift_i, lift_j, weights = stage_cost_own(
        info, gen_count, ref_count, a_own, b_all
    )
    k1b, k2, part = stage_cost_other(a_other, b_all, lift_i, high, mass, b_norms)
    k = (k1a, k1b, k2)
    part, g1 = stage_second(*k, spread(part, "x"), lift_j)
    part, f2 = stage_third(*k, spread(part, ("y", "c")), lift_i)
    part, g3 = stage_fourth(*k, spread(part, "x"), lift_j, g1)
    part = stage_fifth(*k, spread(part, ("y", "c")), lift_i, f2, g3)
    got = spread(part, ("x", "zl"))
    outs = (f32(1, BLOCK),) * 4 + (f32(8, 8, 128),)
    *pots, share = call(last_body, outs, [VMEM, VMEM])(got, weights)
    divergence = jnp.sum(spread(share, ("y", "c"))[:, 0, 0])
    return *(pot.reshape(BLOCK) for pot in pots), divergence


def solution(mesh):
    fine = Mesh(mesh.devices.reshape(4, 4, 2, 4, 4), ("y", "x", "c", "zh", "zl"))
    tile, feat = ("y", "x", "c"), ("zh", "zl")
    return jax.shard_map(
        local,
        mesh=fine,
        in_specs=(P(tile, feat), P(tile, feat), P(), P()),
        out_specs=(P(tile), P(tile), P(tile), P(tile), P()),
        check_vma=False,
    )
```

```python
import functools

import jax
import jax.numpy as jnp
from jax import lax
from jax.experimental import pallas as pl
from jax.experimental.pallas import tpu as pltpu
from jax.sharding import Mesh, PartitionSpec as P

EPSILON = 0.25
LOG2E = 1.4426950408889634
LN2 = 0.6931471805599453
FAR = -1.0e30

BLOCK = 192
D = 1024
NI = 8 * BLOCK
NJ = 4 * BLOCK
RI = NI // 128
RH = RI // 2
RJ = NJ // 128
NEAR = 8
N2 = NI - NEAR * 128
ROOM = 18 * NJ

VMEM = pl.BlockSpec(memory_space=pltpu.VMEM)
HBM = pl.BlockSpec(memory_space=pltpu.HBM)
SMEM = pl.BlockSpec(memory_space=pltpu.SMEM)


def f32(*shape):
    return jax.ShapeDtypeStruct(shape, jnp.float32)


def call(body, outs, ins, scratch=(), out_specs=None, mib=40):
    return pl.pallas_call(
        body,
        out_shape=outs,
        in_specs=ins,
        out_specs=jax.tree.map(lambda _: VMEM, outs) if out_specs is None else out_specs,
        scratch_shapes=list(scratch),
        compiler_params=pltpu.CompilerParams(vmem_limit_bytes=mib * 1024 * 1024),
    )


def merge(got, count):
    parts = [got[n] for n in range(count)]
    high = functools.reduce(jnp.maximum, parts)
    mass = functools.reduce(jnp.add, [jnp.exp2(part - high) for part in parts])
    return high + jnp.log(mass) * LOG2E


def lifted(pot, lift):
    return jnp.where(lift > -1.0e29, pot + lift, FAR)


def tree(op, values):
    values = list(values)
    while len(values) > 1:
        values = [op(*values[n : n + 2]) if n + 1 < len(values) else values[n] for n in range(0, len(values), 2)]
    return values[0]


def fetch(k2_hbm, k2_ref, sems, b):
    rows = pl.ds(b * 128, 128)
    return pltpu.make_async_copy(k2_hbm.at[rows], k2_ref.at[rows], sems.at[b])


def start_fetch(k2_hbm, k2_ref, sems):
    for b in range(RJ):
        fetch(k2_hbm, k2_ref, sems, b).start()


def lanes_block(tiles_of, count, heads, high_ref, mass_ref, base, before=None):
    for group in range(16):
        rows = pl.ds(base + group * 8, 8)
        tiles = tiles_of(rows)
        for v in range(count):
            xs = [heads[v][r : r + 1, :] - tile for r, tile in tiles]
            high = tree(jnp.maximum, xs)
            if before:
                above = before[0][v, rows, :]
                high = jnp.maximum(high, above)
                xs.append(above)
            masses = [jnp.exp2(x - high) for x in xs]
            if before:
                masses[-1] = masses[-1] * before[1][v, rows, :]
            high_ref[v, rows, :] = high
            mass_ref[v, rows, :] = tree(jnp.add, masses)


def near_tile(k1a_ref, k1b_ref, rows, r):
    if r < RH:
        return k1a_ref[rows, r * 128 : (r + 1) * 128]
    return k1b_ref[rows, (r - RH) * 128 : (r - RH + 1) * 128]


def near_tiles(k1a_ref, k1b_ref):
    return lambda rows: [(r, near_tile(k1a_ref, k1b_ref, rows, r)) for r in range(NEAR)]


def far_tiles(k2_ref):
    return lambda rows: [(r, k2_ref[rows, (r - NEAR) * 128 : (r - NEAR + 1) * 128]) for r in range(NEAR, RI)]


def turned(core, value):
    return jnp.where(core > 0.5, jnp.concatenate([value[RH:RI, :], value[0:RH, :]], axis=0), value)


def lanes_result(count, high_ref, mass_ref):
    results = []
    for v in range(count):
        rows_out = []
        for b in range(RJ):
            high = jnp.transpose(high_ref[v, b * 128 : (b + 1) * 128, :])
            mass = jnp.transpose(mass_ref[v, b * 128 : (b + 1) * 128, :])
            top = jnp.max(high, axis=0, keepdims=True)
            total = jnp.sum(mass * jnp.exp2(high - top), axis=0, keepdims=True)
            rows_out.append((top, total))
        top = jnp.concatenate([row[0] for row in rows_out], axis=0)
        total = jnp.concatenate([row[1] for row in rows_out], axis=0)
        results.append(top + jnp.log(total) * LOG2E)
    return results


def reduce_lanes(k1a_ref, k1b_ref, k2_hbm, k2_ref, sems, heads, high_ref, mass_ref):
    count = len(heads)

    def near(b, carry):
        lanes_block(near_tiles(k1a_ref, k1b_ref), count, heads, high_ref, mass_ref, pl.multiple_of(b * 128, 128))
        return carry

    def far(b, carry):
        fetch(k2_hbm, k2_ref, sems, b).wait()
        start = pl.multiple_of(b * 128, 128)
        lanes_block(far_tiles(k2_ref), count, heads, high_ref, mass_ref, start, (high_ref, mass_ref))
        return carry

    lax.fori_loop(0, RJ, near, 0, unroll=2)
    lax.fori_loop(0, RJ, far, 0, unroll=2)
    return lanes_result(count, high_ref, mass_ref)


def reduce_rows(k1a_ref, k1b_ref, k2_hbm, k2_ref, sems, heads, wide_ref, high_ref, mass_ref):
    count = len(heads)
    for v in range(count):
        for b in range(RJ):
            row = jnp.broadcast_to(heads[v][b : b + 1, :], (128, 128))
            wide_ref[v, b * 128 : (b + 1) * 128, :] = jnp.transpose(row)

    def block(b, wides, tile, r):
        spot = pl.ds(pl.multiple_of(b * 8, 8), 8)
        cols = slice(r * 128, (r + 1) * 128)
        tiles = [tile(pl.ds(b * 128 + group * 8, 8)) for group in range(16)]
        for v in range(count):
            xs = [wides[v][group * 8 : group * 8 + 8, :] - tiles[group] for group in range(16)]
            high = tree(jnp.maximum, xs)
            high_ref[v, spot, cols] = high
            mass_ref[v, spot, cols] = tree(jnp.add, [jnp.exp2(x - high) for x in xs])

    def near(b, carry):
        wides = [wide_ref[v, pl.ds(pl.multiple_of(b * 128, 128), 128), :] for v in range(count)]
        for r in range(NEAR):
            block(b, wides, lambda rows: near_tile(k1a_ref, k1b_ref, rows, r), r)
        return carry

    def far(b, carry):
        fetch(k2_hbm, k2_ref, sems, b).wait()
        wides = [wide_ref[v, pl.ds(pl.multiple_of(b * 128, 128), 128), :] for v in range(count)]
        for r in range(NEAR, RI):
            block(b, wides, lambda rows: k2_ref[rows, (r - NEAR) * 128 : (r - NEAR + 1) * 128], r)
        return carry

    lax.fori_loop(0, RJ, near, 0, unroll=3)
    lax.fori_loop(0, RJ, far, 0, unroll=3)
    results = []
    for v in range(count):
        tops, totals = [], []
        for r in range(RI):
            cols = slice(r * 128, (r + 1) * 128)
            high = high_ref[v, :, cols]
            top = jnp.max(high, axis=0, keepdims=True)
            tops.append(top)
            totals.append(jnp.sum(mass_ref[v, :, cols] * jnp.exp2(high - top), axis=0, keepdims=True))
        results.append(jnp.concatenate(tops, axis=0) + jnp.log(jnp.concatenate(totals, axis=0)) * LOG2E)
    return results


def pack_body(gen, ref, out, both, sems):
    copies = [pltpu.make_async_copy(part, both.at[n], sems.at[n]) for n, part in enumerate((gen, ref))]
    for copy in copies:
        copy.start()
    for copy in copies:
        copy.wait()
    wide = jnp.concatenate([both[0].astype(jnp.float32), both[1].astype(jnp.float32)], axis=0)
    out[...] = jnp.transpose(wide).astype(jnp.bfloat16)


def unpack_body(info, raw, a_out, b_out):
    for k in range(D // 128):
        cols = slice(k * 128, (k + 1) * 128)
        even, odd = raw[2 * k], raw[2 * k + 1]
        gen = jnp.concatenate([even[:, :64], odd[:, :64]], axis=1)
        ref = jnp.concatenate([even[:, 64:], odd[:, 64:]], axis=1)
        a = jnp.where(info[0] == 1, gen, ref)
        b_out[:, cols] = jnp.where(info[1] == 1, gen, ref)
        for n in range(4):
            a_out[n, :, cols] = a


def widen_body(own, a_half, out):
    del a_half
    for n in range(4):
        out[n] = own[...]


def norm_parts(values):
    values = values.astype(jnp.float32)
    values = values * values
    return functools.reduce(jnp.add, [values[:, k * 128 : (k + 1) * 128] for k in range(D // 128)])


def masks(info, gen_count, ref_count, lift_i, lift_j, weights):
    c, x, y = info[2], info[3], info[4]

    def total(counts):
        return jnp.full((8, 128), functools.reduce(jnp.add, [counts[n] for n in range(32)]).astype(jnp.float32))

    def number(is_gen, t):
        return jnp.where(is_gen, gen_count[t], ref_count[t])

    def flat(rows):
        shape = (rows, 128)
        return lax.broadcasted_iota(jnp.int32, shape, 0) * 128 + lax.broadcasted_iota(jnp.int32, shape, 1)

    def valid(spots, starts, counts):
        inside = [(spots >= start) & (spots < start + count) for start, count in zip(starts, counts)]
        return functools.reduce(jnp.logical_or, inside)

    a_is_gen, b_is_gen = info[0] == 1, info[1] == 1
    totals = total(gen_count), total(ref_count)
    gen_log, ref_log = (-jnp.log(value) * LOG2E for value in totals)
    counts = [number(a_is_gen, ((n % 4) * 4 + x) * 2 + (c if n < 4 else 1 - c)) for n in range(8)]
    ok = valid(flat(16), [n * BLOCK for n in range(8)], counts)
    log_a = jnp.where(a_is_gen, gen_log, ref_log)
    lift_i[...] = jnp.where(ok, jnp.concatenate([log_a, log_a], axis=0), FAR)
    core = jnp.full((1, 128), c.astype(jnp.float32))
    lift_i[14:15, :] = core
    lift_i[15:16, :] = jnp.full((1, 128), y.astype(jnp.float32))
    here = [(y * 4 + n) * 2 + c for n in range(4)]
    starts = [n * BLOCK for n in range(4)]
    ok = valid(flat(8), starts, [number(b_is_gen, t) for t in here])
    lift_j[...] = jnp.where(ok, jnp.where(b_is_gen, gen_log, ref_log), FAR)
    lift_j[6:7, :] = core
    shift = 64 * lax.rem(y, 2)
    windows = [n * 256 + shift for n in range(4)]
    for n, counts in enumerate((gen_count, ref_count)):
        ok = valid(flat(8), windows, [counts[t] for t in here])
        weights[n * 8 : n * 8 + 8, :] = jnp.where(ok, 1.0 / totals[n], 0.0)
    ok = valid(flat(8), starts, [ref_count[t] for t in here])
    weights[16:24, :] = jnp.where(ok, 1.0 / totals[1], 0.0)
    weights[22:23, :] = jnp.full((1, 128), x.astype(jnp.float32))
    weights[23:24, :] = jnp.full((1, 128), lax.rem(y, 2).astype(jnp.float32))


def a_norms(a_ref):
    rows = []
    for s in range(RH):
        flipped = jnp.transpose(norm_parts(a_ref[s * 128 : (s + 1) * 128, :]))
        rows.append(jnp.sum(flipped, axis=0, keepdims=True) * (0.5 * LOG2E / EPSILON))
    return rows


def cost_tiles(a_ref, b_ref, sq_ref, norms, n):
    inner = lax.dot_general(
        b_ref[...],
        a_ref[n * 256 : (n + 1) * 256, :],
        (((1,), (1,)), ((), ())),
        preferred_element_type=jnp.float32,
    )
    scale = LOG2E / EPSILON
    return [(sq_ref[...] + norms[2 * n + s]) - scale * inner[:, s * 128 : (s + 1) * 128] for s in range(2)]


def reduce_pair(head, source, at, high_ref, mass_ref, base, before):
    heads = [head[base : base + 2, :]]
    pair = lambda rows: [(s, source[rows, at + s * 128 : at + (s + 1) * 128]) for s in range(2)]
    for b in range(RJ):
        lanes_block(pair, 1, heads, high_ref, mass_ref, b * 128, before)


def cost_own_body(
    info, gen_count, ref_count, a_ref, b_ref, k1a_ref, high_ref, mass_ref, sq_ref, lift_i, lift_j, weights
):
    masks(info, gen_count, ref_count, lift_i, lift_j, weights)
    head = lift_i[...]
    norms = a_norms(a_ref)
    for b in range(RJ):
        part = slice(b * 128, (b + 1) * 128)
        total = jnp.sum(norm_parts(b_ref[part, :]), axis=1, keepdims=True) * (0.5 * LOG2E / EPSILON)
        sq_ref[part, :] = jnp.broadcast_to(total, (128, 128))
    for n in range(4):
        if n < 3:
            for s, tile in enumerate(cost_tiles(a_ref, b_ref, sq_ref, norms, n)):
                k1a_ref[:, (2 * n + s) * 128 : (2 * n + s + 1) * 128] = tile
        if n > 0:
            before = (high_ref, mass_ref) if n > 1 else None
            reduce_pair(head, k1a_ref, (n - 1) * 256, high_ref, mass_ref, 2 * n - 2, before)


def cost_other_body(
    a_ref, b_ref, lift_i, high_in, mass_in, sq_ref, k1b_ref, k2_hbm, part_out, k2_ref, high_ref, mass_ref, out_sems
):
    head = lift_i[...]
    norms = a_norms(a_ref)
    stores = [fetch(k2_ref, k2_hbm, out_sems, b) for b in range(RJ)]
    order = [1, 2, 0]
    for step in range(4):
        if step < 3:
            n = order[step]
            target, at = (k1b_ref, 0) if n == 0 else (k2_ref, (n - 1) * 256)
            for s, tile in enumerate(cost_tiles(a_ref, b_ref, sq_ref, norms, n)):
                target[:, at + s * 128 : at + (s + 1) * 128] = tile
        if step > 0:
            n = order[step - 1]
            source, at = (k1b_ref, 0) if n == 0 else (k2_ref, (n - 1) * 256)
            before = (high_ref, mass_ref) if step > 1 else (high_in, mass_in)
            reduce_pair(head, source, at, high_ref, mass_ref, RH + 2 * n, before)
        if step == 1:
            for store in stores:
                store.start()
    (result,) = lanes_result(1, high_ref, mass_ref)
    for n in range(4):
        part_out[n, 0:RJ, :] = result
        part_out[n, RJ:8, :] = jnp.zeros((8 - RJ, 128), jnp.float32)
    for store in stores:
        store.wait()


def second_body(k1a_ref, k1b_ref, k2_hbm, got, lift_j, out, g1_out, k2_ref, sems, wide_ref, high_ref, mass_ref):
    core = lift_j[6:7, :]
    start_fetch(k2_hbm, k2_ref, sems)
    g1 = -merge(got, 4)[0:RJ, :]
    g1_out[...] = g1
    lift = lift_j[0:RJ, :]
    heads = [lift, lifted(g1, lift)]
    results = reduce_rows(k1a_ref, k1b_ref, k2_hbm, k2_ref, sems, heads, wide_ref, high_ref, mass_ref)
    sent = [turned(core, value) for value in results]
    for n in range(8):
        for v in range(2):
            out[n, v * RI : (v + 1) * RI, :] = sent[v]


def third_body(k1a_ref, k1b_ref, k2_hbm, got, lift_i, out, f2_out, k2_ref, sems, high_ref, mass_ref):
    core = lift_i[14:15, :]
    start_fetch(k2_hbm, k2_ref, sems)
    merged = -merge(got, 8)
    f1 = turned(core, merged[0:RI, :])
    f2 = 0.5 * (f1 + turned(core, merged[RI : 2 * RI, :]))
    f2_out[...] = f2
    lift = lift_i[0:RI, :]
    heads = [lifted(f1, lift), lifted(f2, lift)]
    results = reduce_lanes(k1a_ref, k1b_ref, k2_hbm, k2_ref, sems, heads, high_ref, mass_ref)
    for n in range(4):
        for v in range(2):
            out[n, v * 8 : v * 8 + RJ, :] = results[v]
            out[n, v * 8 + RJ : v * 8 + 8, :] = jnp.zeros((8 - RJ, 128), jnp.float32)


def fourth_body(k1a_ref, k1b_ref, k2_hbm, got, lift_j, g1, out, g3_out, k2_ref, sems, wide_ref, high_ref, mass_ref):
    core = lift_j[6:7, :]
    start_fetch(k2_hbm, k2_ref, sems)
    merged = -merge(got, 4)
    g2 = 0.5 * (g1[...] + merged[0:RJ, :])
    g3 = 0.5 * (g2 + merged[8 : 8 + RJ, :])
    g3_out[...] = g3
    lift = lift_j[0:RJ, :]
    heads = [lifted(g2, lift), lifted(g3, lift)]
    results = reduce_rows(k1a_ref, k1b_ref, k2_hbm, k2_ref, sems, heads, wide_ref, high_ref, mass_ref)
    sent = [turned(core, value) for value in results]
    for n in range(8):
        for v in range(2):
            out[n, v * RI : (v + 1) * RI, :] = sent[v]


def fifth_body(k1a_ref, k1b_ref, k2_hbm, got, lift_i, f2, g3, out, k2_ref, sems, high_ref, mass_ref):
    core = lift_i[14:15, :]
    start_fetch(k2_hbm, k2_ref, sems)
    merged = -merge(got, 8)
    f3 = 0.5 * (f2[...] + turned(core, merged[0:RI, :]))
    f4 = 0.5 * (f3 + turned(core, merged[RI : 2 * RI, :]))
    heads = [lifted(f3, lift_i[0:RI, :])]
    (result,) = reduce_lanes(k1a_ref, k1b_ref, k2_hbm, k2_ref, sems, heads, high_ref, mass_ref)
    shifted = result - g3[...]
    along_y = lift_i[15:16, :]
    mine = f4[4:6, :]
    for n, row in ((2, 3), (1, 1), (0, 0)):
        mine = jnp.where(along_y < n + 0.5, f4[row : row + 2, :], mine)
    for n in range(16):
        out[n, 0:RJ, :] = shifted
        out[n, RJ : RJ + 2, :] = mine


def last_body(got, weights, gen_pot, ref_pot, gen_self, ref_self, share):
    g4 = merge([got[n * 4 + 1, 0:RJ, :] for n in range(4)], 4) * (-0.5 * LN2)
    weight = weights[16 : 16 + RJ, :]
    total = jnp.sum(jnp.where(weight > 0.0, g4 * weight, 0.0))
    own = [[got[n * 4 + plane, RJ : RJ + 2, :] * LN2 for n in range(4)] for plane in (1, 0, 3)]
    for n in range(4):
        weight = weights[2 * n : 2 * n + 2, :]
        total += jnp.sum(jnp.where(weight > 0.0, (own[0][n] - own[1][n]) * weight, 0.0))
        weight = weights[8 + 2 * n : 8 + 2 * n + 2, :]
        total -= jnp.sum(jnp.where(weight > 0.0, own[2][n] * weight, 0.0))
    for n in range(8):
        share[n, :, :] = jnp.full((8, 128), total, jnp.float32)

    along_x, odd_y = weights[22:23, :], weights[23:24, :]
    low = lax.broadcasted_iota(jnp.int32, (1, 128), 1) < 64

    def chosen(rows):
        result = rows[0]
        for n in range(1, 4):
            result = jnp.where(along_x > n - 0.5, rows[n], result)
        return result

    def write(out, window, late):
        rolled = jnp.concatenate([window[:, 64:], window[:, :64]], axis=1)
        first = jnp.where(late, jnp.where(low, rolled[0:1, :], rolled[1:2, :]), window[0:1, :])
        second = jnp.where(late, rolled[1:2, :], window[1:2, :])
        out[0:1, 0:128] = first
        out[0:1, 128:192] = second[:, 0:64]

    for out, rows in zip((gen_pot, gen_self, ref_self), own):
        write(out, chosen(rows), odd_y > 0.5)
    odd_x = ((along_x > 0.5) & (along_x < 1.5)) | (along_x > 2.5)
    write(ref_pot, chosen([g4[row : row + 2, :] for row in (0, 1, 3, 4)]), odd_x)


F32 = jnp.float32
BF16 = jnp.bfloat16
STREAM = [pltpu.VMEM((NJ, N2), F32), pltpu.SemaphoreType.DMA((RJ,))]


def lane_scratch(count):
    return [pltpu.VMEM((count, NJ, 128), F32)] * 2


def row_scratch(count):
    return [pltpu.VMEM((count, NJ, 128), F32)] + [pltpu.VMEM((count, 8 * RJ, NI), F32)] * 2


def stage_pack(*args):
    scratch = [pltpu.VMEM((2, 64, BLOCK), BF16), pltpu.SemaphoreType.DMA((2,))]
    out = jax.ShapeDtypeStruct((BLOCK, 128), BF16)
    return call(pack_body, out, [HBM, HBM], scratch, mib=60)(*args)


def bf16(*shape):
    return jax.ShapeDtypeStruct(shape, BF16)


def stage_unpack(*args):
    return call(unpack_body, (bf16(4, BLOCK, D), bf16(BLOCK, D)), [SMEM, VMEM])(*args)


def stage_widen(*args):
    return call(widen_body, bf16(4, BLOCK, D), [VMEM, HBM])(*args)


def stage_cost_own(*args):
    outs = (f32(NJ, NI // 2), f32(1, NJ, 128), f32(1, NJ, 128), f32(NJ, 128))
    outs += (f32(16, 128), f32(8, 128), f32(24, 128))
    return call(cost_own_body, outs, [SMEM] * 3 + [VMEM] * 2)(*args)


def stage_cost_other(*args):
    scratch = [pltpu.VMEM((NJ, N2), F32), *lane_scratch(1), pltpu.SemaphoreType.DMA((RJ,))]
    outs = (f32(NJ, NI // 2 - N2), f32(ROOM, N2), f32(4, 8, 128))
    return call(cost_other_body, outs, [VMEM] * 6, scratch, (VMEM, HBM, VMEM))(*args)


K_SPECS = [VMEM, VMEM, HBM]


def stage_second(*args):
    outs = (f32(8, 2 * RI, 128), f32(RJ, 128))
    return call(second_body, outs, K_SPECS + [VMEM] * 2, STREAM + row_scratch(2))(*args)


def stage_third(*args):
    outs = (f32(4, 16, 128), f32(RI, 128))
    return call(third_body, outs, K_SPECS + [VMEM] * 2, STREAM + lane_scratch(2))(*args)


def stage_fourth(*args):
    outs = (f32(8, 2 * RI, 128), f32(RJ, 128))
    return call(fourth_body, outs, K_SPECS + [VMEM] * 3, STREAM + row_scratch(2))(*args)


def stage_fifth(*args):
    return call(fifth_body, f32(16, 8, 128), K_SPECS + [VMEM] * 4, STREAM + lane_scratch(1))(*args)


def spread(operand, axes):
    return lax.all_to_all(operand, axes, 0, 0, tiled=True)


def local(gen_points, reference_embeddings, gen_count, ref_count):
    y, x, c, zl = (lax.axis_index(name) for name in ("y", "x", "c", "zl"))
    a_is_gen = zl < 3
    b_is_gen = zl == 0
    packed = stage_pack(jnp.transpose(gen_points), jnp.transpose(reference_embeddings))
    raw = lax.all_gather(packed, ("zh", "zl"))

    info = jnp.stack(
        [
            a_is_gen.astype(jnp.int32),
            b_is_gen.astype(jnp.int32),
            c,
            x,
            y,
        ]
    ).astype(jnp.int32)
    a_wide, b_own = stage_unpack(info, raw)
    one = spread(a_wide, "y")
    two = spread(stage_widen(b_own, one), "x")
    a_own, b_all = lax.optimization_barrier((one.reshape(NJ, D), two.reshape(NJ, D)))
    a_other = lax.ppermute(a_own, "c", [(0, 1), (1, 0)])
    k1a, high, mass, b_norms, lift_i, lift_j, weights = stage_cost_own(
        info, gen_count, ref_count, a_own, b_all
    )
    k1b, k2, part = stage_cost_other(a_other, b_all, lift_i, high, mass, b_norms)
    k = (k1a, k1b, k2)
    part, g1 = stage_second(*k, spread(part, "x"), lift_j)
    part, f2 = stage_third(*k, spread(part, ("y", "c")), lift_i)
    part, g3 = stage_fourth(*k, spread(part, "x"), lift_j, g1)
    part = stage_fifth(*k, spread(part, ("y", "c")), lift_i, f2, g3)
    got = spread(part, ("x", "zl"))
    outs = (f32(1, BLOCK),) * 4 + (f32(8, 8, 128),)
    *pots, share = call(last_body, outs, [VMEM, VMEM])(got, weights)
    divergence = jnp.sum(spread(share, ("y", "c"))[:, 0, 0])
    return *(pot.reshape(BLOCK) for pot in pots), divergence


def solution(mesh):
    fine = Mesh(mesh.devices.reshape(4, 4, 2, 4, 4), ("y", "x", "c", "zh", "zl"))
    tile, feat = ("y", "x", "c"), ("zh", "zl")
    return jax.shard_map(
        local,
        mesh=fine,
        in_specs=(P(tile, feat), P(tile, feat), P(), P()),
        out_specs=(P(tile), P(tile), P(tile), P(tile), P()),
        check_vma=False,
    )
```

```python
import functools

import jax
import jax.numpy as jnp
from jax import lax
from jax.experimental import pallas as pl
from jax.experimental.pallas import tpu as pltpu
from jax.sharding import Mesh, PartitionSpec as P

EPSILON = 0.25
LOG2E = 1.4426950408889634
LN2 = 0.6931471805599453
FAR = -1.0e30

BLOCK = 192
D = 1024
NI = 8 * BLOCK
NJ = 4 * BLOCK
RI = NI // 128
RH = RI // 2
RJ = NJ // 128
NEAR = 8
N2 = NI - NEAR * 128
ROOM = 18 * NJ

VMEM = pl.BlockSpec(memory_space=pltpu.VMEM)
HBM = pl.BlockSpec(memory_space=pltpu.HBM)
SMEM = pl.BlockSpec(memory_space=pltpu.SMEM)


def f32(*shape):
    return jax.ShapeDtypeStruct(shape, jnp.float32)


def call(body, outs, ins, scratch=(), out_specs=None, mib=40):
    return pl.pallas_call(
        body,
        out_shape=outs,
        in_specs=ins,
        out_specs=jax.tree.map(lambda _: VMEM, outs) if out_specs is None else out_specs,
        scratch_shapes=list(scratch),
        compiler_params=pltpu.CompilerParams(vmem_limit_bytes=mib * 1024 * 1024),
    )


def merge(got, count):
    parts = [got[n] for n in range(count)]
    high = functools.reduce(jnp.maximum, parts)
    mass = functools.reduce(jnp.add, [jnp.exp2(part - high) for part in parts])
    return high + jnp.log(mass) * LOG2E


def lifted(pot, lift):
    return jnp.where(lift > -1.0e29, pot + lift, FAR)


def tree(op, values):
    values = list(values)
    while len(values) > 1:
        values = [op(*values[n : n + 2]) if n + 1 < len(values) else values[n] for n in range(0, len(values), 2)]
    return values[0]


def fetch(k2_hbm, k2_ref, sems, b):
    rows = pl.ds(b * 128, 128)
    return pltpu.make_async_copy(k2_hbm.at[rows], k2_ref.at[rows], sems.at[b])


def start_fetch(k2_hbm, k2_ref, sems):
    for b in range(RJ):
        fetch(k2_hbm, k2_ref, sems, b).start()


def lanes_block(tiles_of, count, heads, high_ref, mass_ref, base, before=None):
    for group in range(16):
        rows = pl.ds(base + group * 8, 8)
        tiles = tiles_of(rows)
        for v in range(count):
            xs = [heads[v][r : r + 1, :] - tile for r, tile in tiles]
            high = tree(jnp.maximum, xs)
            if before:
                above = before[0][v, rows, :]
                high = jnp.maximum(high, above)
                xs.append(above)
            masses = [jnp.exp2(x - high) for x in xs]
            if before:
                masses[-1] = masses[-1] * before[1][v, rows, :]
            high_ref[v, rows, :] = high
            mass_ref[v, rows, :] = tree(jnp.add, masses)


def near_tile(k1a_ref, k1b_ref, rows, r):
    if r < RH:
        return k1a_ref[rows, r * 128 : (r + 1) * 128]
    return k1b_ref[rows, (r - RH) * 128 : (r - RH + 1) * 128]


def near_tiles(k1a_ref, k1b_ref):
    return lambda rows: [(r, near_tile(k1a_ref, k1b_ref, rows, r)) for r in range(NEAR)]


def far_tiles(k2_ref):
    return lambda rows: [(r, k2_ref[rows, (r - NEAR) * 128 : (r - NEAR + 1) * 128]) for r in range(NEAR, RI)]


def turned(core, value):
    return jnp.where(core > 0.5, jnp.concatenate([value[RH:RI, :], value[0:RH, :]], axis=0), value)


def lanes_result(count, high_ref, mass_ref):
    results = []
    for v in range(count):
        rows_out = []
        for b in range(RJ):
            high = jnp.transpose(high_ref[v, b * 128 : (b + 1) * 128, :])
            mass = jnp.transpose(mass_ref[v, b * 128 : (b + 1) * 128, :])
            top = jnp.max(high, axis=0, keepdims=True)
            total = jnp.sum(mass * jnp.exp2(high - top), axis=0, keepdims=True)
            rows_out.append((top, total))
        top = jnp.concatenate([row[0] for row in rows_out], axis=0)
        total = jnp.concatenate([row[1] for row in rows_out], axis=0)
        results.append(top + jnp.log(total) * LOG2E)
    return results


def reduce_lanes(k1a_ref, k1b_ref, k2_hbm, k2_ref, sems, heads, high_ref, mass_ref):
    count = len(heads)

    def near(b, carry):
        lanes_block(near_tiles(k1a_ref, k1b_ref), count, heads, high_ref, mass_ref, pl.multiple_of(b * 128, 128))
        return carry

    def far(b, carry):
        fetch(k2_hbm, k2_ref, sems, b).wait()
        start = pl.multiple_of(b * 128, 128)
        lanes_block(far_tiles(k2_ref), count, heads, high_ref, mass_ref, start, (high_ref, mass_ref))
        return carry

    lax.fori_loop(0, RJ, near, 0, unroll=2)
    lax.fori_loop(0, RJ, far, 0, unroll=2)
    return lanes_result(count, high_ref, mass_ref)


def reduce_rows(k1a_ref, k1b_ref, k2_hbm, k2_ref, sems, heads, wide_ref, high_ref, mass_ref):
    count = len(heads)
    for v in range(count):
        for b in range(RJ):
            row = jnp.broadcast_to(heads[v][b : b + 1, :], (128, 128))
            wide_ref[v, b * 128 : (b + 1) * 128, :] = jnp.transpose(row)

    def block(b, wides, tile, r):
        spot = pl.ds(pl.multiple_of(b * 8, 8), 8)
        cols = slice(r * 128, (r + 1) * 128)
        tiles = [tile(pl.ds(b * 128 + group * 8, 8)) for group in range(16)]
        for v in range(count):
            xs = [wides[v][group * 8 : group * 8 + 8, :] - tiles[group] for group in range(16)]
            high = tree(jnp.maximum, xs)
            high_ref[v, spot, cols] = high
            mass_ref[v, spot, cols] = tree(jnp.add, [jnp.exp2(x - high) for x in xs])

    def near(b, carry):
        wides = [wide_ref[v, pl.ds(pl.multiple_of(b * 128, 128), 128), :] for v in range(count)]
        for r in range(NEAR):
            block(b, wides, lambda rows: near_tile(k1a_ref, k1b_ref, rows, r), r)
        return carry

    def far(b, carry):
        fetch(k2_hbm, k2_ref, sems, b).wait()
        wides = [wide_ref[v, pl.ds(pl.multiple_of(b * 128, 128), 128), :] for v in range(count)]
        for r in range(NEAR, RI):
            block(b, wides, lambda rows: k2_ref[rows, (r - NEAR) * 128 : (r - NEAR + 1) * 128], r)
        return carry

    lax.fori_loop(0, RJ, near, 0, unroll=2)
    lax.fori_loop(0, RJ, far, 0, unroll=2)
    results = []
    for v in range(count):
        tops, totals = [], []
        for r in range(RI):
            cols = slice(r * 128, (r + 1) * 128)
            high = high_ref[v, :, cols]
            top = jnp.max(high, axis=0, keepdims=True)
            tops.append(top)
            totals.append(jnp.sum(mass_ref[v, :, cols] * jnp.exp2(high - top), axis=0, keepdims=True))
        results.append(jnp.concatenate(tops, axis=0) + jnp.log(jnp.concatenate(totals, axis=0)) * LOG2E)
    return results


def pack_body(gen, ref, out, both, sems):
    copies = [pltpu.make_async_copy(part, both.at[n], sems.at[n]) for n, part in enumerate((gen, ref))]
    for copy in copies:
        copy.start()
    for copy in copies:
        copy.wait()
    wide = jnp.concatenate([both[0].astype(jnp.float32), both[1].astype(jnp.float32)], axis=0)
    out[...] = jnp.transpose(wide).astype(jnp.bfloat16)


def unpack_body(info, raw, a_out, b_out):
    for k in range(D // 128):
        cols = slice(k * 128, (k + 1) * 128)
        even, odd = raw[2 * k], raw[2 * k + 1]
        gen = jnp.concatenate([even[:, :64], odd[:, :64]], axis=1)
        ref = jnp.concatenate([even[:, 64:], odd[:, 64:]], axis=1)
        a = jnp.where(info[0] == 1, gen, ref)
        b_out[:, cols] = jnp.where(info[1] == 1, gen, ref)
        for n in range(4):
            a_out[n, :, cols] = a


def widen_body(own, a_half, out):
    del a_half
    for n in range(4):
        out[n] = own[...]


def norm_parts(values):
    values = values.astype(jnp.float32)
    values = values * values
    return functools.reduce(jnp.add, [values[:, k * 128 : (k + 1) * 128] for k in range(D // 128)])


def masks(info, gen_count, ref_count, lift_i, lift_j, weights):
    c, x, y = info[2], info[3], info[4]

    def total(counts):
        return jnp.full((8, 128), functools.reduce(jnp.add, [counts[n] for n in range(32)]).astype(jnp.float32))

    def number(is_gen, t):
        return jnp.where(is_gen, gen_count[t], ref_count[t])

    def flat(rows):
        shape = (rows, 128)
        return lax.broadcasted_iota(jnp.int32, shape, 0) * 128 + lax.broadcasted_iota(jnp.int32, shape, 1)

    def valid(spots, starts, counts):
        inside = [(spots >= start) & (spots < start + count) for start, count in zip(starts, counts)]
        return functools.reduce(jnp.logical_or, inside)

    a_is_gen, b_is_gen = info[0] == 1, info[1] == 1
    totals = total(gen_count), total(ref_count)
    gen_log, ref_log = (-jnp.log(value) * LOG2E for value in totals)
    counts = [number(a_is_gen, ((n % 4) * 4 + x) * 2 + (c if n < 4 else 1 - c)) for n in range(8)]
    ok = valid(flat(16), [n * BLOCK for n in range(8)], counts)
    log_a = jnp.where(a_is_gen, gen_log, ref_log)
    lift_i[...] = jnp.where(ok, jnp.concatenate([log_a, log_a], axis=0), FAR)
    core = jnp.full((1, 128), c.astype(jnp.float32))
    lift_i[14:15, :] = core
    lift_i[15:16, :] = jnp.full((1, 128), y.astype(jnp.float32))
    here = [(y * 4 + n) * 2 + c for n in range(4)]
    starts = [n * BLOCK for n in range(4)]
    ok = valid(flat(8), starts, [number(b_is_gen, t) for t in here])
    lift_j[...] = jnp.where(ok, jnp.where(b_is_gen, gen_log, ref_log), FAR)
    lift_j[6:7, :] = core
    shift = 64 * lax.rem(y, 2)
    windows = [n * 256 + shift for n in range(4)]
    for n, counts in enumerate((gen_count, ref_count)):
        ok = valid(flat(8), windows, [counts[t] for t in here])
        weights[n * 8 : n * 8 + 8, :] = jnp.where(ok, 1.0 / totals[n], 0.0)
    ok = valid(flat(8), starts, [ref_count[t] for t in here])
    weights[16:24, :] = jnp.where(ok, 1.0 / totals[1], 0.0)
    weights[22:23, :] = jnp.full((1, 128), x.astype(jnp.float32))
    weights[23:24, :] = jnp.full((1, 128), lax.rem(y, 2).astype(jnp.float32))


def a_norms(a_ref):
    rows = []
    for s in range(RH):
        flipped = jnp.transpose(norm_parts(a_ref[s * 128 : (s + 1) * 128, :]))
        rows.append(jnp.sum(flipped, axis=0, keepdims=True) * (0.5 * LOG2E / EPSILON))
    return rows


def cost_tiles(a_ref, b_ref, sq_ref, norms, n):
    inner = lax.dot_general(
        b_ref[...],
        a_ref[n * 256 : (n + 1) * 256, :],
        (((1,), (1,)), ((), ())),
        preferred_element_type=jnp.float32,
    )
    scale = LOG2E / EPSILON
    return [(sq_ref[...] + norms[2 * n + s]) - scale * inner[:, s * 128 : (s + 1) * 128] for s in range(2)]


def reduce_pair(head, source, at, high_ref, mass_ref, base, before):
    heads = [head[base : base + 2, :]]
    pair = lambda rows: [(s, source[rows, at + s * 128 : at + (s + 1) * 128]) for s in range(2)]
    for b in range(RJ):
        lanes_block(pair, 1, heads, high_ref, mass_ref, b * 128, before)


def cost_own_body(
    info, gen_count, ref_count, a_ref, b_ref, k1a_ref, high_ref, mass_ref, sq_ref, lift_i, lift_j, weights
):
    masks(info, gen_count, ref_count, lift_i, lift_j, weights)
    head = lift_i[...]
    norms = a_norms(a_ref)
    for b in range(RJ):
        part = slice(b * 128, (b + 1) * 128)
        total = jnp.sum(norm_parts(b_ref[part, :]), axis=1, keepdims=True) * (0.5 * LOG2E / EPSILON)
        sq_ref[part, :] = jnp.broadcast_to(total, (128, 128))
    for n in range(4):
        if n < 3:
            for s, tile in enumerate(cost_tiles(a_ref, b_ref, sq_ref, norms, n)):
                k1a_ref[:, (2 * n + s) * 128 : (2 * n + s + 1) * 128] = tile
        if n > 0:
            before = (high_ref, mass_ref) if n > 1 else None
            reduce_pair(head, k1a_ref, (n - 1) * 256, high_ref, mass_ref, 2 * n - 2, before)


def cost_other_body(
    a_ref, b_ref, lift_i, high_in, mass_in, sq_ref, k1b_ref, k2_hbm, part_out, k2_ref, high_ref, mass_ref, out_sems
):
    head = lift_i[...]
    norms = a_norms(a_ref)
    stores = [fetch(k2_ref, k2_hbm, out_sems, b) for b in range(RJ)]
    order = [1, 2, 0]
    for step in range(4):
        if step < 3:
            n = order[step]
            target, at = (k1b_ref, 0) if n == 0 else (k2_ref, (n - 1) * 256)
            for s, tile in enumerate(cost_tiles(a_ref, b_ref, sq_ref, norms, n)):
                target[:, at + s * 128 : at + (s + 1) * 128] = tile
        if step > 0:
            n = order[step - 1]
            source, at = (k1b_ref, 0) if n == 0 else (k2_ref, (n - 1) * 256)
            before = (high_ref, mass_ref) if step > 1 else (high_in, mass_in)
            reduce_pair(head, source, at, high_ref, mass_ref, RH + 2 * n, before)
        if step == 1:
            for store in stores:
                store.start()
    (result,) = lanes_result(1, high_ref, mass_ref)
    for n in range(4):
        part_out[n, 0:RJ, :] = result
        part_out[n, RJ:8, :] = jnp.zeros((8 - RJ, 128), jnp.float32)
    for store in stores:
        store.wait()


def second_body(k1a_ref, k1b_ref, k2_hbm, got, lift_j, out, g1_out, k2_ref, sems, wide_ref, high_ref, mass_ref):
    core = lift_j[6:7, :]
    start_fetch(k2_hbm, k2_ref, sems)
    g1 = -merge(got, 4)[0:RJ, :]
    g1_out[...] = g1
    lift = lift_j[0:RJ, :]
    heads = [lift, lifted(g1, lift)]
    results = reduce_rows(k1a_ref, k1b_ref, k2_hbm, k2_ref, sems, heads, wide_ref, high_ref, mass_ref)
    sent = [turned(core, value) for value in results]
    for n in range(8):
        for v in range(2):
            out[n, v * RI : (v + 1) * RI, :] = sent[v]


def third_body(k1a_ref, k1b_ref, k2_hbm, got, lift_i, out, f2_out, k2_ref, sems, high_ref, mass_ref):
    core = lift_i[14:15, :]
    start_fetch(k2_hbm, k2_ref, sems)
    merged = -merge(got, 8)
    f1 = turned(core, merged[0:RI, :])
    f2 = 0.5 * (f1 + turned(core, merged[RI : 2 * RI, :]))
    f2_out[...] = f2
    lift = lift_i[0:RI, :]
    heads = [lifted(f1, lift), lifted(f2, lift)]
    results = reduce_lanes(k1a_ref, k1b_ref, k2_hbm, k2_ref, sems, heads, high_ref, mass_ref)
    for n in range(4):
        for v in range(2):
            out[n, v * 8 : v * 8 + RJ, :] = results[v]
            out[n, v * 8 + RJ : v * 8 + 8, :] = jnp.zeros((8 - RJ, 128), jnp.float32)


def fourth_body(k1a_ref, k1b_ref, k2_hbm, got, lift_j, g1, out, g3_out, k2_ref, sems, wide_ref, high_ref, mass_ref):
    core = lift_j[6:7, :]
    start_fetch(k2_hbm, k2_ref, sems)
    merged = -merge(got, 4)
    g2 = 0.5 * (g1[...] + merged[0:RJ, :])
    g3 = 0.5 * (g2 + merged[8 : 8 + RJ, :])
    g3_out[...] = g3
    lift = lift_j[0:RJ, :]
    heads = [lifted(g2, lift), lifted(g3, lift)]
    results = reduce_rows(k1a_ref, k1b_ref, k2_hbm, k2_ref, sems, heads, wide_ref, high_ref, mass_ref)
    sent = [turned(core, value) for value in results]
    for n in range(8):
        for v in range(2):
            out[n, v * RI : (v + 1) * RI, :] = sent[v]


def fifth_body(k1a_ref, k1b_ref, k2_hbm, got, lift_i, f2, g3, out, k2_ref, sems, high_ref, mass_ref):
    core = lift_i[14:15, :]
    start_fetch(k2_hbm, k2_ref, sems)
    merged = -merge(got, 8)
    f3 = 0.5 * (f2[...] + turned(core, merged[0:RI, :]))
    f4 = 0.5 * (f3 + turned(core, merged[RI : 2 * RI, :]))
    heads = [lifted(f3, lift_i[0:RI, :])]
    (result,) = reduce_lanes(k1a_ref, k1b_ref, k2_hbm, k2_ref, sems, heads, high_ref, mass_ref)
    shifted = result - g3[...]
    along_y = lift_i[15:16, :]
    mine = f4[4:6, :]
    for n, row in ((2, 3), (1, 1), (0, 0)):
        mine = jnp.where(along_y < n + 0.5, f4[row : row + 2, :], mine)
    for n in range(16):
        out[n, 0:RJ, :] = shifted
        out[n, RJ : RJ + 2, :] = mine


def last_body(got, weights, gen_pot, ref_pot, gen_self, ref_self, share):
    g4 = merge([got[n * 4 + 1, 0:RJ, :] for n in range(4)], 4) * (-0.5 * LN2)
    weight = weights[16 : 16 + RJ, :]
    total = jnp.sum(jnp.where(weight > 0.0, g4 * weight, 0.0))
    own = [[got[n * 4 + plane, RJ : RJ + 2, :] * LN2 for n in range(4)] for plane in (1, 0, 3)]
    for n in range(4):
        weight = weights[2 * n : 2 * n + 2, :]
        total += jnp.sum(jnp.where(weight > 0.0, (own[0][n] - own[1][n]) * weight, 0.0))
        weight = weights[8 + 2 * n : 8 + 2 * n + 2, :]
        total -= jnp.sum(jnp.where(weight > 0.0, own[2][n] * weight, 0.0))
    for n in range(8):
        share[n, :, :] = jnp.full((1, 128), total, jnp.float32)

    along_x, odd_y = weights[22:23, :], weights[23:24, :]
    low = lax.broadcasted_iota(jnp.int32, (1, 128), 1) < 64

    def chosen(rows):
        result = rows[0]
        for n in range(1, 4):
            result = jnp.where(along_x > n - 0.5, rows[n], result)
        return result

    def write(out, window, late):
        rolled = jnp.concatenate([window[:, 64:], window[:, :64]], axis=1)
        first = jnp.where(late, jnp.where(low, rolled[0:1, :], rolled[1:2, :]), window[0:1, :])
        second = jnp.where(late, rolled[1:2, :], window[1:2, :])
        out[0:1, 0:128] = first
        out[0:1, 128:192] = second[:, 0:64]

    for out, rows in zip((gen_pot, gen_self, ref_self), own):
        write(out, chosen(rows), odd_y > 0.5)
    odd_x = ((along_x > 0.5) & (along_x < 1.5)) | (along_x > 2.5)
    write(ref_pot, chosen([g4[row : row + 2, :] for row in (0, 1, 3, 4)]), odd_x)


F32 = jnp.float32
BF16 = jnp.bfloat16
STREAM = [pltpu.VMEM((NJ, N2), F32), pltpu.SemaphoreType.DMA((RJ,))]


def lane_scratch(count):
    return [pltpu.VMEM((count, NJ, 128), F32)] * 2


def row_scratch(count):
    return [pltpu.VMEM((count, NJ, 128), F32)] + [pltpu.VMEM((count, 8 * RJ, NI), F32)] * 2


def stage_pack(*args):
    scratch = [pltpu.VMEM((2, 64, BLOCK), BF16), pltpu.SemaphoreType.DMA((2,))]
    out = jax.ShapeDtypeStruct((BLOCK, 128), BF16)
    return call(pack_body, out, [HBM, HBM], scratch, mib=60)(*args)


def bf16(*shape):
    return jax.ShapeDtypeStruct(shape, BF16)


def stage_unpack(*args):
    return call(unpack_body, (bf16(4, BLOCK, D), bf16(BLOCK, D)), [SMEM, VMEM])(*args)


def stage_widen(*args):
    return call(widen_body, bf16(4, BLOCK, D), [VMEM, HBM])(*args)


def stage_cost_own(*args):
    outs = (f32(NJ, NI // 2), f32(1, NJ, 128), f32(1, NJ, 128), f32(NJ, 128))
    outs += (f32(16, 128), f32(8, 128), f32(24, 128))
    return call(cost_own_body, outs, [SMEM] * 3 + [VMEM] * 2)(*args)


def stage_cost_other(*args):
    scratch = [pltpu.VMEM((NJ, N2), F32), *lane_scratch(1), pltpu.SemaphoreType.DMA((RJ,))]
    outs = (f32(NJ, NI // 2 - N2), f32(ROOM, N2), f32(4, 8, 128))
    return call(cost_other_body, outs, [VMEM] * 6, scratch, (VMEM, HBM, VMEM))(*args)


K_SPECS = [VMEM, VMEM, HBM]


def stage_second(*args):
    outs = (f32(8, 2 * RI, 128), f32(RJ, 128))
    return call(second_body, outs, K_SPECS + [VMEM] * 2, STREAM + row_scratch(2))(*args)


def stage_third(*args):
    outs = (f32(4, 16, 128), f32(RI, 128))
    return call(third_body, outs, K_SPECS + [VMEM] * 2, STREAM + lane_scratch(2))(*args)


def stage_fourth(*args):
    outs = (f32(8, 2 * RI, 128), f32(RJ, 128))
    return call(fourth_body, outs, K_SPECS + [VMEM] * 3, STREAM + row_scratch(2))(*args)


def stage_fifth(*args):
    return call(fifth_body, f32(16, 8, 128), K_SPECS + [VMEM] * 4, STREAM + lane_scratch(1))(*args)


def spread(operand, axes):
    return lax.all_to_all(operand, axes, 0, 0, tiled=True)


def local(gen_points, reference_embeddings, gen_count, ref_count):
    y, x, c, zl = (lax.axis_index(name) for name in ("y", "x", "c", "zl"))
    a_is_gen = zl < 3
    b_is_gen = zl == 0
    packed = stage_pack(jnp.transpose(gen_points), jnp.transpose(reference_embeddings))
    raw = lax.all_gather(packed, ("zh", "zl"))

    info = jnp.stack(
        [
            a_is_gen.astype(jnp.int32),
            b_is_gen.astype(jnp.int32),
            c,
            x,
            y,
        ]
    ).astype(jnp.int32)
    a_wide, b_own = stage_unpack(info, raw)
    one = spread(a_wide, "y")
    two = spread(stage_widen(b_own, one), "x")
    a_own, b_all = lax.optimization_barrier((one.reshape(NJ, D), two.reshape(NJ, D)))
    a_other = lax.ppermute(a_own, "c", [(0, 1), (1, 0)])
    k1a, high, mass, b_norms, lift_i, lift_j, weights = stage_cost_own(
        info, gen_count, ref_count, a_own, b_all
    )
    k1b, k2, part = stage_cost_other(a_other, b_all, lift_i, high, mass, b_norms)
    k = (k1a, k1b, k2)
    part, g1 = stage_second(*k, spread(part, "x"), lift_j)
    part, f2 = stage_third(*k, spread(part, ("y", "c")), lift_i)
    part, g3 = stage_fourth(*k, spread(part, "x"), lift_j, g1)
    part = stage_fifth(*k, spread(part, ("y", "c")), lift_i, f2, g3)
    got = spread(part, ("x", "zl"))
    outs = (f32(1, BLOCK),) * 4 + (f32(8, 1, 128),)
    *pots, share = call(last_body, outs, [VMEM, VMEM])(got, weights)
    divergence = jnp.sum(spread(share, ("y", "c"))[:, 0, 0])
    return *(pot.reshape(BLOCK) for pot in pots), divergence


def solution(mesh):
    fine = Mesh(mesh.devices.reshape(4, 4, 2, 4, 4), ("y", "x", "c", "zh", "zl"))
    tile, feat = ("y", "x", "c"), ("zh", "zl")
    return jax.shard_map(
        local,
        mesh=fine,
        in_specs=(P(tile, feat), P(tile, feat), P(), P()),
        out_specs=(P(tile), P(tile), P(tile), P(tile), P()),
        check_vma=False,
    )
```
